32 devices in a mesh: dp: 8 (over z, x), tensor: 4 (over y, core).
Axes of the slice: x: 2, y: 2, z: 4, core: 2. Of those that a mesh axis runs over, the one named last changes fastest.
Arguments:
- inputs: bfloat16 [8, 1024, 2560], P('dp', 'tensor'), may hold values from -6 to 6
- cotangent: bfloat16 [8, 1024, 2560], P('dp', 'tensor'), may hold values from -6 to 6
- document_numbers: int32 [8, 1024], P('dp'), may hold values from 0 to 6, as said below
- sequence_adapter_index: int32 [8], P('dp'), may hold values from 0 to 7
- attention_norm_gain: float32 [2560], replicated, may hold values from 0.25 to 1.75
- query_latent_gain: float32 [768], replicated, may hold values from 0.25 to 1.75
- keyvalue_latent_gain: float32 [256], replicated, may hold values from 0.25 to 1.75
- feedforward_norm_gain: float32 [2560], replicated, may hold values from 0.25 to 1.75
- query_down_matrix: bfloat16 [2560, 768], P('dp'), may hold values from -0.125 to 0.125
- keyvalue_down_matrix: bfloat16 [2560, 288], P('dp'), may hold values from -0.125 to 0.125
- query_up_matrix: bfloat16 [768, 3840], P('dp', 'tensor'), may hold values from -0.21875 to 0.21875
- keyvalue_up_matrix: bfloat16 [256, 5120], P('dp', 'tensor'), may hold values from -0.375 to 0.375
- output_matrix: bfloat16 [2560, 2560], P('tensor', 'dp'), may hold values from -4 to 4
- gate_up_matrix: bfloat16 [2, 2560, 6400], P(None, 'dp', 'tensor'), may hold values from -0.125 to 0.125
- down_matrix: bfloat16 [6400, 2560], P('tensor', 'dp'), may hold values from -0.625 to 0.625
- query_down_adapter_in: bfloat16 [8, 2560, 16], replicated, may hold values from -0.125 to 0.125
- query_down_adapter_out: bfloat16 [8, 16, 768], replicated, may hold values from -0.375 to 0.375
- keyvalue_down_adapter_in: bfloat16 [8, 2560, 16], replicated, may hold values from -0.125 to 0.125
- keyvalue_down_adapter_out: bfloat16 [8, 16, 288], replicated, may hold values from -0.375 to 0.375
- query_up_adapter_in: bfloat16 [8, 768, 16], replicated, may hold values from -0.21875 to 0.21875
- query_up_adapter_out: bfloat16 [8, 16, 3840], P(None, None, 'tensor'), may hold values from -0.375 to 0.375
- keyvalue_up_adapter_in: bfloat16 [8, 256, 16], replicated, may hold values from -0.375 to 0.375
- keyvalue_up_adapter_out: bfloat16 [8, 16, 5120], P(None, None, 'tensor'), may hold values from -0.375 to 0.375
- output_adapter_in: bfloat16 [8, 2560, 16], P(None, 'tensor'), may hold values from -0.125 to 0.125
- output_adapter_out: bfloat16 [8, 16, 2560], replicated, may hold values from -6 to 6
- gate_up_adapter_in: bfloat16 [2, 8, 2560, 16], replicated, may hold values from -0.125 to 0.125
- gate_up_adapter_out: bfloat16 [2, 8, 16, 6400], P(None, None, None, 'tensor'), may hold values from -0.375 to 0.375
- down_adapter_in: bfloat16 [8, 6400, 16], P(None, 'tensor'), may hold values from -0.078125 to 0.078125
- down_adapter_out: bfloat16 [8, 16, 2560], replicated, may hold values from -1.5 to 1.5
Outputs:
- outputs: bfloat16 [8, 1024, 2560], P('dp', 'tensor')
- input_grad: float32 [8, 1024, 2560], P('dp', 'tensor')
- qa_lora_a_grad: float32 [8, 2560, 16], replicated
- qa_lora_b_grad: float32 [8, 16, 768], replicated
- kva_lora_a_grad: float32 [8, 2560, 16], replicated
- kva_lora_b_grad: float32 [8, 16, 288], replicated
- qb_lora_a_grad: float32 [8, 768, 16], replicated
- qb_lora_b_grad: float32 [8, 16, 3840], P(None, None, 'tensor')
- kvb_lora_a_grad: float32 [8, 256, 16], replicated
- kvb_lora_b_grad: float32 [8, 16, 5120], P(None, None, 'tensor')
- out_lora_a_grad: float32 [8, 2560, 16], P(None, 'tensor')
- out_lora_b_grad: float32 [8, 16, 2560], replicated
- gate_up_lora_a_grad: float32 [2, 8, 2560, 16], replicated
- gate_up_lora_b_grad: float32 [2, 8, 16, 6400], P(None, None, None, 'tensor')
- down_lora_a_grad: float32 [8, 6400, 16], P(None, 'tensor')
- down_lora_b_grad: float32 [8, 16, 2560], replicated
The draws below stay inside these ranges and needn't reach their ends.
Inputs may be any that keep to these rules, and one draw needn't show every extreme that they name: `document_numbers`: in each sequence documents are numbered 0, 1, 2 and so on in order, each 60 to 800 tokens long; some sequence holds a document of exactly 800 tokens.
All inputs are finite; a program needn't handle non-finite values.
Results may differ from the reference program's by a relative error of at most 0.025.
Values may be sent and summed in bfloat16 or wider, within the bound.
A program may use at most 256 MiB of HBM per device.

```python
import math
import jax
import jax.numpy as jnp
from jax import lax

MODEL_WIDTH = 2560
HEAD_TOTAL = 40
PLAIN_HEAD_DIM = 64
ROTARY_DIM = 32
VALUE_HEAD_DIM = 64
QUERY_LATENT = 768
KEYVALUE_LATENT = 256
FEEDFWD_HIDDEN = 6400
ADAPTER_RANK = 16
ADAPTER_GROUPS = 8
LEN = 1024
DOC_LEAST = 60
DOC_MOST = 800
DOC_PART = 150
SEQS = 8


def draw_document_numbers(key, part):
    key = jax.random.fold_in(key, 7)
    key_list = jax.random.split(key, 5)
    slot_count = LEN // DOC_PART + 1
    seq_index = jnp.arange(SEQS, dtype=jnp.int32)
    long_doc = jax.random.randint(key_list[0], (SEQS,), DOC_LEAST, DOC_MOST + 1)
    longest = jax.random.randint(key_list[1], (), 0, SEQS)
    shortest = (longest + 1 + jax.random.randint(key_list[2], (), 0, SEQS - 1)) % SEQS
    long_doc = jnp.where(seq_index == longest, DOC_MOST, long_doc)
    long_doc = jnp.where(seq_index == shortest, DOC_LEAST, long_doc)
    remainder = LEN - long_doc
    part_count = jnp.maximum(remainder // DOC_PART, 1)
    base_len = remainder // part_count
    extra_len = remainder % part_count
    slot_index = jnp.arange(slot_count, dtype=jnp.int32)
    lengths = jnp.where(slot_index[None, :] < part_count[:, None], base_len[:, None] + (slot_index[None, :] < extra_len[:, None]).astype(jnp.int32), 0)
    half_room = (base_len - DOC_LEAST) // 2
    shift_draw = jax.random.randint(key_list[3], (SEQS, slot_count), -half_room[:, None], half_room[:, None] + 1)
    paired = slot_index // 2 * 2
    shift_pairs = shift_draw[:, paired]
    pair_sign = 1 - 2 * (slot_index % 2)
    usable = paired[None, :] + 1 < part_count[:, None]
    lengths = lengths + jnp.where(usable, pair_sign[None, :] * shift_pairs, 0)
    insert_at = jax.random.randint(key_list[4], (SEQS,), 0, part_count + 1)
    padded = jnp.concatenate([lengths, jnp.zeros((SEQS, 1), jnp.int32)], axis=1)
    shifted = jnp.concatenate([jnp.zeros((SEQS, 1), jnp.int32), lengths], axis=1)
    slot_spots = jnp.arange(slot_count + 1, dtype=jnp.int32)[None, :]
    doc_lengths = jnp.where(slot_spots < insert_at[:, None], padded, jnp.where(slot_spots == insert_at[:, None], long_doc[:, None], shifted))
    doc_ends = jnp.cumsum(doc_lengths, axis=1)
    places = jnp.arange(LEN, dtype=jnp.int32)
    return jnp.sum((doc_ends[:, :, None] <= places[None, None, :]).astype(jnp.int32), axis=1).astype(jnp.int32)


def place_ends(array, key, low, largest):
    place = [jax.random.randint(jax.random.fold_in(key, axis), (), 0, length) for axis, length in enumerate(array.shape)]
    widest = array.shape.index(max(array.shape))
    beside = place[:widest] + [(place[widest] + 1) % array.shape[widest]] + place[widest + 1:]
    return array.at[tuple(place)].set(low).at[tuple(beside)].set(largest)


def level_of(own_key, extent, cuts, low, high):
    def one(axis_at, blocks):
        heights = jax.random.uniform(jax.random.fold_in(jax.random.fold_in(own_key, 6), axis_at), (blocks,), jnp.float32, low / len(cuts), high / len(cuts))
        return jnp.repeat(jnp.exp(heights), extent[axis_at] // blocks).reshape((-1,) + (1,) * (len(extent) - axis_at - 1))

    level = one(*cuts[0])
    for cut in cuts[1:]:
        level = level * one(*cut)
    return level


def centred(key, dims, deviation, bound, shards=(), held_as=jnp.bfloat16):
    array = deviation * jax.random.normal(key, dims, jnp.float32)
    if shards:
        array = array * level_of(key, dims, shards, -0.22, 0.18)
    return jnp.clip(array, -bound, bound).astype(held_as)


def setup_inputs(seed: int = 0) -> dict:
    splits = jax.random.split(jax.random.key(seed), 30)
    inputs = centred(splits[0], (SEQS, LEN, MODEL_WIDTH), 1.0, 6.0, ((0, 8), (1, 4)))
    cotangent = centred(splits[1], (SEQS, LEN, MODEL_WIDTH), 1.0, 6.0, ((0, 8), (1, 4)))
    document_numbers = draw_document_numbers(jax.random.fold_in(splits[29], 71), 0)
    sequence_adapter_index = place_ends(jax.random.randint(splits[3], (SEQS,), 0, ADAPTER_GROUPS), jax.random.fold_in(splits[3], 1), 0, ADAPTER_GROUPS - 1).astype(jnp.int32)
    attention_norm_gain = jnp.clip(1.0 + 0.15 * jax.random.normal(splits[4], (MODEL_WIDTH,), jnp.float32), 0.25, 1.75)
    query_latent_gain = jnp.clip(1.0 + 0.15 * jax.random.normal(splits[5], (QUERY_LATENT,), jnp.float32), 0.25, 1.75)
    keyvalue_latent_gain = jnp.clip(1.0 + 0.15 * jax.random.normal(splits[6], (KEYVALUE_LATENT,), jnp.float32), 0.25, 1.75)
    feedforward_norm_gain = jnp.clip(1.0 + 0.15 * jax.random.normal(splits[7], (MODEL_WIDTH,), jnp.float32), 0.25, 1.75)
    query_down_matrix = centred(splits[8], (MODEL_WIDTH, QUERY_LATENT), MODEL_WIDTH ** -0.5, 0.125, ((0, 8),))
    keyvalue_down_matrix = centred(splits[9], (MODEL_WIDTH, KEYVALUE_LATENT + ROTARY_DIM), MODEL_WIDTH ** -0.5, 0.125, ((0, 8),))
    query_up_matrix = centred(splits[10], (QUERY_LATENT, HEAD_TOTAL * (PLAIN_HEAD_DIM + ROTARY_DIM)), QUERY_LATENT ** -0.5, 0.21875, ((0, 8), (1, 4)))
    keyvalue_up_matrix = centred(splits[11], (KEYVALUE_LATENT, HEAD_TOTAL * (PLAIN_HEAD_DIM + VALUE_HEAD_DIM)), KEYVALUE_LATENT ** -0.5, 0.375, ((0, 8), (1, 4)))
    output_matrix = centred(splits[12], (HEAD_TOTAL * VALUE_HEAD_DIM, MODEL_WIDTH), (max(HEAD_TOTAL * VALUE_HEAD_DIM // 1024, 1)) ** -0.5, 4.0, ((0, 4), (1, 8)))
    gate_up_matrix = centred(splits[13], (2, MODEL_WIDTH, FEEDFWD_HIDDEN), MODEL_WIDTH ** -0.5, 0.125, ((1, 8), (2, 4)))
    down_matrix = centred(splits[14], (FEEDFWD_HIDDEN, MODEL_WIDTH), (max(FEEDFWD_HIDDEN // 64, 1)) ** -0.5, 0.625, ((0, 4), (1, 8)))
    query_down_adapter_in = centred(splits[15], (ADAPTER_GROUPS, MODEL_WIDTH, ADAPTER_RANK), MODEL_WIDTH ** -0.5, 0.125)
    query_down_adapter_out = centred(splits[16], (ADAPTER_GROUPS, ADAPTER_RANK, QUERY_LATENT), (16 * ADAPTER_RANK) ** -0.5, 0.375)
    keyvalue_down_adapter_in = centred(splits[17], (ADAPTER_GROUPS, MODEL_WIDTH, ADAPTER_RANK), MODEL_WIDTH ** -0.5, 0.125)
    keyvalue_down_adapter_out = centred(splits[18], (ADAPTER_GROUPS, ADAPTER_RANK, KEYVALUE_LATENT + ROTARY_DIM), (16 * ADAPTER_RANK) ** -0.5, 0.375)
    query_up_adapter_in = centred(splits[19], (ADAPTER_GROUPS, QUERY_LATENT, ADAPTER_RANK), QUERY_LATENT ** -0.5, 0.21875)
    query_up_adapter_out = centred(splits[20], (ADAPTER_GROUPS, ADAPTER_RANK, HEAD_TOTAL * (PLAIN_HEAD_DIM + ROTARY_DIM)), (16 * ADAPTER_RANK) ** -0.5, 0.375, ((2, 4),))
    keyvalue_up_adapter_in = centred(splits[21], (ADAPTER_GROUPS, KEYVALUE_LATENT, ADAPTER_RANK), KEYVALUE_LATENT ** -0.5, 0.375)
    keyvalue_up_adapter_out = centred(splits[22], (ADAPTER_GROUPS, ADAPTER_RANK, HEAD_TOTAL * (PLAIN_HEAD_DIM + VALUE_HEAD_DIM)), (16 * ADAPTER_RANK) ** -0.5, 0.375, ((2, 4),))
    output_adapter_in = centred(splits[23], (ADAPTER_GROUPS, HEAD_TOTAL * VALUE_HEAD_DIM, ADAPTER_RANK), (HEAD_TOTAL * VALUE_HEAD_DIM) ** -0.5, 0.125, ((1, 4),))
    output_adapter_out = centred(splits[24], (ADAPTER_GROUPS, ADAPTER_RANK, MODEL_WIDTH), 1 ** -0.5, 6.0)
    gate_up_adapter_in = centred(splits[25], (2, ADAPTER_GROUPS, MODEL_WIDTH, ADAPTER_RANK), MODEL_WIDTH ** -0.5, 0.125)
    gate_up_adapter_out = centred(splits[26], (2, ADAPTER_GROUPS, ADAPTER_RANK, FEEDFWD_HIDDEN), (16 * ADAPTER_RANK) ** -0.5, 0.375, ((3, 4),))
    down_adapter_in = centred(splits[27], (ADAPTER_GROUPS, FEEDFWD_HIDDEN, ADAPTER_RANK), FEEDFWD_HIDDEN ** -0.5, 0.078125, ((1, 4),))
    down_adapter_out = centred(splits[28], (ADAPTER_GROUPS, ADAPTER_RANK, MODEL_WIDTH), ADAPTER_RANK ** -0.5, 1.5)
    return {"inputs": inputs, "cotangent": cotangent, "document_numbers": document_numbers, "sequence_adapter_index": sequence_adapter_index, "attention_norm_gain": attention_norm_gain, "query_latent_gain": query_latent_gain, "keyvalue_latent_gain": keyvalue_latent_gain, "feedforward_norm_gain": feedforward_norm_gain, "query_down_matrix": query_down_matrix, "keyvalue_down_matrix": keyvalue_down_matrix, "query_up_matrix": query_up_matrix, "keyvalue_up_matrix": keyvalue_up_matrix, "output_matrix": output_matrix, "gate_up_matrix": gate_up_matrix, "down_matrix": down_matrix, "query_down_adapter_in": query_down_adapter_in, "query_down_adapter_out": query_down_adapter_out, "keyvalue_down_adapter_in": keyvalue_down_adapter_in, "keyvalue_down_adapter_out": keyvalue_down_adapter_out, "query_up_adapter_in": query_up_adapter_in, "query_up_adapter_out": query_up_adapter_out, "keyvalue_up_adapter_in": keyvalue_up_adapter_in, "keyvalue_up_adapter_out": keyvalue_up_adapter_out, "output_adapter_in": output_adapter_in, "output_adapter_out": output_adapter_out, "gate_up_adapter_in": gate_up_adapter_in, "gate_up_adapter_out": gate_up_adapter_out, "down_adapter_in": down_adapter_in, "down_adapter_out": down_adapter_out}


@jax.custom_vjp
def low(v):
    return lax.optimization_barrier(v.astype(jnp.bfloat16)).astype(jnp.float32)

@jax.custom_vjp
def low_back(v):
    return v

def low_keep(v):
    return (low(v), None)

def low_pass(kept, grad):
    return (grad,)

def back_keep(v):
    return (v, None)

def back_low(kept, grad):
    return (low(grad),)
low.defvjp(low_keep, low_pass)
low_back.defvjp(back_keep, back_low)
NORM_EPS = 1e-05
RESIDUAL = 1.4 / math.sqrt(62.0)
ADAPT_SCALE = 2.0
HIGHEST_PREC = lax.Precision.HIGHEST

def rms_norm(value, gain_vec):
    return value * lax.rsqrt(lax.optimization_barrier(jnp.mean(value * value, axis=-1, keepdims=True)) + NORM_EPS) * gain_vec

def rotate(value, cos_part, sin_part):
    half_dim = value.shape[-1] // 2
    first_half = value[..., :half_dim]
    second = value[..., half_dim:]
    return jnp.concatenate([first_half * cos_part - second * sin_part, second * cos_part + first_half * sin_part], axis=-1)

def rope_tables(segments):
    places = jnp.arange(segments.shape[-1], dtype=jnp.int32)
    begins = jnp.concatenate([jnp.ones_like(segments[:, :1]), (segments[:, 1:] != segments[:, :-1]).astype(jnp.int32)], axis=1)
    first_place = lax.cummax(places[None, :] * begins, axis=1)
    offsets = (places[None, :] - first_place).astype(jnp.float32)
    inv_freq = 10000.0 ** (-2.0 * jnp.arange(ROTARY_DIM // 2, dtype=jnp.float32) / ROTARY_DIM)
    angles = offsets[..., None] * inv_freq
    return (jnp.cos(angles), jnp.sin(angles))

def attend(q_rot, k_rot, values, segments):
    groups = q_rot.shape[0]
    block_rows = min(512, LEN)
    places = jnp.arange(LEN, dtype=jnp.int32)
    score_scale = 1.0 / math.sqrt(PLAIN_HEAD_DIM + ROTARY_DIM)

    def one_block(block_index):
        row_start = block_index * block_rows
        q_part = lax.dynamic_slice_in_dim(q_rot, row_start, block_rows, 1)
        seg_part = lax.dynamic_slice_in_dim(segments, row_start, block_rows, 1)
        row_ids = row_start + jnp.arange(block_rows, dtype=jnp.int32)
        scores = low_back(jnp.einsum('gqhd,gkhd->ghqk', q_part, k_rot, precision=HIGHEST_PREC) * score_scale)
        causal = row_ids[:, None] >= places[None, :]
        allowed = (seg_part[:, None, :, None] == segments[:, None, None, :]) & causal[None, None]
        scores = jnp.where(allowed, scores, -1e+30)
        attn_probs = low(jax.nn.softmax(scores, axis=-1))
        return jnp.einsum('ghqk,gkhd->gqhd', attn_probs, values, precision=HIGHEST_PREC)
    blocks = lax.map(jax.checkpoint(one_block), jnp.arange(LEN // block_rows, dtype=jnp.int32))
    return jnp.moveaxis(blocks, 0, 1).reshape(groups, LEN, HEAD_TOTAL * VALUE_HEAD_DIM)

def layer_forward(inputs, adapter_bundle, frozen, segments, set_rows):
    qa_a, qa_b, kva_a, kva_b, qb_a, qb_b, kvb_a, kvb_b, out_a, out_b, gu_a, gu_b, down_a, down_b = adapter_bundle
    attention_norm_gain, query_latent_gain, keyvalue_latent_gain, feedforward_norm_gain, query_down_matrix, keyvalue_down_matrix, query_up_matrix, keyvalue_up_matrix, output_matrix, gate_up_matrix, down_matrix = frozen
    groups = inputs.shape[0]

    def project(rows_in, weight, table_a, table_b):
        chosen_a = jnp.take(table_a, set_rows, axis=0)
        chosen_b = jnp.take(table_b, set_rows, axis=0)
        reduced = low_back(low(jnp.einsum('gti,gir->gtr', rows_in, chosen_a, precision=HIGHEST_PREC)))
        base_out = jnp.einsum('gti,io->gto', rows_in, weight, precision=HIGHEST_PREC)
        return low_back(base_out + ADAPT_SCALE * jnp.einsum('gtr,gro->gto', reduced, chosen_b, precision=HIGHEST_PREC))
    cos_part, sin_part = rope_tables(segments)
    normed = low(rms_norm(inputs, attention_norm_gain))
    q_latent = project(normed, query_down_matrix, qa_a, qa_b)
    kv_latent = project(normed, keyvalue_down_matrix, kva_a, kva_b)
    q_input = low(rms_norm(q_latent, query_latent_gain))
    kv_input = low(rms_norm(kv_latent[..., :KEYVALUE_LATENT], keyvalue_latent_gain))
    pe_raw = low(kv_latent[..., KEYVALUE_LATENT:])
    queries = project(q_input, query_up_matrix, qb_a, qb_b).reshape(groups, LEN, HEAD_TOTAL, PLAIN_HEAD_DIM + ROTARY_DIM)
    keyvals = project(kv_input, keyvalue_up_matrix, kvb_a, kvb_b).reshape(groups, LEN, HEAD_TOTAL, PLAIN_HEAD_DIM + VALUE_HEAD_DIM)
    q_rot = low(jnp.concatenate([queries[..., :PLAIN_HEAD_DIM], rotate(queries[..., PLAIN_HEAD_DIM:], cos_part[:, :, None], sin_part[:, :, None])], axis=-1))
    pe_rot = rotate(pe_raw, cos_part, sin_part)
    k_rot = low(jnp.concatenate([keyvals[..., :PLAIN_HEAD_DIM], jnp.broadcast_to(pe_rot[:, :, None, :], (groups, LEN, HEAD_TOTAL, ROTARY_DIM))], axis=-1))
    values = low(keyvals[..., PLAIN_HEAD_DIM:])
    head_out = low_back(low(attend(q_rot, k_rot, values, segments)))
    middle = inputs + RESIDUAL * project(head_out, output_matrix, out_a, out_b)
    ffn_in = low(rms_norm(middle, feedforward_norm_gain))
    gate_act = project(ffn_in, gate_up_matrix[0], gu_a[0], gu_b[0])
    up_act = project(ffn_in, gate_up_matrix[1], gu_a[1], gu_b[1])
    hidden = low(jax.nn.silu(gate_act) * up_act)
    return middle + RESIDUAL * project(hidden, down_matrix, down_a, down_b)

def widen_to_tokens(value):
    return value.astype(jnp.float32)

def reference(inputs, cotangent, document_numbers, sequence_adapter_index, attention_norm_gain, query_latent_gain, keyvalue_latent_gain, feedforward_norm_gain, query_down_matrix, keyvalue_down_matrix, query_up_matrix, keyvalue_up_matrix, output_matrix, gate_up_matrix, down_matrix, query_down_adapter_in, query_down_adapter_out, keyvalue_down_adapter_in, keyvalue_down_adapter_out, query_up_adapter_in, query_up_adapter_out, keyvalue_up_adapter_in, keyvalue_up_adapter_out, output_adapter_in, output_adapter_out, gate_up_adapter_in, gate_up_adapter_out, down_adapter_in, down_adapter_out):
    frozen = (widen_to_tokens(attention_norm_gain), widen_to_tokens(query_latent_gain), widen_to_tokens(keyvalue_latent_gain), widen_to_tokens(feedforward_norm_gain), widen_to_tokens(query_down_matrix), widen_to_tokens(keyvalue_down_matrix), widen_to_tokens(query_up_matrix), widen_to_tokens(keyvalue_up_matrix), widen_to_tokens(output_matrix), widen_to_tokens(gate_up_matrix), widen_to_tokens(down_matrix))
    adapter_bundle = (widen_to_tokens(query_down_adapter_in), widen_to_tokens(query_down_adapter_out), widen_to_tokens(keyvalue_down_adapter_in), widen_to_tokens(keyvalue_down_adapter_out), widen_to_tokens(query_up_adapter_in), widen_to_tokens(query_up_adapter_out), widen_to_tokens(keyvalue_up_adapter_in), widen_to_tokens(keyvalue_up_adapter_out), widen_to_tokens(output_adapter_in), widen_to_tokens(output_adapter_out), widen_to_tokens(gate_up_adapter_in), widen_to_tokens(gate_up_adapter_out), widen_to_tokens(down_adapter_in), widen_to_tokens(down_adapter_out))
    group_size = math.gcd(SEQS, 4)
    rounds = SEQS // group_size

    def regroup(value):
        return value.reshape((rounds, group_size) + value.shape[1:])

    def one_group(totals, pieces):
        row_block, grad_block, segments, set_rows = pieces
        result, pullback = jax.vjp(lambda rows_in, adapt_in: layer_forward(rows_in, adapt_in, frozen, segments, set_rows), row_block, adapter_bundle)
        rows_grad, adapt_grad = pullback(grad_block)
        totals = jax.tree.map(lambda left_op, right_op: left_op + right_op, totals, adapt_grad)
        return (totals, (result.astype(jnp.bfloat16), rows_grad))
    zero_grads = jax.tree.map(jnp.zeros_like, adapter_bundle)
    totals, (outputs, input_grad) = lax.scan(one_group, zero_grads, (regroup(widen_to_tokens(inputs)), regroup(widen_to_tokens(cotangent)), regroup(document_numbers), regroup(sequence_adapter_index)))
    outputs = outputs.reshape(SEQS, LEN, MODEL_WIDTH)
    input_grad = input_grad.reshape(SEQS, LEN, MODEL_WIDTH)
    return (outputs, input_grad, totals[0], totals[1], totals[2], totals[3], totals[4], totals[5], totals[6], totals[7], totals[8], totals[9], totals[10], totals[11], totals[12], totals[13])
```

```python
import functools
import math

import jax
import jax.numpy as jnp
from jax import lax
from jax.experimental import pallas as pl
from jax.experimental.pallas import tpu as pltpu
from jax.sharding import PartitionSpec as P

PLAIN_HEAD_DIM = 64
ROTARY_DIM = 32
VALUE_HEAD_DIM = 64
HEAD_LANES = 128
CODE_LANES = 128
RANK = 16
BLOCK_Q = 256
DOC_LANE = 99
DOC_SLOTS = 24

NORM_EPS = 1e-05
RESIDUAL = 1.4 / math.sqrt(62.0)
ADAPT_SCALE = 2.0
SCORE_SCALE = 1.0 / math.sqrt(PLAIN_HEAD_DIM + ROTARY_DIM)
EXP2_SCALE = SCORE_SCALE * math.log2(math.e)
BIG = 1e30
VMEM_LIMIT = 56 * 1024 * 1024
F32 = jnp.float32
BF16 = jnp.bfloat16


def narrow(value):
    return value.astype(BF16)


def dot_nn(a, b):
    return lax.dot_general(a, b, (((1,), (0,)), ((), ())), preferred_element_type=F32)


def dot_nt(a, b):
    return lax.dot_general(a, b, (((1,), (1,)), ((), ())), preferred_element_type=F32)


def dot_tn(a, b):
    return lax.dot_general(a, b, (((0,), (0,)), ((), ())), preferred_element_type=F32)


def normalize(value, gain_vec):
    scale_inv = lax.rsqrt(jnp.mean(value * value, axis=-1, keepdims=True) + NORM_EPS)
    return (value * scale_inv * gain_vec, scale_inv)


def normalize_back(value, scale_inv, gain_vec, grad_in):
    weighted = grad_in * gain_vec
    return scale_inv * weighted - value * scale_inv**3 * jnp.mean(
        value * weighted, axis=-1, keepdims=True
    )


def rope_tables(segments):
    places = jnp.arange(segments.shape[-1], dtype=jnp.int32)
    begins = jnp.concatenate(
        [jnp.ones_like(segments[:, :1]), (segments[:, 1:] != segments[:, :-1]).astype(jnp.int32)],
        axis=1,
    )
    first_place = lax.cummax(places[None, :] * begins, axis=1)
    offsets = (places[None, :] - first_place).astype(F32)
    inv_freq = 10000.0 ** (-2.0 * jnp.arange(ROTARY_DIM // 2, dtype=F32) / ROTARY_DIM)
    angles = offsets[..., None] * inv_freq
    return (jnp.cos(angles)[0], jnp.sin(angles)[0])


def swap(value, axis, bit, size):
    return lax.ppermute(value, axis, [(i, i ^ bit) for i in range(size)])


def place_pieces(sources, copies, outs, name):
    def kernel(*refs):
        src_refs = refs[: len(sources)]
        out_refs = refs[len(sources) : len(sources) + len(outs)]
        sems = refs[-1]
        d = lax.axis_index("dp")
        t = lax.axis_index("tensor")
        started = []
        for n, (src, src_at, out, out_at) in enumerate(copies):
            src_ref = src_refs[src] if src_at is None else src_refs[src].at[src_at]
            copy = pltpu.make_async_copy(src_ref, out_refs[out].at[out_at(d, t)], sems.at[n])
            copy.start()
            started.append(copy)
        for copy in started:
            copy.wait()

    any_spec = pl.BlockSpec(memory_space=pl.ANY)
    moved = sum(s.size * s.dtype.itemsize for s in sources)
    return pl.pallas_call(
        kernel,
        out_shape=[jax.ShapeDtypeStruct(o, BF16) for o in outs],
        in_specs=[any_spec] * len(sources),
        out_specs=[pl.BlockSpec(memory_space=pltpu.VMEM)] * len(outs),
        scratch_shapes=[pltpu.SemaphoreType.DMA((len(copies),))],
        compiler_params=pltpu.CompilerParams(vmem_limit_bytes=VMEM_LIMIT),
        cost_estimate=pl.CostEstimate(flops=0, bytes_accessed=2 * moved, transcendentals=0),
        name=name,
    )(*sources)


def split_three(value):
    high = narrow(value).astype(F32)
    middle = narrow(value - high).astype(F32)
    return high, middle, value - high - middle


def rope_mix(value, cos_l, sin_a, sin_b):
    return (
        value * cos_l
        + pltpu.roll(value, HEAD_LANES - ROTARY_DIM // 2, 1) * sin_a
        + pltpu.roll(value, ROTARY_DIM // 2, 1) * sin_b
    )


def attn_fwd_kernel(
    per_step, q_width, kv_at, xl_ref, wq_ref, wkv_ref, rope_ref, pe_ref, doc_ref, qa_ref, kv_ref, o_ref
):
    length = xl_ref.shape[0]
    lane = lax.broadcasted_iota(jnp.int32, (length, HEAD_LANES), 1)
    q_all = dot_nn(xl_ref[:, :q_width], wq_ref[...])
    kv_all = dot_nn(xl_ref[:, kv_at:], wkv_ref[...])
    kv_ref[...] = narrow(kv_all)
    doc_q = doc_ref[...].astype(F32)
    q_heads, k_heads, kv_turned = [], [], []
    for i in range(per_step):
        span = slice(i * HEAD_LANES, (i + 1) * HEAD_LANES)
        q_one = rope_mix(q_all[:, span], rope_ref[0], rope_ref[1], rope_ref[2]) + doc_q
        q_heads.append(narrow(q_one))
        kv_one = kv_all[:, span]
        k_heads.append(jnp.where(lane < PLAIN_HEAD_DIM, narrow(kv_one), pe_ref[...]))
        kv_turned.append(narrow(kv_one.T))
    key_at = lax.broadcasted_iota(jnp.int32, (BLOCK_Q, BLOCK_Q), 0)
    query_at = lax.broadcasted_iota(jnp.int32, (BLOCK_Q, BLOCK_Q), 1)
    row = lax.broadcasted_iota(jnp.int32, (HEAD_LANES, BLOCK_Q), 0)
    block_lane = lax.broadcasted_iota(jnp.int32, (BLOCK_Q, HEAD_LANES), 1)
    for j in range(length // BLOCK_Q):
        begin, end = j * BLOCK_Q, (j + 1) * BLOCK_Q
        mixed = []
        for i in range(per_step):
            q_part = q_heads[i][begin:end]
            scores = dot_nt(k_heads[i][:end], q_part)
            diag = jnp.where(key_at <= query_at, scores[begin:], -BIG)
            scores = diag if j == 0 else jnp.concatenate([scores[:begin], diag], axis=0)
            top = jnp.max(scores, axis=0, keepdims=True)
            terms = jnp.exp2((scores - top) * EXP2_SCALE)
            total = jnp.sum(terms, axis=0, keepdims=True)
            out_t = dot_nn(kv_turned[i][:, :end], narrow(terms)) * (1.0 / total)
            high, middle, low = split_three(top + jnp.log2(total) * (1.0 / EXP2_SCALE))
            out_t = jnp.where(
                row == 0, -high, jnp.where(row == 1, -middle, jnp.where(row == 2, -low, out_t))
            )
            out_n = out_t.T
            mixed.append(out_n)
            is_lse = (block_lane >= 96) & (block_lane < 99)
            q_saved = jnp.where(is_lse, narrow(pltpu.roll(out_n, 96, 1)), q_part)
            qa_ref[begin:end, i * HEAD_LANES : (i + 1) * HEAD_LANES] = q_saved
        if per_step == 2:
            both = jnp.where(block_lane < 64, pltpu.roll(mixed[0], 64, 1), mixed[1])
            o_ref[begin:end, :] = narrow(both)
        else:
            even = lax.rem(pl.program_id(0), 2) == 0
            moved = jnp.where(even, pltpu.roll(mixed[0], 64, 1), mixed[0])
            mine = (block_lane < 64) == even
            o_ref[begin:end, :] = jnp.where(mine, narrow(moved), o_ref[begin:end, :])


def attn_bwd_kernel(
    per_step, qa_ref, kv_ref, o_ref, do_ref, rope_ref, pe_ref, dq_ref, dkv_ref, dpe_ref, dk_acc, dv_acc
):
    length = qa_ref.shape[0]
    step = pl.program_id(0)
    lane = lax.broadcasted_iota(jnp.int32, (length, HEAD_LANES), 1)
    upper = lane >= 64
    key_at = lax.broadcasted_iota(jnp.int32, (BLOCK_Q, BLOCK_Q), 0)
    query_at = lax.broadcasted_iota(jnp.int32, (BLOCK_Q, BLOCK_Q), 1)
    causal = key_at <= query_at
    out_both = o_ref[...].astype(F32)
    grad_both = do_ref[...].astype(F32)

    @pl.when(step == 0)
    def _():
        dpe_ref[...] = jnp.zeros_like(dpe_ref)

    for i in range(per_step):
        span = slice(i * HEAD_LANES, (i + 1) * HEAD_LANES)
        if per_step == 2:
            turn = i == 0
            grad_one = pltpu.roll(grad_both, 64, 1) if turn else grad_both
            out_one = pltpu.roll(out_both, 64, 1) if turn else out_both
        else:
            even = lax.rem(step, 2) == 0
            grad_one = jnp.where(even, pltpu.roll(grad_both, 64, 1), grad_both)
            out_one = jnp.where(even, pltpu.roll(out_both, 64, 1), out_both)
        grad_one = jnp.where(upper, grad_one, 0.0)
        inner = jnp.sum(jnp.where(upper, grad_one * out_one, 0.0), axis=-1, keepdims=True)
        high, middle, low = split_three(inner)
        grad_aug = jnp.where(
            lane == 0, -high, jnp.where(lane == 1, -middle, jnp.where(lane == 2, -low, grad_one))
        )
        grad_aug = narrow(grad_aug)
        kv_one = kv_ref[:, span]
        ones = jnp.where(lane < 3, 1.0, 0.0).astype(BF16)
        v_aug = jnp.where(upper, kv_one, ones)
        k_aug = jnp.where(lane < 64, kv_one, pe_ref[...])
        k_turned = narrow(k_aug.astype(F32).T)
        for j in reversed(range(length // BLOCK_Q)):
            begin, end = j * BLOCK_Q, (j + 1) * BLOCK_Q
            q_part = qa_ref[begin:end, span]
            probs = jnp.exp2(dot_nt(k_aug[:end], q_part) * EXP2_SCALE)
            diag = jnp.where(causal, probs[begin:], 0.0)
            probs = diag if j == 0 else jnp.concatenate([probs[:begin], diag], axis=0)
            grads = narrow(probs * dot_nt(v_aug[:end], grad_aug[begin:end]))
            dq_part = dot_nn(k_turned[:, :end], grads).T * SCORE_SCALE
            dq_part = rope_mix(
                dq_part,
                rope_ref[0, begin:end, :],
                -rope_ref[1, begin:end, :],
                -rope_ref[2, begin:end, :],
            )
            dq_ref[begin:end, span] = narrow(dq_part)
            dk_part = dot_nn(grads, q_part)
            dv_part = dot_nn(narrow(probs), grad_aug[begin:end])
            if end == length:
                dk_acc[...] = dk_part
                dv_acc[...] = dv_part
            else:
                dk_acc[:end] += dk_part
                dv_acc[:end] += dv_part
        dk_all = dk_acc[...] * SCORE_SCALE
        dkv_ref[:, span] = narrow(jnp.where(upper, dv_acc[...], dk_all))
        dpe_ref[...] += jnp.where(upper & (lane < 96), dk_all, 0.0)


def attend(latents, w_q, w_kv, rope, pe_aug, doc_q, q_width, kv_at):
    length = latents.shape[0]
    heads = w_q.shape[1] // HEAD_LANES
    per_step = 2 if heads % 2 == 0 else 1
    wide = per_step * HEAD_LANES
    whole = lambda a: pl.BlockSpec(a.shape, lambda h: (0,) * a.ndim)
    flops = heads * length * (2 * q_width * 256 + length * 2 * 256)
    return pl.pallas_call(
        functools.partial(attn_fwd_kernel, per_step, q_width, kv_at),
        grid=(heads // per_step,),
        in_specs=[
            whole(latents),
            pl.BlockSpec((w_q.shape[0], wide), lambda h: (0, h)),
            pl.BlockSpec((w_kv.shape[0], wide), lambda h: (0, h)),
            whole(rope),
            whole(pe_aug),
            whole(doc_q),
        ],
        out_specs=[
            pl.BlockSpec((length, wide), lambda h: (0, h)),
            pl.BlockSpec((length, wide), lambda h: (0, h)),
            pl.BlockSpec((length, HEAD_LANES), lambda h: (0, h * per_step // 2)),
        ],
        out_shape=[
            jax.ShapeDtypeStruct((length, heads * HEAD_LANES), BF16),
            jax.ShapeDtypeStruct((length, heads * HEAD_LANES), BF16),
            jax.ShapeDtypeStruct((length, heads * VALUE_HEAD_DIM), BF16),
        ],
        compiler_params=pltpu.CompilerParams(vmem_limit_bytes=VMEM_LIMIT),
        cost_estimate=pl.CostEstimate(
            flops=2 * flops, bytes_accessed=16 * 1024 * 1024, transcendentals=heads * length * length // 2
        ),
        name="attend",
    )(latents, w_q, w_kv, rope, pe_aug, doc_q)


def attend_back(q_aug, kv, heads_out, heads_grad, rope, pe_aug):
    length = q_aug.shape[0]
    heads = q_aug.shape[1] // HEAD_LANES
    per_step = 2 if heads % 2 == 0 else 1
    wide = per_step * HEAD_LANES
    whole = lambda a: pl.BlockSpec(a.shape, lambda h: (0,) * a.ndim)
    columns = pl.BlockSpec((length, wide), lambda h: (0, h))
    packed = pl.BlockSpec((length, HEAD_LANES), lambda h: (0, h * per_step // 2))
    return pl.pallas_call(
        functools.partial(attn_bwd_kernel, per_step),
        grid=(heads // per_step,),
        in_specs=[columns, columns, packed, packed, whole(rope), whole(pe_aug)],
        out_specs=[columns, columns, pl.BlockSpec((length, HEAD_LANES), lambda h: (0, 0))],
        out_shape=[
            jax.ShapeDtypeStruct((length, heads * HEAD_LANES), BF16),
            jax.ShapeDtypeStruct((length, heads * HEAD_LANES), BF16),
            jax.ShapeDtypeStruct((length, HEAD_LANES), F32),
        ],
        scratch_shapes=[
            pltpu.VMEM((length, HEAD_LANES), F32),
            pltpu.VMEM((length, HEAD_LANES), F32),
        ],
        compiler_params=pltpu.CompilerParams(vmem_limit_bytes=VMEM_LIMIT),
        cost_estimate=pl.CostEstimate(
            flops=heads * length * length * 256 * 10,
            bytes_accessed=16 * 1024 * 1024,
            transcendentals=heads * length * length // 2,
        ),
        name="attend_back",
    )(q_aug, kv, heads_out, heads_grad, rope, pe_aug)


def ffn_kernel(main, tail, tail_wide, x_ref, g_ref, w_ref, grad_ref, hid_ref):
    gu_wide = 2 * main + tail_wide
    pre = dot_nn(x_ref[...], w_ref[:, :gu_wide])
    back = dot_nn(g_ref[...], w_ref[:, gu_wide:])

    def middle(gate, up, hid_grad):
        sig = 1.0 / (1.0 + jnp.exp(-gate))
        silu = gate * sig
        gate_grad = hid_grad * up * (sig * (1.0 + gate * (1.0 - sig)))
        return silu * up, gate_grad, hid_grad * silu

    hid, gate_grad, up_grad = middle(pre[:, :main], pre[:, main + tail_wide :], back)
    hid_ref[:, :main] = narrow(hid)
    grad_ref[:, :main] = narrow(gate_grad)
    grad_ref[:, main + tail_wide :] = narrow(up_grad)
    if tail_wide:
        pre_tail = pre[:, main : main + tail_wide]
        back_tail = dot_nn(g_ref[...], w_ref[:, main : main + tail_wide])
        up_tail = pltpu.roll(pre_tail, tail_wide - tail, 1)
        hid_tail = pltpu.roll(back_tail, tail_wide - 2 * tail, 1)
        hid, gate_grad, up_grad = middle(pre_tail, up_tail, hid_tail)
        lane = lax.broadcasted_iota(jnp.int32, pre_tail.shape, 1)
        hid = pltpu.roll(hid, 2 * tail, 1)
        hid = jnp.where((lane >= 2 * tail) & (lane < 3 * tail), hid, 0.0)
        hid_ref[:, main:] = narrow(hid)
        up_grad = pltpu.roll(up_grad, tail, 1)
        both = jnp.where(lane < tail, gate_grad, jnp.where(lane < 2 * tail, up_grad, 0.0))
        grad_ref[:, main : main + tail_wide] = narrow(both)


def ffn_middle(x_rows, g_rows, weight, main, tail, tail_wide):
    rows, depth = x_rows.shape
    block = 256
    width = weight.shape[1]
    return pl.pallas_call(
        functools.partial(ffn_kernel, main, tail, tail_wide),
        grid=(rows // block,),
        in_specs=[
            pl.BlockSpec((block, depth), lambda i: (i, 0)),
            pl.BlockSpec((block, depth), lambda i: (i, 0)),
            pl.BlockSpec((depth, width), lambda i: (0, 0)),
        ],
        out_specs=[
            pl.BlockSpec((block, 2 * main + tail_wide), lambda i: (i, 0)),
            pl.BlockSpec((block, main + tail_wide), lambda i: (i, 0)),
        ],
        out_shape=[
            jax.ShapeDtypeStruct((rows, 2 * main + tail_wide), BF16),
            jax.ShapeDtypeStruct((rows, main + tail_wide), BF16),
        ],
        compiler_params=pltpu.CompilerParams(vmem_limit_bytes=VMEM_LIMIT),
        cost_estimate=pl.CostEstimate(
            flops=2 * rows * depth * (width + tail_wide),
            bytes_accessed=2 * (2 * rows * depth + depth * width + rows * width),
            transcendentals=rows * main,
        ),
        name="ffn_middle",
    )(x_rows, g_rows, weight)


def per_device(
    n_dp,
    n_t,
    inputs,
    cotangent,
    document_numbers,
    sequence_adapter_index,
    attention_norm_gain,
    query_latent_gain,
    keyvalue_latent_gain,
    feedforward_norm_gain,
    query_down_matrix,
    keyvalue_down_matrix,
    query_up_matrix,
    keyvalue_up_matrix,
    output_matrix,
    gate_up_matrix,
    down_matrix,
    query_down_adapter_in,
    query_down_adapter_out,
    keyvalue_down_adapter_in,
    keyvalue_down_adapter_out,
    query_up_adapter_in,
    query_up_adapter_out,
    keyvalue_up_adapter_in,
    keyvalue_up_adapter_out,
    output_adapter_in,
    output_adapter_out,
    gate_up_adapter_in,
    gate_up_adapter_out,
    down_adapter_in,
    down_adapter_out,
):
    d = lax.axis_index("dp")
    t = lax.axis_index("tensor")
    pair = n_dp // 4
    low_bits = [b for b in (1, 2, 4, 8, 16) if b < pair]
    high = n_dp // 2
    y_bits = [b for b in (2, 4, 8, 16) if b < n_t]
    zl = lax.rem(d // pair, 2)
    core = lax.rem(t, 2)
    first = zl == 0
    size = {"dp": n_dp, "tensor": n_t}
    rows = inputs.shape[1]
    width = inputs.shape[2]
    length = document_numbers.shape[1]
    q_lat = query_down_matrix.shape[1]
    kv_all = keyvalue_down_matrix.shape[1]
    kv_lat = kv_all - ROTARY_DIM
    heads = keyvalue_up_matrix.shape[1] // HEAD_LANES
    group_count = query_down_adapter_in.shape[0]
    aug = width + CODE_LANES
    half_rows = rows // 2

    def hop(value, step):
        return swap(value, step[0], step[1], size[step[0]])

    def spread(piece, steps):
        held = {(0, 0): piece}
        for step in steps:
            for key in list(held):
                new = (key[0] ^ step[1], key[1]) if step[0] == "dp" else (key[0], key[1] ^ step[1])
                held[new] = hop(held[key], step)
        return held

    def collect(parts, steps):
        held = dict(parts)
        for step in steps:
            for key in list(held):
                has = (key[0] if step[0] == "dp" else key[1]) & step[1]
                if not has:
                    new = (
                        (key[0] ^ step[1], key[1])
                        if step[0] == "dp"
                        else (key[0], key[1] ^ step[1])
                    )
                    came = hop(narrow(held.pop(new)), step)
                    held[key] = held[key].astype(F32) + came.astype(F32)
        return held[(0, 0)]

    outer_first = [("dp", high), ("dp", pair)] + [("dp", b) for b in reversed(low_bits)]
    inner_first = [("dp", b) for b in low_bits] + [("dp", high), ("dp", pair)]
    t_slow = [("tensor", b) for b in reversed(y_bits)]
    t_core = [("tensor", 1)]

    set_all = lax.all_gather(sequence_adapter_index, "dp", axis=0, tiled=True)
    set_own = sequence_adapter_index[0]
    set_peer = lax.dynamic_index_in_dim(set_all, jnp.bitwise_xor(d, pair), 0, keepdims=False)
    set_even = jnp.where(first, set_own, set_peer)
    set_odd = jnp.where(first, set_peer, set_own)

    def pick(table, index):
        return lax.dynamic_index_in_dim(table, index, 0, keepdims=False)

    def turned(table):
        return jnp.swapaxes(table, -1, -2)

    qa_in, kva_in = pick(turned(query_down_adapter_in), set_own), pick(
        turned(keyvalue_down_adapter_in), set_own
    )
    qa_out, kva_out = pick(query_down_adapter_out, set_own), pick(keyvalue_down_adapter_out, set_own)
    qb_in, kvb_in = pick(turned(query_up_adapter_in), set_own), pick(
        turned(keyvalue_up_adapter_in), set_own
    )
    qb_out, kvb_out = pick(query_up_adapter_out, set_own), pick(keyvalue_up_adapter_out, set_own)
    out_in, out_out = pick(turned(output_adapter_in), set_own), pick(output_adapter_out, set_own)
    gu_in = jnp.concatenate(
        [pick(turned(gate_up_adapter_in[0]), set_own), pick(turned(gate_up_adapter_in[1]), set_own)],
        axis=0,
    )
    down_out = pick(down_adapter_out, set_own)

    down_shard = query_down_matrix.shape[0]
    core_rows = down_shard // 2
    lat_pad = -(-(q_lat + kv_all) // 128) * 128
    down_both = jnp.concatenate([query_down_matrix, keyvalue_down_matrix], axis=1)
    down_mine = lax.dynamic_index_in_dim(
        down_both.reshape(2, core_rows, q_lat + kv_all), core, 0, keepdims=False
    )
    cut = -(-core_rows // 32) * 16
    down_a = spread(down_mine[:cut], outer_first)
    down_b = spread(down_mine[cut:], inner_first)
    sources, copies = [], []
    for held, at, count in ((down_a, 0, cut), (down_b, cut, core_rows - cut)):
        for (r, _), piece in held.items():
            copies.append(
                (
                    len(sources),
                    None,
                    0,
                    lambda dd, tt, r=r, at=at, count=count: (
                        jnp.bitwise_xor(dd, r),
                        pl.ds(at, count),
                    ),
                )
            )
            sources.append(piece)
    (down_core,) = place_pieces(
        sources, copies, [(n_dp, core_rows, q_lat + kv_all)], "place_down_core"
    )
    down_other = hop(down_core, t_core[0])
    (down_full,) = place_pieces(
        [down_core, down_other],
        [
            (0, None, 0, lambda dd, tt: (slice(None), lax.rem(tt, 2))),
            (1, None, 0, lambda dd, tt: (slice(None), 1 - lax.rem(tt, 2))),
        ],
        [(n_dp, 2, core_rows, q_lat + kv_all)],
        "place_down",
    )
    w_down = down_full.reshape(width, q_lat + kv_all)

    qb_rows, kvb_rows = query_up_matrix.shape[0], keyvalue_up_matrix.shape[0]
    head_q = PLAIN_HEAD_DIM + ROTARY_DIM

    def pad_heads(value):
        split = value.reshape(value.shape[0], heads, head_q)
        return jnp.pad(split, ((0, 0), (0, 0), (0, HEAD_LANES - head_q))).reshape(
            value.shape[0], heads * HEAD_LANES
        )

    up_piece = jnp.concatenate([pad_heads(query_up_matrix), keyvalue_up_matrix], axis=0)
    up_held = spread(up_piece, outer_first)
    q_aug_rows = jnp.concatenate(
        [
            narrow(ADAPT_SCALE * pad_heads(qb_out)),
            jnp.zeros((CODE_LANES - RANK, heads * HEAD_LANES), BF16),
        ],
        axis=0,
    )
    kv_aug_rows = jnp.concatenate(
        [
            jnp.zeros((RANK, heads * HEAD_LANES), BF16),
            narrow(ADAPT_SCALE * kvb_out),
            jnp.zeros((CODE_LANES - 2 * RANK, heads * HEAD_LANES), BF16),
        ],
        axis=0,
    )
    sources, copies = [q_aug_rows, kv_aug_rows], [
        (0, None, 0, lambda dd, tt: (pl.ds(q_lat, CODE_LANES),)),
        (1, None, 1, lambda dd, tt: (pl.ds(0, CODE_LANES),)),
    ]
    for (r, _), piece in up_held.items():
        copies.append(
            (
                len(sources),
                pl.ds(0, qb_rows),
                0,
                lambda dd, tt, r=r: (
                    pl.ds(pl.multiple_of(jnp.bitwise_xor(dd, r) * qb_rows, 16), qb_rows),
                ),
            )
        )
        copies.append(
            (
                len(sources),
                pl.ds(qb_rows, kvb_rows),
                1,
                lambda dd, tt, r=r: (
                    pl.ds(
                        pl.multiple_of(CODE_LANES + jnp.bitwise_xor(dd, r) * kvb_rows, 16),
                        kvb_rows,
                    ),
                ),
            )
        )
        sources.append(piece)
    w_q, w_kv = place_pieces(
        sources,
        copies,
        [
            (q_lat + CODE_LANES, heads * HEAD_LANES),
            (CODE_LANES + kv_lat, heads * HEAD_LANES),
        ],
        "place_up",
    )

    def place_rows(held, extra, name):
        count = held[(0, 0)].shape[0]
        sources, copies = [extra], [(0, None, 0, lambda dd, tt: (pl.ds(width, CODE_LANES),))]
        for (r, _), piece in held.items():
            copies.append(
                (
                    len(sources),
                    None,
                    0,
                    lambda dd, tt, r=r: (
                        pl.ds(pl.multiple_of(jnp.bitwise_xor(dd, r) * count, 16), count),
                    ),
                )
            )
            sources.append(piece)
        (full,) = place_pieces(sources, copies, [(aug, extra.shape[1])], name)
        return full

    out_held = spread(output_matrix.T, outer_first)
    out_extra = jnp.concatenate(
        [out_in, jnp.zeros((CODE_LANES - RANK, out_in.shape[1]), BF16)], axis=0
    )
    w_out = place_rows(out_held, out_extra, "place_out")

    hidden = down_matrix.shape[0]
    half = hidden // 2
    main = half // 128 * 128
    tail = half - main
    tail_wide = -(-3 * tail // 128) * 128
    chunks = 2 if (main // 128) % 2 == 0 else 1
    step_wide = main // chunks

    def columns(gate_part, up_part, down_part, chunk):
        at = slice(chunk * step_wide, (chunk + 1) * step_wide)
        out = [gate_part[:, at]]
        if tail and chunk == chunks - 1:
            out += [gate_part[:, main:], up_part[:, main:], down_part[:, main:]]
            if tail_wide > 3 * tail:
                out.append(jnp.zeros((gate_part.shape[0], tail_wide - 3 * tail), BF16))
        out += [up_part[:, at], down_part[:, at]]
        return jnp.concatenate(out, axis=1)

    def halves(value):
        return value[:, :half], value[:, half:]

    down_turned = down_matrix.T
    mats = [halves(gate_up_matrix[0]), halves(gate_up_matrix[1]), halves(down_turned)]
    zero_codes = jnp.zeros((RANK, half), BF16)

    def half_of(value):
        left, right = halves(value)
        return jnp.where(first, left, right)

    extra_parts = []
    for which in (set_even, set_odd):
        gate_b = half_of(pick(gate_up_adapter_out[0], which)) * 2
        up_b = half_of(pick(gate_up_adapter_out[1], which)) * 2
        down_a_t = half_of(pick(turned(down_adapter_in), which))
        extra_parts.append((gate_b, up_b, down_a_t))

    ffn_weights = []
    for chunk in range(chunks):
        left = columns(mats[0][0], mats[1][0], mats[2][0], chunk)
        right = columns(mats[0][1], mats[1][1], mats[2][1], chunk)
        mine = jnp.where(first, left, right)
        other = jnp.where(first, right, left)
        held = {(0, 0): mine, (pair, 0): hop(other, ("dp", pair))}
        for step in [("dp", high)] + [("dp", b) for b in reversed(low_bits)]:
            for key in list(held):
                held[(key[0] ^ step[1], 0)] = hop(held[key], step)
        extra = []
        for gate_b, up_b, down_a_t in extra_parts:
            extra.append(columns(gate_b, zero_codes, down_a_t, chunk))
            extra.append(columns(zero_codes, up_b, zero_codes, chunk))
        extra.append(jnp.zeros((CODE_LANES - 4 * RANK, extra[0].shape[1]), BF16))
        ffn_weights.append(
            place_rows(held, jnp.concatenate(extra, axis=0), "place_ffn_" + str(chunk))
        )

    def code_lanes(codes):
        none = jnp.zeros_like(codes)
        return jnp.concatenate(
            [
                jnp.where(first, codes, none),
                jnp.where(first, none, codes),
                jnp.zeros((codes.shape[0], CODE_LANES - 4 * RANK), codes.dtype),
            ],
            axis=1,
        )

    def own_codes(value):
        lanes = value[:, width:]
        return jnp.where(first, lanes[:, : 2 * RANK], lanes[:, 2 * RANK : 4 * RANK])

    group_a = t_slow + [("dp", pair)]
    group_b = [("dp", pair)] + t_slow
    group_keys = [(p, r) for r in range(n_t) for p in (0, pair)]
    odd_keys = [k for k in group_keys if k[1] & 1]
    even_keys = [k for k in group_keys if not k[1] & 1]
    order = odd_keys + even_keys

    def spread_group(value):
        top = spread(value[:half_rows], group_a + t_core)
        bottom = spread(value[half_rows:], group_b + t_core)
        parts = []
        for key in order:
            parts += [top[key], bottom[key]]
        return jnp.concatenate(parts, axis=0)

    out_grad = cotangent[0].astype(F32)
    ffn_grad = narrow(RESIDUAL * out_grad)
    down_code_grad = narrow(ADAPT_SCALE * dot_nt(ffn_grad, down_out))
    none16 = jnp.zeros((rows, RANK), BF16)
    g_own = jnp.concatenate(
        [ffn_grad, code_lanes(jnp.concatenate([down_code_grad, none16], axis=1))], axis=1
    )
    g_all = spread_group(g_own)

    cos_part, sin_part = rope_tables(document_numbers)
    zeros_l = jnp.zeros((length, PLAIN_HEAD_DIM), F32)
    zeros_r = jnp.zeros((length, HEAD_LANES - 96), F32)
    none_16 = jnp.zeros_like(sin_part)
    rope = jnp.stack(
        [
            jnp.concatenate([zeros_l + 1.0, cos_part, cos_part, zeros_r], axis=1),
            jnp.concatenate([zeros_l, -sin_part, none_16, zeros_r], axis=1),
            jnp.concatenate([zeros_l, none_16, sin_part, zeros_r], axis=1),
        ],
        axis=0,
    )
    lane_ids = jnp.arange(HEAD_LANES, dtype=jnp.int32)[None, :]
    doc_lane = (lane_ids >= DOC_LANE) & (lane_ids < DOC_LANE + DOC_SLOTS)
    is_doc = document_numbers[0][:, None] == lane_ids - DOC_LANE
    doc_q = narrow(jnp.where(doc_lane & is_doc, 1.0, 0.0))
    doc_k = jnp.where(
        doc_lane & ~is_doc, -BIG, jnp.where((lane_ids >= 96) & (lane_ids < 99), 1.0, 0.0)
    )

    residual = inputs[0].astype(F32)
    attn_normed, attn_scale = normalize(residual, attention_norm_gain)
    attn_rows = narrow(attn_normed)
    down_in = jnp.concatenate([qa_in, kva_in], axis=0)
    down_codes_in = narrow(dot_nt(attn_rows, down_in))
    down_b_rows = jnp.concatenate(
        [
            jnp.pad(qa_out, ((0, 0), (0, kv_all))),
            jnp.pad(kva_out, ((0, 0), (q_lat, 0))),
        ],
        axis=0,
    )
    latent = dot_nn(attn_rows, w_down) + ADAPT_SCALE * dot_nn(down_codes_in, down_b_rows)
    q_latent = latent[:, :q_lat]
    kv_latent = latent[:, q_lat : q_lat + kv_lat]
    q_normed, q_scale = normalize(q_latent, query_latent_gain)
    kv_normed, kv_scale = normalize(kv_latent, keyvalue_latent_gain)
    q_input = narrow(q_normed)
    kv_input = narrow(kv_normed)
    pe_input = narrow(latent[:, q_lat + kv_lat :])
    qb_codes = narrow(dot_nt(q_input, qb_in))
    kvb_codes = narrow(dot_nt(kv_input, kvb_in))
    pe_at = q_lat + 2 * RANK
    lat_own = jnp.concatenate(
        [
            q_input,
            qb_codes,
            kvb_codes,
            pe_input,
            jnp.zeros((rows, CODE_LANES - 2 * RANK - ROTARY_DIM), BF16),
            kv_input,
        ],
        axis=1,
    )

    def by_tensor_place(held, name):
        keys = list(held)
        shape = held[keys[0]].shape
        (full,) = place_pieces(
            [held[k] for k in keys],
            [
                (n, None, 0, lambda dd, tt, r=k[1]: (jnp.bitwise_xor(tt, r),))
                for n, k in enumerate(keys)
            ],
            [(n_t,) + shape],
            name,
        )
        return full.reshape((n_t * shape[0],) + shape[1:])

    def relative(value, name):
        blocks = value.reshape(n_t, value.shape[0] // n_t, value.shape[1])
        (full,) = place_pieces(
            [blocks],
            [(0, r, 0, lambda dd, tt, r=r: (jnp.bitwise_xor(tt, r),)) for r in range(n_t)],
            [blocks.shape],
            name,
        )
        return full

    lat_all = by_tensor_place(spread(lat_own, t_slow + t_core), "place_latents")
    pe_rows = lat_all[:, pe_at : pe_at + ROTARY_DIM].astype(F32)
    pe_a, pe_b = pe_rows[:, : ROTARY_DIM // 2], pe_rows[:, ROTARY_DIM // 2 :]
    pe_aug = narrow(
        jnp.concatenate(
            [
                zeros_l,
                pe_a * cos_part - pe_b * sin_part,
                pe_b * cos_part + pe_a * sin_part,
                zeros_r,
            ],
            axis=1,
        )
        + doc_k
    )
    q_aug, kv, head_out = attend(
        lat_all, w_q, w_kv, rope, pe_aug, doc_q, q_lat + CODE_LANES, q_lat
    )
    head_rel = relative(head_out, "place_heads")
    parts = {}
    for r in [r for r in range(n_t) if r & 1] + [r for r in range(n_t) if not r & 1]:
        parts[(0, r)] = dot_nt(head_rel[r], w_out)
    attn_sum = collect(parts, t_core + t_slow[::-1])
    out_codes = narrow(attn_sum[:, width : width + RANK])
    middle = residual + RESIDUAL * (
        attn_sum[:, :width] + ADAPT_SCALE * dot_nn(out_codes, out_out)
    )

    ffn_normed, ffn_scale = normalize(middle, feedforward_norm_gain)
    ffn_rows = narrow(ffn_normed)
    gu_codes = narrow(dot_nt(ffn_rows, gu_in))
    x_own = jnp.concatenate([ffn_rows, code_lanes(gu_codes)], axis=1)
    x_all = spread_group(x_own)
    grads, hids = [], []
    for chunk in range(chunks):
        last = chunk == chunks - 1
        grad_c, hid_c = ffn_middle(
            x_all, g_all, ffn_weights[chunk], step_wide, tail if last else 0, tail_wide if last else 0
        )
        grads.append(grad_c)
        hids.append(hid_c)

    def gu_columns(chunk):
        return grads[chunk].shape[1]

    odd_rows = len(odd_keys) * rows

    def group_parts(terms):
        odd = narrow(terms(slice(0, odd_rows)))
        came = hop(odd, t_core[0])
        chip = terms(slice(odd_rows, 2 * odd_rows)) + came.astype(F32)
        return chip

    def finish(chip, steps_a, steps_b):
        tops, bottoms = {}, {}
        for n, key in enumerate(even_keys):
            piece = chip[n * rows : (n + 1) * rows]
            tops[key] = piece[:half_rows]
            bottoms[key] = piece[half_rows:]
        return collect(tops, steps_a), collect(bottoms, steps_b)

    def ffn_in_terms(at):
        out = dot_nt(grads[0][at], ffn_weights[0][:, : gu_columns(0)])
        for chunk in range(1, chunks):
            out = out + dot_nt(grads[chunk][at], ffn_weights[chunk][:, : gu_columns(chunk)])
        return out

    def down_terms(at):
        out = 0.0
        for chunk in range(chunks):
            weight = ffn_weights[chunk]
            hid = hids[chunk][at]
            out = out + dot_nt(hid[:, :step_wide], weight[:, gu_columns(chunk) :])
            if hid.shape[1] > step_wide:
                out = out + dot_nt(
                    hid[:, step_wide:], weight[:, step_wide : step_wide + tail_wide]
                )
        return out

    ffn_in_halves = finish(group_parts(ffn_in_terms), group_a[::-1], group_b[::-1])
    tops = []
    for n, ffn_in_aug in enumerate(ffn_in_halves):
        at = slice(n * half_rows, (n + 1) * half_rows)
        gu_code_grad = narrow(own_codes(ffn_in_aug))
        ffn_in_grad = ffn_in_aug[:, :width] + dot_nn(gu_code_grad, gu_in)
        middle_grad = out_grad[at] + normalize_back(
            middle[at], ffn_scale[at], feedforward_norm_gain, ffn_in_grad
        )
        attn_grad = narrow(RESIDUAL * middle_grad)
        out_code_grad = narrow(ADAPT_SCALE * dot_nt(attn_grad, out_out))
        attn_grad_aug = jnp.concatenate(
            [attn_grad, out_code_grad, jnp.zeros((half_rows, CODE_LANES - RANK), BF16)], axis=1
        )
        tops.append((gu_code_grad, middle_grad, attn_grad_aug, spread(attn_grad_aug, t_slow + t_core)))
    gu_code_grad = jnp.concatenate([tops[0][0], tops[1][0]], axis=0)
    middle_grad = jnp.concatenate([tops[0][1], tops[1][1]], axis=0)
    attn_grad_aug = jnp.concatenate([tops[0][2], tops[1][2]], axis=0)
    attn_grad = attn_grad_aug[:, :width]

    grad_rel = []
    for r in range(n_t):
        both = jnp.concatenate([tops[0][3][(0, r)], tops[1][3][(0, r)]], axis=0)
        grad_rel.append(both)
    codes_rel = jnp.stack([g[:, width:] for g in grad_rel], axis=0)
    heads_grad = by_tensor_place(
        {(0, r): narrow(dot_nn(grad_rel[r], w_out)) for r in range(n_t)}, "place_heads_grad"
    )
    out_a = dot_tn(codes_rel.reshape(length, CODE_LANES), head_rel.reshape(length, -1))[:RANK]
    dq, dkv, dpe = attend_back(q_aug, kv, head_out, heads_grad, rope, pe_aug)

    down_a_sum, down_b_sum = finish(
        group_parts(down_terms), [("dp", pair)] + t_slow[::-1], [("dp", pair)] + t_slow[::-1]
    )
    ffn_out = jnp.concatenate([down_a_sum, down_b_sum], axis=0)
    down_codes = narrow(own_codes(ffn_out)[:, :RANK])
    outputs = narrow(
        middle
        + RESIDUAL * (ffn_out[:, :width] + ADAPT_SCALE * dot_nn(down_codes, down_out))
    )

    pe_g = dpe[:, PLAIN_HEAD_DIM : PLAIN_HEAD_DIM + ROTARY_DIM]
    pe_ga, pe_gb = pe_g[:, : ROTARY_DIM // 2], pe_g[:, ROTARY_DIM // 2 :]
    pe_grad = jnp.concatenate(
        [pe_ga * cos_part + pe_gb * sin_part, pe_gb * cos_part - pe_ga * sin_part], axis=1
    )
    from_q = dot_nt(dq, w_q)
    from_kv = dot_nt(dkv, w_kv)
    lat_grad = jnp.concatenate(
        [
            from_q[:, :q_lat],
            from_q[:, q_lat:]
            + from_kv[:, :CODE_LANES]
            + jnp.pad(pe_grad, ((0, 0), (2 * RANK, CODE_LANES - 2 * RANK - ROTARY_DIM))),
            from_kv[:, CODE_LANES:],
        ],
        axis=1,
    )
    lat_rel = relative(narrow(lat_grad), "place_latent_grads")
    lat_sum = collect({(0, r): lat_rel[r] for r in range(n_t)}, t_core + t_slow[::-1])
    qb_code_grad = narrow(lat_sum[:, q_lat : q_lat + RANK])
    kvb_code_grad = narrow(lat_sum[:, q_lat + RANK : q_lat + 2 * RANK])
    pe_sum = lat_sum[:, pe_at : pe_at + ROTARY_DIM]
    q_norm_grad = lat_sum[:, :q_lat] + dot_nn(qb_code_grad, qb_in)
    kv_norm_grad = lat_sum[:, q_lat + CODE_LANES :] + dot_nn(kvb_code_grad, kvb_in)
    latent_grad = narrow(
        jnp.concatenate(
            [
                normalize_back(q_latent, q_scale, query_latent_gain, q_norm_grad),
                normalize_back(kv_latent, kv_scale, keyvalue_latent_gain, kv_norm_grad),
                pe_sum,
            ],
            axis=1,
        )
    )
    code_grad = narrow(ADAPT_SCALE * dot_nt(latent_grad, down_b_rows))
    attn_in_grad = dot_nt(latent_grad, w_down) + dot_nn(code_grad, down_in)
    input_grad = middle_grad + normalize_back(
        residual, attn_scale, attention_norm_gain, attn_in_grad
    )

    onehot = narrow(set_all[:, None] == jnp.arange(group_count, dtype=jnp.int32)[None, :])

    def to_sets(terms):
        return jnp.einsum("sk,srn->krn", onehot, terms, preferred_element_type=F32)

    def shared_terms(terms, name):
        count = terms.shape[0] // n_t
        split = relative(narrow(terms), name + "_split")
        own = collect({(0, r): split[r] for r in range(n_t)}, t_core + t_slow[::-1])
        held = spread(narrow(own), outer_first + t_slow + t_core)
        keys = list(held)
        (full,) = place_pieces(
            [held[k] for k in keys],
            [
                (
                    n,
                    None,
                    0,
                    lambda dd, tt, k=k: (jnp.bitwise_xor(dd, k[0]), jnp.bitwise_xor(tt, k[1])),
                )
                for n, k in enumerate(keys)
            ],
            [(n_dp, n_t, count, terms.shape[1])],
            name + "_place",
        )
        return full.reshape(n_dp, n_t * count, terms.shape[1])

    def split_terms(terms, name):
        held = spread(terms, outer_first)
        keys = list(held)
        (full,) = place_pieces(
            [held[k] for k in keys],
            [
                (n, None, 0, lambda dd, tt, k=k: (jnp.bitwise_xor(dd, k[0]),))
                for n, k in enumerate(keys)
            ],
            [(n_dp,) + terms.shape],
            name,
        )
        return full

    gu_a = dot_tn(gu_code_grad, ffn_rows)
    out_b = ADAPT_SCALE * dot_tn(out_codes, attn_grad)
    down_b = ADAPT_SCALE * dot_tn(down_codes, ffn_grad)
    early = shared_terms(jnp.concatenate([gu_a, out_b, down_b], axis=0), "early")

    def uncolumn(parts, at_tail, first_at):
        out = [parts[c][:, first_at(c) : first_at(c) + step_wide] for c in range(chunks)]
        if tail:
            out.append(parts[-1][:, step_wide + at_tail * tail : step_wide + (at_tail + 1) * tail])
        return jnp.concatenate(out, axis=1)

    x_codes, g_codes = x_all[:, width:], g_all[:, width:]
    gu_b = [dot_tn(x_codes, g) for g in grads]
    down_at = [dot_tn(g_codes, h) for h in hids]
    gate_b_all = ADAPT_SCALE * uncolumn(gu_b, 0, lambda c: 0)
    up_b_all = ADAPT_SCALE * uncolumn(gu_b, 1, lambda c: gu_columns(c) - step_wide)
    down_a_all = uncolumn(down_at, 2, lambda c: 0)
    packed = []
    for p in range(2):
        at = 2 * RANK * p
        packed += [
            gate_b_all[at : at + RANK],
            up_b_all[at + RANK : at + 2 * RANK],
            down_a_all[at : at + RANK],
        ]
    hidden_terms = split_terms(narrow(jnp.concatenate(packed, axis=0)), "hidden_place")
    hidden_terms = hidden_terms.reshape(2, 2, pair, 2, 3 * RANK, half)
    hidden_terms = jnp.concatenate([hidden_terms[:, 0], hidden_terms[:, 1]], axis=-1)
    hidden_terms = jnp.moveaxis(hidden_terms, 2, 1).reshape(n_dp, 3 * RANK, hidden)
    hidden_sets = to_sets(hidden_terms)

    lat_codes = lat_all[:, q_lat : q_lat + CODE_LANES]
    qb_b = ADAPT_SCALE * dot_tn(lat_codes, dq)[:RANK]
    kvb_b = ADAPT_SCALE * dot_tn(lat_codes, dkv)[RANK : 2 * RANK]
    head_terms = split_terms(
        narrow(jnp.concatenate([qb_b, kvb_b, out_a], axis=1)), "head_place"
    )
    head_sets = to_sets(head_terms)
    wide = heads * HEAD_LANES
    qb_b_grad = head_sets[:, :, :wide].reshape(group_count, RANK, heads, HEAD_LANES)[..., :head_q]
    qb_b_grad = qb_b_grad.reshape(group_count, RANK, heads * head_q)
    kvb_b_grad = head_sets[:, :, wide : 2 * wide]
    out_a_grad = turned(head_sets[:, :, 2 * wide :])

    down_in_terms = dot_tn(code_grad, attn_rows)
    b_terms = ADAPT_SCALE * dot_tn(down_codes_in, latent_grad)
    qb_a = dot_tn(qb_code_grad, q_input)
    kvb_a = dot_tn(kvb_code_grad, kv_input)
    small = jnp.concatenate([b_terms[:RANK, :q_lat], b_terms[RANK:, q_lat:], qb_a, kvb_a], axis=1)
    small_wide = small.shape[1]
    small = jnp.pad(small, ((0, RANK), (0, width - small_wide)))
    late = shared_terms(jnp.concatenate([down_in_terms, small], axis=0), "late")

    early_sets = to_sets(early)
    late_sets = to_sets(late)
    gu_a_grad = jnp.stack(
        [turned(early_sets[:, :RANK]), turned(early_sets[:, RANK : 2 * RANK])], axis=0
    )
    late_small = late_sets[:, 2 * RANK : 3 * RANK]
    at = [0, q_lat, q_lat + kv_all, 2 * q_lat + kv_all, small_wide]
    return (
        outputs[None],
        input_grad[None],
        turned(late_sets[:, :RANK]),
        late_small[:, :, at[0] : at[1]],
        turned(late_sets[:, RANK : 2 * RANK]),
        late_small[:, :, at[1] : at[2]],
        turned(late_small[:, :, at[2] : at[3]]),
        qb_b_grad,
        turned(late_small[:, :, at[3] : at[4]]),
        kvb_b_grad,
        out_a_grad,
        early_sets[:, 2 * RANK : 3 * RANK],
        gu_a_grad,
        jnp.stack([hidden_sets[:, :RANK], hidden_sets[:, RANK : 2 * RANK]], axis=0),
        turned(hidden_sets[:, 2 * RANK :]),
        early_sets[:, 3 * RANK :],
    )


def solution(mesh):
    return jax.shard_map(
        functools.partial(per_device, mesh.shape["dp"], mesh.shape["tensor"]),
        mesh=mesh,
        in_specs=(
            P("dp", "tensor", None),
            P("dp", "tensor", None),
            P("dp", None),
            P("dp"),
            P(),
            P(),
            P(),
            P(),
            P("dp", None),
            P("dp", None),
            P("dp", "tensor"),
            P("dp", "tensor"),
            P("tensor", "dp"),
            P(None, "dp", "tensor"),
            P("tensor", "dp"),
            P(),
            P(),
            P(),
            P(),
            P(),
            P(None, None, "tensor"),
            P(),
            P(None, None, "tensor"),
            P(None, "tensor", None),
            P(),
            P(),
            P(None, None, None, "tensor"),
            P(None, "tensor", None),
            P(),
        ),
        out_specs=(
            P("dp", "tensor", None),
            P("dp", "tensor", None),
            P(),
            P(),
            P(),
            P(),
            P(),
            P(None, None, "tensor"),
            P(),
            P(None, None, "tensor"),
            P(None, "tensor", None),
            P(),
            P(),
            P(None, None, None, "tensor"),
            P(None, "tensor", None),
            P(),
        ),
        check_vma=False,
    )
```

```python
import functools
import math

import jax
import jax.numpy as jnp
from jax import lax
from jax.experimental import pallas as pl
from jax.experimental.pallas import tpu as pltpu
from jax.sharding import PartitionSpec as P

PLAIN_HEAD_DIM = 64
ROTARY_DIM = 32
VALUE_HEAD_DIM = 64
HEAD_LANES = 128
CODE_LANES = 128
RANK = 16
BLOCK_Q = 256
DOC_LANE = 99
DOC_SLOTS = 24

NORM_EPS = 1e-05
RESIDUAL = 1.4 / math.sqrt(62.0)
ADAPT_SCALE = 2.0
SCORE_SCALE = 1.0 / math.sqrt(PLAIN_HEAD_DIM + ROTARY_DIM)
EXP2_SCALE = SCORE_SCALE * math.log2(math.e)
BIG = 1e30
VMEM_LIMIT = 56 * 1024 * 1024
FREE = pl.CostEstimate(flops=0, bytes_accessed=0, transcendentals=0)
F32 = jnp.float32
BF16 = jnp.bfloat16


def narrow(value):
    return value.astype(BF16)


def dot_nn(a, b):
    return lax.dot_general(a, b, (((1,), (0,)), ((), ())), preferred_element_type=F32)


def dot_nt(a, b):
    return lax.dot_general(a, b, (((1,), (1,)), ((), ())), preferred_element_type=F32)


def dot_tn(a, b):
    return lax.dot_general(a, b, (((0,), (0,)), ((), ())), preferred_element_type=F32)


def normalize(value, gain_vec):
    scale_inv = lax.rsqrt(jnp.mean(value * value, axis=-1, keepdims=True) + NORM_EPS)
    return (value * scale_inv * gain_vec, scale_inv)


def normalize_back(value, scale_inv, gain_vec, grad_in):
    weighted = grad_in * gain_vec
    return scale_inv * weighted - value * scale_inv**3 * jnp.mean(
        value * weighted, axis=-1, keepdims=True
    )


def rope_tables(segments):
    places = jnp.arange(segments.shape[-1], dtype=jnp.int32)
    begins = jnp.concatenate(
        [jnp.ones_like(segments[:, :1]), (segments[:, 1:] != segments[:, :-1]).astype(jnp.int32)],
        axis=1,
    )
    first_place = lax.cummax(places[None, :] * begins, axis=1)
    offsets = (places[None, :] - first_place).astype(F32)
    inv_freq = 10000.0 ** (-2.0 * jnp.arange(ROTARY_DIM // 2, dtype=F32) / ROTARY_DIM)
    angles = offsets[..., None] * inv_freq
    return (jnp.cos(angles)[0], jnp.sin(angles)[0])


def swap(value, axis, bit, size):
    return lax.ppermute(value, axis, [(i, i ^ bit) for i in range(size)])


def place_pieces(sources, copies, outs, name):
    def kernel(*refs):
        src_refs = refs[: len(sources)]
        out_refs = refs[len(sources) : len(sources) + len(outs)]
        sems = refs[-1]
        d = lax.axis_index("dp")
        t = lax.axis_index("tensor")
        started = []
        for n, (src, src_at, out, out_at) in enumerate(copies):
            src_ref = src_refs[src] if src_at is None else src_refs[src].at[src_at]
            copy = pltpu.make_async_copy(src_ref, out_refs[out].at[out_at(d, t)], sems.at[n])
            copy.start()
            started.append(copy)
        for copy in started:
            copy.wait()

    any_spec = pl.BlockSpec(memory_space=pl.ANY)
    moved = sum(s.size * s.dtype.itemsize for s in sources)
    return pl.pallas_call(
        kernel,
        out_shape=[jax.ShapeDtypeStruct(o, BF16) for o in outs],
        in_specs=[any_spec] * len(sources),
        out_specs=[pl.BlockSpec(memory_space=pltpu.VMEM)] * len(outs),
        scratch_shapes=[pltpu.SemaphoreType.DMA((len(copies),))],
        compiler_params=pltpu.CompilerParams(vmem_limit_bytes=VMEM_LIMIT),
        cost_estimate=FREE,
        name=name,
    )(*sources)


class Links:
    def __init__(self, send_sems, recv_sems):
        self.send_sems, self.recv_sems = send_sems, recv_sems
        self.place = {"dp": lax.axis_index("dp"), "tensor": lax.axis_index("tensor")}
        self.copies = []
        self.waited = set()

    def peer(self, step):
        place = dict(self.place)
        place[step[0]] = jnp.bitwise_xor(place[step[0]], step[1])
        return (place["dp"], place["tensor"])

    def greet(self, steps):
        barrier = pltpu.get_barrier_semaphore()
        for step in steps:
            pl.semaphore_signal(
                barrier, inc=1, device_id=self.peer(step), device_id_type=pl.DeviceIdType.MESH
            )
        pl.semaphore_wait(barrier, len(steps))

    def send(self, src, dst, step):
        n = len(self.copies)
        copy = pltpu.make_async_remote_copy(
            src_ref=src,
            dst_ref=dst,
            send_sem=self.send_sems.at[n],
            recv_sem=self.recv_sems.at[n],
            device_id=self.peer(step),
            device_id_type=pl.DeviceIdType.MESH,
        )
        copy.start()
        self.copies.append(copy)
        return n

    def arrived(self, n):
        if n not in self.waited:
            self.copies[n].wait_recv()
            self.waited.add(n)

    def close(self):
        for n, copy in enumerate(self.copies):
            self.arrived(n)
            copy.wait_send()


def flip(key, step):
    return (key[0] ^ step[1], key[1]) if step[0] == "dp" else (key[0], key[1] ^ step[1])


def has_bit(key, step):
    return bool((key[0] if step[0] == "dp" else key[1]) & step[1])


def gather_count(jobs):
    return sum((1 << len(job["steps"])) - 1 for job in jobs)


def run_gathers(links, src_refs, out_refs, jobs):
    d, t = links.place["dp"], links.place["tensor"]

    def landing(job, key):
        at = job["out_at"](jnp.bitwise_xor(d, key[0]), jnp.bitwise_xor(t, key[1]))
        return out_refs[job["out"]].at[at]

    state = []
    for job in jobs:
        src = src_refs[job["src"]]
        if job.get("src_at") is not None:
            src = src.at[job["src_at"]]
        state.append({(0, 0): (src, None)})
    for k in range(max(len(job["steps"]) for job in jobs)):
        for job, held in zip(jobs, state):
            if k >= len(job["steps"]):
                continue
            step = job["steps"][k]
            for key in list(held):
                src, came = held[key]
                if came is not None:
                    links.arrived(came)
                n = links.send(src, landing(job, key), step)
                new = flip(key, step)
                held[new] = (landing(job, new), n)
    return [landing(job, (0, 0)) for job in jobs]


def remote_gather(sources, jobs, extra, outs, name, collective_id):
    steps = []
    for job in jobs:
        steps += [s for s in job["steps"] if s not in steps]
    count = gather_count(jobs)

    def kernel(*refs):
        src_refs = refs[: len(sources)]
        out_refs = refs[len(sources) : len(sources) + len(outs)]
        send_sems, recv_sems, local_sems = refs[len(sources) + len(outs) :]
        links = Links(send_sems, recv_sems)
        links.greet(steps)
        own = run_gathers(links, src_refs, out_refs, jobs)
        local = []
        for job, where in zip(jobs, own):
            src = src_refs[job["src"]]
            if job.get("src_at") is not None:
                src = src.at[job["src_at"]]
            local.append((src, where))
        for src, out, at in extra:
            local.append((src_refs[src], out_refs[out].at[at]))
        started = []
        for n, (src, where) in enumerate(local):
            copy = pltpu.make_async_copy(src, where, local_sems.at[n])
            copy.start()
            started.append(copy)
        links.close()
        for copy in started:
            copy.wait()

    moved = sum(s.size * s.dtype.itemsize for s in sources)
    return pl.pallas_call(
        kernel,
        out_shape=[jax.ShapeDtypeStruct(o, BF16) for o in outs],
        in_specs=[pl.BlockSpec(memory_space=pltpu.VMEM)] * len(sources),
        out_specs=[pl.BlockSpec(memory_space=pl.ANY)] * len(outs),
        scratch_shapes=[
            pltpu.SemaphoreType.DMA((count,)),
            pltpu.SemaphoreType.DMA((count,)),
            pltpu.SemaphoreType.DMA((len(jobs) + len(extra),)),
        ],
        compiler_params=pltpu.CompilerParams(
            collective_id=collective_id, has_side_effects=True, vmem_limit_bytes=VMEM_LIMIT
        ),
        cost_estimate=FREE,
        name=name,
    )(*sources)


def reduce_plan(keys, ways):
    plan = []
    for w, steps in enumerate(ways):
        live = list(keys)
        for k, step in enumerate(steps):
            plan += [(w, k, key) for key in live if has_bit(key, step)]
            live = [key for key in live if not has_bit(key, step)]
    return plan


def remote_reduce(operands, fetched, term, keys, ways, rows, wide, name, collective_id, flops):
    core_step = ("tensor", 1)
    part = rows // len(ways)
    plan = reduce_plan(keys, ways)
    slot = {entry: n for n, entry in enumerate(plan)}
    steps = [core_step] + [s for s in ways[0]]
    count = len(keys) + len(plan)
    n_in = len(operands)

    def kernel(*refs):
        in_refs = refs[:n_in]
        out_ref = refs[n_in]
        held = refs[n_in + 1 : 2 * n_in + 1]
        core_out, core_in, chip, hop_out, hop_in, send_sems, recv_sems, in_sems = refs[2 * n_in + 1 :]
        started = []
        for n in range(n_in):
            shape = fetched[n]
            src = in_refs[n].at[tuple(pl.ds(0, s) for s in shape)]
            copy = pltpu.make_async_copy(src, held[n], in_sems.at[n])
            copy.start()
            started.append(copy)
        links = Links(send_sems, recv_sems)
        links.greet(steps)
        for copy in started:
            copy.wait()
        came = {}

        def send_part(w, k, key):
            entry = (w, k, key)
            came[entry] = links.send(hop_out.at[slot[entry]], hop_in.at[slot[entry]], ways[w][k])

        def so_far(w, k, key):
            total = chip[keys.index(key), w * part : (w + 1) * part, :]
            for j in range(k):
                entry = (w, j, flip(key, ways[w][j]))
                links.arrived(came[entry])
                total = total + hop_in[slot[entry]].astype(F32)
            return total

        for i, key in enumerate(keys):
            core_out[i] = narrow(term(held, links.place, (key[0], key[1] ^ 1)))
            crossing = links.send(core_out.at[i], core_in.at[i], core_step)
            mine = term(held, links.place, key)
            links.arrived(crossing)
            chip[i] = mine + core_in[i].astype(F32)
            for w, way in enumerate(ways):
                if way and has_bit(key, way[0]):
                    hop_out[slot[(w, 0, key)]] = narrow(chip[i, w * part : (w + 1) * part, :])
                    send_part(w, 0, key)
        for k in range(1, len(ways[0])):
            for w in range(len(ways)):
                for entry in plan:
                    if entry[0] == w and entry[1] == k:
                        hop_out[slot[entry]] = narrow(so_far(w, k, entry[2]))
                        send_part(w, k, entry[2])
        for w in range(len(ways)):
            out_ref[w * part : (w + 1) * part, :] = so_far(w, len(ways[w]), (0, 0))
        links.close()

    return pl.pallas_call(
        kernel,
        out_shape=jax.ShapeDtypeStruct((rows, wide), F32),
        in_specs=[pl.BlockSpec(memory_space=pl.ANY)] * n_in,
        out_specs=pl.BlockSpec(memory_space=pltpu.VMEM),
        scratch_shapes=[pltpu.VMEM(s, o.dtype) for s, o in zip(fetched, operands)]
        + [
            pltpu.VMEM((len(keys), rows, wide), BF16),
            pltpu.VMEM((len(keys), rows, wide), BF16),
            pltpu.VMEM((len(keys), rows, wide), F32),
            pltpu.VMEM((max(len(plan), 1), part, wide), BF16),
            pltpu.VMEM((max(len(plan), 1), part, wide), BF16),
            pltpu.SemaphoreType.DMA((count,)),
            pltpu.SemaphoreType.DMA((count,)),
            pltpu.SemaphoreType.DMA((n_in,)),
        ],
        compiler_params=pltpu.CompilerParams(
            collective_id=collective_id, has_side_effects=True, vmem_limit_bytes=VMEM_LIMIT
        ),
        cost_estimate=FREE,
        name=name,
    )(*operands)


def remote_share(terms, parts, jobs_of, outs, n_t, t_steps, steps, name, collective_id):
    count, wide = terms.shape[0] // n_t, terms.shape[1]
    job = dict(
        src=0,
        out=0,
        out_at=lambda dd, tt: (dd, pl.ds(pl.multiple_of(tt * count, 16), count)),
        steps=steps + t_steps[::-1],
    )
    jobs = [job] + jobs_of
    copies = n_t - 1 + gather_count(jobs)
    n_in = 1 + len(parts)
    needed = list(job["steps"])

    def kernel(*refs):
        in_refs, out_refs = refs[:n_in], refs[n_in : n_in + len(outs)]
        own, came_in, went_out, send_sems, recv_sems, local_sems = refs[n_in + len(outs) :]
        links = Links(send_sems, recv_sems)
        links.greet(needed)
        t = links.place["tensor"]
        live = list(range(n_t))
        sums = {
            r: in_refs[0][pl.ds(pl.multiple_of(jnp.bitwise_xor(t, r) * count, 16), count), :].astype(
                F32
            )
            for r in live
        }
        slot = 0
        for step in t_steps:
            sent = []
            for r in live:
                if r & step[1]:
                    went_out[slot] = narrow(sums[r])
                    sent.append((r, slot, links.send(went_out.at[slot], came_in.at[slot], step)))
                    slot += 1
            live = [r for r in live if not r & step[1]]
            for r, at, n in sent:
                links.arrived(n)
                sums[r ^ step[1]] = sums[r ^ step[1]] + came_in[at].astype(F32)
        own[...] = narrow(sums[0])
        sources = [own] + list(in_refs[1:])
        places = run_gathers(links, sources, out_refs, jobs)
        started = []
        for n, (one, where) in enumerate(zip(jobs, places)):
            copy = pltpu.make_async_copy(sources[one["src"]], where, local_sems.at[n])
            copy.start()
            started.append(copy)
        links.close()
        for copy in started:
            copy.wait()

    return pl.pallas_call(
        kernel,
        out_shape=[jax.ShapeDtypeStruct(o, BF16) for o in outs],
        in_specs=[pl.BlockSpec(memory_space=pltpu.VMEM)] * n_in,
        out_specs=[pl.BlockSpec(memory_space=pl.ANY)] * len(outs),
        scratch_shapes=[
            pltpu.VMEM((count, wide), BF16),
            pltpu.VMEM((n_t - 1, count, wide), BF16),
            pltpu.VMEM((n_t - 1, count, wide), BF16),
            pltpu.SemaphoreType.DMA((copies,)),
            pltpu.SemaphoreType.DMA((copies,)),
            pltpu.SemaphoreType.DMA((len(jobs),)),
        ],
        compiler_params=pltpu.CompilerParams(
            collective_id=collective_id, has_side_effects=True, vmem_limit_bytes=VMEM_LIMIT
        ),
        cost_estimate=FREE,
        name=name,
    )(terms, *parts)


def split_three(value):
    high = narrow(value).astype(F32)
    middle = narrow(value - high).astype(F32)
    return high, middle, value - high - middle


def rope_mix(value, cos_l, sin_a, sin_b):
    return (
        value * cos_l
        + pltpu.roll(value, HEAD_LANES - ROTARY_DIM // 2, 1) * sin_a
        + pltpu.roll(value, ROTARY_DIM // 2, 1) * sin_b
    )


def attn_fwd_kernel(
    per_step, q_width, kv_at, xl_ref, wq_ref, wkv_ref, rope_ref, pe_ref, doc_ref, qa_ref, kv_ref, o_ref
):
    length = xl_ref.shape[0]
    lane = lax.broadcasted_iota(jnp.int32, (length, HEAD_LANES), 1)
    q_all = dot_nn(xl_ref[:, :q_width], wq_ref[...])
    kv_all = dot_nn(xl_ref[:, kv_at:], wkv_ref[...])
    kv_ref[...] = narrow(kv_all)
    doc_q = doc_ref[...].astype(F32)
    q_heads, k_heads, kv_turned = [], [], []
    for i in range(per_step):
        span = slice(i * HEAD_LANES, (i + 1) * HEAD_LANES)
        q_one = rope_mix(q_all[:, span], rope_ref[0], rope_ref[1], rope_ref[2]) + doc_q
        q_heads.append(narrow(q_one))
        kv_one = kv_all[:, span]
        k_heads.append(jnp.where(lane < PLAIN_HEAD_DIM, narrow(kv_one), pe_ref[...]))
        kv_turned.append(narrow(kv_one.T))
    key_at = lax.broadcasted_iota(jnp.int32, (BLOCK_Q, BLOCK_Q), 0)
    query_at = lax.broadcasted_iota(jnp.int32, (BLOCK_Q, BLOCK_Q), 1)
    row = lax.broadcasted_iota(jnp.int32, (HEAD_LANES, BLOCK_Q), 0)
    block_lane = lax.broadcasted_iota(jnp.int32, (BLOCK_Q, HEAD_LANES), 1)
    for j in range(length // BLOCK_Q):
        begin, end = j * BLOCK_Q, (j + 1) * BLOCK_Q
        mixed = []
        for i in range(per_step):
            q_part = q_heads[i][begin:end]
            scores = dot_nt(k_heads[i][:end], q_part)
            diag = jnp.where(key_at <= query_at, scores[begin:], -BIG)
            scores = diag if j == 0 else jnp.concatenate([scores[:begin], diag], axis=0)
            top = jnp.max(scores, axis=0, keepdims=True)
            terms = jnp.exp2((scores - top) * EXP2_SCALE)
            total = jnp.sum(terms, axis=0, keepdims=True)
            out_t = dot_nn(kv_turned[i][:, :end], narrow(terms)) * (1.0 / total)
            high, middle, low = split_three(top + jnp.log2(total) * (1.0 / EXP2_SCALE))
            out_t = jnp.where(
                row == 0, -high, jnp.where(row == 1, -middle, jnp.where(row == 2, -low, out_t))
            )
            out_n = out_t.T
            mixed.append(out_n)
            is_lse = (block_lane >= 96) & (block_lane < 99)
            q_saved = jnp.where(is_lse, narrow(pltpu.roll(out_n, 96, 1)), q_part)
            qa_ref[begin:end, i * HEAD_LANES : (i + 1) * HEAD_LANES] = q_saved
        if per_step == 2:
            both = jnp.where(block_lane < 64, pltpu.roll(mixed[0], 64, 1), mixed[1])
            o_ref[begin:end, :] = narrow(both)
        else:
            even = lax.rem(pl.program_id(0), 2) == 0
            moved = jnp.where(even, pltpu.roll(mixed[0], 64, 1), mixed[0])
            mine = (block_lane < 64) == even
            o_ref[begin:end, :] = jnp.where(mine, narrow(moved), o_ref[begin:end, :])


def attn_bwd_kernel(
    per_step, qa_ref, kv_ref, o_ref, do_ref, rope_ref, pe_ref, dq_ref, dkv_ref, dpe_ref, dk_acc, dv_acc
):
    length = qa_ref.shape[0]
    step = pl.program_id(0)
    lane = lax.broadcasted_iota(jnp.int32, (length, HEAD_LANES), 1)
    upper = lane >= 64
    key_at = lax.broadcasted_iota(jnp.int32, (BLOCK_Q, BLOCK_Q), 0)
    query_at = lax.broadcasted_iota(jnp.int32, (BLOCK_Q, BLOCK_Q), 1)
    causal = key_at <= query_at
    out_both = o_ref[...].astype(F32)
    grad_both = do_ref[...].astype(F32)

    @pl.when(step == 0)
    def _():
        dpe_ref[...] = jnp.zeros_like(dpe_ref)

    for i in range(per_step):
        span = slice(i * HEAD_LANES, (i + 1) * HEAD_LANES)
        if per_step == 2:
            turn = i == 0
            grad_one = pltpu.roll(grad_both, 64, 1) if turn else grad_both
            out_one = pltpu.roll(out_both, 64, 1) if turn else out_both
        else:
            even = lax.rem(step, 2) == 0
            grad_one = jnp.where(even, pltpu.roll(grad_both, 64, 1), grad_both)
            out_one = jnp.where(even, pltpu.roll(out_both, 64, 1), out_both)
        grad_one = jnp.where(upper, grad_one, 0.0)
        inner = jnp.sum(jnp.where(upper, grad_one * out_one, 0.0), axis=-1, keepdims=True)
        high, middle, low = split_three(inner)
        grad_aug = jnp.where(
            lane == 0, -high, jnp.where(lane == 1, -middle, jnp.where(lane == 2, -low, grad_one))
        )
        grad_aug = narrow(grad_aug)
        kv_one = kv_ref[:, span]
        ones = jnp.where(lane < 3, 1.0, 0.0).astype(BF16)
        v_aug = jnp.where(upper, kv_one, ones)
        k_aug = jnp.where(lane < 64, kv_one, pe_ref[...])
        k_turned = narrow(k_aug.astype(F32).T)
        for j in reversed(range(length // BLOCK_Q)):
            begin, end = j * BLOCK_Q, (j + 1) * BLOCK_Q
            q_part = qa_ref[begin:end, span]
            probs = jnp.exp2(dot_nt(k_aug[:end], q_part) * EXP2_SCALE)
            diag = jnp.where(causal, probs[begin:], 0.0)
            probs = diag if j == 0 else jnp.concatenate([probs[:begin], diag], axis=0)
            grads = narrow(probs * dot_nt(v_aug[:end], grad_aug[begin:end]))
            dq_part = dot_nn(k_turned[:, :end], grads).T * SCORE_SCALE
            dq_part = rope_mix(
                dq_part,
                rope_ref[0, begin:end, :],
                -rope_ref[1, begin:end, :],
                -rope_ref[2, begin:end, :],
            )
            dq_ref[begin:end, span] = narrow(dq_part)
            dk_part = dot_nn(grads, q_part)
            dv_part = dot_nn(narrow(probs), grad_aug[begin:end])
            if end == length:
                dk_acc[...] = dk_part
                dv_acc[...] = dv_part
            else:
                dk_acc[:end] += dk_part
                dv_acc[:end] += dv_part
        dk_all = dk_acc[...] * SCORE_SCALE
        dkv_ref[:, span] = narrow(jnp.where(upper, dv_acc[...], dk_all))
        dpe_ref[...] += jnp.where(upper & (lane < 96), dk_all, 0.0)


def attend(latents, w_q, w_kv, rope, pe_aug, doc_q, q_width, kv_at):
    length = latents.shape[0]
    heads = w_q.shape[1] // HEAD_LANES
    per_step = 2 if heads % 2 == 0 else 1
    wide = per_step * HEAD_LANES
    whole = lambda a: pl.BlockSpec(a.shape, lambda h: (0,) * a.ndim)
    flops = heads * length * (2 * q_width * 256 + length * 2 * 256)
    return pl.pallas_call(
        functools.partial(attn_fwd_kernel, per_step, q_width, kv_at),
        grid=(heads // per_step,),
        in_specs=[
            whole(latents),
            pl.BlockSpec((w_q.shape[0], wide), lambda h: (0, h)),
            pl.BlockSpec((w_kv.shape[0], wide), lambda h: (0, h)),
            whole(rope),
            whole(pe_aug),
            whole(doc_q),
        ],
        out_specs=[
            pl.BlockSpec((length, wide), lambda h: (0, h)),
            pl.BlockSpec((length, wide), lambda h: (0, h)),
            pl.BlockSpec((length, HEAD_LANES), lambda h: (0, h * per_step // 2)),
        ],
        out_shape=[
            jax.ShapeDtypeStruct((length, heads * HEAD_LANES), BF16),
            jax.ShapeDtypeStruct((length, heads * HEAD_LANES), BF16),
            jax.ShapeDtypeStruct((length, heads * VALUE_HEAD_DIM), BF16),
        ],
        compiler_params=pltpu.CompilerParams(vmem_limit_bytes=VMEM_LIMIT),
        cost_estimate=FREE,
        name="attend",
    )(latents, w_q, w_kv, rope, pe_aug, doc_q)


def attend_back(q_aug, kv, heads_out, heads_grad, rope, pe_aug):
    length = q_aug.shape[0]
    heads = q_aug.shape[1] // HEAD_LANES
    per_step = 2 if heads % 2 == 0 else 1
    wide = per_step * HEAD_LANES
    whole = lambda a: pl.BlockSpec(a.shape, lambda h: (0,) * a.ndim)
    columns = pl.BlockSpec((length, wide), lambda h: (0, h))
    packed = pl.BlockSpec((length, HEAD_LANES), lambda h: (0, h * per_step // 2))
    return pl.pallas_call(
        functools.partial(attn_bwd_kernel, per_step),
        grid=(heads // per_step,),
        in_specs=[columns, columns, packed, packed, whole(rope), whole(pe_aug)],
        out_specs=[columns, columns, pl.BlockSpec((length, HEAD_LANES), lambda h: (0, 0))],
        out_shape=[
            jax.ShapeDtypeStruct((length, heads * HEAD_LANES), BF16),
            jax.ShapeDtypeStruct((length, heads * HEAD_LANES), BF16),
            jax.ShapeDtypeStruct((length, HEAD_LANES), F32),
        ],
        scratch_shapes=[
            pltpu.VMEM((length, HEAD_LANES), F32),
            pltpu.VMEM((length, HEAD_LANES), F32),
        ],
        compiler_params=pltpu.CompilerParams(vmem_limit_bytes=VMEM_LIMIT),
        cost_estimate=FREE,
        name="attend_back",
    )(q_aug, kv, heads_out, heads_grad, rope, pe_aug)


def ffn_kernel(main, tail, tail_wide, x_ref, g_ref, w_ref, grad_ref, hid_ref):
    gu_wide = 2 * main + tail_wide
    pre = dot_nn(x_ref[...], w_ref[:, :gu_wide])
    back = dot_nn(g_ref[...], w_ref[:, gu_wide:])

    def middle(gate, up, hid_grad):
        sig = 1.0 / (1.0 + jnp.exp(-gate))
        silu = gate * sig
        gate_grad = hid_grad * up * (sig * (1.0 + gate * (1.0 - sig)))
        return silu * up, gate_grad, hid_grad * silu

    hid, gate_grad, up_grad = middle(pre[:, :main], pre[:, main + tail_wide :], back)
    hid_ref[:, :main] = narrow(hid)
    grad_ref[:, :main] = narrow(gate_grad)
    grad_ref[:, main + tail_wide :] = narrow(up_grad)
    if tail_wide:
        pre_tail = pre[:, main : main + tail_wide]
        back_tail = dot_nn(g_ref[...], w_ref[:, main : main + tail_wide])
        up_tail = pltpu.roll(pre_tail, tail_wide - tail, 1)
        hid_tail = pltpu.roll(back_tail, tail_wide - 2 * tail, 1)
        hid, gate_grad, up_grad = middle(pre_tail, up_tail, hid_tail)
        lane = lax.broadcasted_iota(jnp.int32, pre_tail.shape, 1)
        hid = pltpu.roll(hid, 2 * tail, 1)
        hid = jnp.where((lane >= 2 * tail) & (lane < 3 * tail), hid, 0.0)
        hid_ref[:, main:] = narrow(hid)
        up_grad = pltpu.roll(up_grad, tail, 1)
        both = jnp.where(lane < tail, gate_grad, jnp.where(lane < 2 * tail, up_grad, 0.0))
        grad_ref[:, main : main + tail_wide] = narrow(both)


def ffn_middle(x_rows, g_rows, weight, main, tail, tail_wide):
    rows, depth = x_rows.shape
    block = 256
    width = weight.shape[1]
    return pl.pallas_call(
        functools.partial(ffn_kernel, main, tail, tail_wide),
        grid=(rows // block,),
        in_specs=[
            pl.BlockSpec((block, depth), lambda i: (i, 0)),
            pl.BlockSpec((block, depth), lambda i: (i, 0)),
            pl.BlockSpec((depth, width), lambda i: (0, 0)),
        ],
        out_specs=[
            pl.BlockSpec((block, 2 * main + tail_wide), lambda i: (i, 0)),
            pl.BlockSpec((block, main + tail_wide), lambda i: (i, 0)),
        ],
        out_shape=[
            jax.ShapeDtypeStruct((rows, 2 * main + tail_wide), BF16),
            jax.ShapeDtypeStruct((rows, main + tail_wide), BF16),
        ],
        compiler_params=pltpu.CompilerParams(vmem_limit_bytes=VMEM_LIMIT),
        cost_estimate=FREE,
        name="ffn_middle",
    )(x_rows, g_rows, weight)


def per_device(
    n_dp,
    n_t,
    inputs,
    cotangent,
    document_numbers,
    sequence_adapter_index,
    attention_norm_gain,
    query_latent_gain,
    keyvalue_latent_gain,
    feedforward_norm_gain,
    query_down_matrix,
    keyvalue_down_matrix,
    query_up_matrix,
    keyvalue_up_matrix,
    output_matrix,
    gate_up_matrix,
    down_matrix,
    query_down_adapter_in,
    query_down_adapter_out,
    keyvalue_down_adapter_in,
    keyvalue_down_adapter_out,
    query_up_adapter_in,
    query_up_adapter_out,
    keyvalue_up_adapter_in,
    keyvalue_up_adapter_out,
    output_adapter_in,
    output_adapter_out,
    gate_up_adapter_in,
    gate_up_adapter_out,
    down_adapter_in,
    down_adapter_out,
):
    d = lax.axis_index("dp")
    t = lax.axis_index("tensor")
    pair = n_dp // 4
    low_bits = [b for b in (1, 2, 4, 8, 16) if b < pair]
    high = n_dp // 2
    y_bits = [b for b in (2, 4, 8, 16) if b < n_t]
    zl = lax.rem(d // pair, 2)
    core = lax.rem(t, 2)
    first = zl == 0
    size = {"dp": n_dp, "tensor": n_t}
    rows = inputs.shape[1]
    width = inputs.shape[2]
    length = document_numbers.shape[1]
    q_lat = query_down_matrix.shape[1]
    kv_all = keyvalue_down_matrix.shape[1]
    kv_lat = kv_all - ROTARY_DIM
    heads = keyvalue_up_matrix.shape[1] // HEAD_LANES
    group_count = query_down_adapter_in.shape[0]
    aug = width + CODE_LANES
    half_rows = rows // 2

    def hop(value, step):
        return swap(value, step[0], step[1], size[step[0]])

    outer_first = [("dp", high), ("dp", pair)] + [("dp", b) for b in reversed(low_bits)]
    inner_first = [("dp", b) for b in low_bits] + [("dp", high), ("dp", pair)]
    t_slow = [("tensor", b) for b in reversed(y_bits)]
    t_core = [("tensor", 1)]

    set_own = sequence_adapter_index[0]

    def pick(table, index):
        return lax.dynamic_index_in_dim(table, index, 0, keepdims=False)

    def turned(table):
        return jnp.swapaxes(table, -1, -2)

    qa_in, kva_in = pick(turned(query_down_adapter_in), set_own), pick(
        turned(keyvalue_down_adapter_in), set_own
    )
    qa_out, kva_out = pick(query_down_adapter_out, set_own), pick(keyvalue_down_adapter_out, set_own)
    qb_in, kvb_in = pick(turned(query_up_adapter_in), set_own), pick(
        turned(keyvalue_up_adapter_in), set_own
    )
    qb_out, kvb_out = pick(query_up_adapter_out, set_own), pick(keyvalue_up_adapter_out, set_own)
    out_in, out_out = pick(turned(output_adapter_in), set_own), pick(output_adapter_out, set_own)
    gu_in = jnp.concatenate(
        [pick(turned(gate_up_adapter_in[0]), set_own), pick(turned(gate_up_adapter_in[1]), set_own)],
        axis=0,
    )
    down_out = pick(down_adapter_out, set_own)

    def code_lanes(codes):
        none = jnp.zeros_like(codes)
        return jnp.concatenate(
            [
                jnp.where(first, codes, none),
                jnp.where(first, none, codes),
                jnp.zeros((codes.shape[0], CODE_LANES - 4 * RANK), codes.dtype),
            ],
            axis=1,
        )

    def own_codes(value):
        lanes = value[:, width:]
        return jnp.where(first, lanes[:, : 2 * RANK], lanes[:, 2 * RANK : 4 * RANK])

    out_grad = cotangent[0].astype(F32)
    ffn_grad = narrow(RESIDUAL * out_grad)
    down_code_grad = narrow(ADAPT_SCALE * dot_nt(ffn_grad, down_out))
    none16 = jnp.zeros((rows, RANK), BF16)
    g_own = jnp.concatenate(
        [ffn_grad, code_lanes(jnp.concatenate([down_code_grad, none16], axis=1))], axis=1
    )

    down_shard = query_down_matrix.shape[0]
    core_rows = down_shard // 2
    down_both = jnp.concatenate([query_down_matrix, keyvalue_down_matrix], axis=1)
    down_mine = lax.dynamic_index_in_dim(
        down_both.reshape(2, core_rows, q_lat + kv_all), core, 0, keepdims=False
    )
    cut = -(-core_rows // 32) * 16
    qb_rows, kvb_rows = query_up_matrix.shape[0], keyvalue_up_matrix.shape[0]
    head_q = PLAIN_HEAD_DIM + ROTARY_DIM

    def pad_heads(value):
        split = value.reshape(value.shape[0], heads, head_q)
        return jnp.pad(split, ((0, 0), (0, 0), (0, HEAD_LANES - head_q))).reshape(
            value.shape[0], heads * HEAD_LANES
        )

    q_aug_rows = jnp.concatenate(
        [
            narrow(ADAPT_SCALE * pad_heads(qb_out)),
            jnp.zeros((CODE_LANES - RANK, heads * HEAD_LANES), BF16),
        ],
        axis=0,
    )
    kv_aug_rows = jnp.concatenate(
        [
            jnp.zeros((RANK, heads * HEAD_LANES), BF16),
            narrow(ADAPT_SCALE * kvb_out),
            jnp.zeros((CODE_LANES - 2 * RANK, heads * HEAD_LANES), BF16),
        ],
        axis=0,
    )
    out_extra = jnp.concatenate(
        [out_in, jnp.zeros((CODE_LANES - RANK, out_in.shape[1]), BF16)], axis=0
    )
    out_rows = output_matrix.shape[1]

    def rows_at(start, step, count):
        return lambda dd, tt: (pl.ds(pl.multiple_of(start + dd * step, 16), count),)

    def group_block(dd, tt):
        return lax.rem(dd // pair, 2) * n_t + tt

    def group_jobs(src, out):
        return [
            dict(
                src=src,
                src_at=pl.ds(at, half_rows),
                out=out,
                out_at=lambda dd, tt, at=at: (
                    pl.ds(pl.multiple_of(group_block(dd, tt) * rows + at, 16), half_rows),
                ),
                steps=steps + t_core,
            )
            for at, steps in ((0, group_a), (half_rows, group_b))
        ]

    group_a = t_slow + [("dp", pair)]
    group_b = [("dp", pair)] + t_slow
    jobs = [
        dict(
            src=0,
            src_at=pl.ds(at, count),
            out=0,
            out_at=lambda dd, tt, at=at, count=count: (dd, lax.rem(tt, 2), pl.ds(at, count)),
            steps=steps + t_core,
        )
        for at, count, steps in (
            (0, cut, outer_first),
            (cut, core_rows - cut, inner_first),
        )
    ]
    jobs += [
        dict(src=1, out=1, out_at=rows_at(0, qb_rows, qb_rows), steps=outer_first),
        dict(src=2, out=2, out_at=rows_at(CODE_LANES, kvb_rows, kvb_rows), steps=outer_first),
        dict(src=3, out=3, out_at=rows_at(0, out_rows, out_rows), steps=outer_first),
    ]
    jobs += group_jobs(4, 4)
    jobs.append(dict(src=8, out=5, out_at=lambda dd, tt: (dd,), steps=outer_first))
    set_mark = jnp.full((16, 128), sequence_adapter_index[0].astype(F32)).astype(BF16)
    w_down, w_q, w_kv, w_out, g_all, set_marks = remote_gather(
        [
            down_mine,
            pad_heads(query_up_matrix),
            keyvalue_up_matrix,
            output_matrix.T,
            g_own,
            q_aug_rows,
            kv_aug_rows,
            out_extra,
            set_mark,
        ],
        jobs,
        [
            (5, 1, (pl.ds(q_lat, CODE_LANES),)),
            (6, 2, (pl.ds(0, CODE_LANES),)),
            (7, 3, (pl.ds(width, CODE_LANES),)),
        ],
        [
            (n_dp, 2, core_rows, q_lat + kv_all),
            (q_lat + CODE_LANES, heads * HEAD_LANES),
            (CODE_LANES + kv_lat, heads * HEAD_LANES),
            (aug, heads * VALUE_HEAD_DIM),
            (2 * n_t * rows, aug),
            (n_dp, 16, 128),
        ],
        "gather_weights",
        1,
    )
    set_all = set_marks[:, 0, 0].astype(jnp.int32)
    set_peer = lax.dynamic_index_in_dim(set_all, jnp.bitwise_xor(d, pair), 0, keepdims=False)
    set_even = jnp.where(first, set_own, set_peer)
    set_odd = jnp.where(first, set_peer, set_own)
    w_down = w_down.reshape(width, q_lat + kv_all)

    hidden = down_matrix.shape[0]
    half = hidden // 2
    main = half // 128 * 128
    tail = half - main
    tail_wide = -(-3 * tail // 128) * 128
    chunks = 2 if (main // 128) % 2 == 0 else 1
    step_wide = main // chunks

    def columns(gate_part, up_part, down_part, chunk):
        at = slice(chunk * step_wide, (chunk + 1) * step_wide)
        out = [gate_part[:, at]]
        if tail and chunk == chunks - 1:
            out += [gate_part[:, main:], up_part[:, main:], down_part[:, main:]]
            if tail_wide > 3 * tail:
                out.append(jnp.zeros((gate_part.shape[0], tail_wide - 3 * tail), BF16))
        out += [up_part[:, at], down_part[:, at]]
        return jnp.concatenate(out, axis=1)

    def halves(value):
        return value[:, :half], value[:, half:]

    down_turned = down_matrix.T
    mats = [halves(gate_up_matrix[0]), halves(gate_up_matrix[1]), halves(down_turned)]
    zero_codes = jnp.zeros((RANK, half), BF16)

    def half_of(value):
        left, right = halves(value)
        return jnp.where(first, left, right)

    extra_parts = []
    for which in (set_even, set_odd):
        gate_b = half_of(pick(gate_up_adapter_out[0], which)) * 2
        up_b = half_of(pick(gate_up_adapter_out[1], which)) * 2
        down_a_t = half_of(pick(turned(down_adapter_in), which))
        extra_parts.append((gate_b, up_b, down_a_t))

    z_count = n_dp // pair
    ffn_columns, ffn_known = [], []
    for chunk in range(chunks):
        left = columns(mats[0][0], mats[1][0], mats[2][0], chunk)
        right = columns(mats[0][1], mats[1][1], mats[2][1], chunk)
        mine = jnp.where(first, left, right)
        other = jnp.where(first, right, left)
        held = {
            0: mine,
            pair: hop(other, ("dp", pair)),
            high: hop(mine, ("dp", high)),
            high ^ pair: hop(other, ("dp", high ^ pair)),
        }
        count, wide = mine.shape
        (column,) = place_pieces(
            list(held.values()),
            [
                (n, None, 0, lambda dd, tt, r=r: (jnp.bitwise_xor(dd, r) // pair,))
                for n, r in enumerate(held)
            ],
            [(z_count, count, wide)],
            "place_column_" + str(chunk),
        )
        ffn_columns.append(column)
    w_down, ffn_columns = lax.optimization_barrier((w_down, ffn_columns))
    for column in ffn_columns:
        known = {0: column}
        for b in reversed(low_bits):
            for r in list(known):
                known[r ^ b] = hop(known[r], ("dp", b))
        ffn_known.append(known)
    cos_part, sin_part = rope_tables(document_numbers)
    zeros_l = jnp.zeros((length, PLAIN_HEAD_DIM), F32)
    zeros_r = jnp.zeros((length, HEAD_LANES - 96), F32)
    none_16 = jnp.zeros_like(sin_part)
    rope = jnp.stack(
        [
            jnp.concatenate([zeros_l + 1.0, cos_part, cos_part, zeros_r], axis=1),
            jnp.concatenate([zeros_l, -sin_part, none_16, zeros_r], axis=1),
            jnp.concatenate([zeros_l, none_16, sin_part, zeros_r], axis=1),
        ],
        axis=0,
    )
    lane_ids = jnp.arange(HEAD_LANES, dtype=jnp.int32)[None, :]
    doc_lane = (lane_ids >= DOC_LANE) & (lane_ids < DOC_LANE + DOC_SLOTS)
    is_doc = document_numbers[0][:, None] == lane_ids - DOC_LANE
    doc_q = narrow(jnp.where(doc_lane & is_doc, 1.0, 0.0))
    doc_k = jnp.where(
        doc_lane & ~is_doc, -BIG, jnp.where((lane_ids >= 96) & (lane_ids < 99), 1.0, 0.0)
    )

    residual = inputs[0].astype(F32)
    attn_normed, attn_scale = normalize(residual, attention_norm_gain)
    attn_rows = narrow(attn_normed)
    down_in = jnp.concatenate([qa_in, kva_in], axis=0)
    down_codes_in = narrow(dot_nt(attn_rows, down_in))
    down_b_rows = jnp.concatenate(
        [
            jnp.pad(qa_out, ((0, 0), (0, kv_all))),
            jnp.pad(kva_out, ((0, 0), (q_lat, 0))),
        ],
        axis=0,
    )
    latent = dot_nn(attn_rows, w_down) + ADAPT_SCALE * dot_nn(down_codes_in, down_b_rows)
    q_latent = latent[:, :q_lat]
    kv_latent = latent[:, q_lat : q_lat + kv_lat]
    q_normed, q_scale = normalize(q_latent, query_latent_gain)
    kv_normed, kv_scale = normalize(kv_latent, keyvalue_latent_gain)
    q_input = narrow(q_normed)
    kv_input = narrow(kv_normed)
    pe_input = narrow(latent[:, q_lat + kv_lat :])
    qb_codes = narrow(dot_nt(q_input, qb_in))
    kvb_codes = narrow(dot_nt(kv_input, kvb_in))
    pe_at = q_lat + 2 * RANK
    lat_own = jnp.concatenate(
        [
            q_input,
            qb_codes,
            kvb_codes,
            pe_input,
            jnp.zeros((rows, CODE_LANES - 2 * RANK - ROTARY_DIM), BF16),
            kv_input,
        ],
        axis=1,
    )

    def token_jobs(src, out, parts):
        count = rows // parts
        return [
            dict(
                src=src,
                src_at=pl.ds(n * count, count),
                out=out,
                out_at=lambda dd, tt, n=n: (
                    pl.ds(pl.multiple_of(tt * rows + n * count, 16), count),
                ),
                steps=t_slow + t_core,
            )
            for n in range(parts)
        ]

    def relative(value, name):
        blocks = value.reshape(n_t, value.shape[0] // n_t, value.shape[1])
        (full,) = place_pieces(
            [blocks],
            [(0, r, 0, lambda dd, tt, r=r: (jnp.bitwise_xor(tt, r),)) for r in range(n_t)],
            [blocks.shape],
            name,
        )
        return full

    (lat_all,) = remote_gather(
        [lat_own], token_jobs(0, 0, 2), [], [(length, lat_own.shape[1])], "gather_latents", 2
    )
    pe_rows = lat_all[:, pe_at : pe_at + ROTARY_DIM].astype(F32)
    pe_a, pe_b = pe_rows[:, : ROTARY_DIM // 2], pe_rows[:, ROTARY_DIM // 2 :]
    pe_aug = narrow(
        jnp.concatenate(
            [
                zeros_l,
                pe_a * cos_part - pe_b * sin_part,
                pe_b * cos_part + pe_a * sin_part,
                zeros_r,
            ],
            axis=1,
        )
        + doc_k
    )
    q_aug, kv, head_out = attend(
        lat_all, w_q, w_kv, rope, pe_aug, doc_q, q_lat + CODE_LANES, q_lat
    )
    tensor_keys = [(0, r) for r in reversed(range(0, n_t, 2))]

    def token_rows(key, place):
        at = jnp.bitwise_xor(place["tensor"], key[1]) * rows
        return pl.ds(pl.multiple_of(at, 16), rows)

    def out_term(held, place, key):
        return dot_nt(held[0][token_rows(key, place), :], held[1][...])

    head_out, ffn_known[0] = lax.optimization_barrier((head_out, ffn_known[0]))
    attn_sum = remote_reduce(
        [head_out, w_out],
        [head_out.shape, w_out.shape],
        out_term,
        tensor_keys,
        [t_slow[::-1]],
        rows,
        aug,
        "reduce_out",
        3,
        2 * length * head_out.shape[1] * aug,
    )
    out_codes = narrow(attn_sum[:, width : width + RANK])
    middle = residual + RESIDUAL * (
        attn_sum[:, :width] + ADAPT_SCALE * dot_nn(out_codes, out_out)
    )

    ffn_normed, ffn_scale = normalize(middle, feedforward_norm_gain)
    ffn_rows = narrow(ffn_normed)
    gu_codes = narrow(dot_nt(ffn_rows, gu_in))
    x_own = jnp.concatenate([ffn_rows, code_lanes(gu_codes)], axis=1)
    x_own, ffn_known = lax.optimization_barrier((x_own, ffn_known))
    ffn_weights = []
    for chunk, known in enumerate(ffn_known):
        count, wide = known[0].shape[1:]
        extra = []
        for gate_b, up_b, down_a_t in extra_parts:
            extra.append(columns(gate_b, zero_codes, down_a_t, chunk))
            extra.append(columns(zero_codes, up_b, zero_codes, chunk))
        extra.append(jnp.zeros((CODE_LANES - 4 * RANK, extra[0].shape[1]), BF16))
        sources, copies = [jnp.concatenate(extra, axis=0)], [
            (0, None, 0, lambda dd, tt: (pl.ds(width, CODE_LANES),))
        ]
        for r, piece in known.items():
            for z in range(z_count):
                copies.append(
                    (
                        len(sources),
                        z,
                        0,
                        lambda dd, tt, r=r, z=z: (
                            pl.ds(
                                pl.multiple_of(
                                    (z * pair + lax.rem(jnp.bitwise_xor(dd, r), pair)) * count, 16
                                ),
                                count,
                            ),
                        ),
                    )
                )
            sources.append(piece)
        (full,) = place_pieces(sources, copies, [(aug, wide)], "place_ffn_" + str(chunk))
        ffn_weights.append(full)

    (x_all,) = remote_gather(
        [x_own], group_jobs(0, 0), [], [(2 * n_t * rows, aug)], "gather_rows", 4
    )
    grads, hids = [], []
    for chunk in range(chunks):
        last = chunk == chunks - 1
        grad_c, hid_c = ffn_middle(
            x_all, g_all, ffn_weights[chunk], step_wide, tail if last else 0, tail_wide if last else 0
        )
        grads.append(grad_c)
        hids.append(hid_c)

    def gu_columns(chunk):
        return grads[chunk].shape[1]

    group_keys = [
        (p, r) for p in (pair, 0) for r in reversed(range(0, n_t, 2))
    ]

    def ffn_in_term(held, place, key):
        block = group_block(
            jnp.bitwise_xor(place["dp"], key[0]), jnp.bitwise_xor(place["tensor"], key[1])
        )
        at = pl.ds(pl.multiple_of(block * rows, 16), rows)
        out = dot_nt(held[0][at, :], held[chunks][...])
        for chunk in range(1, chunks):
            out = out + dot_nt(held[chunk][at, :], held[chunks + chunk][...])
        return out

    ffn_in_sum = remote_reduce(
        grads + ffn_weights,
        [g.shape for g in grads] + [(aug, gu_columns(c)) for c in range(chunks)],
        ffn_in_term,
        group_keys,
        [group_a[::-1], group_b[::-1]],
        rows,
        aug,
        "reduce_ffn_in",
        5,
        2 * 2 * length * sum(g.shape[1] for g in grads) * aug,
    )

    def down_terms(hid_rows):
        out = 0.0
        for chunk, hid in enumerate(hid_rows):
            weight = ffn_weights[chunk]
            out = out + dot_nt(hid[:, :step_wide], weight[:, gu_columns(chunk) :])
            if hid.shape[1] > step_wide:
                out = out + dot_nt(
                    hid[:, step_wide:], weight[:, step_wide : step_wide + tail_wide]
                )
        return out

    gu_code_grad = narrow(own_codes(ffn_in_sum))
    ffn_in_grad = ffn_in_sum[:, :width] + dot_nn(gu_code_grad, gu_in)
    middle_grad = out_grad + normalize_back(
        middle, ffn_scale, feedforward_norm_gain, ffn_in_grad
    )
    attn_grad = narrow(RESIDUAL * middle_grad)
    out_code_grad = narrow(ADAPT_SCALE * dot_nt(attn_grad, out_out))
    attn_grad_aug = jnp.concatenate(
        [attn_grad, out_code_grad, jnp.zeros((rows, CODE_LANES - RANK), BF16)], axis=1
    )

    (grad_all,) = remote_gather(
        [attn_grad_aug], token_jobs(0, 0, 2), [], [(length, aug)], "gather_grad", 6
    )
    heads_grad = narrow(dot_nn(grad_all, w_out))
    out_a = dot_tn(grad_all[:, width:], head_out)[:RANK]
    dq, dkv, dpe = attend_back(q_aug, kv, head_out, heads_grad, rope, pe_aug)

    hid_rel = place_pieces(
        hids,
        [
            (
                c,
                pl.ds(b * rows, rows),
                c,
                lambda dd, tt, b=b: (
                    jnp.bitwise_xor(lax.rem(dd // pair, 2), b // n_t) * n_t
                    + jnp.bitwise_xor(tt, b % n_t),
                ),
            )
            for c in range(chunks)
            for b in range(2 * n_t)
        ],
        [(2 * n_t, rows, h.shape[1]) for h in hids],
        "place_hidden",
    )
    hid_rel = [h.reshape(2, n_t // 2, 2, rows, h.shape[2]) for h in hid_rel]
    hid_odd = [h[:, :, 1].reshape(n_t * rows, -1) for h in hid_rel]
    hid_even = [h[:, :, 0].reshape(n_t * rows, -1) for h in hid_rel]
    came = hop(narrow(down_terms(hid_odd)), t_core[0])
    chip = down_terms(hid_even) + came.astype(F32)
    chip = chip.reshape(2, n_t // 2, rows, aug)
    ffn_out = chip[0] + hop(narrow(chip[1]), ("dp", pair)).astype(F32)
    left = n_t // 2
    while left > 1:
        ffn_out = ffn_out[: left // 2] + hop(
            narrow(ffn_out[left // 2 :]), ("tensor", left)
        ).astype(F32)
        left //= 2
    ffn_out = ffn_out[0]
    down_codes = narrow(own_codes(ffn_out)[:, :RANK])
    outputs = narrow(
        middle
        + RESIDUAL * (ffn_out[:, :width] + ADAPT_SCALE * dot_nn(down_codes, down_out))
    )

    pe_g = dpe[:, PLAIN_HEAD_DIM : PLAIN_HEAD_DIM + ROTARY_DIM]
    pe_ga, pe_gb = pe_g[:, : ROTARY_DIM // 2], pe_g[:, ROTARY_DIM // 2 :]
    pe_grad = jnp.concatenate(
        [pe_ga * cos_part + pe_gb * sin_part, pe_gb * cos_part - pe_ga * sin_part], axis=1
    )
    pe_padded = jnp.pad(pe_grad, ((0, 0), (2 * RANK, CODE_LANES - 2 * RANK - ROTARY_DIM)))
    lat_wide = q_lat + CODE_LANES + kv_lat

    def latent_term(held, place, key):
        at = token_rows(key, place)
        from_q = dot_nt(held[0][at, :], held[2][...])
        from_kv = dot_nt(held[1][at, :], held[3][...])
        return jnp.concatenate(
            [
                from_q[:, :q_lat],
                from_q[:, q_lat:] + from_kv[:, :CODE_LANES] + held[4][at, :],
                from_kv[:, CODE_LANES:],
            ],
            axis=1,
        )

    operands = [dq, dkv, w_q, w_kv, pe_padded]
    lat_sum = remote_reduce(
        operands,
        [o.shape for o in operands],
        latent_term,
        tensor_keys,
        [t_slow[::-1]],
        rows,
        lat_wide,
        "reduce_latents",
        7,
        2 * length * dq.shape[1] * lat_wide,
    )
    qb_code_grad = narrow(lat_sum[:, q_lat : q_lat + RANK])
    kvb_code_grad = narrow(lat_sum[:, q_lat + RANK : q_lat + 2 * RANK])
    pe_sum = lat_sum[:, pe_at : pe_at + ROTARY_DIM]
    q_norm_grad = lat_sum[:, :q_lat] + dot_nn(qb_code_grad, qb_in)
    kv_norm_grad = lat_sum[:, q_lat + CODE_LANES :] + dot_nn(kvb_code_grad, kvb_in)
    latent_grad = narrow(
        jnp.concatenate(
            [
                normalize_back(q_latent, q_scale, query_latent_gain, q_norm_grad),
                normalize_back(kv_latent, kv_scale, keyvalue_latent_gain, kv_norm_grad),
                pe_sum,
            ],
            axis=1,
        )
    )
    code_grad = narrow(ADAPT_SCALE * dot_nt(latent_grad, down_b_rows))
    attn_in_grad = dot_nt(latent_grad, w_down) + dot_nn(code_grad, down_in)
    input_grad = middle_grad + normalize_back(
        residual, attn_scale, attention_norm_gain, attn_in_grad
    )

    onehot = narrow(set_all[:, None] == jnp.arange(group_count, dtype=jnp.int32)[None, :])

    def to_sets(terms):
        return jnp.einsum("sk,srn->krn", onehot, terms, preferred_element_type=F32)

    def dp_job(src, out):
        return dict(src=src, out=out, out_at=lambda dd, tt: (dd,), steps=outer_first)

    t_steps = t_core + t_slow[::-1]

    gu_a = dot_tn(gu_code_grad, ffn_rows)
    out_b = ADAPT_SCALE * dot_tn(out_codes, attn_grad)
    down_b = ADAPT_SCALE * dot_tn(down_codes, ffn_grad)
    early_terms = jnp.concatenate([gu_a, out_b, down_b], axis=0)

    def uncolumn(parts, at_tail, first_at):
        out = [parts[c][:, first_at(c) : first_at(c) + step_wide] for c in range(chunks)]
        if tail:
            out.append(parts[-1][:, step_wide + at_tail * tail : step_wide + (at_tail + 1) * tail])
        return jnp.concatenate(out, axis=1)

    x_codes, g_codes = x_all[:, width:], g_all[:, width:]
    gu_b = [dot_tn(x_codes, g) for g in grads]
    down_at = [dot_tn(g_codes, h) for h in hids]
    gate_b_all = ADAPT_SCALE * uncolumn(gu_b, 0, lambda c: 0)
    up_b_all = ADAPT_SCALE * uncolumn(gu_b, 1, lambda c: gu_columns(c) - step_wide)
    down_a_all = uncolumn(down_at, 2, lambda c: 0)
    packed = []
    for p in range(2):
        at = 2 * RANK * p
        packed += [
            gate_b_all[at : at + RANK],
            up_b_all[at + RANK : at + 2 * RANK],
            down_a_all[at : at + RANK],
        ]
    hidden_own = narrow(jnp.concatenate(packed, axis=0))
    early, hidden_terms = remote_share(
        narrow(early_terms),
        [hidden_own],
        [dp_job(1, 1)],
        [(n_dp,) + early_terms.shape, (n_dp,) + hidden_own.shape],
        n_t,
        t_steps,
        outer_first,
        "share_early",
        8,
    )
    hidden_terms = hidden_terms.reshape(2, 2, pair, 2, 3 * RANK, half)
    hidden_terms = jnp.concatenate([hidden_terms[:, 0], hidden_terms[:, 1]], axis=-1)
    hidden_terms = jnp.moveaxis(hidden_terms, 2, 1).reshape(n_dp, 3 * RANK, hidden)
    hidden_sets = to_sets(hidden_terms)

    lat_codes = lat_all[:, q_lat : q_lat + CODE_LANES]
    qb_b = ADAPT_SCALE * dot_tn(lat_codes, dq)[:RANK]
    kvb_b = ADAPT_SCALE * dot_tn(lat_codes, dkv)[RANK : 2 * RANK]
    head_own = narrow(jnp.concatenate([qb_b, kvb_b, out_a], axis=1))
    down_in_terms = dot_tn(code_grad, attn_rows)
    b_terms = ADAPT_SCALE * dot_tn(down_codes_in, latent_grad)
    qb_a = dot_tn(qb_code_grad, q_input)
    kvb_a = dot_tn(kvb_code_grad, kv_input)
    small = jnp.concatenate([b_terms[:RANK, :q_lat], b_terms[RANK:, q_lat:], qb_a, kvb_a], axis=1)
    small_wide = small.shape[1]
    small = jnp.pad(small, ((0, RANK), (0, width - small_wide)))
    late_terms = jnp.concatenate([down_in_terms, small], axis=0)
    late, head_terms = remote_share(
        narrow(late_terms),
        [head_own],
        [dp_job(1, 1)],
        [(n_dp,) + late_terms.shape, (n_dp,) + head_own.shape],
        n_t,
        t_steps,
        outer_first,
        "share_late",
        9,
    )
    head_sets = to_sets(head_terms)
    wide = heads * HEAD_LANES
    qb_b_grad = head_sets[:, :, :wide].reshape(group_count, RANK, heads, HEAD_LANES)[..., :head_q]
    qb_b_grad = qb_b_grad.reshape(group_count, RANK, heads * head_q)
    kvb_b_grad = head_sets[:, :, wide : 2 * wide]
    out_a_grad = turned(head_sets[:, :, 2 * wide :])

    early_sets = to_sets(early)
    late_sets = to_sets(late)
    gu_a_grad = jnp.stack(
        [turned(early_sets[:, :RANK]), turned(early_sets[:, RANK : 2 * RANK])], axis=0
    )
    late_small = late_sets[:, 2 * RANK : 3 * RANK]
    at = [0, q_lat, q_lat + kv_all, 2 * q_lat + kv_all, small_wide]
    return (
        outputs[None],
        input_grad[None],
        turned(late_sets[:, :RANK]),
        late_small[:, :, at[0] : at[1]],
        turned(late_sets[:, RANK : 2 * RANK]),
        late_small[:, :, at[1] : at[2]],
        turned(late_small[:, :, at[2] : at[3]]),
        qb_b_grad,
        turned(late_small[:, :, at[3] : at[4]]),
        kvb_b_grad,
        out_a_grad,
        early_sets[:, 2 * RANK : 3 * RANK],
        gu_a_grad,
        jnp.stack([hidden_sets[:, :RANK], hidden_sets[:, RANK : 2 * RANK]], axis=0),
        turned(hidden_sets[:, 2 * RANK :]),
        early_sets[:, 3 * RANK :],
    )


def solution(mesh):
    return jax.shard_map(
        functools.partial(per_device, mesh.shape["dp"], mesh.shape["tensor"]),
        mesh=mesh,
        in_specs=(
            P("dp", "tensor", None),
            P("dp", "tensor", None),
            P("dp", None),
            P("dp"),
            P(),
            P(),
            P(),
            P(),
            P("dp", None),
            P("dp", None),
            P("dp", "tensor"),
            P("dp", "tensor"),
            P("tensor", "dp"),
            P(None, "dp", "tensor"),
            P("tensor", "dp"),
            P(),
            P(),
            P(),
            P(),
            P(),
            P(None, None, "tensor"),
            P(),
            P(None, None, "tensor"),
            P(None, "tensor", None),
            P(),
            P(),
            P(None, None, None, "tensor"),
            P(None, "tensor", None),
            P(),
        ),
        out_specs=(
            P("dp", "tensor", None),
            P("dp", "tensor", None),
            P(),
            P(),
            P(),
            P(),
            P(),
            P(None, None, "tensor"),
            P(),
            P(None, None, "tensor"),
            P(None, "tensor", None),
            P(),
            P(),
            P(None, None, None, "tensor"),
            P(None, "tensor", None),
            P(),
        ),
        check_vma=False,
    )
```

```python
import functools
import math

import jax
import jax.numpy as jnp
from jax import lax
from jax.experimental import pallas as pl
from jax.experimental.pallas import tpu as pltpu
from jax.sharding import PartitionSpec as P

PLAIN_HEAD_DIM = 64
ROTARY_DIM = 32
VALUE_HEAD_DIM = 64
HEAD_LANES = 128
CODE_LANES = 128
RANK = 16
BLOCK_Q = 256
DOC_LANE = 99
DOC_SLOTS = 24

NORM_EPS = 1e-05
RESIDUAL = 1.4 / math.sqrt(62.0)
ADAPT_SCALE = 2.0
SCORE_SCALE = 1.0 / math.sqrt(PLAIN_HEAD_DIM + ROTARY_DIM)
EXP2_SCALE = SCORE_SCALE * math.log2(math.e)
BIG = 1e30
VMEM_LIMIT = 60 * 1024 * 1024
FREE = pl.CostEstimate(flops=0, bytes_accessed=0, transcendentals=0)
F32 = jnp.float32
BF16 = jnp.bfloat16


def narrow(value):
    return value.astype(BF16)


def dot_nn(a, b):
    return lax.dot_general(a, b, (((1,), (0,)), ((), ())), preferred_element_type=F32)


def dot_nt(a, b):
    return lax.dot_general(a, b, (((1,), (1,)), ((), ())), preferred_element_type=F32)


def dot_tn(a, b):
    return lax.dot_general(a, b, (((0,), (0,)), ((), ())), preferred_element_type=F32)


def normalize(value, gain_vec):
    scale_inv = lax.rsqrt(jnp.mean(value * value, axis=-1, keepdims=True) + NORM_EPS)
    return (value * scale_inv * gain_vec, scale_inv)


def normalize_back(value, scale_inv, gain_vec, grad_in):
    weighted = grad_in * gain_vec
    return scale_inv * weighted - value * scale_inv**3 * jnp.mean(
        value * weighted, axis=-1, keepdims=True
    )


def rope_tables(segments):
    places = jnp.arange(segments.shape[-1], dtype=jnp.int32)
    begins = jnp.concatenate(
        [jnp.ones_like(segments[:, :1]), (segments[:, 1:] != segments[:, :-1]).astype(jnp.int32)],
        axis=1,
    )
    first_place = lax.cummax(places[None, :] * begins, axis=1)
    offsets = (places[None, :] - first_place).astype(F32)
    inv_freq = 10000.0 ** (-2.0 * jnp.arange(ROTARY_DIM // 2, dtype=F32) / ROTARY_DIM)
    angles = offsets[..., None] * inv_freq
    return (jnp.cos(angles)[0], jnp.sin(angles)[0])


def swap(value, axis, bit, size):
    return lax.ppermute(value, axis, [(i, i ^ bit) for i in range(size)])


class Links:
    def __init__(self, send_sems, recv_sems):
        self.send_sems, self.recv_sems = send_sems, recv_sems
        self.place = {"dp": lax.axis_index("dp"), "tensor": lax.axis_index("tensor")}
        self.copies = []
        self.waited = set()

    def peer(self, step):
        place = dict(self.place)
        place[step[0]] = jnp.bitwise_xor(place[step[0]], step[1])
        return (place["dp"], place["tensor"])

    def greet(self, steps):
        barrier = pltpu.get_barrier_semaphore()
        for step in steps:
            pl.semaphore_signal(
                barrier, inc=1, device_id=self.peer(step), device_id_type=pl.DeviceIdType.MESH
            )
        pl.semaphore_wait(barrier, len(steps))

    def prepare(self, src, dst, step):
        n = len(self.copies)
        copy = pltpu.make_async_remote_copy(
            src_ref=src,
            dst_ref=dst,
            send_sem=self.send_sems.at[n],
            recv_sem=self.recv_sems.at[n],
            device_id=self.peer(step),
            device_id_type=pl.DeviceIdType.MESH,
        )
        self.copies.append(copy)
        return n

    def send(self, src, dst, step):
        n = self.prepare(src, dst, step)
        self.copies[n].start()
        return n

    def arrived(self, n):
        if n not in self.waited:
            self.copies[n].wait_recv()
            self.waited.add(n)

    def close(self):
        for n, copy in enumerate(self.copies):
            self.arrived(n)
            copy.wait_send()


class Riders:
    def __init__(self, links, riders, in_refs, out_refs):
        self.links = links
        self.rounds = []
        d = links.place["dp"]
        for rider in riders:
            full = out_refs[rider["out"]]
            if rider["kind"] == "plain":
                src = in_refs[rider["src"]]
                if rider["src_at"] is not None:
                    src = src.at[rider["src_at"]]
                self.add(0, src, full, rider["step"])
                continue
            count, pair, high = rider["count"], rider["pair"], rider["high"]
            if rider["kind"] == "one":
                begin, size = rider["rows"]
                here = full.at[pl.ds(pl.multiple_of(d * count + begin, 16), size)]
                for name, bit in (("other", pair), ("mine", high), ("other", high ^ pair)):
                    src = in_refs[rider[name]].at[pl.ds(begin, size)]
                    self.add(0, src, here, ("dp", bit))
            else:
                held = [0]
                for k, step in enumerate(rider["steps"]):
                    for key in list(held):
                        low = jnp.bitwise_xor(lax.rem(d, pair), key)
                        at = pl.multiple_of((rider["z"] * pair + low) * count, 16)
                        here = full.at[pl.ds(at, count)]
                        self.add(k, here, here, step)
                        held.append(key ^ step[1])

    def add(self, k, src, dst, step):
        while len(self.rounds) <= k:
            self.rounds.append([])
        self.rounds[k].append(self.links.prepare(src, dst, step))

    def start(self):
        if self.rounds:
            for n in self.rounds[0]:
                self.links.copies[n].start()

    def finish(self):
        for k, numbers in enumerate(self.rounds):
            if k:
                for n in numbers:
                    self.links.copies[n].start()
            for n in numbers:
                self.links.arrived(n)


def rider_steps(riders):
    steps = []
    for rider in riders:
        if rider["kind"] == "plain":
            steps.append(rider["step"])
        elif rider["kind"] == "one":
            pair, high = rider["pair"], rider["high"]
            steps += [("dp", pair), ("dp", high), ("dp", high ^ pair)]
        else:
            steps += rider["steps"]
    return steps


def rider_count(riders):
    total = 0
    for rider in riders:
        if rider["kind"] == "plain":
            total += 1
        elif rider["kind"] == "one":
            total += 3
        else:
            total += (1 << len(rider["steps"])) - 1
    return total


def distinct(steps):
    out = []
    for step in steps:
        if step not in out:
            out.append(step)
    return out


def flip(key, step):
    return (key[0] ^ step[1], key[1]) if step[0] == "dp" else (key[0], key[1] ^ step[1])


def has_bit(key, step):
    return bool((key[0] if step[0] == "dp" else key[1]) & step[1])


def gather_count(jobs):
    return sum((1 << len(job["steps"])) - 1 for job in jobs)


def run_gathers(links, src_refs, out_refs, jobs, between=None):
    d, t = links.place["dp"], links.place["tensor"]

    def landing(job, key):
        at = job["out_at"](jnp.bitwise_xor(d, key[0]), jnp.bitwise_xor(t, key[1]))
        return out_refs[job["out"]].at[at]

    state = []
    for job in jobs:
        src = src_refs[job["src"]]
        if job.get("src_at") is not None:
            src = src.at[job["src_at"]]
        state.append({(0, 0): (src, None)})
    for k in range(max(len(job["steps"]) for job in jobs)):
        for job, held in zip(jobs, state):
            if k >= len(job["steps"]):
                continue
            step = job["steps"][k]
            for key in list(held):
                src, came = held[key]
                if came is not None:
                    links.arrived(came)
                n = links.send(src, landing(job, key), step)
                new = flip(key, step)
                held[new] = (landing(job, new), n)
        if between is not None:
            between(k)
    return [landing(job, (0, 0)) for job in jobs]


def remote_gather(
    sources, jobs, extra, outs, name, collective_id, riders=(), aliases=(), distant=(), rider_round=0
):
    steps = distinct([s for job in jobs for s in job["steps"]] + rider_steps(riders))
    count = gather_count(jobs) + rider_count(riders)
    aliases = dict(aliases)

    def kernel(*refs):
        src_refs = refs[: len(sources)]
        out_refs = refs[len(sources) : len(sources) + len(outs)]
        send_sems, recv_sems, local_sems = refs[len(sources) + len(outs) :]
        links = Links(send_sems, recv_sems)
        d, t = links.place["dp"], links.place["tensor"]
        links.greet(steps)
        ride = Riders(links, riders, src_refs, out_refs)
        local = []
        for job in jobs:
            src = src_refs[job["src"]]
            if job.get("src_at") is not None:
                src = src.at[job["src_at"]]
            local.append((src, out_refs[job["out"]].at[job["out_at"](d, t)]))
        for src, out, at in extra:
            local.append((src_refs[src], out_refs[out].at[at(d, t)]))
        started = []
        for n, (src, where) in enumerate(local):
            copy = pltpu.make_async_copy(src, where, local_sems.at[n])
            copy.start()
            started.append(copy)

        def between(k):
            if k == rider_round:
                ride.start()

        run_gathers(links, src_refs, out_refs, jobs, between)
        ride.finish()
        links.close()
        for copy in started:
            copy.wait()

    return pl.pallas_call(
        kernel,
        out_shape=[jax.ShapeDtypeStruct(o, BF16) for o in outs],
        in_specs=[
            pl.BlockSpec(memory_space=pl.ANY if n in aliases or n in distant else pltpu.VMEM)
            for n in range(len(sources))
        ],
        out_specs=[pl.BlockSpec(memory_space=pl.ANY)] * len(outs),
        scratch_shapes=[
            pltpu.SemaphoreType.DMA((count,)),
            pltpu.SemaphoreType.DMA((count,)),
            pltpu.SemaphoreType.DMA((len(jobs) + len(extra),)),
        ],
        input_output_aliases=aliases,
        compiler_params=pltpu.CompilerParams(
            collective_id=collective_id, has_side_effects=True, vmem_limit_bytes=VMEM_LIMIT
        ),
        cost_estimate=FREE,
        name=name,
    )(*sources)


def reduce_plan(keys, ways):
    plan = []
    for w, steps in enumerate(ways):
        live = list(keys)
        for k, step in enumerate(steps):
            plan += [(w, k, key) for key in live if has_bit(key, step)]
            live = [key for key in live if not has_bit(key, step)]
    return plan


def remote_reduce(
    operands, fetched, term, keys, ways, rows, wide, name, collective_id, riders=(), ridden=(), carried=()
):
    core_step = ("tensor", 1)
    part = rows // len(ways)
    plan = reduce_plan(keys, ways)
    slot = {entry: n for n, entry in enumerate(plan)}
    steps = distinct([core_step] + [s for s in ways[0]] + rider_steps(riders))
    count = len(keys) + len(plan) + rider_count(riders)
    n_in = len(operands)
    n_all = n_in + len(ridden) + len(carried)

    def kernel(*refs):
        in_refs = refs[:n_in]
        out_ref = refs[n_all]
        ride_in = refs[n_in:n_all]
        ride_out = refs[n_all + 1 : n_all + 1 + len(ridden)]
        scratch = refs[n_all + 1 + len(ridden) :]
        held = scratch[:n_in]
        core_out, core_in, chip, hop_out, hop_in, send_sems, recv_sems, in_sems = scratch[n_in:]
        started = []
        for n in range(n_in):
            shape = fetched[n]
            src = in_refs[n].at[tuple(pl.ds(0, s) for s in shape)]
            copy = pltpu.make_async_copy(src, held[n], in_sems.at[n])
            copy.start()
            started.append(copy)
        links = Links(send_sems, recv_sems)
        links.greet(steps)
        ride = Riders(links, riders, ride_in, ride_out)
        ride.start()
        for copy in started:
            copy.wait()
        came = {}

        def send_part(w, k, key):
            entry = (w, k, key)
            came[entry] = links.send(hop_out.at[slot[entry]], hop_in.at[slot[entry]], ways[w][k])

        def so_far(w, k, key):
            total = chip[keys.index(key), w * part : (w + 1) * part, :]
            for j in range(k):
                entry = (w, j, flip(key, ways[w][j]))
                links.arrived(came[entry])
                total = total + hop_in[slot[entry]].astype(F32)
            return total

        for i, key in enumerate(keys):
            core_out[i] = narrow(term(held, links.place, (key[0], key[1] ^ 1)))
            crossing = links.send(core_out.at[i], core_in.at[i], core_step)
            mine = term(held, links.place, key)
            links.arrived(crossing)
            chip[i] = mine + core_in[i].astype(F32)
            for w, way in enumerate(ways):
                if way and has_bit(key, way[0]):
                    hop_out[slot[(w, 0, key)]] = narrow(chip[i, w * part : (w + 1) * part, :])
                    send_part(w, 0, key)
        for k in range(1, len(ways[0])):
            for w in range(len(ways)):
                for entry in plan:
                    if entry[0] == w and entry[1] == k:
                        hop_out[slot[entry]] = narrow(so_far(w, k, entry[2]))
                        send_part(w, k, entry[2])
        for w in range(len(ways)):
            out_ref[w * part : (w + 1) * part, :] = so_far(w, len(ways[w]), (0, 0))
        ride.finish()
        links.close()

    any_spec = pl.BlockSpec(memory_space=pl.ANY)
    return pl.pallas_call(
        kernel,
        out_shape=[jax.ShapeDtypeStruct((rows, wide), F32)]
        + [jax.ShapeDtypeStruct(r.shape, r.dtype) for r in ridden],
        in_specs=[any_spec] * n_all,
        out_specs=[pl.BlockSpec(memory_space=pltpu.VMEM)] + [any_spec] * len(ridden),
        input_output_aliases={n_in + n: 1 + n for n in range(len(ridden))},
        scratch_shapes=[pltpu.VMEM(s, o.dtype) for s, o in zip(fetched, operands)]
        + [
            pltpu.VMEM((len(keys), rows, wide), BF16),
            pltpu.VMEM((len(keys), rows, wide), BF16),
            pltpu.VMEM((len(keys), rows, wide), F32),
            pltpu.VMEM((max(len(plan), 1), part, wide), BF16),
            pltpu.VMEM((max(len(plan), 1), part, wide), BF16),
            pltpu.SemaphoreType.DMA((count,)),
            pltpu.SemaphoreType.DMA((count,)),
            pltpu.SemaphoreType.DMA((n_in,)),
        ],
        compiler_params=pltpu.CompilerParams(
            collective_id=collective_id, has_side_effects=True, vmem_limit_bytes=VMEM_LIMIT
        ),
        cost_estimate=FREE,
        name=name,
    )(*operands, *ridden, *carried)


def remote_share(terms, parts, jobs_of, outs, n_t, t_steps, steps, name, collective_id):
    count, wide = terms.shape[0] // n_t, terms.shape[1]
    job = dict(
        src=0,
        out=0,
        out_at=lambda dd, tt: (dd, pl.ds(pl.multiple_of(tt * count, 16), count)),
        steps=steps + t_steps[::-1],
    )
    jobs = [job] + jobs_of
    copies = n_t - 1 + gather_count(jobs)
    n_in = 1 + len(parts)
    needed = list(job["steps"])

    def kernel(*refs):
        in_refs, out_refs = refs[:n_in], refs[n_in : n_in + len(outs)]
        own, came_in, went_out, send_sems, recv_sems, local_sems = refs[n_in + len(outs) :]
        links = Links(send_sems, recv_sems)
        links.greet(needed)
        t = links.place["tensor"]
        live = list(range(n_t))
        sums = {
            r: in_refs[0][pl.ds(pl.multiple_of(jnp.bitwise_xor(t, r) * count, 16), count), :].astype(
                F32
            )
            for r in live
        }
        slot = 0
        for step in t_steps:
            sent = []
            for r in live:
                if r & step[1]:
                    went_out[slot] = narrow(sums[r])
                    sent.append((r, slot, links.send(went_out.at[slot], came_in.at[slot], step)))
                    slot += 1
            live = [r for r in live if not r & step[1]]
            for r, at, n in sent:
                links.arrived(n)
                sums[r ^ step[1]] = sums[r ^ step[1]] + came_in[at].astype(F32)
        own[...] = narrow(sums[0])
        sources = [own] + list(in_refs[1:])
        places = run_gathers(links, sources, out_refs, jobs)
        started = []
        for n, (one, where) in enumerate(zip(jobs, places)):
            copy = pltpu.make_async_copy(sources[one["src"]], where, local_sems.at[n])
            copy.start()
            started.append(copy)
        links.close()
        for copy in started:
            copy.wait()

    return pl.pallas_call(
        kernel,
        out_shape=[jax.ShapeDtypeStruct(o, BF16) for o in outs],
        in_specs=[pl.BlockSpec(memory_space=pltpu.VMEM)] * n_in,
        out_specs=[pl.BlockSpec(memory_space=pl.ANY)] * len(outs),
        scratch_shapes=[
            pltpu.VMEM((count, wide), BF16),
            pltpu.VMEM((n_t - 1, count, wide), BF16),
            pltpu.VMEM((n_t - 1, count, wide), BF16),
            pltpu.SemaphoreType.DMA((copies,)),
            pltpu.SemaphoreType.DMA((copies,)),
            pltpu.SemaphoreType.DMA((len(jobs),)),
        ],
        compiler_params=pltpu.CompilerParams(
            collective_id=collective_id, has_side_effects=True, vmem_limit_bytes=VMEM_LIMIT
        ),
        cost_estimate=FREE,
        name=name,
    )(terms, *parts)


def split_three(value):
    high = narrow(value).astype(F32)
    middle = narrow(value - high).astype(F32)
    return high, middle, value - high - middle


def rope_mix(value, cos_l, sin_a, sin_b):
    return (
        value * cos_l
        + pltpu.roll(value, HEAD_LANES - ROTARY_DIM // 2, 1) * sin_a
        + pltpu.roll(value, ROTARY_DIM // 2, 1) * sin_b
    )


def attn_fwd_kernel(
    per_step, q_width, kv_at, xl_ref, wq_ref, wkv_ref, rope_ref, pe_ref, doc_ref, qa_ref, kv_ref, o_ref
):
    length = xl_ref.shape[0]
    lane = lax.broadcasted_iota(jnp.int32, (length, HEAD_LANES), 1)
    q_all = dot_nn(xl_ref[:, :q_width], wq_ref[...])
    kv_all = dot_nn(xl_ref[:, kv_at:], wkv_ref[...])
    kv_ref[...] = narrow(kv_all)
    doc_q = doc_ref[...].astype(F32)
    q_heads, k_heads, kv_turned = [], [], []
    for i in range(per_step):
        span = slice(i * HEAD_LANES, (i + 1) * HEAD_LANES)
        q_one = rope_mix(q_all[:, span], rope_ref[0], rope_ref[1], rope_ref[2]) + doc_q
        q_heads.append(narrow(q_one))
        kv_one = kv_all[:, span]
        k_heads.append(jnp.where(lane < PLAIN_HEAD_DIM, narrow(kv_one), pe_ref[...]))
        kv_turned.append(narrow(kv_one.T))
    key_at = lax.broadcasted_iota(jnp.int32, (BLOCK_Q, BLOCK_Q), 0)
    query_at = lax.broadcasted_iota(jnp.int32, (BLOCK_Q, BLOCK_Q), 1)
    row = lax.broadcasted_iota(jnp.int32, (HEAD_LANES, BLOCK_Q), 0)
    block_lane = lax.broadcasted_iota(jnp.int32, (BLOCK_Q, HEAD_LANES), 1)
    for j in range(length // BLOCK_Q):
        begin, end = j * BLOCK_Q, (j + 1) * BLOCK_Q
        mixed = []
        for i in range(per_step):
            q_part = q_heads[i][begin:end]
            scores = dot_nt(k_heads[i][:end], q_part)
            diag = jnp.where(key_at <= query_at, scores[begin:], -BIG)
            scores = diag if j == 0 else jnp.concatenate([scores[:begin], diag], axis=0)
            top = jnp.max(scores, axis=0, keepdims=True)
            terms = jnp.exp2((scores - top) * EXP2_SCALE)
            total = jnp.sum(terms, axis=0, keepdims=True)
            out_t = dot_nn(kv_turned[i][:, :end], narrow(terms)) * (1.0 / total)
            high, middle, low = split_three(top + jnp.log2(total) * (1.0 / EXP2_SCALE))
            out_t = jnp.where(
                row == 0, -high, jnp.where(row == 1, -middle, jnp.where(row == 2, -low, out_t))
            )
            out_n = out_t.T
            mixed.append(out_n)
            is_lse = (block_lane >= 96) & (block_lane < 99)
            q_saved = jnp.where(is_lse, narrow(pltpu.roll(out_n, 96, 1)), q_part)
            qa_ref[begin:end, i * HEAD_LANES : (i + 1) * HEAD_LANES] = q_saved
        if per_step == 2:
            both = jnp.where(block_lane < 64, pltpu.roll(mixed[0], 64, 1), mixed[1])
            o_ref[begin:end, :] = narrow(both)
        else:
            even = lax.rem(pl.program_id(0), 2) == 0
            moved = jnp.where(even, pltpu.roll(mixed[0], 64, 1), mixed[0])
            mine = (block_lane < 64) == even
            o_ref[begin:end, :] = jnp.where(mine, narrow(moved), o_ref[begin:end, :])


def attn_bwd_kernel(
    per_step, qa_ref, kv_ref, o_ref, do_ref, rope_ref, pe_ref, dq_ref, dkv_ref, dpe_ref, dk_acc, dv_acc
):
    length = qa_ref.shape[0]
    step = pl.program_id(0)
    lane = lax.broadcasted_iota(jnp.int32, (length, HEAD_LANES), 1)
    upper = lane >= 64
    key_at = lax.broadcasted_iota(jnp.int32, (BLOCK_Q, BLOCK_Q), 0)
    query_at = lax.broadcasted_iota(jnp.int32, (BLOCK_Q, BLOCK_Q), 1)
    causal = key_at <= query_at
    out_both = o_ref[...].astype(F32)
    grad_both = do_ref[...].astype(F32)

    @pl.when(step == 0)
    def _():
        dpe_ref[...] = jnp.zeros_like(dpe_ref)

    for i in range(per_step):
        span = slice(i * HEAD_LANES, (i + 1) * HEAD_LANES)
        if per_step == 2:
            turn = i == 0
            grad_one = pltpu.roll(grad_both, 64, 1) if turn else grad_both
            out_one = pltpu.roll(out_both, 64, 1) if turn else out_both
        else:
            even = lax.rem(step, 2) == 0
            grad_one = jnp.where(even, pltpu.roll(grad_both, 64, 1), grad_both)
            out_one = jnp.where(even, pltpu.roll(out_both, 64, 1), out_both)
        grad_one = jnp.where(upper, grad_one, 0.0)
        inner = jnp.sum(jnp.where(upper, grad_one * out_one, 0.0), axis=-1, keepdims=True)
        high, middle, low = split_three(inner)
        grad_aug = jnp.where(
            lane == 0, -high, jnp.where(lane == 1, -middle, jnp.where(lane == 2, -low, grad_one))
        )
        grad_aug = narrow(grad_aug)
        kv_one = kv_ref[:, span]
        ones = jnp.where(lane < 3, 1.0, 0.0).astype(BF16)
        v_aug = jnp.where(upper, kv_one, ones)
        k_aug = jnp.where(lane < 64, kv_one, pe_ref[...])
        k_turned = narrow(k_aug.astype(F32).T)
        for j in reversed(range(length // BLOCK_Q)):
            begin, end = j * BLOCK_Q, (j + 1) * BLOCK_Q
            q_part = qa_ref[begin:end, span]
            probs = jnp.exp2(dot_nt(k_aug[:end], q_part) * EXP2_SCALE)
            diag = jnp.where(causal, probs[begin:], 0.0)
            probs = diag if j == 0 else jnp.concatenate([probs[:begin], diag], axis=0)
            grads = narrow(probs * dot_nt(v_aug[:end], grad_aug[begin:end]))
            dq_part = dot_nn(k_turned[:, :end], grads).T * SCORE_SCALE
            dq_part = rope_mix(
                dq_part,
                rope_ref[0, begin:end, :],
                -rope_ref[1, begin:end, :],
                -rope_ref[2, begin:end, :],
            )
            dq_ref[begin:end, span] = narrow(dq_part)
            dk_part = dot_nn(grads, q_part)
            dv_part = dot_nn(narrow(probs), grad_aug[begin:end])
            if end == length:
                dk_acc[...] = dk_part
                dv_acc[...] = dv_part
            else:
                dk_acc[:end] += dk_part
                dv_acc[:end] += dv_part
        dk_all = dk_acc[...] * SCORE_SCALE
        dkv_ref[:, span] = narrow(jnp.where(upper, dv_acc[...], dk_all))
        dpe_ref[...] += jnp.where(upper & (lane < 96), dk_all, 0.0)


def ridden_call(
    kernel, grid, arrays, in_specs, out_shape, out_specs, scratch, riders, ridden, carried, fresh, name, collective_id
):
    steps = distinct(rider_steps(riders))
    count = rider_count(riders)
    n_in, n_out = len(arrays), len(out_shape)
    n_ride_in = len(ridden) + len(carried)
    n_ride_out = len(ridden) + len(fresh)

    def body(*refs):
        own_in, rest = refs[:n_in], refs[n_in:]
        ride_in, rest = rest[:n_ride_in], rest[n_ride_in:]
        own_out, rest = rest[:n_out], rest[n_out:]
        ride_out, rest = rest[:n_ride_out], rest[n_ride_out:]
        send_sems, recv_sems = rest[-2:]
        own_scratch = rest[:-2]
        links = Links(send_sems, recv_sems)
        ride = Riders(links, riders, ride_in, ride_out)

        @pl.when(pl.program_id(0) == 0)
        def _():
            links.greet(steps)
            ride.start()

        kernel(*own_in, *own_out, *own_scratch)

        @pl.when(pl.program_id(0) == grid[0] - 1)
        def _():
            ride.finish()
            links.close()

    any_spec = pl.BlockSpec(memory_space=pl.ANY)
    return pl.pallas_call(
        body,
        grid=grid,
        in_specs=list(in_specs) + [any_spec] * n_ride_in,
        out_specs=list(out_specs) + [any_spec] * n_ride_out,
        out_shape=list(out_shape)
        + [jax.ShapeDtypeStruct(r.shape, r.dtype) for r in ridden]
        + [jax.ShapeDtypeStruct(f, BF16) for f in fresh],
        scratch_shapes=list(scratch)
        + [pltpu.SemaphoreType.DMA((count,)), pltpu.SemaphoreType.DMA((count,))],
        input_output_aliases={n_in + n: n_out + n for n in range(len(ridden))},
        compiler_params=pltpu.CompilerParams(
            collective_id=collective_id, has_side_effects=True, vmem_limit_bytes=VMEM_LIMIT
        ),
        cost_estimate=FREE,
        name=name,
    )(*arrays, *ridden, *carried)


def attend(latents, w_q, w_kv, rope, pe_aug, doc_q, q_width, kv_at, riders, ridden, carried):
    length = latents.shape[0]
    heads = w_q.shape[1] // HEAD_LANES
    per_step = 2 if heads % 2 == 0 else 1
    wide = per_step * HEAD_LANES
    whole = lambda a: pl.BlockSpec(a.shape, lambda h: (0,) * a.ndim)
    return ridden_call(
        functools.partial(attn_fwd_kernel, per_step, q_width, kv_at),
        (heads // per_step,),
        [latents, w_q, w_kv, rope, pe_aug, doc_q],
        [
            whole(latents),
            pl.BlockSpec((w_q.shape[0], wide), lambda h: (0, h)),
            pl.BlockSpec((w_kv.shape[0], wide), lambda h: (0, h)),
            whole(rope),
            whole(pe_aug),
            whole(doc_q),
        ],
        [
            jax.ShapeDtypeStruct((length, heads * HEAD_LANES), BF16),
            jax.ShapeDtypeStruct((length, heads * HEAD_LANES), BF16),
            jax.ShapeDtypeStruct((length, heads * VALUE_HEAD_DIM), BF16),
        ],
        [
            pl.BlockSpec((length, wide), lambda h: (0, h)),
            pl.BlockSpec((length, wide), lambda h: (0, h)),
            pl.BlockSpec((length, HEAD_LANES), lambda h: (0, h * per_step // 2)),
        ],
        [],
        riders,
        ridden,
        carried,
        [],
        "attend",
        10,
    )


def attend_back(q_aug, kv, heads_out, heads_grad, rope, pe_aug, riders, carried, fresh):
    length = q_aug.shape[0]
    heads = q_aug.shape[1] // HEAD_LANES
    per_step = 2 if heads % 2 == 0 else 1
    wide = per_step * HEAD_LANES
    whole = lambda a: pl.BlockSpec(a.shape, lambda h: (0,) * a.ndim)
    columns = pl.BlockSpec((length, wide), lambda h: (0, h))
    packed = pl.BlockSpec((length, HEAD_LANES), lambda h: (0, h * per_step // 2))
    arrays = [q_aug, kv, heads_out, heads_grad, rope, pe_aug]
    in_specs = [columns, columns, packed, packed, whole(rope), whole(pe_aug)]
    out_shape = [
        jax.ShapeDtypeStruct((length, heads * HEAD_LANES), BF16),
        jax.ShapeDtypeStruct((length, heads * HEAD_LANES), BF16),
        jax.ShapeDtypeStruct((length, HEAD_LANES), F32),
    ]
    out_specs = [columns, columns, pl.BlockSpec((length, HEAD_LANES), lambda h: (0, 0))]
    scratch = [pltpu.VMEM((length, HEAD_LANES), F32), pltpu.VMEM((length, HEAD_LANES), F32)]
    kernel = functools.partial(attn_bwd_kernel, per_step)
    grid = (heads // per_step,)
    if riders:
        return ridden_call(
            kernel, grid, arrays, in_specs, out_shape, out_specs, scratch, riders, [], carried, fresh, "attend_back", 11
        )
    return pl.pallas_call(
        kernel,
        grid=grid,
        in_specs=in_specs,
        out_specs=out_specs,
        out_shape=out_shape,
        scratch_shapes=scratch,
        compiler_params=pltpu.CompilerParams(vmem_limit_bytes=VMEM_LIMIT),
        cost_estimate=FREE,
        name="attend_back",
    )(*arrays)


def gate_middle(gate, up, hid_grad):
    sig = 1.0 / (1.0 + jnp.exp(-gate))
    silu = gate * sig
    gate_grad = hid_grad * up * (sig * (1.0 + gate * (1.0 - sig)))
    return silu * up, gate_grad, hid_grad * silu


def tail_middle(pre, back, tail):
    wide = pre.shape[1]
    up = pltpu.roll(pre, wide - tail, 1)
    hid_grad = pltpu.roll(back, wide - 2 * tail, 1)
    hid, gate_grad, up_grad = gate_middle(pre, up, hid_grad)
    lane = lax.broadcasted_iota(jnp.int32, pre.shape, 1)
    hid = jnp.where((lane >= 2 * tail) & (lane < 3 * tail), pltpu.roll(hid, 2 * tail, 1), 0.0)
    both = jnp.where(
        lane < tail, gate_grad, jnp.where(lane < 2 * tail, pltpu.roll(up_grad, tail, 1), 0.0)
    )
    return hid, both


def remote_ffn(x_own, g_all, weights, mains, tail, tail_wide, slow, block_of, riders, name, collective_id):
    rows, aug = x_own.shape
    total = g_all.shape[0]
    blocks = total // rows
    width = aug - CODE_LANES
    chunks = len(mains)
    tails = [0] * (chunks - 1) + [tail_wide]
    gu = [2 * m + w for m, w in zip(mains, tails)]
    core_step = ("tensor", 1)
    keys = [(0, 0)]
    for step in slow:
        keys += [flip(key, step) for key in keys]
    bits_of = {key: [s for s in slow if has_bit(key, s)] for key in keys}
    keys.sort(key=lambda k: len(bits_of[k]))

    def part_rows(key, step):
        n = len(bits_of[key])
        i = bits_of[key].index(step)
        size = -(-rows // (16 * n)) * 16
        begin = i * size
        return begin, min(size, rows - begin)

    count = len(keys) + sum(len(bits_of[k]) for k in keys) + rider_count(riders)
    steps = distinct([core_step] + slow + rider_steps(riders))

    def kernel(x_ref, g_ref, *refs):
        refs = refs[chunks:]
        codes_ref = refs[0]
        grad_refs = refs[1 : 1 + chunks]
        hid_refs = refs[1 + chunks : 1 + 2 * chunks]
        w_refs = refs[1 + 2 * chunks : 1 + 3 * chunks]
        x_held, back_held, g_held = refs[1 + 3 * chunks : 4 + 3 * chunks]
        w_held = refs[4 + 3 * chunks : 4 + 4 * chunks]
        send_sems, recv_sems, w_sems, g_sems = refs[4 + 4 * chunks :]
        links = Links(send_sems, recv_sems)
        place = links.place
        fetch = [
            pltpu.make_async_copy(w_refs[c], w_held[c], w_sems.at[c]) for c in range(chunks)
        ]
        fetch[0].start()
        links.greet(steps)

        def landing(key):
            return x_held.at[block_of(key, place)]

        arrivals = {key: [] for key in keys}

        def pass_on(key, src):
            for step in slow:
                if has_bit(key, step):
                    continue
                there = flip(key, step)
                begin, size = part_rows(there, step)
                at = pl.ds(begin, size)
                n = links.send(src.at[at], landing(key).at[at], step)
                arrivals[there].append(n)

        crossing = {}
        pass_on((0, 0), x_ref)
        crossing[(0, 0)] = links.send(x_ref, landing((0, 0)), core_step)
        ride = Riders(links, riders, w_refs, w_refs)
        ride.start()
        x_held[block_of((0, 0), place)] = x_ref[...]

        def g_copy(b, slot):
            at = pl.ds(pl.multiple_of(b * rows, 16), rows)
            return pltpu.make_async_copy(g_ref.at[at], g_held.at[slot], g_sems.at[slot])

        def over_blocks(work):
            g_copy(0, 0).start()

            def one(b, carry):
                slot = lax.rem(b, 2)

                @pl.when(b + 1 < blocks)
                def _():
                    g_copy(b + 1, 1 - slot).start()

                g_copy(b, slot).wait()
                work(b, g_held[slot])
                return carry

            lax.fori_loop(0, blocks, one, 0)

        fetch[0].wait()

        def back_first(b, g_rows):
            back_held[b] = dot_nn(g_rows, w_held[0][:, gu[0] :])

        over_blocks(back_first)

        def rows_at(b):
            return pl.ds(pl.multiple_of(b * rows, 16), rows)

        def forward(b, c, back):
            main = mains[c]
            x_rows = x_held[b]
            pre = dot_nn(x_rows, w_held[c][:, : gu[c]])
            hid, gate_grad, up_grad = gate_middle(pre[:, :main], pre[:, gu[c] - main :], back)
            at = rows_at(b)
            hid_refs[c][at, :main] = narrow(hid)
            grad_refs[c][at, :main] = narrow(gate_grad)
            grad_refs[c][at, gu[c] - main :] = narrow(up_grad)
            return pre

        def first_chunk(key):
            def one(i, carry):
                other = (key[0], key[1] + i)
                b = block_of(other, place)
                forward(b, 0, back_held[b])
                return carry

            lax.fori_loop(0, 2, one, 0)

        links.arrived(crossing[(0, 0)])
        first_chunk((0, 0))
        for level in range(1, len(slow) + 1):
            here = [key for key in keys if len(bits_of[key]) == level]
            for key in here:
                for n in arrivals[key]:
                    links.arrived(n)
                pass_on(key, landing(key))
                crossing[key] = links.send(landing(key), landing(key), core_step)
            for key in here:
                links.arrived(crossing[key])
                first_chunk(key)
        ride.finish()
        for c in range(1, chunks):
            fetch[c].start()
            fetch[c].wait()

            def later(b, g_rows, c=c):
                main = mains[c]
                back = dot_nn(g_rows, w_held[c][:, gu[c] :])
                pre = forward(b, c, back)
                if tails[c]:
                    at_tail = slice(main, main + tail_wide)
                    hid, both = tail_middle(
                        pre[:, at_tail], dot_nn(g_rows, w_held[c][:, at_tail]), tail
                    )
                    at = rows_at(b)
                    hid_refs[c][at, main:] = narrow(hid)
                    grad_refs[c][at, at_tail] = narrow(both)

            over_blocks(later)
        for b in range(blocks):
            codes_ref[b * rows : (b + 1) * rows, :] = x_held[b, :, width:]
        links.close()

    any_spec = pl.BlockSpec(memory_space=pl.ANY)
    vmem_spec = pl.BlockSpec(memory_space=pltpu.VMEM)
    outs = pl.pallas_call(
        kernel,
        in_specs=[vmem_spec, any_spec] + [any_spec] * chunks,
        out_specs=[vmem_spec] * (1 + 2 * chunks) + [any_spec] * chunks,
        out_shape=[jax.ShapeDtypeStruct((total, CODE_LANES), BF16)]
        + [jax.ShapeDtypeStruct((total, g), BF16) for g in gu]
        + [jax.ShapeDtypeStruct((total, m + w), BF16) for m, w in zip(mains, tails)]
        + [jax.ShapeDtypeStruct(w.shape, BF16) for w in weights],
        scratch_shapes=[
            pltpu.VMEM((blocks, rows, aug), BF16),
            pltpu.VMEM((blocks, rows, mains[0]), F32),
            pltpu.VMEM((2, rows, aug), BF16),
        ]
        + [pltpu.VMEM(w.shape, BF16) for w in weights]
        + [
            pltpu.SemaphoreType.DMA((count,)),
            pltpu.SemaphoreType.DMA((count,)),
            pltpu.SemaphoreType.DMA((chunks,)),
            pltpu.SemaphoreType.DMA((2,)),
        ],
        input_output_aliases={2 + c: 1 + 2 * chunks + c for c in range(chunks)},
        compiler_params=pltpu.CompilerParams(
            collective_id=collective_id, has_side_effects=True, vmem_limit_bytes=VMEM_LIMIT
        ),
        cost_estimate=FREE,
        name=name,
    )(x_own, g_all, *weights)
    return (
        outs[0],
        outs[1 : 1 + chunks],
        outs[1 + chunks : 1 + 2 * chunks],
        outs[1 + 2 * chunks :],
    )


def remote_ffn_back(grads, hids, weights, mains, tail_wide, keys, ways, block_of, rows, name, collective_id):
    aug = weights[0].shape[0]
    chunks = len(mains)
    tails = [0] * (chunks - 1) + [tail_wide]
    gu = [2 * m + w for m, w in zip(mains, tails)]
    core_step = ("tensor", 1)
    part = rows // len(ways)
    plan = reduce_plan(keys, ways)
    later = [entry for entry in plan if entry[1] > 0]
    slot = {entry: n for n, entry in enumerate(plan)}
    later_slot = {entry: n for n, entry in enumerate(later)}
    steps = distinct([core_step] + ways[0])
    count = 2 * len(keys) + len(plan)
    operands = list(grads) + list(hids) + list(weights)

    def kernel(*refs):
        n_in = len(operands)
        in_refs = refs[:n_in]
        out_ref, terms_ref = refs[n_in : n_in + 2]
        held = refs[n_in + 2 : 2 * n_in + 2]
        rest = refs[2 * n_in + 2 :]
        core_out, core_in, chip, hop_out, hop_in, stage, send_sems, recv_sems, in_sems, out_sems, free = rest
        g_held, h_held, w_held = held[:chunks], held[chunks : 2 * chunks], held[2 * chunks :]
        started = []
        order = [n for c in range(chunks) for n in (c, 2 * chunks + c)] + list(range(chunks, 2 * chunks))
        for n in order:
            copy = pltpu.make_async_copy(in_refs[n], held[n], in_sems.at[n])
            copy.start()
            started.append(copy)
        links = Links(send_sems, recv_sems)
        place = links.place
        links.greet(steps)
        for copy in started:
            copy.wait()
        came = {}

        def rows_of(key):
            return pl.ds(pl.multiple_of(block_of(key, place) * rows, 16), rows)

        def in_term(key):
            at = rows_of(key)
            out = dot_nt(g_held[0][at, :], w_held[0][:, : gu[0]])
            for c in range(1, chunks):
                out = out + dot_nt(g_held[c][at, :], w_held[c][:, : gu[c]])
            return out

        def down_term(key):
            at = rows_of(key)
            out = 0.0
            for c in range(chunks):
                out = out + dot_nt(h_held[c][at, : mains[c]], w_held[c][:, gu[c] :])
                if tails[c]:
                    out = out + dot_nt(
                        h_held[c][at, mains[c] :], w_held[c][:, mains[c] : mains[c] + tails[c]]
                    )
            return out

        def so_far(w, k, key):
            if key == (0, 0):
                total = out_ref[w * part : (w + 1) * part, :]
            else:
                total = chip[keys.index(key), w * part : (w + 1) * part, :].astype(F32)
            for j in range(k):
                entry = (w, j, flip(key, ways[w][j]))
                links.arrived(came[entry])
                total = total + hop_in[slot[entry]].astype(F32)
            return total

        crossings = []

        def cross(i, value):
            n = len(crossings)
            if n >= 2:
                links.copies[crossings[n - 2]].wait_send()
            core_out[n % 2] = narrow(value)
            crossings.append(links.send(core_out.at[n % 2], core_in.at[i], core_step))
            return crossings[-1]

        for i, key in enumerate(keys):
            crossing = cross(i, in_term((key[0], key[1] ^ 1)))
            mine = in_term(key)
            links.arrived(crossing)
            mine = mine + core_in[i].astype(F32)
            if key == (0, 0):
                out_ref[...] = mine
            else:
                chip[i] = narrow(mine)
                for w, way in enumerate(ways):
                    if has_bit(key, way[0]):
                        at = slice(w * part, (w + 1) * part)
                        entry = (w, 0, key)
                        came[entry] = links.send(
                            chip.at[i, pl.ds(w * part, part)], hop_in.at[slot[entry]], way[0]
                        )
        pl.semaphore_signal(
            free, inc=1, device_id=links.peer(core_step), device_id_type=pl.DeviceIdType.MESH
        )
        pl.semaphore_wait(free, 1)
        stored = []
        for i, key in enumerate(keys):
            crossing = cross(i, down_term((key[0], key[1] ^ 1)))
            mine = down_term(key)
            links.arrived(crossing)
            if i >= 2:
                stored[i - 2].wait()
            stage[i % 2] = narrow(mine + core_in[i].astype(F32))
            copy = pltpu.make_async_copy(stage.at[i % 2], terms_ref.at[i], out_sems.at[i])
            copy.start()
            stored.append(copy)
            if i == len(keys) // 2 - 1:
                for k in range(1, len(ways[0])):
                    for w in range(len(ways)):
                        for entry in plan:
                            if entry[0] == w and entry[1] == k:
                                hop_out[later_slot[entry]] = narrow(so_far(w, k, entry[2]))
                                came[entry] = links.send(
                                    hop_out.at[later_slot[entry]],
                                    hop_in.at[slot[entry]],
                                    ways[w][k],
                                )
        for w in range(len(ways)):
            out_ref[w * part : (w + 1) * part, :] = so_far(w, len(ways[w]), (0, 0))
        for copy in stored[max(0, len(keys) - 2) :]:
            copy.wait()
        for n, copy in enumerate(links.copies):
            links.arrived(n)
            if n not in crossings[:-2]:
                copy.wait_send()

    any_spec = pl.BlockSpec(memory_space=pl.ANY)
    return pl.pallas_call(
        kernel,
        out_shape=[
            jax.ShapeDtypeStruct((rows, aug), F32),
            jax.ShapeDtypeStruct((len(keys), rows, aug), BF16),
        ],
        in_specs=[any_spec] * len(operands),
        out_specs=[pl.BlockSpec(memory_space=pltpu.VMEM), any_spec],
        scratch_shapes=[pltpu.VMEM(o.shape, o.dtype) for o in operands]
        + [
            pltpu.VMEM((2, rows, aug), BF16),
            pltpu.VMEM((len(keys), rows, aug), BF16),
            pltpu.VMEM((len(keys) - 1, rows, aug), BF16),
            pltpu.VMEM((max(len(later), 1), part, aug), BF16),
            pltpu.VMEM((len(plan), part, aug), BF16),
            pltpu.VMEM((2, rows, aug), BF16),
            pltpu.SemaphoreType.DMA((count,)),
            pltpu.SemaphoreType.DMA((count,)),
            pltpu.SemaphoreType.DMA((len(operands),)),
            pltpu.SemaphoreType.DMA((len(keys),)),
            pltpu.SemaphoreType.REGULAR,
        ],
        compiler_params=pltpu.CompilerParams(
            collective_id=collective_id, has_side_effects=True, vmem_limit_bytes=VMEM_LIMIT
        ),
        cost_estimate=FREE,
        name=name,
    )(*operands)


def per_device(
    n_dp,
    n_t,
    inputs,
    cotangent,
    document_numbers,
    sequence_adapter_index,
    attention_norm_gain,
    query_latent_gain,
    keyvalue_latent_gain,
    feedforward_norm_gain,
    query_down_matrix,
    keyvalue_down_matrix,
    query_up_matrix,
    keyvalue_up_matrix,
    output_matrix,
    gate_up_matrix,
    down_matrix,
    query_down_adapter_in,
    query_down_adapter_out,
    keyvalue_down_adapter_in,
    keyvalue_down_adapter_out,
    query_up_adapter_in,
    query_up_adapter_out,
    keyvalue_up_adapter_in,
    keyvalue_up_adapter_out,
    output_adapter_in,
    output_adapter_out,
    gate_up_adapter_in,
    gate_up_adapter_out,
    down_adapter_in,
    down_adapter_out,
):
    d = lax.axis_index("dp")
    t = lax.axis_index("tensor")
    pair = n_dp // 4
    low_bits = [b for b in (1, 2, 4, 8, 16) if b < pair]
    high = n_dp // 2
    y_bits = [b for b in (2, 4, 8, 16) if b < n_t]
    zl = lax.rem(d // pair, 2)
    core = lax.rem(t, 2)
    first = zl == 0
    size = {"dp": n_dp, "tensor": n_t}
    rows = inputs.shape[1]
    width = inputs.shape[2]
    length = document_numbers.shape[1]
    q_lat = query_down_matrix.shape[1]
    kv_all = keyvalue_down_matrix.shape[1]
    kv_lat = kv_all - ROTARY_DIM
    heads = keyvalue_up_matrix.shape[1] // HEAD_LANES
    group_count = query_down_adapter_in.shape[0]
    aug = width + CODE_LANES
    half_rows = rows // 2

    def hop(value, step):
        return swap(value, step[0], step[1], size[step[0]])

    outer_first = [("dp", high), ("dp", pair)] + [("dp", b) for b in reversed(low_bits)]
    inner_first = [("dp", b) for b in low_bits] + [("dp", high), ("dp", pair)]
    t_slow = [("tensor", b) for b in reversed(y_bits)]
    t_core = [("tensor", 1)]

    set_own = sequence_adapter_index[0]

    def pick(table, index):
        return lax.dynamic_index_in_dim(table, index, 0, keepdims=False)

    def turned(table):
        return jnp.swapaxes(table, -1, -2)

    qa_in, kva_in = pick(turned(query_down_adapter_in), set_own), pick(
        turned(keyvalue_down_adapter_in), set_own
    )
    qa_out, kva_out = pick(query_down_adapter_out, set_own), pick(keyvalue_down_adapter_out, set_own)
    qb_in, kvb_in = pick(turned(query_up_adapter_in), set_own), pick(
        turned(keyvalue_up_adapter_in), set_own
    )
    qb_out, kvb_out = pick(query_up_adapter_out, set_own), pick(keyvalue_up_adapter_out, set_own)
    out_in, out_out = pick(turned(output_adapter_in), set_own), pick(output_adapter_out, set_own)
    gu_in = jnp.concatenate(
        [pick(turned(gate_up_adapter_in[0]), set_own), pick(turned(gate_up_adapter_in[1]), set_own)],
        axis=0,
    )
    down_out = pick(down_adapter_out, set_own)

    hidden = down_matrix.shape[0]
    half = hidden // 2
    tiles = half // 128
    main = tiles * 128
    tail = half - main
    tail_wide = -(-3 * tail // 128) * 128
    first_tiles = (2 * tiles + 2) // 3
    mains = [first_tiles * 128, main - first_tiles * 128]
    chunks = len(mains)
    tails = [0] * (chunks - 1) + [tail_wide]
    gu_wide = [2 * m + w for m, w in zip(mains, tails)]

    def columns(gate_part, up_part, down_part, chunk):
        begin = sum(mains[:chunk])
        at = slice(begin, begin + mains[chunk])
        out = [gate_part[:, at]]
        if tail and chunk == chunks - 1:
            out += [gate_part[:, main:], up_part[:, main:], down_part[:, main:]]
            if tail_wide > 3 * tail:
                out.append(jnp.zeros((gate_part.shape[0], tail_wide - 3 * tail), BF16))
        out += [up_part[:, at], down_part[:, at]]
        return jnp.concatenate(out, axis=1)

    def halves(value):
        return value[:, :half], value[:, half:]

    mats = [halves(gate_up_matrix[0]), halves(gate_up_matrix[1]), halves(down_matrix.T)]
    ffn_mine, ffn_other = [], []
    for chunk in range(chunks):
        left = columns(mats[0][0], mats[1][0], mats[2][0], chunk)
        right = columns(mats[0][1], mats[1][1], mats[2][1], chunk)
        ffn_mine.append(jnp.where(first, left, right))
        ffn_other.append(jnp.where(first, right, left))
    ffn_rows_each = gate_up_matrix.shape[1]
    z_count = n_dp // pair
    ffn_wide = [m.shape[1] for m in ffn_mine]

    def ride_one(out, mine, other, begin, size):
        return dict(
            kind="one",
            out=out,
            mine=mine,
            other=other,
            rows=(begin, size),
            count=ffn_rows_each,
            pair=pair,
            high=high,
        )

    def ride_two(out, z):
        return dict(
            kind="two",
            out=out,
            z=z,
            count=ffn_rows_each,
            pair=pair,
            high=high,
            steps=[("dp", b) for b in reversed(low_bits)],
        )

    def code_lanes(codes):
        none = jnp.zeros_like(codes)
        return jnp.concatenate(
            [
                jnp.where(first, codes, none),
                jnp.where(first, none, codes),
                jnp.zeros((codes.shape[0], CODE_LANES - 4 * RANK), codes.dtype),
            ],
            axis=1,
        )

    def own_codes(value):
        lanes = value[:, width:]
        return jnp.where(first, lanes[:, : 2 * RANK], lanes[:, 2 * RANK : 4 * RANK])

    out_grad = cotangent[0].astype(F32)
    ffn_grad = narrow(RESIDUAL * out_grad)
    down_code_grad = narrow(ADAPT_SCALE * dot_nt(ffn_grad, down_out))
    none16 = jnp.zeros((rows, RANK), BF16)
    g_own = jnp.concatenate(
        [ffn_grad, code_lanes(jnp.concatenate([down_code_grad, none16], axis=1))], axis=1
    )

    down_shard = query_down_matrix.shape[0]
    shares = n_t if down_shard % (16 * n_t) == 0 else 2
    share_rows = down_shard // shares
    down_both = jnp.concatenate([query_down_matrix, keyvalue_down_matrix], axis=1)
    down_mine = lax.dynamic_index_in_dim(
        down_both.reshape(shares, share_rows, q_lat + kv_all), lax.rem(t, shares), 0, keepdims=False
    )
    qb_rows, kvb_rows = query_up_matrix.shape[0], keyvalue_up_matrix.shape[0]
    head_q = PLAIN_HEAD_DIM + ROTARY_DIM

    def pad_heads(value):
        split = value.reshape(value.shape[0], heads, head_q)
        return jnp.pad(split, ((0, 0), (0, 0), (0, HEAD_LANES - head_q))).reshape(
            value.shape[0], heads * HEAD_LANES
        )

    q_aug_rows = jnp.concatenate(
        [
            narrow(ADAPT_SCALE * pad_heads(qb_out)),
            jnp.zeros((CODE_LANES - RANK, heads * HEAD_LANES), BF16),
        ],
        axis=0,
    )
    kv_aug_rows = jnp.concatenate(
        [
            jnp.zeros((RANK, heads * HEAD_LANES), BF16),
            narrow(ADAPT_SCALE * kvb_out),
            jnp.zeros((CODE_LANES - 2 * RANK, heads * HEAD_LANES), BF16),
        ],
        axis=0,
    )
    out_extra = jnp.concatenate(
        [out_in, jnp.zeros((CODE_LANES - RANK, out_in.shape[1]), BF16)], axis=0
    )
    out_rows = output_matrix.shape[1]

    def rows_at(start, step, count):
        return lambda dd, tt: (pl.ds(pl.multiple_of(start + dd * step, 16), count),)

    def group_block(dd, tt):
        return lax.rem(dd // pair, 2) * n_t + tt

    def group_jobs(src, out, ways):
        return [
            dict(
                src=src,
                src_at=pl.ds(at, half_rows),
                out=out,
                out_at=lambda dd, tt, at=at: (
                    pl.ds(pl.multiple_of(group_block(dd, tt) * rows + at, 16), half_rows),
                ),
                steps=steps + t_core,
            )
            for at, steps in zip((0, half_rows), ways)
        ]

    group_a = t_slow + [("dp", pair)]
    group_b = [("dp", pair)] + t_slow
    jobs = [
        dict(
            src=0,
            out=0,
            out_at=lambda dd, tt: (dd, lax.rem(tt, shares)),
            steps=outer_first + (t_slow if shares == n_t else []) + t_core,
        )
    ]
    jobs += [
        dict(src=1, out=1, out_at=rows_at(0, qb_rows, qb_rows), steps=outer_first),
        dict(src=2, out=2, out_at=rows_at(CODE_LANES, kvb_rows, kvb_rows), steps=outer_first),
        dict(src=3, out=3, out_at=rows_at(0, out_rows, out_rows), steps=outer_first),
    ]
    jobs += group_jobs(4, 4, (group_b, group_b))
    jobs.append(dict(src=8, out=5, out_at=lambda dd, tt: (dd,), steps=outer_first))
    set_mark = jnp.full((16, 128), sequence_adapter_index[0].astype(F32)).astype(BF16)
    w_down, w_q, w_kv, w_out, g_all, set_marks, w_ffn0, w_ffn1 = remote_gather(
        [
            down_mine,
            pad_heads(query_up_matrix),
            keyvalue_up_matrix,
            output_matrix.T,
            g_own,
            q_aug_rows,
            kv_aug_rows,
            out_extra,
            set_mark,
            ffn_mine[0],
            ffn_other[0],
            ffn_mine[1],
        ],
        jobs,
        [
            (5, 1, lambda dd, tt: (pl.ds(q_lat, CODE_LANES),)),
            (6, 2, lambda dd, tt: (pl.ds(0, CODE_LANES),)),
            (7, 3, lambda dd, tt: (pl.ds(width, CODE_LANES),)),
            (9, 6, rows_at(0, ffn_rows_each, ffn_rows_each)),
            (11, 7, rows_at(0, ffn_rows_each, ffn_rows_each)),
        ],
        [
            (n_dp, shares, share_rows, q_lat + kv_all),
            (q_lat + CODE_LANES, heads * HEAD_LANES),
            (CODE_LANES + kv_lat, heads * HEAD_LANES),
            (aug, heads * VALUE_HEAD_DIM),
            (2 * n_t * rows, aug),
            (n_dp, 16, 128),
            (aug, ffn_wide[0]),
            (aug, ffn_wide[1]),
        ],
        "gather_weights",
        1,
        riders=[ride_one(6, 9, 10, 0, ffn_rows_each)],
        rider_round=1,
    )
    set_all = set_marks[:, 0, 0].astype(jnp.int32)
    set_peer = lax.dynamic_index_in_dim(set_all, jnp.bitwise_xor(d, pair), 0, keepdims=False)
    set_even = jnp.where(first, set_own, set_peer)
    set_odd = jnp.where(first, set_peer, set_own)
    w_down = w_down.reshape(width, q_lat + kv_all)
    zero_codes = jnp.zeros((RANK, half), BF16)

    def half_of(value):
        left, right = halves(value)
        return jnp.where(first, left, right)

    extra_parts = []
    for which in (set_even, set_odd):
        gate_b = half_of(pick(gate_up_adapter_out[0], which)) * 2
        up_b = half_of(pick(gate_up_adapter_out[1], which)) * 2
        down_a_t = half_of(pick(turned(down_adapter_in), which))
        extra_parts.append((gate_b, up_b, down_a_t))
    ffn_extra = []
    for chunk in range(chunks):
        extra = []
        for gate_b, up_b, down_a_t in extra_parts:
            extra.append(columns(gate_b, zero_codes, down_a_t, chunk))
            extra.append(columns(zero_codes, up_b, zero_codes, chunk))
        extra.append(jnp.zeros((CODE_LANES - 4 * RANK, extra[0].shape[1]), BF16))
        ffn_extra.append(jnp.concatenate(extra, axis=0))
    cut_a = ffn_rows_each // 64 * 16
    cut_b = ffn_rows_each // 48 * 32

    cos_part, sin_part = rope_tables(document_numbers)
    zeros_l = jnp.zeros((length, PLAIN_HEAD_DIM), F32)
    zeros_r = jnp.zeros((length, HEAD_LANES - 96), F32)
    none_16 = jnp.zeros_like(sin_part)
    rope = jnp.stack(
        [
            jnp.concatenate([zeros_l + 1.0, cos_part, cos_part, zeros_r], axis=1),
            jnp.concatenate([zeros_l, -sin_part, none_16, zeros_r], axis=1),
            jnp.concatenate([zeros_l, none_16, sin_part, zeros_r], axis=1),
        ],
        axis=0,
    )
    lane_ids = jnp.arange(HEAD_LANES, dtype=jnp.int32)[None, :]
    doc_lane = (lane_ids >= DOC_LANE) & (lane_ids < DOC_LANE + DOC_SLOTS)
    is_doc = document_numbers[0][:, None] == lane_ids - DOC_LANE
    doc_q = narrow(jnp.where(doc_lane & is_doc, 1.0, 0.0))
    doc_k = jnp.where(
        doc_lane & ~is_doc, -BIG, jnp.where((lane_ids >= 96) & (lane_ids < 99), 1.0, 0.0)
    )

    residual = inputs[0].astype(F32)
    attn_normed, attn_scale = normalize(residual, attention_norm_gain)
    attn_rows = narrow(attn_normed)
    down_in = jnp.concatenate([qa_in, kva_in], axis=0)
    down_codes_in = narrow(dot_nt(attn_rows, down_in))
    down_b_rows = jnp.concatenate(
        [
            jnp.pad(qa_out, ((0, 0), (0, kv_all))),
            jnp.pad(kva_out, ((0, 0), (q_lat, 0))),
        ],
        axis=0,
    )
    latent = dot_nn(attn_rows, w_down) + ADAPT_SCALE * dot_nn(down_codes_in, down_b_rows)
    q_latent = latent[:, :q_lat]
    kv_latent = latent[:, q_lat : q_lat + kv_lat]
    q_normed, q_scale = normalize(q_latent, query_latent_gain)
    kv_normed, kv_scale = normalize(kv_latent, keyvalue_latent_gain)
    q_input = narrow(q_normed)
    kv_input = narrow(kv_normed)
    pe_input = narrow(latent[:, q_lat + kv_lat :])
    qb_codes = narrow(dot_nt(q_input, qb_in))
    kvb_codes = narrow(dot_nt(kv_input, kvb_in))
    pe_at = q_lat + 2 * RANK
    lat_own = jnp.concatenate(
        [
            q_input,
            qb_codes,
            kvb_codes,
            pe_input,
            jnp.zeros((rows, CODE_LANES - 2 * RANK - ROTARY_DIM), BF16),
            kv_input,
        ],
        axis=1,
    )

    def token_jobs(src, out, parts):
        count = rows // parts
        return [
            dict(
                src=src,
                src_at=pl.ds(n * count, count),
                out=out,
                out_at=lambda dd, tt, n=n: (
                    pl.ds(pl.multiple_of(tt * rows + n * count, 16), count),
                ),
                steps=t_slow + t_core,
            )
            for n in range(parts)
        ]

    lat_all, w_ffn0, w_ffn1 = remote_gather(
        [lat_own, ffn_extra[0], ffn_extra[1], w_ffn0, w_ffn1, ffn_mine[1], ffn_other[1]],
        token_jobs(0, 0, 2),
        [
            (1, 1, lambda dd, tt: (pl.ds(width, CODE_LANES),)),
            (2, 2, lambda dd, tt: (pl.ds(width, CODE_LANES),)),
        ],
        [(length, lat_own.shape[1]), (aug, ffn_wide[0]), (aug, ffn_wide[1])],
        "gather_latents",
        2,
        riders=[ride_two(1, 0), ride_one(2, 5, 6, 0, cut_a)],
        aliases={3: 1, 4: 2},
        distant=(5, 6),
    )
    pe_rows = lat_all[:, pe_at : pe_at + ROTARY_DIM].astype(F32)
    pe_a, pe_b = pe_rows[:, : ROTARY_DIM // 2], pe_rows[:, ROTARY_DIM // 2 :]
    pe_aug = narrow(
        jnp.concatenate(
            [
                zeros_l,
                pe_a * cos_part - pe_b * sin_part,
                pe_b * cos_part + pe_a * sin_part,
                zeros_r,
            ],
            axis=1,
        )
        + doc_k
    )
    q_aug, kv, head_out, w_ffn0, w_ffn1 = attend(
        lat_all,
        w_q,
        w_kv,
        rope,
        pe_aug,
        doc_q,
        q_lat + CODE_LANES,
        q_lat,
        [ride_two(0, 1), ride_one(1, 2, 3, cut_a, cut_b - cut_a)],
        [w_ffn0, w_ffn1],
        [ffn_mine[1], ffn_other[1]],
    )
    tensor_keys = [(0, r) for r in reversed(range(0, n_t, 2))]

    def token_rows(key, place):
        at = jnp.bitwise_xor(place["tensor"], key[1]) * rows
        return pl.ds(pl.multiple_of(at, 16), rows)

    def out_term(held, place, key):
        return dot_nt(held[0][token_rows(key, place), :], held[1][...])

    attn_sum, w_ffn0, w_ffn1 = remote_reduce(
        [head_out, w_out],
        [head_out.shape, w_out.shape],
        out_term,
        tensor_keys,
        [t_slow[::-1]],
        rows,
        aug,
        "reduce_out",
        3,
        riders=[ride_two(0, z) for z in range(2, z_count)]
        + [ride_one(1, 2, 3, cut_b, ffn_rows_each - cut_b)],
        ridden=[w_ffn0, w_ffn1],
        carried=[ffn_mine[1], ffn_other[1]],
    )
    out_codes = narrow(attn_sum[:, width : width + RANK])
    middle = residual + RESIDUAL * (
        attn_sum[:, :width] + ADAPT_SCALE * dot_nn(out_codes, out_out)
    )

    ffn_normed, ffn_scale = normalize(middle, feedforward_norm_gain)
    ffn_rows = narrow(ffn_normed)
    gu_codes = narrow(dot_nt(ffn_rows, gu_in))
    x_own = jnp.concatenate([ffn_rows, code_lanes(gu_codes)], axis=1)

    def group_block_of(key, place):
        return group_block(
            jnp.bitwise_xor(place["dp"], key[0]), jnp.bitwise_xor(place["tensor"], key[1])
        )

    x_codes, grads, hids, ffn_weights = remote_ffn(
        x_own,
        g_all,
        [w_ffn0, w_ffn1],
        mains,
        tail,
        tail_wide,
        t_slow + [("dp", pair)],
        group_block_of,
        [ride_two(1, z) for z in range(z_count)],
        "feed_forward",
        4,
    )
    group_keys = [(p, r) for p in (pair, 0) for r in reversed(range(0, n_t, 2))]
    ffn_in_sum, down_chip = remote_ffn_back(
        grads,
        hids,
        ffn_weights,
        mains,
        tail_wide,
        group_keys,
        [group_a[::-1], group_b[::-1]],
        group_block_of,
        rows,
        "feed_forward_back",
        5,
    )
    gu_code_grad = narrow(own_codes(ffn_in_sum))
    ffn_in_grad = ffn_in_sum[:, :width] + dot_nn(gu_code_grad, gu_in)
    middle_grad = out_grad + normalize_back(
        middle, ffn_scale, feedforward_norm_gain, ffn_in_grad
    )
    attn_grad = narrow(RESIDUAL * middle_grad)
    out_code_grad = narrow(ADAPT_SCALE * dot_nt(attn_grad, out_out))
    attn_grad_aug = jnp.concatenate(
        [attn_grad, out_code_grad, jnp.zeros((rows, CODE_LANES - RANK), BF16)], axis=1
    )

    ride_down = n_t == 4
    sent = remote_gather(
        [attn_grad_aug] + ([down_chip] if ride_down else []),
        token_jobs(0, 0, 2),
        [],
        [(length, aug)] + ([(rows, aug)] if ride_down else []),
        "gather_grad",
        6,
        riders=[dict(kind="plain", src=1, src_at=0, out=1, step=("dp", pair))] if ride_down else [],
        distant=(1,),
    )
    grad_all = sent[0]
    heads_grad = narrow(dot_nn(grad_all, w_out))
    out_a = dot_tn(grad_all[:, width:], head_out)[:RANK]
    if ride_down:
        down_far = narrow(down_chip[2].astype(F32) + sent[1].astype(F32))
        dq, dkv, dpe, came_pair, came_y = attend_back(
            q_aug,
            kv,
            head_out,
            heads_grad,
            rope,
            pe_aug,
            [
                dict(kind="plain", src=0, src_at=1, out=0, step=("dp", pair)),
                dict(kind="plain", src=1, src_at=None, out=1, step=("tensor", 2)),
            ],
            [down_chip, down_far],
            [(rows, aug), (rows, aug)],
        )
        ffn_out = down_chip[3].astype(F32) + came_pair.astype(F32) + came_y.astype(F32)
    else:
        dq, dkv, dpe = attend_back(q_aug, kv, head_out, heads_grad, rope, pe_aug, [], [], [])
        places = n_t // 2
        ffn_out = down_chip[places:].astype(F32) + hop(down_chip[:places], ("dp", pair)).astype(F32)
        while places > 1:
            places //= 2
            ffn_out = ffn_out[places:] + hop(narrow(ffn_out[:places]), ("tensor", 2 * places)).astype(
                F32
            )
        ffn_out = ffn_out[0]
    down_codes = narrow(own_codes(ffn_out)[:, :RANK])
    outputs = narrow(
        middle + RESIDUAL * (ffn_out[:, :width] + ADAPT_SCALE * dot_nn(down_codes, down_out))
    )

    pe_g = dpe[:, PLAIN_HEAD_DIM : PLAIN_HEAD_DIM + ROTARY_DIM]
    pe_ga, pe_gb = pe_g[:, : ROTARY_DIM // 2], pe_g[:, ROTARY_DIM // 2 :]
    pe_grad = jnp.concatenate(
        [pe_ga * cos_part + pe_gb * sin_part, pe_gb * cos_part - pe_ga * sin_part], axis=1
    )
    pe_padded = jnp.pad(pe_grad, ((0, 0), (2 * RANK, CODE_LANES - 2 * RANK - ROTARY_DIM)))
    lat_wide = q_lat + CODE_LANES + kv_lat

    def latent_term(held, place, key):
        at = token_rows(key, place)
        from_q = dot_nt(held[0][at, :], held[2][...])
        from_kv = dot_nt(held[1][at, :], held[3][...])
        return jnp.concatenate(
            [
                from_q[:, :q_lat],
                from_q[:, q_lat:] + from_kv[:, :CODE_LANES] + held[4][at, :],
                from_kv[:, CODE_LANES:],
            ],
            axis=1,
        )

    operands = [dq, dkv, w_q, w_kv, pe_padded]
    (lat_sum,) = remote_reduce(
        operands,
        [o.shape for o in operands],
        latent_term,
        tensor_keys,
        [t_slow[::-1]],
        rows,
        lat_wide,
        "reduce_latents",
        7,
    )
    qb_code_grad = narrow(lat_sum[:, q_lat : q_lat + RANK])
    kvb_code_grad = narrow(lat_sum[:, q_lat + RANK : q_lat + 2 * RANK])
    pe_sum = lat_sum[:, pe_at : pe_at + ROTARY_DIM]
    q_norm_grad = lat_sum[:, :q_lat] + dot_nn(qb_code_grad, qb_in)
    kv_norm_grad = lat_sum[:, q_lat + CODE_LANES :] + dot_nn(kvb_code_grad, kvb_in)
    latent_grad = narrow(
        jnp.concatenate(
            [
                normalize_back(q_latent, q_scale, query_latent_gain, q_norm_grad),
                normalize_back(kv_latent, kv_scale, keyvalue_latent_gain, kv_norm_grad),
                pe_sum,
            ],
            axis=1,
        )
    )
    code_grad = narrow(ADAPT_SCALE * dot_nt(latent_grad, down_b_rows))
    attn_in_grad = dot_nt(latent_grad, w_down) + dot_nn(code_grad, down_in)
    input_grad = middle_grad + normalize_back(
        residual, attn_scale, attention_norm_gain, attn_in_grad
    )

    onehot = narrow(set_all[:, None] == jnp.arange(group_count, dtype=jnp.int32)[None, :])

    def to_sets(terms):
        return jnp.einsum("sk,srn->krn", onehot, terms, preferred_element_type=F32)

    def dp_job(src, out):
        return dict(src=src, out=out, out_at=lambda dd, tt: (dd,), steps=outer_first)

    t_steps = t_core + t_slow[::-1]

    gu_a = dot_tn(gu_code_grad, ffn_rows)
    out_b = ADAPT_SCALE * dot_tn(out_codes, attn_grad)
    down_b = ADAPT_SCALE * dot_tn(down_codes, ffn_grad)
    early_terms = jnp.concatenate([gu_a, out_b, down_b], axis=0)

    def uncolumn(parts, at_tail, first_at):
        out = [parts[c][:, first_at(c) : first_at(c) + mains[c]] for c in range(chunks)]
        if tail:
            at = mains[-1] + at_tail * tail
            out.append(parts[-1][:, at : at + tail])
        return jnp.concatenate(out, axis=1)

    g_codes = g_all[:, width:]
    gu_b = [dot_tn(x_codes, g) for g in grads]
    down_at = [dot_tn(g_codes, h) for h in hids]
    gate_b_all = ADAPT_SCALE * uncolumn(gu_b, 0, lambda c: 0)
    up_b_all = ADAPT_SCALE * uncolumn(gu_b, 1, lambda c: gu_wide[c] - mains[c])
    down_a_all = uncolumn(down_at, 2, lambda c: 0)
    packed = []
    for p in range(2):
        at = 2 * RANK * p
        packed += [
            gate_b_all[at : at + RANK],
            up_b_all[at + RANK : at + 2 * RANK],
            down_a_all[at : at + RANK],
        ]
    hidden_own = narrow(jnp.concatenate(packed, axis=0))
    early, hidden_terms = remote_share(
        narrow(early_terms),
        [hidden_own],
        [dp_job(1, 1)],
        [(n_dp,) + early_terms.shape, (n_dp,) + hidden_own.shape],
        n_t,
        t_steps,
        outer_first,
        "share_early",
        8,
    )
    hidden_terms = hidden_terms.reshape(2, 2, pair, 2, 3 * RANK, half)
    hidden_terms = jnp.concatenate([hidden_terms[:, 0], hidden_terms[:, 1]], axis=-1)
    hidden_terms = jnp.moveaxis(hidden_terms, 2, 1).reshape(n_dp, 3 * RANK, hidden)
    hidden_sets = to_sets(hidden_terms)

    lat_codes = lat_all[:, q_lat : q_lat + CODE_LANES]
    qb_b = ADAPT_SCALE * dot_tn(lat_codes, dq)[:RANK]
    kvb_b = ADAPT_SCALE * dot_tn(lat_codes, dkv)[RANK : 2 * RANK]
    head_own = narrow(jnp.concatenate([qb_b, kvb_b, out_a], axis=1))
    down_in_terms = dot_tn(code_grad, attn_rows)
    b_terms = ADAPT_SCALE * dot_tn(down_codes_in, latent_grad)
    qb_a = dot_tn(qb_code_grad, q_input)
    kvb_a = dot_tn(kvb_code_grad, kv_input)
    small = jnp.concatenate([b_terms[:RANK, :q_lat], b_terms[RANK:, q_lat:], qb_a, kvb_a], axis=1)
    small_wide = small.shape[1]
    small = jnp.pad(small, ((0, RANK), (0, width - small_wide)))
    late_terms = jnp.concatenate([down_in_terms, small], axis=0)
    late, head_terms = remote_share(
        narrow(late_terms),
        [head_own],
        [dp_job(1, 1)],
        [(n_dp,) + late_terms.shape, (n_dp,) + head_own.shape],
        n_t,
        t_steps,
        outer_first,
        "share_late",
        9,
    )
    head_sets = to_sets(head_terms)
    wide = heads * HEAD_LANES
    qb_b_grad = head_sets[:, :, :wide].reshape(group_count, RANK, heads, HEAD_LANES)[..., :head_q]
    qb_b_grad = qb_b_grad.reshape(group_count, RANK, heads * head_q)
    kvb_b_grad = head_sets[:, :, wide : 2 * wide]
    out_a_grad = turned(head_sets[:, :, 2 * wide :])

    early_sets = to_sets(early)
    late_sets = to_sets(late)
    gu_a_grad = jnp.stack(
        [turned(early_sets[:, :RANK]), turned(early_sets[:, RANK : 2 * RANK])], axis=0
    )
    late_small = late_sets[:, 2 * RANK : 3 * RANK]
    at = [0, q_lat, q_lat + kv_all, 2 * q_lat + kv_all, small_wide]
    return (
        outputs[None],
        input_grad[None],
        turned(late_sets[:, :RANK]),
        late_small[:, :, at[0] : at[1]],
        turned(late_sets[:, RANK : 2 * RANK]),
        late_small[:, :, at[1] : at[2]],
        turned(late_small[:, :, at[2] : at[3]]),
        qb_b_grad,
        turned(late_small[:, :, at[3] : at[4]]),
        kvb_b_grad,
        out_a_grad,
        early_sets[:, 2 * RANK : 3 * RANK],
        gu_a_grad,
        jnp.stack([hidden_sets[:, :RANK], hidden_sets[:, RANK : 2 * RANK]], axis=0),
        turned(hidden_sets[:, 2 * RANK :]),
        early_sets[:, 3 * RANK :],
    )


def solution(mesh):
    return jax.shard_map(
        functools.partial(per_device, mesh.shape["dp"], mesh.shape["tensor"]),
        mesh=mesh,
        in_specs=(
            P("dp", "tensor", None),
            P("dp", "tensor", None),
            P("dp", None),
            P("dp"),
            P(),
            P(),
            P(),
            P(),
            P("dp", None),
            P("dp", None),
            P("dp", "tensor"),
            P("dp", "tensor"),
            P("tensor", "dp"),
            P(None, "dp", "tensor"),
            P("tensor", "dp"),
            P(),
            P(),
            P(),
            P(),
            P(),
            P(None, None, "tensor"),
            P(),
            P(None, None, "tensor"),
            P(None, "tensor", None),
            P(),
            P(),
            P(None, None, None, "tensor"),
            P(None, "tensor", None),
            P(),
        ),
        out_specs=(
            P("dp", "tensor", None),
            P("dp", "tensor", None),
            P(),
            P(),
            P(),
            P(),
            P(),
            P(None, None, "tensor"),
            P(),
            P(None, None, "tensor"),
            P(None, "tensor", None),
            P(),
            P(),
            P(None, None, None, "tensor"),
            P(None, "tensor", None),
            P(),
        ),
        check_vma=False,
    )
```

```python
import functools
import math

import jax
import jax.numpy as jnp
from jax import lax
from jax.experimental import pallas as pl
from jax.experimental.pallas import tpu as pltpu
from jax.sharding import PartitionSpec as P

PLAIN_HEAD_DIM = 64
ROTARY_DIM = 32
VALUE_HEAD_DIM = 64
HEAD_LANES = 128
CODE_LANES = 128
RANK = 16
BLOCK_Q = 256
DOC_LANE = 99
DOC_SLOTS = 24

NORM_EPS = 1e-05
RESIDUAL = 1.4 / math.sqrt(62.0)
ADAPT_SCALE = 2.0
SCORE_SCALE = 1.0 / math.sqrt(PLAIN_HEAD_DIM + ROTARY_DIM)
EXP2_SCALE = SCORE_SCALE * math.log2(math.e)
BIG = 1e30
VMEM_LIMIT = 60 * 1024 * 1024
FREE = pl.CostEstimate(flops=0, bytes_accessed=0, transcendentals=0)
F32 = jnp.float32
BF16 = jnp.bfloat16


def narrow(value):
    return value.astype(BF16)


def dot_nn(a, b):
    return lax.dot_general(a, b, (((1,), (0,)), ((), ())), preferred_element_type=F32)


def dot_nt(a, b):
    return lax.dot_general(a, b, (((1,), (1,)), ((), ())), preferred_element_type=F32)


def dot_tn(a, b):
    return lax.dot_general(a, b, (((0,), (0,)), ((), ())), preferred_element_type=F32)


def normalize(value, gain_vec):
    scale_inv = lax.rsqrt(jnp.mean(value * value, axis=-1, keepdims=True) + NORM_EPS)
    return (value * scale_inv * gain_vec, scale_inv)


def normalize_back(value, scale_inv, gain_vec, grad_in):
    weighted = grad_in * gain_vec
    return scale_inv * weighted - value * scale_inv**3 * jnp.mean(
        value * weighted, axis=-1, keepdims=True
    )


def rope_tables(segments):
    places = jnp.arange(segments.shape[-1], dtype=jnp.int32)
    begins = jnp.concatenate(
        [jnp.ones_like(segments[:, :1]), (segments[:, 1:] != segments[:, :-1]).astype(jnp.int32)],
        axis=1,
    )
    first_place = lax.cummax(places[None, :] * begins, axis=1)
    offsets = (places[None, :] - first_place).astype(F32)
    inv_freq = 10000.0 ** (-2.0 * jnp.arange(ROTARY_DIM // 2, dtype=F32) / ROTARY_DIM)
    angles = offsets[..., None] * inv_freq
    return (jnp.cos(angles)[0], jnp.sin(angles)[0])


def swap(value, axis, bit, size):
    return lax.ppermute(value, axis, [(i, i ^ bit) for i in range(size)])


class Links:
    def __init__(self, send_sems, recv_sems):
        self.send_sems, self.recv_sems = send_sems, recv_sems
        self.place = {"dp": lax.axis_index("dp"), "tensor": lax.axis_index("tensor")}
        self.copies = []
        self.waited = set()

    def peer(self, step):
        place = dict(self.place)
        place[step[0]] = jnp.bitwise_xor(place[step[0]], step[1])
        return (place["dp"], place["tensor"])

    def greet(self, steps):
        barrier = pltpu.get_barrier_semaphore()
        for step in steps:
            pl.semaphore_signal(
                barrier, inc=1, device_id=self.peer(step), device_id_type=pl.DeviceIdType.MESH
            )
        pl.semaphore_wait(barrier, len(steps))

    def prepare(self, src, dst, step):
        n = len(self.copies)
        copy = pltpu.make_async_remote_copy(
            src_ref=src,
            dst_ref=dst,
            send_sem=self.send_sems.at[n],
            recv_sem=self.recv_sems.at[n],
            device_id=self.peer(step),
            device_id_type=pl.DeviceIdType.MESH,
        )
        self.copies.append(copy)
        return n

    def send(self, src, dst, step):
        n = self.prepare(src, dst, step)
        self.copies[n].start()
        return n

    def arrived(self, n):
        if n not in self.waited:
            self.copies[n].wait_recv()
            self.waited.add(n)

    def close(self):
        for n, copy in enumerate(self.copies):
            self.arrived(n)
            copy.wait_send()


class Riders:
    def __init__(self, links, riders, in_refs, out_refs):
        self.links = links
        self.rounds = []
        d = links.place["dp"]
        for rider in riders:
            full = out_refs[rider["out"]]
            if rider["kind"] == "plain":
                src = in_refs[rider["src"]]
                if rider["src_at"] is not None:
                    src = src.at[rider["src_at"]]
                self.add(0, src, full, rider["step"])
                continue
            count, pair, high = rider["count"], rider["pair"], rider["high"]
            if rider["kind"] == "one":
                begin, size = rider["rows"]
                here = full.at[pl.ds(pl.multiple_of(d * count + begin, 16), size)]
                for name, bit in (("other", pair), ("mine", high), ("other", high ^ pair)):
                    src = in_refs[rider[name]].at[pl.ds(begin, size)]
                    self.add(0, src, here, ("dp", bit))
            else:
                held = [0]
                for k, step in enumerate(rider["steps"]):
                    for key in list(held):
                        place = jnp.bitwise_xor(d, rider["z"] * pair + key)
                        at = pl.multiple_of(place * count, 16)
                        here = full.at[pl.ds(at, count)]
                        self.add(k, here, here, step)
                        held.append(key ^ step[1])

    def add(self, k, src, dst, step):
        while len(self.rounds) <= k:
            self.rounds.append([])
        self.rounds[k].append(self.links.prepare(src, dst, step))

    def start(self):
        if self.rounds:
            for n in self.rounds[0]:
                self.links.copies[n].start()

    def finish(self):
        for k, numbers in enumerate(self.rounds):
            if k:
                for n in numbers:
                    self.links.copies[n].start()
            for n in numbers:
                self.links.arrived(n)


def rider_steps(riders):
    steps = []
    for rider in riders:
        if rider["kind"] == "plain":
            steps.append(rider["step"])
        elif rider["kind"] == "one":
            pair, high = rider["pair"], rider["high"]
            steps += [("dp", pair), ("dp", high), ("dp", high ^ pair)]
        else:
            steps += rider["steps"]
    return steps


def rider_count(riders):
    total = 0
    for rider in riders:
        if rider["kind"] == "plain":
            total += 1
        elif rider["kind"] == "one":
            total += 3
        else:
            total += (1 << len(rider["steps"])) - 1
    return total


def distinct(steps):
    out = []
    for step in steps:
        if step not in out:
            out.append(step)
    return out


def flip(key, step):
    return (key[0] ^ step[1], key[1]) if step[0] == "dp" else (key[0], key[1] ^ step[1])


def has_bit(key, step):
    return bool((key[0] if step[0] == "dp" else key[1]) & step[1])


def gather_count(jobs):
    return sum((1 << len(job["steps"])) - 1 for job in jobs)


def gather_rounds(links, src_refs, out_refs, jobs):
    d, t = links.place["dp"], links.place["tensor"]

    def landing(job, key):
        at = job["out_at"](jnp.bitwise_xor(d, key[0]), jnp.bitwise_xor(t, key[1]))
        return out_refs[job["out"]].at[at]

    state = []
    for job in jobs:
        src = src_refs[job["src"]]
        if job.get("src_at") is not None:
            src = src.at[job["src_at"]]
        state.append({(0, 0): (src, None)})
    for k in range(max(len(job["steps"]) for job in jobs)):
        for job, held in zip(jobs, state):
            if k >= len(job["steps"]):
                continue
            step = job["steps"][k]
            for key in list(held):
                src, came = held[key]
                if came is not None:
                    links.arrived(came)
                n = links.send(src, landing(job, key), step)
                new = flip(key, step)
                held[new] = (landing(job, new), n)
        yield k


def remote_gather(
    sources,
    jobs,
    extra,
    outs,
    name,
    collective_id,
    riders=(),
    aliases=(),
    distant=(),
    order=(),
    near_outs=(),
    scratch=(),
    work=None,
    late=(),
):
    steps = distinct([s for job in jobs for s in job["steps"]] + rider_steps(riders))
    count = gather_count(jobs) + rider_count(riders)
    aliases = dict(aliases)
    n_src, n_out, n_near = len(sources), len(outs), len(near_outs)

    def kernel(*refs):
        src_refs, refs = refs[:n_src], refs[n_src:]
        out_refs, refs = refs[:n_out], refs[n_out:]
        near, refs = refs[: n_near + len(scratch)], refs[n_near + len(scratch) :]
        send_sems, recv_sems, local_sems = refs
        all_src, all_out = list(src_refs) + list(near), list(out_refs) + list(near)
        links = Links(send_sems, recv_sems)
        d, t = links.place["dp"], links.place["tensor"]
        links.greet(steps)
        ride = Riders(links, riders, src_refs, out_refs)
        local = []

        def keep(src, where):
            copy = pltpu.make_async_copy(src, where, local_sems.at[len(local)])
            copy.start()
            local.append(copy)
            return copy

        for src, out, at in extra:
            keep(all_src[src], all_out[out].at[at(d, t)])
        groups = {}
        for job in jobs:
            groups.setdefault(job.get("group", 0), []).append(job)
        turns = {}
        sent = {g: [] for g in groups}
        kept = {g: [] for g in groups}

        def advance(group):
            before = len(links.copies)
            if group not in turns:
                turns[group] = gather_rounds(links, all_src, all_out, groups[group])
                for job in groups[group]:
                    src = all_src[job["src"]]
                    if job.get("src_at") is not None:
                        src = src.at[job["src_at"]]
                    kept[group].append(keep(src, all_out[job["out"]].at[job["out_at"](d, t)]))
            going = next(turns[group], None) is not None
            sent[group] += range(before, len(links.copies))
            return going

        waited = set()
        if "ride" not in order:
            ride.start()
        for turn in order:
            if turn == "ride":
                ride.start()
            elif turn == "work":
                work(all_src)
                for src, out in late:
                    keep(all_src[src], all_out[out])
            elif isinstance(turn, tuple):
                for n in sent[turn[1]]:
                    links.arrived(n)
                for copy in kept[turn[1]]:
                    copy.wait()
                waited.add(turn[1])
            else:
                advance(turn)
        for group in groups:
            while advance(group):
                pass
        ride.finish()
        links.close()
        done = [copy for group in waited for copy in kept[group]]
        for copy in local:
            if not any(copy is other for other in done):
                copy.wait()

    vmem = pl.BlockSpec(memory_space=pltpu.VMEM)
    far = pl.BlockSpec(memory_space=pl.ANY)
    return pl.pallas_call(
        kernel,
        out_shape=[jax.ShapeDtypeStruct(o, BF16) for o in outs] + list(near_outs),
        in_specs=[far if n in aliases or n in distant else vmem for n in range(n_src)],
        out_specs=[far] * n_out + [vmem] * n_near,
        scratch_shapes=[pltpu.VMEM(o.shape, o.dtype) for o in scratch]
        + [
            pltpu.SemaphoreType.DMA((count,)),
            pltpu.SemaphoreType.DMA((count,)),
            pltpu.SemaphoreType.DMA((len(jobs) + len(extra) + len(late),)),
        ],
        input_output_aliases=aliases,
        compiler_params=pltpu.CompilerParams(
            collective_id=collective_id, has_side_effects=True, vmem_limit_bytes=VMEM_LIMIT
        ),
        cost_estimate=FREE,
        name=name,
    )(*sources)


def reduce_plan(keys, ways):
    plan = []
    for w, steps in enumerate(ways):
        live = list(keys)
        for k, step in enumerate(steps):
            plan += [(w, k, key) for key in live if has_bit(key, step)]
            live = [key for key in live if not has_bit(key, step)]
    return plan


def remote_reduce(
    operands, fetched, term, keys, ways, rows, wide, name, collective_id, riders=(), ridden=(), carried=(), jobs=(), job_sources=(), job_outs=()
):
    core_step = ("tensor", 1)
    part = rows // len(ways)
    plan = reduce_plan(keys, ways)
    slot = {entry: n for n, entry in enumerate(plan)}
    steps = distinct(
        [core_step]
        + [s for s in ways[0]]
        + rider_steps(riders)
        + [s for job in jobs for s in job["steps"]]
    )
    count = len(keys) + len(plan) + rider_count(riders) + gather_count(jobs)
    n_in = len(operands)
    n_ride = n_in + len(ridden) + len(carried)
    n_all = n_ride + len(job_sources)
    n_jobs = len(job_outs)

    def kernel(*refs):
        in_refs = refs[:n_in]
        out_ref = refs[n_all]
        ride_in = refs[n_in:n_ride]
        job_in = refs[n_ride:n_all]
        ride_out = refs[n_all + 1 : n_all + 1 + len(ridden)]
        job_out = refs[n_all + 1 + len(ridden) : n_all + 1 + len(ridden) + n_jobs]
        scratch = refs[n_all + 1 + len(ridden) + n_jobs :]
        held = scratch[:n_in]
        core_out, core_in, chip, hop_out, hop_in, send_sems, recv_sems, in_sems, job_sems = scratch[
            n_in:
        ]
        started = []
        for n in range(n_in):
            shape = fetched[n]
            src = in_refs[n].at[tuple(pl.ds(0, s) for s in shape)]
            copy = pltpu.make_async_copy(src, held[n], in_sems.at[n])
            copy.start()
            started.append(copy)
        links = Links(send_sems, recv_sems)
        links.greet(steps)
        ride = Riders(links, riders, ride_in, ride_out)
        ride.start()
        rounds = gather_rounds(links, job_in, job_out, jobs) if jobs else iter(())
        next(rounds, None)
        placed = []
        for n, job in enumerate(jobs):
            at = job["out_at"](links.place["dp"], links.place["tensor"])
            copy = pltpu.make_async_copy(
                job_in[job["src"]], job_out[job["out"]].at[at], job_sems.at[n]
            )
            copy.start()
            placed.append(copy)
        for copy in started:
            copy.wait()
        came = {}

        def send_part(w, k, key):
            entry = (w, k, key)
            came[entry] = links.send(hop_out.at[slot[entry]], hop_in.at[slot[entry]], ways[w][k])

        def so_far(w, k, key):
            total = chip[keys.index(key), w * part : (w + 1) * part, :]
            for j in range(k):
                entry = (w, j, flip(key, ways[w][j]))
                links.arrived(came[entry])
                total = total + hop_in[slot[entry]].astype(F32)
            return total

        for i, key in enumerate(keys):
            core_out[i] = narrow(term(held, links.place, (key[0], key[1] ^ 1)))
            crossing = links.send(core_out.at[i], core_in.at[i], core_step)
            mine = term(held, links.place, key)
            links.arrived(crossing)
            chip[i] = mine + core_in[i].astype(F32)
            for w, way in enumerate(ways):
                if way and has_bit(key, way[0]):
                    hop_out[slot[(w, 0, key)]] = narrow(chip[i, w * part : (w + 1) * part, :])
                    send_part(w, 0, key)
            next(rounds, None)
        for k in range(1, len(ways[0])):
            for w in range(len(ways)):
                for entry in plan:
                    if entry[0] == w and entry[1] == k:
                        hop_out[slot[entry]] = narrow(so_far(w, k, entry[2]))
                        send_part(w, k, entry[2])
        for w in range(len(ways)):
            out_ref[w * part : (w + 1) * part, :] = so_far(w, len(ways[w]), (0, 0))
        for _ in rounds:
            pass
        ride.finish()
        links.close()
        for copy in placed:
            copy.wait()

    any_spec = pl.BlockSpec(memory_space=pl.ANY)
    return pl.pallas_call(
        kernel,
        out_shape=[jax.ShapeDtypeStruct((rows, wide), F32)]
        + [jax.ShapeDtypeStruct(r.shape, r.dtype) for r in ridden]
        + [jax.ShapeDtypeStruct(o, BF16) for o in job_outs],
        in_specs=[any_spec] * n_ride + [pl.BlockSpec(memory_space=pltpu.VMEM)] * len(job_sources),
        out_specs=[pl.BlockSpec(memory_space=pltpu.VMEM)] + [any_spec] * (len(ridden) + n_jobs),
        input_output_aliases={n_in + n: 1 + n for n in range(len(ridden))},
        scratch_shapes=[pltpu.VMEM(s, o.dtype) for s, o in zip(fetched, operands)]
        + [
            pltpu.VMEM((len(keys), rows, wide), BF16),
            pltpu.VMEM((len(keys), rows, wide), BF16),
            pltpu.VMEM((len(keys), rows, wide), F32),
            pltpu.VMEM((max(len(plan), 1), part, wide), BF16),
            pltpu.VMEM((max(len(plan), 1), part, wide), BF16),
            pltpu.SemaphoreType.DMA((count,)),
            pltpu.SemaphoreType.DMA((count,)),
            pltpu.SemaphoreType.DMA((n_in,)),
            pltpu.SemaphoreType.DMA((max(len(jobs), 1),)),
        ],
        compiler_params=pltpu.CompilerParams(
            collective_id=collective_id, has_side_effects=True, vmem_limit_bytes=VMEM_LIMIT
        ),
        cost_estimate=FREE,
        name=name,
    )(*operands, *ridden, *carried, *job_sources)


class Share:
    def __init__(self, links, n_t, orders, source, out, own, sums, came, went, terms, fetch_sem):
        self.links, self.terms, self.own = links, terms, own
        self.fetch = pltpu.make_async_copy(source, terms, fetch_sem.at[0])
        self.sums, self.came, self.went = sums, came, went
        self.count = terms.shape[0] // n_t
        self.wide = terms.shape[1] // len(orders)
        count = self.count
        t_steps = [("tensor", 1 << b) for b in range(n_t.bit_length() - 1)]
        self.rounds = []
        live, slot = list(range(n_t)), 0
        before = []
        for k, step in enumerate(t_steps):
            sent = []
            for r in live:
                if r & step[1]:
                    src = terms.at[self.block(r)] if k == 0 else went.at[slot]
                    sent.append((r, slot, links.prepare(src, came.at[slot], step)))
                    slot += 1
            live = [r for r in live if not r & step[1]]
            self.rounds.append(functools.partial(self.scatter, k, list(live), before, sent, step))
            before = [(r ^ step[1], at, n) for r, at, n in sent]
        d, t = links.place["dp"], links.place["tensor"]

        def landing(p, key):
            rows = pl.ds(pl.multiple_of(jnp.bitwise_xor(t, key[1]) * count, 16), count)
            return out.at[p, jnp.bitwise_xor(d, key[0]), rows]

        self.places = [landing(p, (0, 0)) for p in range(len(orders))]
        held = [{(0, 0): (own.at[p], None)} for p in range(len(orders))]
        seen = set()
        for k in range(len(orders[0])):
            work = []
            for p, order in enumerate(orders):
                step = order[k]
                for key in list(held[p]):
                    src, needs = held[p][key]
                    n = links.prepare(src, landing(p, key), step)
                    work.append((None if needs in seen else needs, n))
                    seen.add(needs)
                    new = flip(key, step)
                    held[p][new] = (landing(p, new), n)
            self.rounds.append(functools.partial(self.gather, k, before, work))

    def block(self, r):
        at = jnp.bitwise_xor(self.links.place["tensor"], r) * self.count
        return pl.ds(pl.multiple_of(at, 16), self.count)

    def scatter(self, k, live, before, sent, step):
        if k == 0:
            self.fetch.start()
            self.fetch.wait()
            for r in live:
                self.sums[r] = self.terms[self.block(r), :].astype(F32)
        self.add(before)
        for r, at, n in sent:
            if k:
                self.went[at] = narrow(self.sums[r])
            self.links.copies[n].start()

    def add(self, before):
        for r, at, n in before:
            self.links.arrived(n)
            self.sums[r] = self.sums[r] + self.came[at].astype(F32)

    def gather(self, k, before, work):
        if k == 0:
            self.add(before)
            for p in range(self.own.shape[0]):
                self.own[p] = narrow(self.sums[0, :, p * self.wide : (p + 1) * self.wide])
        for needs, n in work:
            if needs is not None:
                self.links.copies[needs].wait_recv()
                self.links.waited.add(needs)
            self.links.copies[n].start()

    def keep(self, sems):
        return [
            pltpu.make_async_copy(self.own.at[p], where, sems.at[p])
            for p, where in enumerate(self.places)
        ]


def share_shapes(shape, n_t, orders):
    count, parts = shape[0] // n_t, len(orders)
    copies = n_t - 1 + parts * ((1 << len(orders[0])) - 1)
    scratch = [
        pltpu.VMEM((parts, count, shape[1] // parts), BF16),
        pltpu.VMEM((n_t, count, shape[1]), F32),
        pltpu.VMEM((n_t - 1, count, shape[1]), BF16),
        pltpu.VMEM((n_t - 1, count, shape[1]), BF16),
        pltpu.VMEM(shape, BF16),
        pltpu.SemaphoreType.DMA((1,)),
        pltpu.SemaphoreType.DMA((parts,)),
    ]
    return scratch, copies


def remote_share(terms, n_dp, n_t, orders, name, collective_id):
    scratch, copies = share_shapes(terms.shape, n_t, orders)
    parts = len(orders)

    def kernel(source, out_ref, *refs):
        own_sems, send_sems, recv_sems = refs[-3:]
        links = Links(send_sems, recv_sems)
        links.greet(orders[0])
        share = Share(links, n_t, orders, source, out_ref, *refs[:-3])
        for one in share.rounds:
            one()
        kept = share.keep(own_sems)
        for copy in kept:
            copy.start()
        links.close()
        for copy in kept:
            copy.wait()

    return pl.pallas_call(
        kernel,
        out_shape=jax.ShapeDtypeStruct((parts, n_dp, terms.shape[0], terms.shape[1] // parts), BF16),
        in_specs=[pl.BlockSpec(memory_space=pl.ANY)],
        out_specs=pl.BlockSpec(memory_space=pl.ANY),
        scratch_shapes=scratch
        + [pltpu.SemaphoreType.DMA((copies,)), pltpu.SemaphoreType.DMA((copies,))],
        compiler_params=pltpu.CompilerParams(
            collective_id=collective_id, has_side_effects=True, vmem_limit_bytes=VMEM_LIMIT
        ),
        cost_estimate=FREE,
        name=name,
    )(terms)


def set_sums(set_ids, sources, acc_shape, add, outs, put, groups, name):
    n_src = len(sources)
    count = set_ids.shape[0]

    def kernel(ids_ref, *refs):
        src_refs, out_refs, acc = refs[:n_src], refs[n_src:-1], refs[-1]
        k = pl.program_id(0)
        acc[...] = jnp.zeros_like(acc)
        for s in range(count):

            @pl.when(ids_ref[s] == k)
            def _(s=s):
                add(s, src_refs, acc)

        put(acc, out_refs)

    out_specs = []
    for before, after in outs:
        lead = len(before)
        block = tuple(before) + (1,) + tuple(after)
        out_specs.append(
            pl.BlockSpec(
                block, lambda k, ids, lead=lead, n=len(after): (0,) * lead + (k,) + (0,) * n
            )
        )
    return pl.pallas_call(
        kernel,
        grid_spec=pltpu.PrefetchScalarGridSpec(
            num_scalar_prefetch=1,
            grid=(groups,),
            in_specs=[
                pl.BlockSpec(a.shape, lambda k, ids, n=a.ndim: (0,) * n) for a in sources
            ],
            out_specs=out_specs,
            scratch_shapes=[pltpu.VMEM(acc_shape, F32)],
        ),
        out_shape=[
            jax.ShapeDtypeStruct(tuple(before) + (groups,) + tuple(after), F32)
            for before, after in outs
        ],
        compiler_params=pltpu.CompilerParams(vmem_limit_bytes=VMEM_LIMIT),
        cost_estimate=FREE,
        name=name,
    )(set_ids, *sources)


def split_three(value):
    high = narrow(value).astype(F32)
    middle = narrow(value - high).astype(F32)
    return high, middle, value - high - middle


def rope_mix(value, cos_l, sin_a, sin_b):
    return (
        value * cos_l
        + pltpu.roll(value, HEAD_LANES - ROTARY_DIM // 2, 1) * sin_a
        + pltpu.roll(value, ROTARY_DIM // 2, 1) * sin_b
    )


def attn_fwd_kernel(
    per_step, q_width, kv_at, xl_ref, wq_ref, wkv_ref, rope_ref, pe_ref, doc_ref, qa_ref, kv_ref, o_ref
):
    length = xl_ref.shape[0]
    lane = lax.broadcasted_iota(jnp.int32, (length, HEAD_LANES), 1)
    q_all = dot_nn(xl_ref[:, :q_width], wq_ref[...])
    kv_all = dot_nn(xl_ref[:, kv_at:], wkv_ref[...])
    kv_ref[...] = narrow(kv_all)
    doc_q = doc_ref[...].astype(F32)
    q_heads, k_heads, kv_turned = [], [], []
    for i in range(per_step):
        span = slice(i * HEAD_LANES, (i + 1) * HEAD_LANES)
        q_one = rope_mix(q_all[:, span], rope_ref[0], rope_ref[1], rope_ref[2]) + doc_q
        q_heads.append(narrow(q_one))
        kv_one = kv_all[:, span]
        k_heads.append(jnp.where(lane < PLAIN_HEAD_DIM, narrow(kv_one), pe_ref[...]))
        kv_turned.append(narrow(kv_one.T))
    key_at = lax.broadcasted_iota(jnp.int32, (BLOCK_Q, BLOCK_Q), 0)
    query_at = lax.broadcasted_iota(jnp.int32, (BLOCK_Q, BLOCK_Q), 1)
    row = lax.broadcasted_iota(jnp.int32, (HEAD_LANES, BLOCK_Q), 0)
    block_lane = lax.broadcasted_iota(jnp.int32, (BLOCK_Q, HEAD_LANES), 1)
    for j in range(length // BLOCK_Q):
        begin, end = j * BLOCK_Q, (j + 1) * BLOCK_Q
        mixed = []
        for i in range(per_step):
            q_part = q_heads[i][begin:end]
            scores = dot_nt(k_heads[i][:end], q_part)
            diag = jnp.where(key_at <= query_at, scores[begin:], -BIG)
            scores = diag if j == 0 else jnp.concatenate([scores[:begin], diag], axis=0)
            top = jnp.max(scores, axis=0, keepdims=True)
            terms = jnp.exp2((scores - top) * EXP2_SCALE)
            total = jnp.sum(terms, axis=0, keepdims=True)
            out_t = dot_nn(kv_turned[i][:, :end], narrow(terms)) * (1.0 / total)
            high, middle, low = split_three(top + jnp.log2(total) * (1.0 / EXP2_SCALE))
            out_t = jnp.where(
                row == 0, -high, jnp.where(row == 1, -middle, jnp.where(row == 2, -low, out_t))
            )
            out_n = out_t.T
            mixed.append(out_n)
            is_lse = (block_lane >= 96) & (block_lane < 99)
            q_saved = jnp.where(is_lse, narrow(pltpu.roll(out_n, 96, 1)), q_part)
            qa_ref[begin:end, i * HEAD_LANES : (i + 1) * HEAD_LANES] = q_saved
        if per_step == 2:
            both = jnp.where(block_lane < 64, pltpu.roll(mixed[0], 64, 1), mixed[1])
            o_ref[begin:end, :] = narrow(both)
        else:
            even = lax.rem(pl.program_id(0), 2) == 0
            moved = jnp.where(even, pltpu.roll(mixed[0], 64, 1), mixed[0])
            mine = (block_lane < 64) == even
            o_ref[begin:end, :] = jnp.where(mine, narrow(moved), o_ref[begin:end, :])


def attn_bwd_kernel(
    per_step, qa_ref, kv_ref, o_ref, do_ref, rope_ref, pe_ref, dq_ref, dkv_ref, dpe_ref, dk_acc, dv_acc
):
    length = qa_ref.shape[0]
    step = pl.program_id(0)
    lane = lax.broadcasted_iota(jnp.int32, (length, HEAD_LANES), 1)
    upper = lane >= 64
    key_at = lax.broadcasted_iota(jnp.int32, (BLOCK_Q, BLOCK_Q), 0)
    query_at = lax.broadcasted_iota(jnp.int32, (BLOCK_Q, BLOCK_Q), 1)
    causal = key_at <= query_at
    out_both = o_ref[...].astype(F32)
    grad_both = do_ref[...].astype(F32)

    @pl.when(step == 0)
    def _():
        dpe_ref[...] = jnp.zeros_like(dpe_ref)

    for i in range(per_step):
        span = slice(i * HEAD_LANES, (i + 1) * HEAD_LANES)
        if per_step == 2:
            turn = i == 0
            grad_one = pltpu.roll(grad_both, 64, 1) if turn else grad_both
            out_one = pltpu.roll(out_both, 64, 1) if turn else out_both
        else:
            even = lax.rem(step, 2) == 0
            grad_one = jnp.where(even, pltpu.roll(grad_both, 64, 1), grad_both)
            out_one = jnp.where(even, pltpu.roll(out_both, 64, 1), out_both)
        grad_one = jnp.where(upper, grad_one, 0.0)
        inner = jnp.sum(jnp.where(upper, grad_one * out_one, 0.0), axis=-1, keepdims=True)
        high, middle, low = split_three(inner)
        grad_aug = jnp.where(
            lane == 0, -high, jnp.where(lane == 1, -middle, jnp.where(lane == 2, -low, grad_one))
        )
        grad_aug = narrow(grad_aug)
        kv_one = kv_ref[:, span]
        ones = jnp.where(lane < 3, 1.0, 0.0).astype(BF16)
        v_aug = jnp.where(upper, kv_one, ones)
        k_aug = jnp.where(lane < 64, kv_one, pe_ref[...])
        k_turned = narrow(k_aug.astype(F32).T)
        for j in reversed(range(length // BLOCK_Q)):
            begin, end = j * BLOCK_Q, (j + 1) * BLOCK_Q
            q_part = qa_ref[begin:end, span]
            probs = jnp.exp2(dot_nt(k_aug[:end], q_part) * EXP2_SCALE)
            diag = jnp.where(causal, probs[begin:], 0.0)
            probs = diag if j == 0 else jnp.concatenate([probs[:begin], diag], axis=0)
            grads = narrow(probs * dot_nt(v_aug[:end], grad_aug[begin:end]))
            dq_part = dot_nn(k_turned[:, :end], grads).T * SCORE_SCALE
            dq_part = rope_mix(
                dq_part,
                rope_ref[0, begin:end, :],
                -rope_ref[1, begin:end, :],
                -rope_ref[2, begin:end, :],
            )
            dq_ref[begin:end, span] = narrow(dq_part)
            dk_part = dot_nn(grads, q_part)
            dv_part = dot_nn(narrow(probs), grad_aug[begin:end])
            if end == length:
                dk_acc[...] = dk_part
                dv_acc[...] = dv_part
            else:
                dk_acc[:end] += dk_part
                dv_acc[:end] += dv_part
        dk_all = dk_acc[...] * SCORE_SCALE
        dkv_ref[:, span] = narrow(jnp.where(upper, dv_acc[...], dk_all))
        dpe_ref[...] += jnp.where(upper & (lane < 96), dk_all, 0.0)


def ridden_call(
    kernel,
    grid,
    arrays,
    in_specs,
    out_shape,
    out_specs,
    scratch,
    riders,
    ridden,
    carried,
    fresh,
    name,
    collective_id,
):
    steps = distinct(rider_steps(riders))
    count = rider_count(riders)
    n_in, n_out = len(arrays), len(out_shape)
    n_ride_in = len(ridden) + len(carried)
    n_ride_out = len(ridden) + len(fresh)
    def body(*refs):
        own_in, rest = refs[:n_in], refs[n_in:]
        ride_in, rest = rest[:n_ride_in], rest[n_ride_in:]
        own_out, rest = rest[:n_out], rest[n_out:]
        ride_out, rest = rest[:n_ride_out], rest[n_ride_out:]
        send_sems, recv_sems = rest[-2:]
        links = Links(send_sems, recv_sems)
        ride = Riders(links, riders, ride_in, ride_out)

        @pl.when(pl.program_id(0) == 0)
        def _():
            links.greet(steps)
            ride.start()

        kernel(*own_in, *own_out, *rest[:-2])

        @pl.when(pl.program_id(0) == grid[0] - 1)
        def _():
            ride.finish()
            links.close()

    any_spec = pl.BlockSpec(memory_space=pl.ANY)
    return pl.pallas_call(
        body,
        grid=grid,
        in_specs=list(in_specs) + [any_spec] * n_ride_in,
        out_specs=list(out_specs) + [any_spec] * n_ride_out,
        out_shape=list(out_shape)
        + [jax.ShapeDtypeStruct(r.shape, r.dtype) for r in ridden]
        + [jax.ShapeDtypeStruct(f, BF16) for f in fresh],
        scratch_shapes=list(scratch)
        + [pltpu.SemaphoreType.DMA((count,)), pltpu.SemaphoreType.DMA((count,))],
        input_output_aliases={n_in + n: n_out + n for n in range(len(ridden))},
        compiler_params=pltpu.CompilerParams(
            collective_id=collective_id, has_side_effects=True, vmem_limit_bytes=VMEM_LIMIT
        ),
        cost_estimate=FREE,
        name=name,
    )(*arrays, *ridden, *carried)


def attend(latents, w_q, w_kv, rope, pe_aug, doc_q, q_width, kv_at, riders, ridden, carried):
    length = latents.shape[0]
    heads = w_q.shape[1] // HEAD_LANES
    per_step = 2 if heads % 2 == 0 else 1
    wide = per_step * HEAD_LANES
    whole = lambda a: pl.BlockSpec(a.shape, lambda h: (0,) * a.ndim)
    return ridden_call(
        functools.partial(attn_fwd_kernel, per_step, q_width, kv_at),
        (heads // per_step,),
        [latents, w_q, w_kv, rope, pe_aug, doc_q],
        [
            whole(latents),
            pl.BlockSpec((w_q.shape[0], wide), lambda h: (0, h)),
            pl.BlockSpec((w_kv.shape[0], wide), lambda h: (0, h)),
            whole(rope),
            whole(pe_aug),
            whole(doc_q),
        ],
        [
            jax.ShapeDtypeStruct((length, heads * HEAD_LANES), BF16),
            jax.ShapeDtypeStruct((length, heads * HEAD_LANES), BF16),
            jax.ShapeDtypeStruct((length, heads * VALUE_HEAD_DIM), BF16),
        ],
        [
            pl.BlockSpec((length, wide), lambda h: (0, h)),
            pl.BlockSpec((length, wide), lambda h: (0, h)),
            pl.BlockSpec((length, HEAD_LANES), lambda h: (0, h * per_step // 2)),
        ],
        [],
        riders,
        ridden,
        carried,
        [],
        "attend",
        10,
    )


def attend_back(q_aug, kv, heads_out, heads_grad, rope, pe_aug, riders, ridden, carried, fresh):
    length = q_aug.shape[0]
    heads = q_aug.shape[1] // HEAD_LANES
    per_step = 2 if heads % 2 == 0 else 1
    wide = per_step * HEAD_LANES
    whole = lambda a: pl.BlockSpec(a.shape, lambda h: (0,) * a.ndim)
    columns = pl.BlockSpec((length, wide), lambda h: (0, h))
    packed = pl.BlockSpec((length, HEAD_LANES), lambda h: (0, h * per_step // 2))
    arrays = [q_aug, kv, heads_out, heads_grad, rope, pe_aug]
    in_specs = [columns, columns, packed, packed, whole(rope), whole(pe_aug)]
    out_shape = [
        jax.ShapeDtypeStruct((length, heads * HEAD_LANES), BF16),
        jax.ShapeDtypeStruct((length, heads * HEAD_LANES), BF16),
        jax.ShapeDtypeStruct((length, HEAD_LANES), F32),
    ]
    out_specs = [columns, columns, pl.BlockSpec((length, HEAD_LANES), lambda h: (0, 0))]
    scratch = [pltpu.VMEM((length, HEAD_LANES), F32), pltpu.VMEM((length, HEAD_LANES), F32)]
    return ridden_call(
        functools.partial(attn_bwd_kernel, per_step),
        (heads // per_step,),
        arrays,
        in_specs,
        out_shape,
        out_specs,
        scratch,
        riders,
        ridden,
        carried,
        fresh,
        "attend_back",
        11,
    )


def gate_middle(gate, up, hid_grad):
    sig = 1.0 / (1.0 + jnp.exp(-gate))
    silu = gate * sig
    gate_grad = hid_grad * up * (sig * (1.0 + gate * (1.0 - sig)))
    return silu * up, gate_grad, hid_grad * silu


def tail_middle(pre, back, tail):
    wide = pre.shape[1]
    up = pltpu.roll(pre, wide - tail, 1)
    hid_grad = pltpu.roll(back, wide - 2 * tail, 1)
    hid, gate_grad, up_grad = gate_middle(pre, up, hid_grad)
    lane = lax.broadcasted_iota(jnp.int32, pre.shape, 1)
    hid = jnp.where((lane >= 2 * tail) & (lane < 3 * tail), pltpu.roll(hid, 2 * tail, 1), 0.0)
    both = jnp.where(
        lane < tail, gate_grad, jnp.where(lane < 2 * tail, pltpu.roll(up_grad, tail, 1), 0.0)
    )
    return hid, both


def remote_ffn(x_own, g_all, weights, extras, mains, tail, tail_wide, slow, block_of, riders, name, collective_id):
    rows, aug = x_own.shape
    total = g_all.shape[0]
    blocks = total // rows
    width = aug - CODE_LANES
    chunks = len(mains)
    tails = [0] * (chunks - 1) + [tail_wide]
    gu = [2 * m + w for m, w in zip(mains, tails)]
    core_step = ("tensor", 1)
    keys = [(0, 0)]
    for step in slow:
        keys += [flip(key, step) for key in keys]
    bits_of = {key: [s for s in slow if has_bit(key, s)] for key in keys}
    keys.sort(key=lambda k: len(bits_of[k]))

    def part_rows(key, step):
        n = len(bits_of[key])
        i = bits_of[key].index(step)
        size = -(-rows // (16 * n)) * 16
        begin = i * size
        return begin, min(size, rows - begin)

    count = len(keys) + sum(len(bits_of[k]) for k in keys) + rider_count(riders)
    steps = distinct([core_step] + slow + rider_steps(riders))

    def kernel(x_ref, g_ref, *refs):
        e_refs = refs[chunks : 2 * chunks]
        refs = refs[2 * chunks :]
        codes_ref = refs[0]
        grad_refs = refs[1 : 1 + chunks]
        hid_refs = refs[1 + chunks : 1 + 2 * chunks]
        w_refs = refs[1 + 2 * chunks : 1 + 3 * chunks]
        x_held, back_held, g_held = refs[1 + 3 * chunks : 4 + 3 * chunks]
        w_held = refs[4 + 3 * chunks : 4 + 4 * chunks]
        send_sems, recv_sems, w_sems, g_sems = refs[4 + 4 * chunks :]
        links = Links(send_sems, recv_sems)
        place = links.place
        fetch = [
            pltpu.make_async_copy(w_refs[c], w_held[c].at[pl.ds(0, width)], w_sems.at[c])
            for c in range(chunks)
        ]
        fetch_extra = [
            pltpu.make_async_copy(
                e_refs[c], w_held[c].at[pl.ds(width, CODE_LANES)], w_sems.at[chunks + c]
            )
            for c in range(chunks)
        ]
        fetch[0].start()
        for copy in fetch_extra:
            copy.start()
        links.greet(steps)

        def landing(key):
            return x_held.at[block_of(key, place)]

        arrivals = {key: [] for key in keys}

        def pass_on(key, src):
            for step in slow:
                if has_bit(key, step):
                    continue
                there = flip(key, step)
                begin, size = part_rows(there, step)
                at = pl.ds(begin, size)
                n = links.send(src.at[at], landing(key).at[at], step)
                arrivals[there].append(n)

        crossing = {}
        pass_on((0, 0), x_ref)
        crossing[(0, 0)] = links.send(x_ref, landing((0, 0)), core_step)
        ride = Riders(links, riders, w_refs, w_refs)
        ride.start()
        x_held[block_of((0, 0), place)] = x_ref[...]

        def g_copy(b, slot):
            at = pl.ds(pl.multiple_of(b * rows, 16), rows)
            return pltpu.make_async_copy(g_ref.at[at], g_held.at[slot], g_sems.at[slot])

        def over_blocks(work):
            g_copy(0, 0).start()

            def one(b, carry):
                slot = lax.rem(b, 2)

                @pl.when(b + 1 < blocks)
                def _():
                    g_copy(b + 1, 1 - slot).start()

                g_copy(b, slot).wait()
                work(b, g_held[slot])
                return carry

            lax.fori_loop(0, blocks, one, 0)

        fetch[0].wait()
        for copy in fetch_extra:
            copy.wait()

        def back_first(b, g_rows):
            back_held[b] = dot_nn(g_rows, w_held[0][:, gu[0] :])

        over_blocks(back_first)

        def rows_at(b):
            return pl.ds(pl.multiple_of(b * rows, 16), rows)

        def forward(b, c, back):
            main = mains[c]
            x_rows = x_held[b]
            pre = dot_nn(x_rows, w_held[c][:, : gu[c]])
            hid, gate_grad, up_grad = gate_middle(pre[:, :main], pre[:, gu[c] - main :], back)
            at = rows_at(b)
            hid_refs[c][at, :main] = narrow(hid)
            grad_refs[c][at, :main] = narrow(gate_grad)
            grad_refs[c][at, gu[c] - main :] = narrow(up_grad)
            return pre

        def first_chunk(key):
            def one(i, carry):
                other = (key[0], key[1] + i)
                b = block_of(other, place)
                forward(b, 0, back_held[b])
                return carry

            lax.fori_loop(0, 2, one, 0)

        links.arrived(crossing[(0, 0)])
        first_chunk((0, 0))
        for level in range(1, len(slow) + 1):
            here = [key for key in keys if len(bits_of[key]) == level]
            for key in here:
                for n in arrivals[key]:
                    links.arrived(n)
                pass_on(key, landing(key))
                crossing[key] = links.send(landing(key), landing(key), core_step)
            for key in here:
                links.arrived(crossing[key])
                first_chunk(key)
        ride.finish()
        for c in range(1, chunks):
            fetch[c].start()
            fetch[c].wait()

            def later(b, g_rows, c=c):
                main = mains[c]
                back = dot_nn(g_rows, w_held[c][:, gu[c] :])
                pre = forward(b, c, back)
                if tails[c]:
                    at_tail = slice(main, main + tail_wide)
                    hid, both = tail_middle(
                        pre[:, at_tail], dot_nn(g_rows, w_held[c][:, at_tail]), tail
                    )
                    at = rows_at(b)
                    hid_refs[c][at, main:] = narrow(hid)
                    grad_refs[c][at, at_tail] = narrow(both)

            over_blocks(later)
        for b in range(blocks):
            codes_ref[b * rows : (b + 1) * rows, :] = x_held[b, :, width:]
        links.close()

    any_spec = pl.BlockSpec(memory_space=pl.ANY)
    vmem_spec = pl.BlockSpec(memory_space=pltpu.VMEM)
    outs = pl.pallas_call(
        kernel,
        in_specs=[vmem_spec, any_spec] + [any_spec] * (2 * chunks),
        out_specs=[vmem_spec] * (1 + 2 * chunks) + [any_spec] * chunks,
        out_shape=[jax.ShapeDtypeStruct((total, CODE_LANES), BF16)]
        + [jax.ShapeDtypeStruct((total, g), BF16) for g in gu]
        + [jax.ShapeDtypeStruct((total, m + w), BF16) for m, w in zip(mains, tails)]
        + [jax.ShapeDtypeStruct(w.shape, BF16) for w in weights],
        scratch_shapes=[
            pltpu.VMEM((blocks, rows, aug), BF16),
            pltpu.VMEM((blocks, rows, mains[0]), F32),
            pltpu.VMEM((2, rows, aug), BF16),
        ]
        + [pltpu.VMEM((aug, w.shape[1]), BF16) for w in weights]
        + [
            pltpu.SemaphoreType.DMA((count,)),
            pltpu.SemaphoreType.DMA((count,)),
            pltpu.SemaphoreType.DMA((2 * chunks,)),
            pltpu.SemaphoreType.DMA((2,)),
        ],
        input_output_aliases={2 + c: 1 + 2 * chunks + c for c in range(chunks)},
        compiler_params=pltpu.CompilerParams(
            collective_id=collective_id, has_side_effects=True, vmem_limit_bytes=VMEM_LIMIT
        ),
        cost_estimate=FREE,
        name=name,
    )(x_own, g_all, *weights, *extras)
    return (
        outs[0],
        outs[1 : 1 + chunks],
        outs[1 + chunks : 1 + 2 * chunks],
        outs[1 + 2 * chunks :],
    )


def remote_ffn_back(
    grads, hids, weights, extras, x_codes, g_codes, mains, tail_wide, keys, ways, block_of, rows, name, collective_id
):
    width = weights[0].shape[0]
    aug = width + CODE_LANES
    chunks = len(mains)
    tails = [0] * (chunks - 1) + [tail_wide]
    gu = [2 * m + w for m, w in zip(mains, tails)]
    core_step = ("tensor", 1)
    part = rows // len(ways)
    plan = reduce_plan(keys, ways)
    later = [entry for entry in plan if entry[1] > 0]
    slot = {entry: n for n, entry in enumerate(plan)}
    later_slot = {entry: n for n, entry in enumerate(later)}
    steps = distinct([core_step] + ways[0])
    count = 2 * len(keys) + len(plan)
    operands = list(grads) + list(hids) + list(weights) + [x_codes, g_codes]
    shapes = [o.shape for o in operands]
    for c in range(chunks):
        shapes[2 * chunks + c] = (aug, weights[c].shape[1])

    def kernel(*refs):
        n_in = len(operands)
        in_refs, e_refs, refs = refs[:n_in], refs[n_in : n_in + chunks], refs[n_in + chunks :]
        refs = in_refs + refs
        out_ref, terms_ref = refs[n_in : n_in + 2]
        gu_refs = refs[n_in + 2 : n_in + 2 + chunks]
        down_refs = refs[n_in + 2 + chunks : n_in + 2 + 2 * chunks]
        held = refs[n_in + 2 + 2 * chunks : 2 * n_in + 2 + 2 * chunks]
        rest = refs[2 * n_in + 2 + 2 * chunks :]
        core_out, core_in, chip, hop_out, hop_in, stage, send_sems, recv_sems, in_sems, out_sems, free = rest
        g_held, h_held = held[:chunks], held[chunks : 2 * chunks]
        w_held = held[2 * chunks : 3 * chunks]
        started = []
        order = [n for c in range(chunks) for n in (2 * chunks + c, c)]
        order += list(range(chunks, 2 * chunks)) + [3 * chunks, 3 * chunks + 1]
        for n in order:
            is_weight = 2 * chunks <= n < 3 * chunks
            to = held[n].at[pl.ds(0, width)] if is_weight else held[n]
            copy = pltpu.make_async_copy(in_refs[n], to, in_sems.at[n])
            copy.start()
            started.append(copy)
        for c in range(chunks):
            copy = pltpu.make_async_copy(
                e_refs[c], w_held[c].at[pl.ds(width, CODE_LANES)], in_sems.at[n_in + c]
            )
            copy.start()
            started.append(copy)
        links = Links(send_sems, recv_sems)
        place = links.place
        links.greet(steps)
        for copy in started[: 2 * chunks] + started[n_in:]:
            copy.wait()
        came = {}

        def rows_of(key):
            return pl.ds(pl.multiple_of(block_of(key, place) * rows, 16), rows)

        def in_term(key):
            at = rows_of(key)
            out = dot_nt(g_held[0][at, :], w_held[0][:, : gu[0]])
            for c in range(1, chunks):
                out = out + dot_nt(g_held[c][at, :], w_held[c][:, : gu[c]])
            return out

        def down_term(key):
            at = rows_of(key)
            out = 0.0
            for c in range(chunks):
                out = out + dot_nt(h_held[c][at, : mains[c]], w_held[c][:, gu[c] :])
                if tails[c]:
                    out = out + dot_nt(
                        h_held[c][at, mains[c] :], w_held[c][:, mains[c] : mains[c] + tails[c]]
                    )
            return out

        def so_far(w, k, key):
            if key == (0, 0):
                total = out_ref[w * part : (w + 1) * part, :]
            else:
                total = chip[keys.index(key), w * part : (w + 1) * part, :].astype(F32)
            for j in range(k):
                entry = (w, j, flip(key, ways[w][j]))
                links.arrived(came[entry])
                total = total + hop_in[slot[entry]].astype(F32)
            return total

        crossings = []

        def cross(i, value):
            n = len(crossings)
            if n >= 2:
                links.copies[crossings[n - 2]].wait_send()
            core_out[n % 2] = narrow(value)
            crossings.append(links.send(core_out.at[n % 2], core_in.at[i], core_step))
            return crossings[-1]

        for i, key in enumerate(keys):
            crossing = cross(i, in_term((key[0], key[1] ^ 1)))
            mine = in_term(key)
            links.arrived(crossing)
            mine = mine + core_in[i].astype(F32)
            if key == (0, 0):
                out_ref[...] = mine
            else:
                chip[i] = narrow(mine)
                for w, way in enumerate(ways):
                    if has_bit(key, way[0]):
                        at = slice(w * part, (w + 1) * part)
                        entry = (w, 0, key)
                        came[entry] = links.send(
                            chip.at[i, pl.ds(w * part, part)], hop_in.at[slot[entry]], way[0]
                        )
        pl.semaphore_signal(
            free, inc=1, device_id=links.peer(core_step), device_id_type=pl.DeviceIdType.MESH
        )
        pl.semaphore_wait(free, 1)
        for copy in started[2 * chunks : n_in]:
            copy.wait()
        stored = []
        for i, key in enumerate(keys):
            crossing = cross(i, down_term((key[0], key[1] ^ 1)))
            mine = down_term(key)
            links.arrived(crossing)
            if i >= 2:
                stored[i - 2].wait()
            stage[i % 2] = narrow(mine + core_in[i].astype(F32))
            copy = pltpu.make_async_copy(stage.at[i % 2], terms_ref.at[i], out_sems.at[i])
            copy.start()
            stored.append(copy)
            if i == len(keys) // 2 - 1:
                for k in range(1, len(ways[0])):
                    for w in range(len(ways)):
                        for entry in plan:
                            if entry[0] == w and entry[1] == k:
                                hop_out[later_slot[entry]] = narrow(so_far(w, k, entry[2]))
                                came[entry] = links.send(
                                    hop_out.at[later_slot[entry]],
                                    hop_in.at[slot[entry]],
                                    ways[w][k],
                                )
        x_held, gc_held = held[3 * chunks :]
        for c in range(chunks):
            gu_refs[c][...] = dot_tn(x_held[...], g_held[c][...])
            down_refs[c][...] = dot_tn(gc_held[...], h_held[c][...])
        for w in range(len(ways)):
            out_ref[w * part : (w + 1) * part, :] = so_far(w, len(ways[w]), (0, 0))
        for copy in stored[max(0, len(keys) - 2) :]:
            copy.wait()
        for n, copy in enumerate(links.copies):
            links.arrived(n)
            if n not in crossings[:-2]:
                copy.wait_send()

    any_spec = pl.BlockSpec(memory_space=pl.ANY)
    return pl.pallas_call(
        kernel,
        out_shape=[
            jax.ShapeDtypeStruct((rows, aug), F32),
            jax.ShapeDtypeStruct((len(keys), rows, aug), BF16),
        ]
        + [jax.ShapeDtypeStruct((CODE_LANES, g.shape[1]), F32) for g in grads]
        + [jax.ShapeDtypeStruct((CODE_LANES, h.shape[1]), F32) for h in hids],
        in_specs=[any_spec] * (len(operands) + chunks),
        out_specs=[pl.BlockSpec(memory_space=pltpu.VMEM), any_spec]
        + [pl.BlockSpec(memory_space=pltpu.VMEM)] * (2 * chunks),
        scratch_shapes=[pltpu.VMEM(n, o.dtype) for n, o in zip(shapes, operands)]
        + [
            pltpu.VMEM((2, rows, aug), BF16),
            pltpu.VMEM((len(keys), rows, aug), BF16),
            pltpu.VMEM((len(keys) - 1, rows, aug), BF16),
            pltpu.VMEM((max(len(later), 1), part, aug), BF16),
            pltpu.VMEM((len(plan), part, aug), BF16),
            pltpu.VMEM((2, rows, aug), BF16),
            pltpu.SemaphoreType.DMA((count,)),
            pltpu.SemaphoreType.DMA((count,)),
            pltpu.SemaphoreType.DMA((len(operands) + chunks,)),
            pltpu.SemaphoreType.DMA((len(keys),)),
            pltpu.SemaphoreType.REGULAR,
        ],
        compiler_params=pltpu.CompilerParams(
            collective_id=collective_id, has_side_effects=True, vmem_limit_bytes=VMEM_LIMIT
        ),
        cost_estimate=FREE,
        name=name,
    )(*operands, *extras)


def ffn_extras(places, gate_up_out, down_in, mains, tail, tail_wide):
    half = down_in.shape[2] // 2
    chunks = len(mains)
    tails = [0] * (chunks - 1) + [tail_wide]
    wide = [3 * m + w for m, w in zip(mains, tails)]

    def kernel(places_ref, gu_ref, down_ref, *outs):
        for out in outs:
            out[...] = jnp.zeros_like(out)
        lower = places_ref[2] == 0
        for p in range(2):
            which = places_ref[p]

            def half_of(value):
                return jnp.where(lower, value[:, :half], value[:, half:])

            parts = [
                half_of(gu_ref[0, which]) * 2,
                half_of(gu_ref[1, which]) * 2,
                half_of(down_ref[which]),
            ]
            for kind, value in enumerate(parts):
                top = 2 * RANK * p + (RANK if kind == 1 else 0)
                at_rows = slice(top, top + RANK)
                begin = 0
                for c in range(chunks):
                    main = mains[c]
                    at = [0, main + tails[c], 2 * main + tails[c]][kind]
                    outs[c][at_rows, at : at + main] = value[:, begin : begin + main]
                    begin += main
                if tail:
                    at = mains[-1] + kind * tail
                    outs[-1][at_rows, at : at + tail] = value[:, begin:]

    return pl.pallas_call(
        kernel,
        grid_spec=pltpu.PrefetchScalarGridSpec(
            num_scalar_prefetch=1,
            grid=(1,),
            in_specs=[
                pl.BlockSpec(a.shape, lambda i, ids, n=a.ndim: (0,) * n)
                for a in (gate_up_out, down_in)
            ],
            out_specs=[pl.BlockSpec((CODE_LANES, w), lambda i, ids: (0, 0)) for w in wide],
        ),
        out_shape=[jax.ShapeDtypeStruct((CODE_LANES, w), BF16) for w in wide],
        compiler_params=pltpu.CompilerParams(vmem_limit_bytes=VMEM_LIMIT),
        cost_estimate=FREE,
        name="ffn_extras",
    )(places, gate_up_out, down_in)


def per_device(
    n_dp,
    n_t,
    inputs,
    cotangent,
    document_numbers,
    sequence_adapter_index,
    attention_norm_gain,
    query_latent_gain,
    keyvalue_latent_gain,
    feedforward_norm_gain,
    query_down_matrix,
    keyvalue_down_matrix,
    query_up_matrix,
    keyvalue_up_matrix,
    output_matrix,
    gate_up_matrix,
    down_matrix,
    query_down_adapter_in,
    query_down_adapter_out,
    keyvalue_down_adapter_in,
    keyvalue_down_adapter_out,
    query_up_adapter_in,
    query_up_adapter_out,
    keyvalue_up_adapter_in,
    keyvalue_up_adapter_out,
    output_adapter_in,
    output_adapter_out,
    gate_up_adapter_in,
    gate_up_adapter_out,
    down_adapter_in,
    down_adapter_out,
):
    d = lax.axis_index("dp")
    t = lax.axis_index("tensor")
    pair = n_dp // 4
    low_bits = [b for b in (1, 2, 4, 8, 16) if b < pair]
    high = n_dp // 2
    y_bits = [b for b in (2, 4, 8, 16) if b < n_t]
    zl = lax.rem(d // pair, 2)
    core = lax.rem(t, 2)
    first = zl == 0
    size = {"dp": n_dp, "tensor": n_t}
    rows = inputs.shape[1]
    width = inputs.shape[2]
    length = document_numbers.shape[1]
    q_lat = query_down_matrix.shape[1]
    kv_all = keyvalue_down_matrix.shape[1]
    kv_lat = kv_all - ROTARY_DIM
    heads = keyvalue_up_matrix.shape[1] // HEAD_LANES
    group_count = query_down_adapter_in.shape[0]
    aug = width + CODE_LANES
    half_rows = rows // 2

    def hop(value, step):
        return swap(value, step[0], step[1], size[step[0]])

    outer_first = [("dp", high), ("dp", pair)] + [("dp", b) for b in reversed(low_bits)]
    inner_first = [("dp", b) for b in low_bits] + [("dp", high), ("dp", pair)]
    t_slow = [("tensor", b) for b in reversed(y_bits)]
    t_core = [("tensor", 1)]

    set_own = sequence_adapter_index[0]

    def pick(table, index):
        return lax.dynamic_index_in_dim(table, index, 0, keepdims=False)

    def turned(table):
        return jnp.swapaxes(table, -1, -2)

    qa_in, kva_in = pick(turned(query_down_adapter_in), set_own), pick(
        turned(keyvalue_down_adapter_in), set_own
    )
    qa_out, kva_out = pick(query_down_adapter_out, set_own), pick(keyvalue_down_adapter_out, set_own)
    qb_in, kvb_in = pick(turned(query_up_adapter_in), set_own), pick(
        turned(keyvalue_up_adapter_in), set_own
    )
    qb_out, kvb_out = pick(query_up_adapter_out, set_own), pick(keyvalue_up_adapter_out, set_own)
    out_in, out_out = pick(turned(output_adapter_in), set_own), pick(output_adapter_out, set_own)
    gu_in = jnp.concatenate(
        [pick(turned(gate_up_adapter_in[0]), set_own), pick(turned(gate_up_adapter_in[1]), set_own)],
        axis=0,
    )
    down_out = pick(down_adapter_out, set_own)

    hidden = down_matrix.shape[0]
    half = hidden // 2
    tiles = half // 128
    main = tiles * 128
    tail = half - main
    tail_wide = -(-3 * tail // 128) * 128
    first_tiles = (2 * tiles + 2) // 3
    mains = [first_tiles * 128, main - first_tiles * 128]
    chunks = len(mains)
    tails = [0] * (chunks - 1) + [tail_wide]
    gu_wide = [2 * m + w for m, w in zip(mains, tails)]

    def columns(gate_part, up_part, down_part, chunk):
        begin = sum(mains[:chunk])
        at = slice(begin, begin + mains[chunk])
        out = [gate_part[:, at]]
        if tail and chunk == chunks - 1:
            out += [gate_part[:, main:], up_part[:, main:], down_part[:, main:]]
            if tail_wide > 3 * tail:
                out.append(jnp.zeros((gate_part.shape[0], tail_wide - 3 * tail), BF16))
        out += [up_part[:, at], down_part[:, at]]
        return jnp.concatenate(out, axis=1)

    def halves(value):
        return value[:, :half], value[:, half:]

    mats = [halves(gate_up_matrix[0]), halves(gate_up_matrix[1]), halves(down_matrix.T)]
    ffn_mine, ffn_other = [], []
    for chunk in range(chunks):
        left = columns(mats[0][0], mats[1][0], mats[2][0], chunk)
        right = columns(mats[0][1], mats[1][1], mats[2][1], chunk)
        ffn_mine.append(jnp.where(first, left, right))
        ffn_other.append(jnp.where(first, right, left))
    ffn_rows_each = gate_up_matrix.shape[1]
    z_count = n_dp // pair
    ffn_wide = [m.shape[1] for m in ffn_mine]

    def ride_one(out, mine, other, begin, size):
        return dict(
            kind="one",
            out=out,
            mine=mine,
            other=other,
            rows=(begin, size),
            count=ffn_rows_each,
            pair=pair,
            high=high,
        )

    def ride_two(out, z):
        return dict(
            kind="two",
            out=out,
            z=z,
            count=ffn_rows_each,
            pair=pair,
            high=high,
            steps=[("dp", b) for b in reversed(low_bits)],
        )

    def code_lanes(codes):
        none = jnp.zeros_like(codes)
        return jnp.concatenate(
            [
                jnp.where(first, codes, none),
                jnp.where(first, none, codes),
                jnp.zeros((codes.shape[0], CODE_LANES - 4 * RANK), codes.dtype),
            ],
            axis=1,
        )

    def own_codes(value):
        lanes = value[:, width:]
        return jnp.where(first, lanes[:, : 2 * RANK], lanes[:, 2 * RANK : 4 * RANK])

    out_grad = cotangent[0].astype(F32)
    ffn_grad = narrow(RESIDUAL * out_grad)
    down_code_grad = narrow(ADAPT_SCALE * dot_nt(ffn_grad, down_out))
    none16 = jnp.zeros((rows, RANK), BF16)
    g_own = jnp.concatenate(
        [ffn_grad, code_lanes(jnp.concatenate([down_code_grad, none16], axis=1))], axis=1
    )

    down_shard = query_down_matrix.shape[0]
    shares = n_t if down_shard % (16 * n_t) == 0 else 2
    share_rows = down_shard // shares
    down_wide = -(-(q_lat + kv_all) // 128) * 128
    down_pad = down_wide - q_lat - kv_all
    down_both = jnp.concatenate(
        [query_down_matrix, keyvalue_down_matrix, jnp.zeros((down_shard, down_pad), BF16)], axis=1
    )
    down_mine = lax.dynamic_index_in_dim(
        down_both.reshape(shares, share_rows, down_wide), lax.rem(t, shares), 0, keepdims=False
    )
    down_in = jnp.concatenate([qa_in, kva_in], axis=0)
    down_b_rows = jnp.concatenate(
        [
            jnp.pad(qa_out, ((0, 0), (0, down_wide - q_lat))),
            jnp.pad(kva_out, ((0, 0), (q_lat, down_pad))),
        ],
        axis=0,
    )
    qb_in_wide = jnp.pad(qb_in, ((0, CODE_LANES - RANK), (0, 0)))
    kvb_in_wide = jnp.pad(kvb_in, ((RANK, CODE_LANES - 2 * RANK), (0, 0)))
    qb_rows, kvb_rows = query_up_matrix.shape[0], keyvalue_up_matrix.shape[0]
    head_q = PLAIN_HEAD_DIM + ROTARY_DIM

    def pad_heads(value):
        split = value.reshape(value.shape[0], heads, head_q)
        return jnp.pad(split, ((0, 0), (0, 0), (0, HEAD_LANES - head_q))).reshape(
            value.shape[0], heads * HEAD_LANES
        )

    q_aug_rows = jnp.concatenate(
        [
            narrow(ADAPT_SCALE * pad_heads(qb_out)),
            jnp.zeros((CODE_LANES - RANK, heads * HEAD_LANES), BF16),
        ],
        axis=0,
    )
    kv_aug_rows = jnp.concatenate(
        [
            jnp.zeros((RANK, heads * HEAD_LANES), BF16),
            narrow(ADAPT_SCALE * kvb_out),
            jnp.zeros((CODE_LANES - 2 * RANK, heads * HEAD_LANES), BF16),
        ],
        axis=0,
    )
    out_extra = jnp.concatenate(
        [out_in, jnp.zeros((CODE_LANES - RANK, out_in.shape[1]), BF16)], axis=0
    )
    out_rows = output_matrix.shape[1]

    def rows_at(start, step, count):
        return lambda dd, tt: (pl.ds(pl.multiple_of(start + dd * step, 16), count),)

    def group_block(dd, tt):
        return lax.rem(dd // pair, 2) * n_t + tt

    def group_jobs(src, out, ways):
        return [
            dict(
                src=src,
                src_at=pl.ds(at, half_rows),
                out=out,
                out_at=lambda dd, tt, at=at: (
                    pl.ds(pl.multiple_of(group_block(dd, tt) * rows + at, 16), half_rows),
                ),
                steps=steps + t_core,
                group="rows",
            )
            for at, steps in zip((0, half_rows), ways)
        ]

    group_a = t_slow + [("dp", pair)]
    group_b = [("dp", pair)] + t_slow
    pe_at = q_lat + 2 * RANK
    lat_wide = q_lat + CODE_LANES + kv_lat

    def token_jobs(src, out, parts, group=0):
        count = rows // parts
        return [
            dict(
                src=src,
                src_at=pl.ds(n * count, count),
                out=out,
                out_at=lambda dd, tt, n=n: (
                    pl.ds(pl.multiple_of(tt * rows + n * count, 16), count),
                ),
                steps=t_slow + t_core,
                group=group,
            )
            for n in range(parts)
        ]

    def latent_work(refs):
        x_ref, norm_ref, q_norm_ref, kv_norm_ref, in_ref, b_ref, qb_ref, kvb_ref = refs[12:20]
        latent_ref, codes_ref, w_ref, own_ref = refs[20:24]
        x_f = x_ref[...].astype(F32)
        scale = lax.rsqrt(jnp.mean(x_f * x_f, axis=-1, keepdims=True) + NORM_EPS)
        h_rows = narrow(x_f * scale * norm_ref[...])
        codes = narrow(dot_nt(h_rows, in_ref[...]))
        latent = dot_nn(h_rows, w_ref[...]) + ADAPT_SCALE * dot_nn(codes, b_ref[...])
        latent_ref[...] = latent
        codes_ref[...] = codes
        q_part = latent[:, :q_lat]
        kv_part = latent[:, q_lat : q_lat + kv_lat]
        q_scale = lax.rsqrt(jnp.mean(q_part * q_part, axis=-1, keepdims=True) + NORM_EPS)
        kv_scale = lax.rsqrt(jnp.mean(kv_part * kv_part, axis=-1, keepdims=True) + NORM_EPS)
        q_in = narrow(q_part * q_scale * q_norm_ref[...])
        kv_in = narrow(kv_part * kv_scale * kv_norm_ref[...])
        own_ref[:, :q_lat] = q_in
        own_ref[:, q_lat + CODE_LANES :] = kv_in
        code_block = dot_nt(q_in, qb_ref[...]) + dot_nt(kv_in, kvb_ref[...])
        pe_block = pltpu.roll(latent[:, q_lat + kv_lat :], 2 * RANK, 1)
        lane = lax.broadcasted_iota(jnp.int32, code_block.shape, 1)
        own_ref[:, q_lat : q_lat + CODE_LANES] = narrow(
            jnp.where(lane < 2 * RANK, code_block, pe_block)
        )

    down_steps = outer_first + (t_slow if shares == n_t else []) + t_core
    n_start_outs = 9
    latent_at, w_at, lat_own_at = n_start_outs, n_start_outs + 2, n_start_outs + 3
    n_start_sources = 20
    jobs = [
        dict(
            src=0,
            out=w_at,
            out_at=lambda dd, tt: (
                pl.ds(
                    pl.multiple_of(dd * down_shard + lax.rem(tt, shares) * share_rows, 16), share_rows
                ),
            ),
            steps=down_steps,
            group="down",
        ),
        dict(src=1, out=1, out_at=rows_at(0, qb_rows, qb_rows), steps=outer_first, group="up"),
        dict(src=2, out=2, out_at=rows_at(CODE_LANES, kvb_rows, kvb_rows), steps=outer_first, group="up"),
        dict(src=8, out=5, out_at=lambda dd, tt: (dd,), steps=outer_first, group="up"),
        dict(src=3, out=3, out_at=rows_at(0, out_rows, out_rows), steps=outer_first, group="out"),
    ]
    low_steps = [("dp", b) for b in reversed(low_bits)]
    for src, out in ((9, 6), (11, 7)):
        jobs.append(
            dict(
                src=src,
                out=out,
                out_at=rows_at(0, ffn_rows_each, ffn_rows_each),
                steps=low_steps,
                group="own",
            )
        )
    jobs += group_jobs(4, 4, (group_b, group_b))
    jobs += token_jobs(n_start_sources + 3, 8, 2, "latents")
    set_mark = jnp.full((16, 128), sequence_adapter_index[0].astype(F32)).astype(BF16)
    w_down, w_q, w_kv, w_out, g_all, set_marks, w_ffn0, w_ffn1, lat_all, latent, down_codes_in = (
        remote_gather(
            [
                down_mine,
                pad_heads(query_up_matrix),
                keyvalue_up_matrix,
                output_matrix.T,
                g_own,
                q_aug_rows,
                kv_aug_rows,
                out_extra,
                set_mark,
                ffn_mine[0],
                ffn_other[0],
                ffn_mine[1],
                inputs[0],
                attention_norm_gain[None],
                query_latent_gain[None],
                keyvalue_latent_gain[None],
                down_in,
                down_b_rows,
                qb_in_wide,
                kvb_in_wide,
            ],
            jobs,
            [
                (5, 1, lambda dd, tt: (pl.ds(q_lat, CODE_LANES),)),
                (6, 2, lambda dd, tt: (pl.ds(0, CODE_LANES),)),
                (7, 3, lambda dd, tt: (pl.ds(width, CODE_LANES),)),
            ],
            [
                (width, down_wide),
                (q_lat + CODE_LANES, heads * HEAD_LANES),
                (CODE_LANES + kv_lat, heads * HEAD_LANES),
                (aug, heads * VALUE_HEAD_DIM),
                (2 * n_t * rows, aug),
                (n_dp, 16, 128),
                (width, ffn_wide[0]),
                (width, ffn_wide[1]),
                (length, lat_wide),
            ],
            "gather_start",
            1,
            riders=[ride_one(6, 9, 10, 0, ffn_rows_each)],
            order=["down", "up", "out", "down", "up", "down", "own", "out", "rows", "down"]
            + ["up", "out", "ride"]
            + ["down"] * (len(down_steps) - 4)
            + [("all", "down"), "work", "latents", "rows"]
            + ["latents"] * len(t_slow)
            + ["rows"],
            near_outs=[
                jax.ShapeDtypeStruct((rows, down_wide), F32),
                jax.ShapeDtypeStruct((rows, 2 * RANK), BF16),
            ],
            scratch=[
                jax.ShapeDtypeStruct((width, down_wide), BF16),
                jax.ShapeDtypeStruct((rows, lat_wide), BF16),
            ],
            work=latent_work,
            late=[(n_start_sources + 2, 0)],
        )
    )
    set_all = set_marks[:, 0, 0].astype(jnp.int32)
    set_peer = lax.dynamic_index_in_dim(set_all, jnp.bitwise_xor(d, pair), 0, keepdims=False)
    set_even = jnp.where(first, set_own, set_peer)
    set_odd = jnp.where(first, set_peer, set_own)
    ffn_extra = ffn_extras(
        jnp.stack([set_even, set_odd, zl]).astype(jnp.int32),
        gate_up_adapter_out,
        turned(down_adapter_in),
        mains,
        tail,
        tail_wide,
    )
    cut_a = ffn_rows_each // 48 * 16

    cos_part, sin_part = rope_tables(document_numbers)
    zeros_l = jnp.zeros((length, PLAIN_HEAD_DIM), F32)
    zeros_r = jnp.zeros((length, HEAD_LANES - 96), F32)
    none_16 = jnp.zeros_like(sin_part)
    rope = jnp.stack(
        [
            jnp.concatenate([zeros_l + 1.0, cos_part, cos_part, zeros_r], axis=1),
            jnp.concatenate([zeros_l, -sin_part, none_16, zeros_r], axis=1),
            jnp.concatenate([zeros_l, none_16, sin_part, zeros_r], axis=1),
        ],
        axis=0,
    )
    lane_ids = jnp.arange(HEAD_LANES, dtype=jnp.int32)[None, :]
    doc_lane = (lane_ids >= DOC_LANE) & (lane_ids < DOC_LANE + DOC_SLOTS)
    is_doc = document_numbers[0][:, None] == lane_ids - DOC_LANE
    doc_q = narrow(jnp.where(doc_lane & is_doc, 1.0, 0.0))
    doc_k = jnp.where(
        doc_lane & ~is_doc, -BIG, jnp.where((lane_ids >= 96) & (lane_ids < 99), 1.0, 0.0)
    )

    residual = inputs[0].astype(F32)
    attn_normed, attn_scale = normalize(residual, attention_norm_gain)
    attn_rows = narrow(attn_normed)
    q_latent = latent[:, :q_lat]
    kv_latent = latent[:, q_lat : q_lat + kv_lat]
    q_normed, q_scale = normalize(q_latent, query_latent_gain)
    kv_normed, kv_scale = normalize(kv_latent, keyvalue_latent_gain)
    q_input = narrow(q_normed)
    kv_input = narrow(kv_normed)
    pe_rows = lat_all[:, pe_at : pe_at + ROTARY_DIM].astype(F32)
    pe_a, pe_b = pe_rows[:, : ROTARY_DIM // 2], pe_rows[:, ROTARY_DIM // 2 :]
    pe_aug = narrow(
        jnp.concatenate(
            [
                zeros_l,
                pe_a * cos_part - pe_b * sin_part,
                pe_b * cos_part + pe_a * sin_part,
                zeros_r,
            ],
            axis=1,
        )
        + doc_k
    )
    q_aug, kv, head_out, w_ffn0, w_ffn1 = attend(
        lat_all,
        w_q,
        w_kv,
        rope,
        pe_aug,
        doc_q,
        q_lat + CODE_LANES,
        q_lat,
        [ride_two(0, 1), ride_one(1, 2, 3, 0, cut_a)],
        [w_ffn0, w_ffn1],
        [ffn_mine[1], ffn_other[1]],
    )
    tensor_keys = [(0, r) for r in reversed(range(0, n_t, 2))]

    def token_rows(key, place):
        at = jnp.bitwise_xor(place["tensor"], key[1]) * rows
        return pl.ds(pl.multiple_of(at, 16), rows)

    def out_term(held, place, key):
        return dot_nt(held[0][token_rows(key, place), :], held[1][...])

    attn_sum, w_ffn0, w_ffn1 = remote_reduce(
        [head_out, w_out],
        [head_out.shape, w_out.shape],
        out_term,
        tensor_keys,
        [t_slow[::-1]],
        rows,
        aug,
        "reduce_out",
        3,
        riders=[ride_two(0, z) for z in range(2, z_count)]
        + [ride_one(1, 2, 3, cut_a, ffn_rows_each - cut_a)],
        ridden=[w_ffn0, w_ffn1],
        carried=[ffn_mine[1], ffn_other[1]],
    )
    out_codes = narrow(attn_sum[:, width : width + RANK])
    middle = residual + RESIDUAL * (
        attn_sum[:, :width] + ADAPT_SCALE * dot_nn(out_codes, out_out)
    )

    ffn_normed, ffn_scale = normalize(middle, feedforward_norm_gain)
    ffn_rows = narrow(ffn_normed)
    gu_codes = narrow(dot_nt(ffn_rows, gu_in))
    x_own = jnp.concatenate([ffn_rows, code_lanes(gu_codes)], axis=1)

    def group_block_of(key, place):
        return group_block(
            jnp.bitwise_xor(place["dp"], key[0]), jnp.bitwise_xor(place["tensor"], key[1])
        )

    x_codes, grads, hids, ffn_weights = remote_ffn(
        x_own,
        g_all,
        [w_ffn0, w_ffn1],
        ffn_extra,
        mains,
        tail,
        tail_wide,
        t_slow + [("dp", pair)],
        group_block_of,
        [ride_two(1, z) for z in range(1, z_count)],
        "feed_forward",
        4,
    )
    group_keys = [(p, r) for p in (pair, 0) for r in reversed(range(0, n_t, 2))]
    ffn_in_sum, down_chip, *code_terms = remote_ffn_back(
        grads,
        hids,
        ffn_weights,
        ffn_extra,
        x_codes,
        g_all[:, width:],
        mains,
        tail_wide,
        group_keys,
        [group_a[::-1], group_b[::-1]],
        group_block_of,
        rows,
        "feed_forward_back",
        5,
    )
    gu_code_grad = narrow(own_codes(ffn_in_sum))
    ffn_in_grad = ffn_in_sum[:, :width] + dot_nn(gu_code_grad, gu_in)
    middle_grad = out_grad + normalize_back(
        middle, ffn_scale, feedforward_norm_gain, ffn_in_grad
    )
    attn_grad = narrow(RESIDUAL * middle_grad)
    out_code_grad = narrow(ADAPT_SCALE * dot_nt(attn_grad, out_out))
    attn_grad_aug = jnp.concatenate(
        [attn_grad, out_code_grad, jnp.zeros((rows, CODE_LANES - RANK), BF16)], axis=1
    )

    def uncolumn(parts, at_tail, first_at):
        out = [parts[c][:, first_at(c) : first_at(c) + mains[c]] for c in range(chunks)]
        if tail:
            at = mains[-1] + at_tail * tail
            out.append(parts[-1][:, at : at + tail])
        return jnp.concatenate(out, axis=1)

    gu_b, down_at = code_terms[:chunks], code_terms[chunks:]
    gate_b_all = ADAPT_SCALE * uncolumn(gu_b, 0, lambda c: 0)
    up_b_all = ADAPT_SCALE * uncolumn(gu_b, 1, lambda c: gu_wide[c] - mains[c])
    down_a_all = uncolumn(down_at, 2, lambda c: 0)
    packed = []
    for p in range(2):
        at = 2 * RANK * p
        packed += [
            gate_b_all[at : at + RANK],
            up_b_all[at + RANK : at + 2 * RANK],
            down_a_all[at : at + RANK],
        ]
    hidden_own = narrow(jnp.concatenate(packed, axis=0))

    def dp_job(src, out):
        return dict(src=src, out=out, out_at=lambda dd, tt: (dd,), steps=outer_first)

    ride_down = n_t == 4
    sent = remote_gather(
        [attn_grad_aug, hidden_own] + ([down_chip] if ride_down else []),
        token_jobs(0, 0, 2)
        + [
            dict(
                src=1,
                out=1,
                out_at=rows_at(0, hidden_own.shape[0], hidden_own.shape[0]),
                steps=[("dp", high), ("dp", pair)],
                group="hidden",
            )
        ],
        [],
        [(length, aug), (n_dp * hidden_own.shape[0], hidden_own.shape[1])] + ([(rows, aug)] if ride_down else []),
        "gather_grad",
        6,
        riders=[dict(kind="plain", src=2, src_at=0, out=2, step=("dp", pair))] if ride_down else [],
        distant=(2,),
        order=[0, "hidden", "hidden", "ride"],
    )
    hidden_terms = sent[1]
    grad_all = sent[0]
    heads_grad = narrow(dot_nn(grad_all, w_out))
    out_a = dot_tn(grad_all[:, width:], head_out)[:RANK]
    hidden_ride = [
        dict(
            kind="two",
            out=0,
            z=z,
            count=hidden_own.shape[0],
            pair=pair,
            high=high,
            steps=[("dp", b) for b in reversed(low_bits)],
        )
        for z in range(z_count)
    ]
    if ride_down:
        down_far = narrow(down_chip[2].astype(F32) + sent[2].astype(F32))
        dq, dkv, dpe, hidden_terms, came_pair, came_y = attend_back(
            q_aug,
            kv,
            head_out,
            heads_grad,
            rope,
            pe_aug,
            [
                dict(kind="plain", src=1, src_at=1, out=1, step=("dp", pair)),
                dict(kind="plain", src=2, src_at=None, out=2, step=("tensor", 2)),
            ]
            + hidden_ride,
            [hidden_terms],
            [down_chip, down_far],
            [(rows, aug), (rows, aug)],
        )
    else:
        dq, dkv, dpe, hidden_terms = attend_back(
            q_aug, kv, head_out, heads_grad, rope, pe_aug, hidden_ride, [hidden_terms], [], []
        )
        places = n_t // 2
        ffn_out = down_chip[places:].astype(F32) + hop(down_chip[:places], ("dp", pair)).astype(F32)
        while places > 1:
            places //= 2
            ffn_out = ffn_out[places:] + hop(narrow(ffn_out[:places]), ("tensor", 2 * places)).astype(
                F32
            )
        ffn_out = ffn_out[0]
    pe_g = dpe[:, PLAIN_HEAD_DIM : PLAIN_HEAD_DIM + ROTARY_DIM]
    pe_ga, pe_gb = pe_g[:, : ROTARY_DIM // 2], pe_g[:, ROTARY_DIM // 2 :]
    pe_grad = jnp.concatenate(
        [pe_ga * cos_part + pe_gb * sin_part, pe_gb * cos_part - pe_ga * sin_part], axis=1
    )
    pe_padded = jnp.pad(pe_grad, ((0, 0), (2 * RANK, CODE_LANES - 2 * RANK - ROTARY_DIM)))
    def latent_term(held, place, key):
        at = token_rows(key, place)
        from_q = dot_nt(held[0][at, :], held[2][...])
        from_kv = dot_nt(held[1][at, :], held[3][...])
        return jnp.concatenate(
            [
                from_q[:, :q_lat],
                from_q[:, q_lat:] + from_kv[:, :CODE_LANES] + held[4][at, :],
                from_kv[:, CODE_LANES:],
            ],
            axis=1,
        )

    lat_codes = lat_all[:, q_lat : q_lat + CODE_LANES]
    qb_b = ADAPT_SCALE * dot_tn(lat_codes, dq)[:RANK]
    kvb_b = ADAPT_SCALE * dot_tn(lat_codes, dkv)[RANK : 2 * RANK]
    head_own = narrow(jnp.concatenate([qb_b, kvb_b, out_a], axis=1))
    operands = [dq, dkv, w_q, w_kv, pe_padded]
    lat_sum, head_terms = remote_reduce(
        operands,
        [o.shape for o in operands],
        latent_term,
        tensor_keys,
        [t_slow[::-1]],
        rows,
        lat_wide,
        "reduce_latents",
        7,
        jobs=[dp_job(0, 0)],
        job_sources=[head_own],
        job_outs=[(n_dp,) + head_own.shape],
    )
    if ride_down:
        ffn_out = (
            down_chip[3].astype(F32)
            + came_pair.astype(F32)
            + came_y.astype(F32)
        )
    down_codes = narrow(own_codes(ffn_out)[:, :RANK])
    outputs = narrow(
        middle + RESIDUAL * (ffn_out[:, :width] + ADAPT_SCALE * dot_nn(down_codes, down_out))
    )
    qb_code_grad = narrow(lat_sum[:, q_lat : q_lat + RANK])
    kvb_code_grad = narrow(lat_sum[:, q_lat + RANK : q_lat + 2 * RANK])
    pe_sum = lat_sum[:, pe_at : pe_at + ROTARY_DIM]
    q_norm_grad = lat_sum[:, :q_lat] + dot_nn(qb_code_grad, qb_in)
    kv_norm_grad = lat_sum[:, q_lat + CODE_LANES :] + dot_nn(kvb_code_grad, kvb_in)
    latent_grad = narrow(
        jnp.concatenate(
            [
                normalize_back(q_latent, q_scale, query_latent_gain, q_norm_grad),
                normalize_back(kv_latent, kv_scale, keyvalue_latent_gain, kv_norm_grad),
                pe_sum,
                jnp.zeros((rows, down_pad), F32),
            ],
            axis=1,
        )
    )
    code_grad = narrow(ADAPT_SCALE * dot_nt(latent_grad, down_b_rows))
    attn_in_grad = dot_nt(latent_grad, w_down) + dot_nn(code_grad, down_in)
    input_grad = middle_grad + normalize_back(
        residual, attn_scale, attention_norm_gain, attn_in_grad
    )

    gu_a = dot_tn(gu_code_grad, ffn_rows)
    out_b = ADAPT_SCALE * dot_tn(out_codes, attn_grad)
    down_b = ADAPT_SCALE * dot_tn(down_codes, ffn_grad)
    table_orders = [outer_first + t_slow + t_core, t_slow + outer_first + t_core]
    down_in_terms = dot_tn(code_grad, attn_rows)
    b_terms = ADAPT_SCALE * dot_tn(down_codes_in, latent_grad)
    qb_a = dot_tn(qb_code_grad, q_input)
    kvb_a = dot_tn(kvb_code_grad, kv_input)
    small = [b_terms[:RANK, :q_lat], b_terms[RANK:, q_lat : q_lat + kv_all], qb_a, kvb_a]
    small_at = [0]
    padded = []
    for value in small:
        wide = -(-value.shape[1] // 128) * 128
        padded.append(jnp.pad(value, ((0, 0), (0, wide - value.shape[1]))))
        small_at.append(small_at[-1] + wide)
    small_rows = jnp.pad(
        jnp.concatenate(padded, axis=1), ((0, 0), (0, width - small_at[-1]))
    )
    shared = jnp.concatenate([gu_a, out_b, down_b, down_in_terms, small_rows], axis=0)
    shared = jnp.pad(shared, ((0, -shared.shape[0] % (16 * n_t)), (0, 0)))
    shared_terms = remote_share(
        narrow(shared),
        n_dp,
        n_t,
        table_orders,
        "share",
        8,
    )
    part_wide = width // 2

    def add_shared(s, refs, acc):
        for p in range(2):
            at = slice(p * part_wide, (p + 1) * part_wide)
            acc[:, at] += refs[0][p, s].astype(F32)

    def put_shared(acc, outs):
        outs[0][0, 0] = acc[:RANK, :]
        outs[0][1, 0] = acc[RANK : 2 * RANK, :]
        for n in range(4):
            outs[1 + n][0] = acc[(2 + n) * RANK : (3 + n) * RANK, :]
        for n, value in enumerate(small):
            at = small_at[n]
            outs[5 + n][0] = acc[6 * RANK : 7 * RANK, at : at + value.shape[1]]

    shared_sets = set_sums(
        set_all,
        [shared_terms],
        (shared.shape[0], width),
        add_shared,
        [((2,), (RANK, width))]
        + [((), (RANK, width))] * 4
        + [((), (RANK, value.shape[1])) for value in small],
        put_shared,
        group_count,
        "sum_shared",
    )
    gu_a_t, out_b_grad, down_b_grad, qa_a_t, kva_a_t, qa_b_grad, kva_b_grad, qb_a_t, kvb_a_t = (
        shared_sets
    )
    wide = heads * HEAD_LANES
    head_wide = head_own.shape[1]

    def add_split(s, refs, acc):
        which = (s // pair) % 2
        base = s - which * pair
        for h in range(2):
            acc[: 3 * RANK, h * half : (h + 1) * half] += refs[0][
                base + h * pair, which * 3 * RANK : (which + 1) * 3 * RANK, :
            ].astype(F32)
        acc[3 * RANK :, :head_wide] += refs[1][s].astype(F32)

    def put_split(acc, outs):
        outs[0][0, 0] = acc[:RANK, :hidden]
        outs[0][1, 0] = acc[RANK : 2 * RANK, :hidden]
        outs[1][0] = acc[2 * RANK : 3 * RANK, :hidden]
        for h in range(heads):
            outs[2][0, :, h * head_q : (h + 1) * head_q] = acc[
                3 * RANK :, h * HEAD_LANES : h * HEAD_LANES + head_q
            ]
        outs[3][0] = acc[3 * RANK :, wide : 2 * wide]
        outs[4][0] = acc[3 * RANK :, 2 * wide : head_wide]

    gu_b_grad, down_a_t, qb_b_grad, kvb_b_grad, out_a_t = set_sums(
        set_all,
        [hidden_terms.reshape((n_dp,) + hidden_own.shape), head_terms],
        (4 * RANK, max(hidden, -(-head_wide // 128) * 128)),
        add_split,
        [
            ((2,), (RANK, hidden)),
            ((), (RANK, hidden)),
            ((), (RANK, heads * head_q)),
            ((), (RANK, wide)),
            ((), (RANK, head_wide - 2 * wide)),
        ],
        put_split,
        group_count,
        "sum_split",
    )
    return (
        outputs[None],
        input_grad[None],
        turned(qa_a_t),
        qa_b_grad,
        turned(kva_a_t),
        kva_b_grad,
        turned(qb_a_t),
        qb_b_grad,
        turned(kvb_a_t),
        kvb_b_grad,
        turned(out_a_t),
        out_b_grad,
        turned(gu_a_t),
        gu_b_grad,
        turned(down_a_t),
        down_b_grad,
    )


def solution(mesh):
    return jax.shard_map(
        functools.partial(per_device, mesh.shape["dp"], mesh.shape["tensor"]),
        mesh=mesh,
        in_specs=(
            P("dp", "tensor", None),
            P("dp", "tensor", None),
            P("dp", None),
            P("dp"),
            P(),
            P(),
            P(),
            P(),
            P("dp", None),
            P("dp", None),
            P("dp", "tensor"),
            P("dp", "tensor"),
            P("tensor", "dp"),
            P(None, "dp", "tensor"),
            P("tensor", "dp"),
            P(),
            P(),
            P(),
            P(),
            P(),
            P(None, None, "tensor"),
            P(),
            P(None, None, "tensor"),
            P(None, "tensor", None),
            P(),
            P(),
            P(None, None, None, "tensor"),
            P(None, "tensor", None),
            P(),
        ),
        out_specs=(
            P("dp", "tensor", None),
            P("dp", "tensor", None),
            P(),
            P(),
            P(),
            P(),
            P(),
            P(None, None, "tensor"),
            P(),
            P(None, None, "tensor"),
            P(None, "tensor", None),
            P(),
            P(),
            P(None, None, None, "tensor"),
            P(None, "tensor", None),
            P(),
        ),
        check_vma=False,
    )
```

```python
import functools
import math

import jax
import jax.numpy as jnp
from jax import lax
from jax.experimental import pallas as pl
from jax.experimental.pallas import tpu as pltpu
from jax.sharding import PartitionSpec as P

PLAIN_HEAD_DIM = 64
ROTARY_DIM = 32
VALUE_HEAD_DIM = 64
HEAD_LANES = 128
CODE_LANES = 128
RANK = 16
BLOCK_Q = 256
DOC_LANE = 99
DOC_SLOTS = 24

NORM_EPS = 1e-05
RESIDUAL = 1.4 / math.sqrt(62.0)
ADAPT_SCALE = 2.0
SCORE_SCALE = 1.0 / math.sqrt(PLAIN_HEAD_DIM + ROTARY_DIM)
EXP2_SCALE = SCORE_SCALE * math.log2(math.e)
BIG = 1e30
VMEM_LIMIT = 60 * 1024 * 1024
FREE = pl.CostEstimate(flops=0, bytes_accessed=0, transcendentals=0)
F32 = jnp.float32
BF16 = jnp.bfloat16


def narrow(value):
    return value.astype(BF16)


def dot_nn(a, b):
    return lax.dot_general(a, b, (((1,), (0,)), ((), ())), preferred_element_type=F32)


def dot_nt(a, b):
    return lax.dot_general(a, b, (((1,), (1,)), ((), ())), preferred_element_type=F32)


def dot_tn(a, b):
    return lax.dot_general(a, b, (((0,), (0,)), ((), ())), preferred_element_type=F32)


def normalize(value, gain_vec):
    scale_inv = lax.rsqrt(jnp.mean(value * value, axis=-1, keepdims=True) + NORM_EPS)
    return (value * scale_inv * gain_vec, scale_inv)


def normalize_back(value, scale_inv, gain_vec, grad_in):
    weighted = grad_in * gain_vec
    return scale_inv * weighted - value * scale_inv**3 * jnp.mean(
        value * weighted, axis=-1, keepdims=True
    )


def rope_tables(segments):
    places = jnp.arange(segments.shape[-1], dtype=jnp.int32)
    begins = jnp.concatenate(
        [jnp.ones_like(segments[:, :1]), (segments[:, 1:] != segments[:, :-1]).astype(jnp.int32)],
        axis=1,
    )
    first_place = lax.cummax(places[None, :] * begins, axis=1)
    offsets = (places[None, :] - first_place).astype(F32)
    inv_freq = 10000.0 ** (-2.0 * jnp.arange(ROTARY_DIM // 2, dtype=F32) / ROTARY_DIM)
    angles = offsets[..., None] * inv_freq
    return (jnp.cos(angles)[0], jnp.sin(angles)[0])


def swap(value, axis, bit, size):
    return lax.ppermute(value, axis, [(i, i ^ bit) for i in range(size)])


class Links:
    def __init__(self, send_sems, recv_sems):
        self.send_sems, self.recv_sems = send_sems, recv_sems
        self.place = {"dp": lax.axis_index("dp"), "tensor": lax.axis_index("tensor")}
        self.copies = []
        self.waited = set()

    def peer(self, step):
        place = dict(self.place)
        place[step[0]] = jnp.bitwise_xor(place[step[0]], step[1])
        return (place["dp"], place["tensor"])

    def greet(self, steps):
        barrier = pltpu.get_barrier_semaphore()
        for step in steps:
            pl.semaphore_signal(
                barrier, inc=1, device_id=self.peer(step), device_id_type=pl.DeviceIdType.MESH
            )
        pl.semaphore_wait(barrier, len(steps))

    def prepare(self, src, dst, step):
        n = len(self.copies)
        copy = pltpu.make_async_remote_copy(
            src_ref=src,
            dst_ref=dst,
            send_sem=self.send_sems.at[n],
            recv_sem=self.recv_sems.at[n],
            device_id=self.peer(step),
            device_id_type=pl.DeviceIdType.MESH,
        )
        self.copies.append(copy)
        return n

    def send(self, src, dst, step):
        n = self.prepare(src, dst, step)
        self.copies[n].start()
        return n

    def arrived(self, n):
        if n not in self.waited:
            self.copies[n].wait_recv()
            self.waited.add(n)

    def close(self):
        for n, copy in enumerate(self.copies):
            self.arrived(n)
            copy.wait_send()


class Riders:
    def __init__(self, links, riders, in_refs, out_refs):
        self.links = links
        self.rounds = []
        d = links.place["dp"]
        for rider in riders:
            full = out_refs[rider["out"]]
            if rider["kind"] == "plain":
                src = in_refs[rider["src"]]
                if rider["src_at"] is not None:
                    src = src.at[rider["src_at"]]
                self.add(0, src, full, rider["step"])
                continue
            count, pair, high = rider["count"], rider["pair"], rider["high"]
            if rider["kind"] == "one":
                begin, size = rider["rows"]
                here = full.at[pl.ds(pl.multiple_of(d * count + begin, 16), size)]
                for name, bit in (("other", pair), ("mine", high), ("other", high ^ pair)):
                    src = in_refs[rider[name]].at[pl.ds(begin, size)]
                    self.add(0, src, here, ("dp", bit))
            else:
                held = [0]
                for k, step in enumerate(rider["steps"]):
                    for key in list(held):
                        place = jnp.bitwise_xor(d, rider["z"] * pair + key)
                        begin, size = rider.get("rows", (0, count))
                        at = pl.multiple_of(place * count + begin, 16)
                        here = full.at[pl.ds(at, size)]
                        self.add(k, here, here, step)
                        held.append(key ^ step[1])

    def add(self, k, src, dst, step):
        while len(self.rounds) <= k:
            self.rounds.append([])
        self.rounds[k].append(self.links.prepare(src, dst, step))

    def start(self):
        if self.rounds:
            for n in self.rounds[0]:
                self.links.copies[n].start()

    def finish(self):
        for k, numbers in enumerate(self.rounds):
            if k:
                for n in numbers:
                    self.links.copies[n].start()
            for n in numbers:
                self.links.arrived(n)


def rider_steps(riders):
    steps = []
    for rider in riders:
        if rider["kind"] == "plain":
            steps.append(rider["step"])
        elif rider["kind"] == "one":
            pair, high = rider["pair"], rider["high"]
            steps += [("dp", pair), ("dp", high), ("dp", high ^ pair)]
        else:
            steps += rider["steps"]
    return steps


def rider_count(riders):
    total = 0
    for rider in riders:
        if rider["kind"] == "plain":
            total += 1
        elif rider["kind"] == "one":
            total += 3
        else:
            total += (1 << len(rider["steps"])) - 1
    return total


def distinct(steps):
    out = []
    for step in steps:
        if step not in out:
            out.append(step)
    return out


def flip(key, step):
    return (key[0] ^ step[1], key[1]) if step[0] == "dp" else (key[0], key[1] ^ step[1])


def has_bit(key, step):
    return bool((key[0] if step[0] == "dp" else key[1]) & step[1])


def gather_count(jobs):
    return sum((1 << len(job["steps"])) - 1 for job in jobs)


def gather_rounds(links, src_refs, out_refs, jobs):
    d, t = links.place["dp"], links.place["tensor"]

    def landing(job, key):
        at = job["out_at"](jnp.bitwise_xor(d, key[0]), jnp.bitwise_xor(t, key[1]))
        return out_refs[job["out"]].at[at]

    state = []
    for job in jobs:
        src = src_refs[job["src"]]
        if job.get("src_at") is not None:
            src = src.at[job["src_at"]]
        state.append({(0, 0): (src, None)})
    for k in range(max(len(job["steps"]) for job in jobs)):
        for job, held in zip(jobs, state):
            if k >= len(job["steps"]):
                continue
            step = job["steps"][k]
            for key in list(held):
                src, came = held[key]
                if came is not None:
                    links.arrived(came)
                n = links.send(src, landing(job, key), step)
                new = flip(key, step)
                held[new] = (landing(job, new), n)
        yield k


def remote_gather(
    sources,
    jobs,
    extra,
    outs,
    name,
    collective_id,
    riders=(),
    aliases=(),
    distant=(),
    order=(),
    near_outs=(),
    scratch=(),
    work=None,
    late=(),
):
    steps = distinct([s for job in jobs for s in job["steps"]] + rider_steps(riders))
    count = gather_count(jobs) + rider_count(riders)
    aliases = dict(aliases)
    n_src, n_out, n_near = len(sources), len(outs), len(near_outs)

    def kernel(*refs):
        src_refs, refs = refs[:n_src], refs[n_src:]
        out_refs, refs = refs[:n_out], refs[n_out:]
        near, refs = refs[: n_near + len(scratch)], refs[n_near + len(scratch) :]
        send_sems, recv_sems, local_sems = refs
        all_src, all_out = list(src_refs) + list(near), list(out_refs) + list(near)
        links = Links(send_sems, recv_sems)
        d, t = links.place["dp"], links.place["tensor"]
        links.greet(steps)
        ride = Riders(links, riders, src_refs, out_refs)
        local = []

        def keep(src, where):
            copy = pltpu.make_async_copy(src, where, local_sems.at[len(local)])
            copy.start()
            local.append(copy)
            return copy

        for src, out, at in extra:
            keep(all_src[src], all_out[out].at[at(d, t)])
        groups = {}
        for job in jobs:
            groups.setdefault(job.get("group", 0), []).append(job)
        turns = {}
        sent = {g: [] for g in groups}
        kept = {g: [] for g in groups}

        def advance(group):
            before = len(links.copies)
            if group not in turns:
                turns[group] = gather_rounds(links, all_src, all_out, groups[group])
                for job in groups[group]:
                    src = all_src[job["src"]]
                    if job.get("src_at") is not None:
                        src = src.at[job["src_at"]]
                    kept[group].append(keep(src, all_out[job["out"]].at[job["out_at"](d, t)]))
            going = next(turns[group], None) is not None
            sent[group] += range(before, len(links.copies))
            return going

        waited = set()
        if "ride" not in order:
            ride.start()
        for turn in order:
            if turn == "ride":
                ride.start()
            elif callable(turn):
                turn(all_src)
            elif turn == "work":
                work(all_src)
                for src, out in late:
                    keep(all_src[src], all_out[out])
            elif isinstance(turn, tuple):
                for n in sent[turn[1]]:
                    links.arrived(n)
                for copy in kept[turn[1]]:
                    copy.wait()
                waited.add(turn[1])
            else:
                advance(turn)
        for group in groups:
            while advance(group):
                pass
        ride.finish()
        links.close()
        done = [copy for group in waited for copy in kept[group]]
        for copy in local:
            if not any(copy is other for other in done):
                copy.wait()

    vmem = pl.BlockSpec(memory_space=pltpu.VMEM)
    far = pl.BlockSpec(memory_space=pl.ANY)
    return pl.pallas_call(
        kernel,
        out_shape=[jax.ShapeDtypeStruct(o, BF16) for o in outs] + list(near_outs),
        in_specs=[far if n in aliases or n in distant else vmem for n in range(n_src)],
        out_specs=[far] * n_out + [vmem] * n_near,
        scratch_shapes=[pltpu.VMEM(o.shape, o.dtype) for o in scratch]
        + [
            pltpu.SemaphoreType.DMA((count,)),
            pltpu.SemaphoreType.DMA((count,)),
            pltpu.SemaphoreType.DMA((len(jobs) + len(extra) + len(late),)),
        ],
        input_output_aliases=aliases,
        compiler_params=pltpu.CompilerParams(
            collective_id=collective_id, has_side_effects=True, vmem_limit_bytes=VMEM_LIMIT
        ),
        cost_estimate=FREE,
        name=name,
    )(*sources)


def reduce_plan(keys, ways):
    plan = []
    for w, steps in enumerate(ways):
        live = list(keys)
        for k, step in enumerate(steps):
            plan += [(w, k, key) for key in live if has_bit(key, step)]
            live = [key for key in live if not has_bit(key, step)]
    return plan


def remote_reduce(
    operands, fetched, term, keys, ways, rows, wide, name, collective_id, riders=(), ridden=(), carried=(), jobs=(), job_sources=(), job_outs=(), after=None, after_in=(), after_out=()
):
    core_step = ("tensor", 1)
    part = rows // len(ways)
    plan = reduce_plan(keys, ways)
    slot = {entry: n for n, entry in enumerate(plan)}
    steps = distinct(
        [core_step]
        + [s for s in ways[0]]
        + rider_steps(riders)
        + [s for job in jobs for s in job["steps"]]
    )
    count = len(keys) + len(plan) + rider_count(riders) + gather_count(jobs)
    n_in = len(operands)
    n_ride = n_in + len(ridden) + len(carried)
    n_all = n_ride + len(job_sources)
    n_jobs = len(job_outs)
    after_out = list(after_out) or [jax.ShapeDtypeStruct((rows, wide), F32)]
    n_own = len(after_out)

    def kernel(*refs):
        in_refs = refs[:n_in]
        own_out = refs[n_all + len(after_in) : n_all + len(after_in) + n_own]
        extra_in = refs[n_all : n_all + len(after_in)]
        refs = refs[:n_all] + refs[n_all + len(after_in) + n_own - 1 :]
        ride_in = refs[n_in:n_ride]
        job_in = refs[n_ride:n_all]
        ride_out = refs[n_all + 1 : n_all + 1 + len(ridden)]
        job_out = refs[n_all + 1 + len(ridden) : n_all + 1 + len(ridden) + n_jobs]
        scratch = refs[n_all + 1 + len(ridden) + n_jobs :]
        held = scratch[:n_in]
        core_out, core_in, chip, hop_out, hop_in, send_sems, recv_sems, in_sems, job_sems = scratch[
            n_in:
        ]
        started = []
        for n in range(n_in):
            shape = fetched[n]
            src = in_refs[n].at[tuple(pl.ds(0, s) for s in shape)]
            copy = pltpu.make_async_copy(src, held[n], in_sems.at[n])
            copy.start()
            started.append(copy)
        links = Links(send_sems, recv_sems)
        links.greet(steps)
        ride = Riders(links, riders, ride_in, ride_out)
        ride.start()
        rounds = gather_rounds(links, job_in, job_out, jobs) if jobs else iter(())
        next(rounds, None)
        placed = []
        for n, job in enumerate(jobs):
            at = job["out_at"](links.place["dp"], links.place["tensor"])
            copy = pltpu.make_async_copy(
                job_in[job["src"]], job_out[job["out"]].at[at], job_sems.at[n]
            )
            copy.start()
            placed.append(copy)
        for copy in started:
            copy.wait()
        came = {}

        def send_part(w, k, key):
            entry = (w, k, key)
            came[entry] = links.send(hop_out.at[slot[entry]], hop_in.at[slot[entry]], ways[w][k])

        def so_far(w, k, key):
            total = chip[keys.index(key), w * part : (w + 1) * part, :]
            for j in range(k):
                entry = (w, j, flip(key, ways[w][j]))
                links.arrived(came[entry])
                total = total + hop_in[slot[entry]].astype(F32)
            return total

        for i, key in enumerate(keys):
            core_out[i] = narrow(term(held, links.place, (key[0], key[1] ^ 1)))
            crossing = links.send(core_out.at[i], core_in.at[i], core_step)
            mine = term(held, links.place, key)
            links.arrived(crossing)
            chip[i] = mine + core_in[i].astype(F32)
            for w, way in enumerate(ways):
                if way and has_bit(key, way[0]):
                    hop_out[slot[(w, 0, key)]] = narrow(chip[i, w * part : (w + 1) * part, :])
                    send_part(w, 0, key)
            next(rounds, None)
        for k in range(1, len(ways[0])):
            for w in range(len(ways)):
                for entry in plan:
                    if entry[0] == w and entry[1] == k:
                        hop_out[slot[entry]] = narrow(so_far(w, k, entry[2]))
                        send_part(w, k, entry[2])
        for w in range(len(ways)):
            total = so_far(w, len(ways[w]), (0, 0))
            if after is None:
                own_out[0][w * part : (w + 1) * part, :] = total
            else:
                after(slice(w * part, (w + 1) * part), total, extra_in, own_out)
        for _ in rounds:
            pass
        ride.finish()
        links.close()
        for copy in placed:
            copy.wait()

    any_spec = pl.BlockSpec(memory_space=pl.ANY)
    return pl.pallas_call(
        kernel,
        out_shape=after_out
        + [jax.ShapeDtypeStruct(r.shape, r.dtype) for r in ridden]
        + [jax.ShapeDtypeStruct(o, BF16) for o in job_outs],
        in_specs=[any_spec] * n_ride
        + [pl.BlockSpec(memory_space=pltpu.VMEM)] * (len(job_sources) + len(after_in)),
        out_specs=[pl.BlockSpec(memory_space=pltpu.VMEM)] * n_own
        + [any_spec] * (len(ridden) + n_jobs),
        input_output_aliases={n_in + n: n_own + n for n in range(len(ridden))},
        scratch_shapes=[pltpu.VMEM(s, o.dtype) for s, o in zip(fetched, operands)]
        + [
            pltpu.VMEM((len(keys), rows, wide), BF16),
            pltpu.VMEM((len(keys), rows, wide), BF16),
            pltpu.VMEM((len(keys), rows, wide), F32),
            pltpu.VMEM((max(len(plan), 1), part, wide), BF16),
            pltpu.VMEM((max(len(plan), 1), part, wide), BF16),
            pltpu.SemaphoreType.DMA((count,)),
            pltpu.SemaphoreType.DMA((count,)),
            pltpu.SemaphoreType.DMA((n_in,)),
            pltpu.SemaphoreType.DMA((max(len(jobs), 1),)),
        ],
        compiler_params=pltpu.CompilerParams(
            collective_id=collective_id, has_side_effects=True, vmem_limit_bytes=VMEM_LIMIT
        ),
        cost_estimate=FREE,
        name=name,
    )(*operands, *ridden, *carried, *job_sources, *after_in)


class Share:
    def __init__(self, links, n_t, orders, source, out, own, sums, came, went, terms, fetch_sem):
        self.links, self.terms, self.own = links, terms, own
        self.fetch = pltpu.make_async_copy(source, terms, fetch_sem.at[0])
        self.sums, self.came, self.went = sums, came, went
        self.count = terms.shape[0] // n_t
        self.wide = terms.shape[1] // len(orders)
        count = self.count
        t_steps = [("tensor", 1 << b) for b in range(n_t.bit_length() - 1)]
        self.rounds = []
        live, slot = list(range(n_t)), 0
        before = []
        for k, step in enumerate(t_steps):
            sent = []
            for r in live:
                if r & step[1]:
                    src = terms.at[self.block(r)] if k == 0 else went.at[slot]
                    sent.append((r, slot, links.prepare(src, came.at[slot], step)))
                    slot += 1
            live = [r for r in live if not r & step[1]]
            self.rounds.append(functools.partial(self.scatter, k, list(live), before, sent, step))
            before = [(r ^ step[1], at, n) for r, at, n in sent]
        d, t = links.place["dp"], links.place["tensor"]

        def landing(p, key):
            rows = pl.ds(pl.multiple_of(jnp.bitwise_xor(t, key[1]) * count, 16), count)
            return out.at[p, jnp.bitwise_xor(d, key[0]), rows]

        self.places = [landing(p, (0, 0)) for p in range(len(orders))]
        held = [{(0, 0): (own.at[p], None)} for p in range(len(orders))]
        seen = set()
        for k in range(len(orders[0])):
            work = []
            for p, order in enumerate(orders):
                step = order[k]
                for key in list(held[p]):
                    src, needs = held[p][key]
                    n = links.prepare(src, landing(p, key), step)
                    work.append((None if needs in seen else needs, n))
                    seen.add(needs)
                    new = flip(key, step)
                    held[p][new] = (landing(p, new), n)
            self.rounds.append(functools.partial(self.gather, k, before, work))

    def block(self, r):
        at = jnp.bitwise_xor(self.links.place["tensor"], r) * self.count
        return pl.ds(pl.multiple_of(at, 16), self.count)

    def scatter(self, k, live, before, sent, step):
        if k == 0:
            self.fetch.start()
            self.fetch.wait()
            for r in live:
                self.sums[r] = self.terms[self.block(r), :].astype(F32)
        self.add(before)
        for r, at, n in sent:
            if k:
                self.went[at] = narrow(self.sums[r])
            self.links.copies[n].start()

    def add(self, before):
        for r, at, n in before:
            self.links.arrived(n)
            self.sums[r] = self.sums[r] + self.came[at].astype(F32)

    def gather(self, k, before, work):
        if k == 0:
            self.add(before)
            for p in range(self.own.shape[0]):
                self.own[p] = narrow(self.sums[0, :, p * self.wide : (p + 1) * self.wide])
        for needs, n in work:
            if needs is not None:
                self.links.copies[needs].wait_recv()
                self.links.waited.add(needs)
            self.links.copies[n].start()

    def keep(self, sems):
        return [
            pltpu.make_async_copy(self.own.at[p], where, sems.at[p])
            for p, where in enumerate(self.places)
        ]


def share_shapes(shape, n_t, orders):
    count, parts = shape[0] // n_t, len(orders)
    copies = n_t - 1 + parts * ((1 << len(orders[0])) - 1)
    scratch = [
        pltpu.VMEM((parts, count, shape[1] // parts), BF16),
        pltpu.VMEM((n_t, count, shape[1]), F32),
        pltpu.VMEM((n_t - 1, count, shape[1]), BF16),
        pltpu.VMEM((n_t - 1, count, shape[1]), BF16),
        pltpu.VMEM(shape, BF16),
        pltpu.SemaphoreType.DMA((1,)),
        pltpu.SemaphoreType.DMA((parts,)),
    ]
    return scratch, copies


def remote_share(terms, n_dp, n_t, orders, name, collective_id, work_in, work_out, work):
    scratch, copies = share_shapes(terms.shape, n_t, orders)
    parts = len(orders)

    n_in, n_work = len(work_in), len(work_out)

    def kernel(source, *refs):
        work_refs = refs[:n_in] + refs[n_in + 1 : n_in + 1 + n_work]
        out_ref = refs[n_in]
        refs = refs[n_in + 1 + n_work :]
        own_sems, send_sems, recv_sems = refs[-3:]
        links = Links(send_sems, recv_sems)
        links.greet(orders[0])
        share = Share(links, n_t, orders, source, out_ref, *refs[:-3])
        for k, one in enumerate(share.rounds):
            one()
            if k == len(share.rounds) - 2:
                work(work_refs)
        kept = share.keep(own_sems)
        for copy in kept:
            copy.start()
        links.close()
        for copy in kept:
            copy.wait()

    return pl.pallas_call(
        kernel,
        out_shape=[
            jax.ShapeDtypeStruct((parts, n_dp, terms.shape[0], terms.shape[1] // parts), BF16)
        ]
        + list(work_out),
        in_specs=[pl.BlockSpec(memory_space=pl.ANY)]
        + [pl.BlockSpec(memory_space=pltpu.VMEM)] * n_in,
        out_specs=[pl.BlockSpec(memory_space=pl.ANY)]
        + [pl.BlockSpec(memory_space=pltpu.VMEM)] * n_work,
        scratch_shapes=scratch
        + [pltpu.SemaphoreType.DMA((copies,)), pltpu.SemaphoreType.DMA((copies,))],
        compiler_params=pltpu.CompilerParams(
            collective_id=collective_id, has_side_effects=True, vmem_limit_bytes=VMEM_LIMIT
        ),
        cost_estimate=FREE,
        name=name,
    )(terms, *work_in)


def set_sums(set_ids, sources, acc_shape, add, outs, put, groups, name):
    n_src = len(sources)
    count = set_ids.shape[0]

    def kernel(ids_ref, *refs):
        src_refs, out_refs, acc = refs[:n_src], refs[n_src:-1], refs[-1]
        k = pl.program_id(0)
        acc[...] = jnp.zeros_like(acc)
        for s in range(count):

            @pl.when(ids_ref[s] == k)
            def _(s=s):
                add(s, src_refs, acc)

        put(acc, out_refs)

    out_specs = []
    for before, after in outs:
        lead = len(before)
        block = tuple(before) + (1,) + tuple(after)
        out_specs.append(
            pl.BlockSpec(
                block, lambda k, ids, lead=lead, n=len(after): (0,) * lead + (k,) + (0,) * n
            )
        )
    return pl.pallas_call(
        kernel,
        grid_spec=pltpu.PrefetchScalarGridSpec(
            num_scalar_prefetch=1,
            grid=(groups,),
            in_specs=[
                pl.BlockSpec(a.shape, lambda k, ids, n=a.ndim: (0,) * n) for a in sources
            ],
            out_specs=out_specs,
            scratch_shapes=[pltpu.VMEM(acc_shape, F32)],
        ),
        out_shape=[
            jax.ShapeDtypeStruct(tuple(before) + (groups,) + tuple(after), F32)
            for before, after in outs
        ],
        compiler_params=pltpu.CompilerParams(vmem_limit_bytes=VMEM_LIMIT),
        cost_estimate=FREE,
        name=name,
    )(set_ids, *sources)


def split_three(value):
    high = narrow(value).astype(F32)
    middle = narrow(value - high).astype(F32)
    return high, middle, value - high - middle


def rope_mix(value, cos_l, sin_a, sin_b):
    return (
        value * cos_l
        + pltpu.roll(value, HEAD_LANES - ROTARY_DIM // 2, 1) * sin_a
        + pltpu.roll(value, ROTARY_DIM // 2, 1) * sin_b
    )


def attn_fwd_kernel(
    per_step, q_width, kv_at, xl_ref, wq_ref, wkv_ref, rope_ref, pe_ref, doc_ref, qa_ref, kv_ref, o_ref
):
    length = xl_ref.shape[0]
    lane = lax.broadcasted_iota(jnp.int32, (length, HEAD_LANES), 1)
    q_all = dot_nn(xl_ref[:, :q_width], wq_ref[...])
    kv_all = dot_nn(xl_ref[:, kv_at:], wkv_ref[...])
    kv_ref[...] = narrow(kv_all)
    doc_q = doc_ref[...].astype(F32)
    q_heads, k_heads, kv_turned = [], [], []
    for i in range(per_step):
        span = slice(i * HEAD_LANES, (i + 1) * HEAD_LANES)
        q_one = rope_mix(q_all[:, span], rope_ref[0], rope_ref[1], rope_ref[2]) + doc_q
        q_heads.append(narrow(q_one))
        kv_one = kv_all[:, span]
        k_heads.append(jnp.where(lane < PLAIN_HEAD_DIM, narrow(kv_one), pe_ref[...]))
        kv_turned.append(narrow(kv_one.T))
    key_at = lax.broadcasted_iota(jnp.int32, (BLOCK_Q, BLOCK_Q), 0)
    query_at = lax.broadcasted_iota(jnp.int32, (BLOCK_Q, BLOCK_Q), 1)
    row = lax.broadcasted_iota(jnp.int32, (HEAD_LANES, BLOCK_Q), 0)
    block_lane = lax.broadcasted_iota(jnp.int32, (BLOCK_Q, HEAD_LANES), 1)
    for j in range(length // BLOCK_Q):
        begin, end = j * BLOCK_Q, (j + 1) * BLOCK_Q
        mixed = []
        for i in range(per_step):
            q_part = q_heads[i][begin:end]
            scores = dot_nt(k_heads[i][:end], q_part)
            diag = jnp.where(key_at <= query_at, scores[begin:], -BIG)
            scores = diag if j == 0 else jnp.concatenate([scores[:begin], diag], axis=0)
            top = jnp.max(scores, axis=0, keepdims=True)
            terms = jnp.exp2((scores - top) * EXP2_SCALE)
            total = jnp.sum(terms, axis=0, keepdims=True)
            out_t = dot_nn(kv_turned[i][:, :end], narrow(terms)) * (1.0 / total)
            high, middle, low = split_three(top + jnp.log2(total) * (1.0 / EXP2_SCALE))
            out_t = jnp.where(
                row == 0, -high, jnp.where(row == 1, -middle, jnp.where(row == 2, -low, out_t))
            )
            out_n = out_t.T
            mixed.append(out_n)
            is_lse = (block_lane >= 96) & (block_lane < 99)
            q_saved = jnp.where(is_lse, narrow(pltpu.roll(out_n, 96, 1)), q_part)
            qa_ref[begin:end, i * HEAD_LANES : (i + 1) * HEAD_LANES] = q_saved
        if per_step == 2:
            both = jnp.where(block_lane < 64, pltpu.roll(mixed[0], 64, 1), mixed[1])
            o_ref[begin:end, :] = narrow(both)
        else:
            even = lax.rem(pl.program_id(0), 2) == 0
            moved = jnp.where(even, pltpu.roll(mixed[0], 64, 1), mixed[0])
            mine = (block_lane < 64) == even
            o_ref[begin:end, :] = jnp.where(mine, narrow(moved), o_ref[begin:end, :])


def attn_bwd_kernel(
    per_step, qa_ref, kv_ref, o_ref, do_ref, rope_ref, pe_ref, dq_ref, dkv_ref, dpe_ref, dk_acc, dv_acc
):
    length = qa_ref.shape[0]
    step = pl.program_id(0)
    lane = lax.broadcasted_iota(jnp.int32, (length, HEAD_LANES), 1)
    upper = lane >= 64
    key_at = lax.broadcasted_iota(jnp.int32, (BLOCK_Q, BLOCK_Q), 0)
    query_at = lax.broadcasted_iota(jnp.int32, (BLOCK_Q, BLOCK_Q), 1)
    causal = key_at <= query_at
    out_both = o_ref[...].astype(F32)
    grad_both = do_ref[...].astype(F32)

    @pl.when(step == 0)
    def _():
        dpe_ref[...] = jnp.zeros_like(dpe_ref)

    for i in range(per_step):
        span = slice(i * HEAD_LANES, (i + 1) * HEAD_LANES)
        if per_step == 2:
            turn = i == 0
            grad_one = pltpu.roll(grad_both, 64, 1) if turn else grad_both
            out_one = pltpu.roll(out_both, 64, 1) if turn else out_both
        else:
            even = lax.rem(step, 2) == 0
            grad_one = jnp.where(even, pltpu.roll(grad_both, 64, 1), grad_both)
            out_one = jnp.where(even, pltpu.roll(out_both, 64, 1), out_both)
        grad_one = jnp.where(upper, grad_one, 0.0)
        inner = jnp.sum(jnp.where(upper, grad_one * out_one, 0.0), axis=-1, keepdims=True)
        high, middle, low = split_three(inner)
        grad_aug = jnp.where(
            lane == 0, -high, jnp.where(lane == 1, -middle, jnp.where(lane == 2, -low, grad_one))
        )
        grad_aug = narrow(grad_aug)
        kv_one = kv_ref[:, span]
        ones = jnp.where(lane < 3, 1.0, 0.0).astype(BF16)
        v_aug = jnp.where(upper, kv_one, ones)
        k_aug = jnp.where(lane < 64, kv_one, pe_ref[...])
        k_turned = narrow(k_aug.astype(F32).T)
        for j in reversed(range(length // BLOCK_Q)):
            begin, end = j * BLOCK_Q, (j + 1) * BLOCK_Q
            q_part = qa_ref[begin:end, span]
            probs = jnp.exp2(dot_nt(k_aug[:end], q_part) * EXP2_SCALE)
            diag = jnp.where(causal, probs[begin:], 0.0)
            probs = diag if j == 0 else jnp.concatenate([probs[:begin], diag], axis=0)
            grads = narrow(probs * dot_nt(v_aug[:end], grad_aug[begin:end]))
            dq_part = dot_nn(k_turned[:, :end], grads).T * SCORE_SCALE
            dq_part = rope_mix(
                dq_part,
                rope_ref[0, begin:end, :],
                -rope_ref[1, begin:end, :],
                -rope_ref[2, begin:end, :],
            )
            dq_ref[begin:end, span] = narrow(dq_part)
            dk_part = dot_nn(grads, q_part)
            dv_part = dot_nn(narrow(probs), grad_aug[begin:end])
            if end == length:
                dk_acc[...] = dk_part
                dv_acc[...] = dv_part
            else:
                dk_acc[:end] += dk_part
                dv_acc[:end] += dv_part
        dk_all = dk_acc[...] * SCORE_SCALE
        dkv_ref[:, span] = narrow(jnp.where(upper, dv_acc[...], dk_all))
        dpe_ref[...] += jnp.where(upper & (lane < 96), dk_all, 0.0)


def ridden_call(
    kernel,
    grid,
    arrays,
    in_specs,
    out_shape,
    out_specs,
    scratch,
    riders,
    ridden,
    carried,
    fresh,
    name,
    collective_id,
):
    steps = distinct(rider_steps(riders))
    count = rider_count(riders)
    n_in, n_out = len(arrays), len(out_shape)
    n_ride_in = len(ridden) + len(carried)
    n_ride_out = len(ridden) + len(fresh)
    def body(*refs):
        own_in, rest = refs[:n_in], refs[n_in:]
        ride_in, rest = rest[:n_ride_in], rest[n_ride_in:]
        own_out, rest = rest[:n_out], rest[n_out:]
        ride_out, rest = rest[:n_ride_out], rest[n_ride_out:]
        send_sems, recv_sems = rest[-2:]
        links = Links(send_sems, recv_sems)
        ride = Riders(links, riders, ride_in, ride_out)

        @pl.when(pl.program_id(0) == 0)
        def _():
            links.greet(steps)
            ride.start()

        kernel(*own_in, *own_out, *rest[:-2])

        @pl.when(pl.program_id(0) == grid[0] - 1)
        def _():
            ride.finish()
            links.close()

    any_spec = pl.BlockSpec(memory_space=pl.ANY)
    return pl.pallas_call(
        body,
        grid=grid,
        in_specs=list(in_specs) + [any_spec] * n_ride_in,
        out_specs=list(out_specs) + [any_spec] * n_ride_out,
        out_shape=list(out_shape)
        + [jax.ShapeDtypeStruct(r.shape, r.dtype) for r in ridden]
        + [jax.ShapeDtypeStruct(f, BF16) for f in fresh],
        scratch_shapes=list(scratch)
        + [pltpu.SemaphoreType.DMA((count,)), pltpu.SemaphoreType.DMA((count,))],
        input_output_aliases={n_in + n: n_out + n for n in range(len(ridden))},
        compiler_params=pltpu.CompilerParams(
            collective_id=collective_id, has_side_effects=True, vmem_limit_bytes=VMEM_LIMIT
        ),
        cost_estimate=FREE,
        name=name,
    )(*arrays, *ridden, *carried)


def attend(latents, w_q, w_kv, rope, pe_aug, doc_q, q_width, kv_at, riders, ridden, carried):
    length = latents.shape[0]
    heads = w_q.shape[1] // HEAD_LANES
    per_step = 2 if heads % 2 == 0 else 1
    wide = per_step * HEAD_LANES
    whole = lambda a: pl.BlockSpec(a.shape, lambda h: (0,) * a.ndim)
    return ridden_call(
        functools.partial(attn_fwd_kernel, per_step, q_width, kv_at),
        (heads // per_step,),
        [latents, w_q, w_kv, rope, pe_aug, doc_q],
        [
            whole(latents),
            pl.BlockSpec((w_q.shape[0], wide), lambda h: (0, h)),
            pl.BlockSpec((w_kv.shape[0], wide), lambda h: (0, h)),
            whole(rope),
            whole(pe_aug),
            whole(doc_q),
        ],
        [
            jax.ShapeDtypeStruct((length, heads * HEAD_LANES), BF16),
            jax.ShapeDtypeStruct((length, heads * HEAD_LANES), BF16),
            jax.ShapeDtypeStruct((length, heads * VALUE_HEAD_DIM), BF16),
        ],
        [
            pl.BlockSpec((length, wide), lambda h: (0, h)),
            pl.BlockSpec((length, wide), lambda h: (0, h)),
            pl.BlockSpec((length, HEAD_LANES), lambda h: (0, h * per_step // 2)),
        ],
        [],
        riders,
        ridden,
        carried,
        [],
        "attend",
        10,
    )


def attend_back(q_aug, kv, heads_out, heads_grad, rope, pe_aug, riders, ridden, carried, fresh):
    length = q_aug.shape[0]
    heads = q_aug.shape[1] // HEAD_LANES
    per_step = 2 if heads % 2 == 0 else 1
    wide = per_step * HEAD_LANES
    whole = lambda a: pl.BlockSpec(a.shape, lambda h: (0,) * a.ndim)
    columns = pl.BlockSpec((length, wide), lambda h: (0, h))
    packed = pl.BlockSpec((length, HEAD_LANES), lambda h: (0, h * per_step // 2))
    arrays = [q_aug, kv, heads_out, heads_grad, rope, pe_aug]
    in_specs = [columns, columns, packed, packed, whole(rope), whole(pe_aug)]
    out_shape = [
        jax.ShapeDtypeStruct((length, heads * HEAD_LANES), BF16),
        jax.ShapeDtypeStruct((length, heads * HEAD_LANES), BF16),
        jax.ShapeDtypeStruct((length, HEAD_LANES), F32),
    ]
    out_specs = [columns, columns, pl.BlockSpec((length, HEAD_LANES), lambda h: (0, 0))]
    scratch = [pltpu.VMEM((length, HEAD_LANES), F32), pltpu.VMEM((length, HEAD_LANES), F32)]
    return ridden_call(
        functools.partial(attn_bwd_kernel, per_step),
        (heads // per_step,),
        arrays,
        in_specs,
        out_shape,
        out_specs,
        scratch,
        riders,
        ridden,
        carried,
        fresh,
        "attend_back",
        11,
    )


def gate_middle(gate, up, hid_grad):
    sig = 1.0 / (1.0 + jnp.exp(-gate))
    silu = gate * sig
    gate_grad = hid_grad * up * (sig * (1.0 + gate * (1.0 - sig)))
    return silu * up, gate_grad, hid_grad * silu


def tail_middle(pre, back, tail):
    wide = pre.shape[1]
    up = pltpu.roll(pre, wide - tail, 1)
    hid_grad = pltpu.roll(back, wide - 2 * tail, 1)
    hid, gate_grad, up_grad = gate_middle(pre, up, hid_grad)
    lane = lax.broadcasted_iota(jnp.int32, pre.shape, 1)
    hid = jnp.where((lane >= 2 * tail) & (lane < 3 * tail), pltpu.roll(hid, 2 * tail, 1), 0.0)
    both = jnp.where(
        lane < tail, gate_grad, jnp.where(lane < 2 * tail, pltpu.roll(up_grad, tail, 1), 0.0)
    )
    return hid, both


def remote_ffn(x_own, g_all, weights, extras, mains, tail, tail_wide, slow, block_of, riders, name, collective_id):
    rows, aug = x_own.shape
    total = g_all.shape[0]
    blocks = total // rows
    both = 2 * rows
    width = aug - CODE_LANES
    chunks = len(mains)
    tails = [0] * (chunks - 1) + [tail_wide]
    gu = [2 * m + w for m, w in zip(mains, tails)]
    core_step = ("tensor", 1)
    keys = [(0, 0)]
    for step in slow:
        keys += [flip(key, step) for key in keys]
    bits_of = {key: [s for s in slow if has_bit(key, s)] for key in keys}
    keys.sort(key=lambda k: len(bits_of[k]))

    def part_rows(key, step):
        n = len(bits_of[key])
        i = bits_of[key].index(step)
        size = -(-rows // (16 * n)) * 16
        begin = i * size
        return begin, min(size, rows - begin)

    count = len(keys) + sum(len(bits_of[k]) for k in keys) + rider_count(riders)
    steps = distinct([core_step] + slow + rider_steps(riders))

    def kernel(x_ref, g_ref, *refs):
        e_refs = refs[chunks : 2 * chunks]
        refs = refs[2 * chunks :]
        codes_ref = refs[0]
        grad_refs = refs[1 : 1 + chunks]
        hid_refs = refs[1 + chunks : 1 + 2 * chunks]
        w_refs = refs[1 + 2 * chunks : 1 + 3 * chunks]
        x_held, back_held, g_held = refs[1 + 3 * chunks : 4 + 3 * chunks]
        w_held = refs[4 + 3 * chunks : 4 + 4 * chunks]
        send_sems, recv_sems, w_sems, g_sems = refs[4 + 4 * chunks :]
        links = Links(send_sems, recv_sems)
        place = links.place
        fetch = [
            pltpu.make_async_copy(w_refs[c], w_held[c].at[pl.ds(0, width)], w_sems.at[c])
            for c in range(chunks)
        ]
        fetch_extra = [
            pltpu.make_async_copy(
                e_refs[c], w_held[c].at[pl.ds(width, CODE_LANES)], w_sems.at[chunks + c]
            )
            for c in range(chunks)
        ]
        fetch[0].start()
        for copy in fetch_extra:
            copy.start()
        links.greet(steps)

        def landing(key):
            at = pl.multiple_of(block_of(key, place) * rows, 16)
            return x_held.at[pl.ds(at, rows)]

        arrivals = {key: [] for key in keys}

        def pass_on(key, src):
            for step in slow:
                if has_bit(key, step):
                    continue
                there = flip(key, step)
                begin, size = part_rows(there, step)
                at = pl.ds(begin, size)
                n = links.send(src.at[at], landing(key).at[at], step)
                arrivals[there].append(n)

        crossing = {}
        pass_on((0, 0), x_ref)
        crossing[(0, 0)] = links.send(x_ref, landing((0, 0)), core_step)
        ride = Riders(links, riders, w_refs, w_refs)
        ride.start()
        x_held[pl.ds(pl.multiple_of(block_of((0, 0), place) * rows, 16), rows), :] = x_ref[...]

        def g_copy(b, slot):
            at = pl.ds(pl.multiple_of(b * both, 16), both)
            return pltpu.make_async_copy(g_ref.at[at], g_held.at[slot], g_sems.at[slot])

        def over_blocks(work):
            g_copy(0, 0).start()

            def one(b, carry):
                slot = lax.rem(b, 2)

                @pl.when(b + 1 < blocks // 2)
                def _():
                    g_copy(b + 1, 1 - slot).start()

                g_copy(b, slot).wait()
                work(b, g_held[slot])
                return carry

            lax.fori_loop(0, blocks // 2, one, 0)

        fetch[0].wait()
        for copy in fetch_extra:
            copy.wait()

        def back_first(b, g_rows):
            back_held[b] = dot_nn(g_rows, w_held[0][:, gu[0] :])

        over_blocks(back_first)

        def forward(b, c, back):
            main = mains[c]
            at = pl.ds(pl.multiple_of(b * both, 16), both)
            pre = dot_nn(x_held[at, :], w_held[c][:, : gu[c]])
            hid, gate_grad, up_grad = gate_middle(pre[:, :main], pre[:, gu[c] - main :], back)
            hid_refs[c][at, :main] = narrow(hid)
            grad_refs[c][at, :main] = narrow(gate_grad)
            grad_refs[c][at, gu[c] - main :] = narrow(up_grad)
            return pre, at

        def first_chunk(key):
            b = block_of(key, place) // 2
            forward(b, 0, back_held[b])

        links.arrived(crossing[(0, 0)])
        first_chunk((0, 0))
        for level in range(1, len(slow) + 1):
            here = [key for key in keys if len(bits_of[key]) == level]
            for key in here:
                for n in arrivals[key]:
                    links.arrived(n)
                pass_on(key, landing(key))
                crossing[key] = links.send(landing(key), landing(key), core_step)
            for key in here:
                links.arrived(crossing[key])
                first_chunk(key)
        ride.finish()
        for c in range(1, chunks):
            fetch[c].start()
            fetch[c].wait()

            def later(b, g_rows, c=c):
                main = mains[c]
                back = dot_nn(g_rows, w_held[c][:, gu[c] :])
                pre, at = forward(b, c, back)
                if tails[c]:
                    at_tail = slice(main, main + tail_wide)
                    hid, both = tail_middle(
                        pre[:, at_tail], dot_nn(g_rows, w_held[c][:, at_tail]), tail
                    )
                    hid_refs[c][at, main:] = narrow(hid)
                    grad_refs[c][at, at_tail] = narrow(both)

            over_blocks(later)
        codes_ref[...] = x_held[:, width:]
        links.close()

    any_spec = pl.BlockSpec(memory_space=pl.ANY)
    vmem_spec = pl.BlockSpec(memory_space=pltpu.VMEM)
    outs = pl.pallas_call(
        kernel,
        in_specs=[vmem_spec, any_spec] + [any_spec] * (2 * chunks),
        out_specs=[vmem_spec] * (1 + 2 * chunks) + [any_spec] * chunks,
        out_shape=[jax.ShapeDtypeStruct((total, CODE_LANES), BF16)]
        + [jax.ShapeDtypeStruct((total, g), BF16) for g in gu]
        + [jax.ShapeDtypeStruct((total, m + w), BF16) for m, w in zip(mains, tails)]
        + [jax.ShapeDtypeStruct(w.shape, BF16) for w in weights],
        scratch_shapes=[
            pltpu.VMEM((total, aug), BF16),
            pltpu.VMEM((blocks // 2, both, mains[0]), F32),
            pltpu.VMEM((2, both, aug), BF16),
        ]
        + [pltpu.VMEM((aug, w.shape[1]), BF16) for w in weights]
        + [
            pltpu.SemaphoreType.DMA((count,)),
            pltpu.SemaphoreType.DMA((count,)),
            pltpu.SemaphoreType.DMA((2 * chunks,)),
            pltpu.SemaphoreType.DMA((2,)),
        ],
        input_output_aliases={2 + c: 1 + 2 * chunks + c for c in range(chunks)},
        compiler_params=pltpu.CompilerParams(
            collective_id=collective_id, has_side_effects=True, vmem_limit_bytes=VMEM_LIMIT
        ),
        cost_estimate=FREE,
        name=name,
    )(x_own, g_all, *weights, *extras)
    return (
        outs[0],
        outs[1 : 1 + chunks],
        outs[1 + chunks : 1 + 2 * chunks],
        outs[1 + 2 * chunks :],
    )


def remote_ffn_back(
    grads, hids, weights, extras, x_codes, g_codes, mains, tail_wide, keys, ways, block_of, rows, name, collective_id
):
    width = weights[0].shape[0]
    aug = width + CODE_LANES
    chunks = len(mains)
    tails = [0] * (chunks - 1) + [tail_wide]
    gu = [2 * m + w for m, w in zip(mains, tails)]
    core_step = ("tensor", 1)
    part = rows // len(ways)
    plan = reduce_plan(keys, ways)
    later = [entry for entry in plan if entry[1] > 0]
    slot = {entry: n for n, entry in enumerate(plan)}
    later_slot = {entry: n for n, entry in enumerate(later)}
    steps = distinct([core_step] + ways[0])
    count = 2 * len(keys) + len(plan)
    operands = list(grads) + list(hids) + list(weights) + [x_codes, g_codes]
    shapes = [o.shape for o in operands]
    for c in range(chunks):
        shapes[2 * chunks + c] = (aug, weights[c].shape[1])

    def kernel(*refs):
        n_in = len(operands)
        in_refs, e_refs, refs = refs[:n_in], refs[n_in : n_in + chunks], refs[n_in + chunks :]
        refs = in_refs + refs
        out_ref, terms_ref = refs[n_in : n_in + 2]
        gu_refs = refs[n_in + 2 : n_in + 2 + chunks]
        down_refs = refs[n_in + 2 + chunks : n_in + 2 + 2 * chunks]
        held = refs[n_in + 2 + 2 * chunks : 2 * n_in + 2 + 2 * chunks]
        rest = refs[2 * n_in + 2 + 2 * chunks :]
        core_out, core_in, chip, hop_out, hop_in, stage, send_sems, recv_sems, in_sems, out_sems, free = rest
        g_held, h_held = held[:chunks], held[chunks : 2 * chunks]
        w_held = held[2 * chunks : 3 * chunks]
        started = []
        order = [n for c in range(chunks) for n in (2 * chunks + c, c)]
        order += list(range(chunks, 2 * chunks)) + [3 * chunks, 3 * chunks + 1]
        for n in order:
            is_weight = 2 * chunks <= n < 3 * chunks
            to = held[n].at[pl.ds(0, width)] if is_weight else held[n]
            copy = pltpu.make_async_copy(in_refs[n], to, in_sems.at[n])
            copy.start()
            started.append(copy)
        for c in range(chunks):
            copy = pltpu.make_async_copy(
                e_refs[c], w_held[c].at[pl.ds(width, CODE_LANES)], in_sems.at[n_in + c]
            )
            copy.start()
            started.append(copy)
        links = Links(send_sems, recv_sems)
        place = links.place
        links.greet(steps)
        for copy in started[: 2 * chunks] + started[n_in:]:
            copy.wait()
        came = {}

        def rows_of(key):
            return pl.ds(pl.multiple_of(block_of(key, place) * rows, 16), rows)

        def in_term(key):
            at = rows_of(key)
            out = dot_nt(g_held[0][at, :], w_held[0][:, : gu[0]])
            for c in range(1, chunks):
                out = out + dot_nt(g_held[c][at, :], w_held[c][:, : gu[c]])
            return out

        def down_term(key):
            at = rows_of(key)
            out = 0.0
            for c in range(chunks):
                out = out + dot_nt(h_held[c][at, : mains[c]], w_held[c][:, gu[c] :])
                if tails[c]:
                    out = out + dot_nt(
                        h_held[c][at, mains[c] :], w_held[c][:, mains[c] : mains[c] + tails[c]]
                    )
            return out

        def so_far(w, k, key):
            if key == (0, 0):
                total = out_ref[w * part : (w + 1) * part, :]
            else:
                total = chip[keys.index(key), w * part : (w + 1) * part, :].astype(F32)
            for j in range(k):
                entry = (w, j, flip(key, ways[w][j]))
                links.arrived(came[entry])
                total = total + hop_in[slot[entry]].astype(F32)
            return total

        crossings = []

        def cross(i, value):
            n = len(crossings)
            if n >= 2:
                links.copies[crossings[n - 2]].wait_send()
            core_out[n % 2] = narrow(value)
            crossings.append(links.send(core_out.at[n % 2], core_in.at[i], core_step))
            return crossings[-1]

        for i, key in enumerate(keys):
            crossing = cross(i, in_term((key[0], key[1] ^ 1)))
            mine = in_term(key)
            links.arrived(crossing)
            mine = mine + core_in[i].astype(F32)
            if key == (0, 0):
                out_ref[...] = mine
            else:
                chip[i] = narrow(mine)
                for w, way in enumerate(ways):
                    if has_bit(key, way[0]):
                        at = slice(w * part, (w + 1) * part)
                        entry = (w, 0, key)
                        came[entry] = links.send(
                            chip.at[i, pl.ds(w * part, part)], hop_in.at[slot[entry]], way[0]
                        )
        pl.semaphore_signal(
            free, inc=1, device_id=links.peer(core_step), device_id_type=pl.DeviceIdType.MESH
        )
        pl.semaphore_wait(free, 1)
        for copy in started[2 * chunks : n_in]:
            copy.wait()
        stored = []
        for i, key in enumerate(keys):
            crossing = cross(i, down_term((key[0], key[1] ^ 1)))
            mine = down_term(key)
            links.arrived(crossing)
            if i >= 2:
                stored[i - 2].wait()
            stage[i % 2] = narrow(mine + core_in[i].astype(F32))
            copy = pltpu.make_async_copy(stage.at[i % 2], terms_ref.at[i], out_sems.at[i])
            copy.start()
            stored.append(copy)
            if i == len(keys) // 2 - 1:
                for k in range(1, len(ways[0])):
                    for w in range(len(ways)):
                        for entry in plan:
                            if entry[0] == w and entry[1] == k:
                                hop_out[later_slot[entry]] = narrow(so_far(w, k, entry[2]))
                                came[entry] = links.send(
                                    hop_out.at[later_slot[entry]],
                                    hop_in.at[slot[entry]],
                                    ways[w][k],
                                )
        x_held, gc_held = held[3 * chunks :]
        for c in range(chunks):
            gu_refs[c][...] = dot_tn(x_held[...], g_held[c][...])
            down_refs[c][...] = dot_tn(gc_held[...], h_held[c][...])
        for w in range(len(ways)):
            out_ref[w * part : (w + 1) * part, :] = so_far(w, len(ways[w]), (0, 0))
        for copy in stored[max(0, len(keys) - 2) :]:
            copy.wait()
        for n, copy in enumerate(links.copies):
            links.arrived(n)
            if n not in crossings[:-2]:
                copy.wait_send()

    any_spec = pl.BlockSpec(memory_space=pl.ANY)
    return pl.pallas_call(
        kernel,
        out_shape=[
            jax.ShapeDtypeStruct((rows, aug), F32),
            jax.ShapeDtypeStruct((len(keys), rows, aug), BF16),
        ]
        + [jax.ShapeDtypeStruct((CODE_LANES, g.shape[1]), F32) for g in grads]
        + [jax.ShapeDtypeStruct((CODE_LANES, h.shape[1]), F32) for h in hids],
        in_specs=[any_spec] * (len(operands) + chunks),
        out_specs=[pl.BlockSpec(memory_space=pltpu.VMEM), any_spec]
        + [pl.BlockSpec(memory_space=pltpu.VMEM)] * (2 * chunks),
        scratch_shapes=[pltpu.VMEM(n, o.dtype) for n, o in zip(shapes, operands)]
        + [
            pltpu.VMEM((2, rows, aug), BF16),
            pltpu.VMEM((len(keys), rows, aug), BF16),
            pltpu.VMEM((len(keys) - 1, rows, aug), BF16),
            pltpu.VMEM((max(len(later), 1), part, aug), BF16),
            pltpu.VMEM((len(plan), part, aug), BF16),
            pltpu.VMEM((2, rows, aug), BF16),
            pltpu.SemaphoreType.DMA((count,)),
            pltpu.SemaphoreType.DMA((count,)),
            pltpu.SemaphoreType.DMA((len(operands) + chunks,)),
            pltpu.SemaphoreType.DMA((len(keys),)),
            pltpu.SemaphoreType.REGULAR,
        ],
        compiler_params=pltpu.CompilerParams(
            collective_id=collective_id, has_side_effects=True, vmem_limit_bytes=VMEM_LIMIT
        ),
        cost_estimate=FREE,
        name=name,
    )(*operands, *extras)


def ffn_extras(places, gate_up_out, down_in, mains, tail, tail_wide):
    half = down_in.shape[2] // 2
    chunks = len(mains)
    tails = [0] * (chunks - 1) + [tail_wide]
    wide = [3 * m + w for m, w in zip(mains, tails)]

    def kernel(places_ref, gu_ref, down_ref, *outs):
        for out in outs:
            out[...] = jnp.zeros_like(out)
        lower = places_ref[2] == 0
        for p in range(2):
            which = places_ref[p]

            def half_of(value):
                return jnp.where(lower, value[:, :half], value[:, half:])

            parts = [
                half_of(gu_ref[0, which]) * 2,
                half_of(gu_ref[1, which]) * 2,
                half_of(down_ref[which]),
            ]
            for kind, value in enumerate(parts):
                top = 2 * RANK * p + (RANK if kind == 1 else 0)
                at_rows = slice(top, top + RANK)
                begin = 0
                for c in range(chunks):
                    main = mains[c]
                    at = [0, main + tails[c], 2 * main + tails[c]][kind]
                    outs[c][at_rows, at : at + main] = value[:, begin : begin + main]
                    begin += main
                if tail:
                    at = mains[-1] + kind * tail
                    outs[-1][at_rows, at : at + tail] = value[:, begin:]

    return pl.pallas_call(
        kernel,
        grid_spec=pltpu.PrefetchScalarGridSpec(
            num_scalar_prefetch=1,
            grid=(1,),
            in_specs=[
                pl.BlockSpec(a.shape, lambda i, ids, n=a.ndim: (0,) * n)
                for a in (gate_up_out, down_in)
            ],
            out_specs=[pl.BlockSpec((CODE_LANES, w), lambda i, ids: (0, 0)) for w in wide],
        ),
        out_shape=[jax.ShapeDtypeStruct((CODE_LANES, w), BF16) for w in wide],
        compiler_params=pltpu.CompilerParams(vmem_limit_bytes=VMEM_LIMIT),
        cost_estimate=FREE,
        name="ffn_extras",
    )(places, gate_up_out, down_in)


def chunk_places(mains, tail, tail_wide):
    out = []
    begin = 0
    for c, main in enumerate(mains):
        wide = tail_wide if c == len(mains) - 1 else 0
        for kind, at in enumerate((0, main + wide, 2 * main + wide)):
            out.append((kind, c, at, begin, main))
        begin += main
    if tail:
        for kind in range(3):
            out.append((kind, len(mains) - 1, mains[-1] + kind * tail, begin, tail))
    return out


def prepare(places, tables, shards, sizes, mains, tail, tail_wide):
    heads, head_q, shares, down_wide = sizes
    qa_in, kva_in, qb_in, kvb_in, out_in, gu_in, qa_out, kva_out, qb_out, kvb_out, out_out, down_out = (
        tables
    )
    q_down, kv_down, q_up, gate_up, down_t, cotangent = shards
    width, q_lat, kv_all = qa_in.shape[2], q_down.shape[1], kv_down.shape[1]
    rows = cotangent.shape[0]
    share_rows = q_down.shape[0] // shares
    wide = heads * HEAD_LANES
    half = down_t.shape[1] // 2
    wides = [3 * m for m in mains[:-1]] + [3 * mains[-1] + tail_wide]

    def kernel(places_ref, *refs):
        ins, outs = refs[: len(tables) + len(shards)], refs[len(tables) + len(shards) :]
        qa_i, kva_i, qb_i, kvb_i, out_i, gu_i, qa_o, kva_o, qb_o, kvb_o, out_o, down_o = ins[
            : len(tables)
        ]
        qd, kvd, qu, gu_w, down_w, cot = ins[len(tables) :]
        down_in_o, down_b_o, qb_w, kvb_w, q_aug, kv_aug, out_x, gu_lanes, out_p, down_p, gu_p = outs[:11]
        mine_d, q_pad, g_own = outs[11:14]
        pieces = outs[14:]
        first = places_ref[1] == 0
        for out in (down_b_o, qb_w, kvb_w, q_aug, kv_aug, out_x, gu_lanes, out_p, gu_p, mine_d, q_pad):
            out[...] = jnp.zeros_like(out)
        for out in pieces:
            out[...] = jnp.zeros_like(out)
        down_in_o[:RANK, :] = qa_i[0]
        down_in_o[RANK:, :] = kva_i[0]
        down_b_o[:RANK, :q_lat] = qa_o[0]
        down_b_o[RANK:, q_lat : q_lat + kv_all] = kva_o[0]
        qb_w[:RANK, :] = qb_i[0]
        kvb_w[RANK : 2 * RANK, :] = kvb_i[0]
        out_x[:RANK, :] = out_i[0]
        kv_aug[RANK : 2 * RANK, :] = narrow(kvb_o[0].astype(F32) * ADAPT_SCALE)
        q_out = narrow(qb_o[0].astype(F32) * ADAPT_SCALE)
        q_up_all = qu[...]
        for h in range(heads):
            at = slice(h * HEAD_LANES, h * HEAD_LANES + head_q)
            q_aug[:RANK, at] = q_out[:, h * head_q : (h + 1) * head_q]
            q_pad[:, at] = q_up_all[:, h * head_q : (h + 1) * head_q]
        for n in range(2):
            both = gu_i[n, 0]
            none = jnp.zeros_like(both)
            gu_p[n * RANK : (n + 1) * RANK, :] = both
            gu_lanes[n * RANK : (n + 1) * RANK, :] = jnp.where(first, both, none)
            gu_lanes[(2 + n) * RANK : (3 + n) * RANK, :] = jnp.where(first, none, both)
        out_p[:RANK, :] = out_o[0]
        down_p[...] = down_o[0]
        mine_d[:, :q_lat] = qd[...]
        mine_d[:, q_lat : q_lat + kv_all] = kvd[...]
        grad = narrow(RESIDUAL * cot[...].astype(F32))
        g_own[:, :width] = grad
        codes = dot_nt(grad, jnp.concatenate([down_o[0]] * 8, axis=0)) * ADAPT_SCALE
        lane = lax.broadcasted_iota(jnp.int32, codes.shape, 1)
        begin = jnp.where(first, 0, 2 * RANK)
        g_own[:, width:] = narrow(jnp.where((lane >= begin) & (lane < begin + RANK), codes, 0.0))
        sources = [gu_w[0], gu_w[1], down_w[...]]
        sides = [(v[:, :half], v[:, half:]) for v in sources]
        for kind, c, at, begin, count in chunk_places(mains, tail, tail_wide):
            left = sides[kind][0][:, begin : begin + count]
            right = sides[kind][1][:, begin : begin + count]
            pieces[2 * c][:, at : at + count] = jnp.where(first, left, right)
            pieces[2 * c + 1][:, at : at + count] = jnp.where(first, right, left)

    def picked(table):
        if table.ndim == 4:
            return pl.BlockSpec((2, 1) + table.shape[2:], lambda i, ids: (0, ids[0], 0, 0))
        return pl.BlockSpec((1,) + table.shape[1:], lambda i, ids: (ids[0], 0, 0))

    def shared(shard):
        return pl.BlockSpec((share_rows, shard.shape[1]), lambda i, ids: (ids[2], 0))

    def whole(shape):
        return pl.BlockSpec(shape, lambda i, ids: (0,) * len(shape))

    out_shapes = [
        (2 * RANK, width),
        (2 * RANK, down_wide),
        (CODE_LANES, qb_in.shape[2]),
        (CODE_LANES, kvb_in.shape[2]),
        (CODE_LANES, wide),
        (CODE_LANES, wide),
        (CODE_LANES, out_in.shape[2]),
        (CODE_LANES, width),
        (CODE_LANES, width),
        (RANK, width),
        (CODE_LANES, width),
        (share_rows, down_wide),
        (q_up.shape[0], wide),
        (rows, width + CODE_LANES),
    ]
    for w in wides:
        out_shapes += [(down_t.shape[0], w)] * 2
    return pl.pallas_call(
        kernel,
        grid_spec=pltpu.PrefetchScalarGridSpec(
            num_scalar_prefetch=1,
            grid=(1,),
            in_specs=[picked(a) for a in tables]
            + [shared(q_down), shared(kv_down)]
            + [whole(a.shape) for a in shards[2:]],
            out_specs=[whole(o) for o in out_shapes],
        ),
        out_shape=[jax.ShapeDtypeStruct(o, BF16) for o in out_shapes],
        compiler_params=pltpu.CompilerParams(vmem_limit_bytes=VMEM_LIMIT),
        cost_estimate=FREE,
        name="prepare",
    )(places, *tables, *shards)


def per_device(
    n_dp,
    n_t,
    inputs,
    cotangent,
    document_numbers,
    sequence_adapter_index,
    attention_norm_gain,
    query_latent_gain,
    keyvalue_latent_gain,
    feedforward_norm_gain,
    query_down_matrix,
    keyvalue_down_matrix,
    query_up_matrix,
    keyvalue_up_matrix,
    output_matrix,
    gate_up_matrix,
    down_matrix,
    query_down_adapter_in,
    query_down_adapter_out,
    keyvalue_down_adapter_in,
    keyvalue_down_adapter_out,
    query_up_adapter_in,
    query_up_adapter_out,
    keyvalue_up_adapter_in,
    keyvalue_up_adapter_out,
    output_adapter_in,
    output_adapter_out,
    gate_up_adapter_in,
    gate_up_adapter_out,
    down_adapter_in,
    down_adapter_out,
):
    d = lax.axis_index("dp")
    t = lax.axis_index("tensor")
    pair = n_dp // 4
    low_bits = [b for b in (1, 2, 4, 8, 16) if b < pair]
    high = n_dp // 2
    y_bits = [b for b in (2, 4, 8, 16) if b < n_t]
    zl = lax.rem(d // pair, 2)
    core = lax.rem(t, 2)
    first = zl == 0
    size = {"dp": n_dp, "tensor": n_t}
    rows = inputs.shape[1]
    width = inputs.shape[2]
    length = document_numbers.shape[1]
    q_lat = query_down_matrix.shape[1]
    kv_all = keyvalue_down_matrix.shape[1]
    kv_lat = kv_all - ROTARY_DIM
    heads = keyvalue_up_matrix.shape[1] // HEAD_LANES
    group_count = query_down_adapter_in.shape[0]
    aug = width + CODE_LANES
    half_rows = rows // 2

    def hop(value, step):
        return swap(value, step[0], step[1], size[step[0]])

    outer_first = [("dp", high), ("dp", pair)] + [("dp", b) for b in reversed(low_bits)]
    inner_first = [("dp", b) for b in low_bits] + [("dp", high), ("dp", pair)]
    t_slow = [("tensor", b) for b in reversed(y_bits)]
    t_core = [("tensor", 1)]

    set_own = sequence_adapter_index[0]

    def pick(table, index):
        return lax.dynamic_index_in_dim(table, index, 0, keepdims=False)

    def turned(table):
        return jnp.swapaxes(table, -1, -2)

    hidden = down_matrix.shape[0]
    half = hidden // 2
    tiles = half // 128
    main = tiles * 128
    tail = half - main
    tail_wide = -(-3 * tail // 128) * 128
    first_tiles = (2 * tiles + 2) // 3
    mains = [first_tiles * 128, main - first_tiles * 128]
    chunks = len(mains)
    tails = [0] * (chunks - 1) + [tail_wide]
    gu_wide = [2 * m + w for m, w in zip(mains, tails)]

    head_q = PLAIN_HEAD_DIM + ROTARY_DIM
    down_shard = query_down_matrix.shape[0]
    shares = n_t if down_shard % (16 * n_t) == 0 else 2
    share_rows = down_shard // shares
    down_wide = -(-(q_lat + kv_all) // 128) * 128
    down_pad = down_wide - q_lat - kv_all
    (
        down_in,
        down_b_rows,
        qb_in_wide,
        kvb_in_wide,
        q_aug_rows,
        kv_aug_rows,
        out_extra,
        gu_in_lanes,
        out_out_wide,
        down_out,
        gu_in_wide,
        down_mine,
        q_up_mine,
        g_own,
        *ffn_pieces,
    ) = prepare(
        jnp.stack([set_own, zl, lax.rem(t, shares)]).astype(jnp.int32),
        [
            turned(query_down_adapter_in),
            turned(keyvalue_down_adapter_in),
            turned(query_up_adapter_in),
            turned(keyvalue_up_adapter_in),
            turned(output_adapter_in),
            turned(gate_up_adapter_in),
            query_down_adapter_out,
            keyvalue_down_adapter_out,
            query_up_adapter_out,
            keyvalue_up_adapter_out,
            output_adapter_out,
            down_adapter_out,
        ],
        [
            query_down_matrix,
            keyvalue_down_matrix,
            query_up_matrix,
            gate_up_matrix,
            down_matrix.T,
            cotangent[0],
        ],
        (heads, head_q, shares, down_wide),
        mains,
        tail,
        tail_wide,
    )
    qb_in, kvb_in = qb_in_wide[:RANK], kvb_in_wide[RANK : 2 * RANK]
    out_out, gu_in = out_out_wide[:RANK], gu_in_wide[: 2 * RANK]
    ffn_mine, ffn_other = ffn_pieces[::2], ffn_pieces[1::2]
    ffn_rows_each = gate_up_matrix.shape[1]
    z_count = n_dp // pair
    ffn_wide = [m.shape[1] for m in ffn_mine]

    def ride_one(out, mine, other, begin, size):
        return dict(
            kind="one",
            out=out,
            mine=mine,
            other=other,
            rows=(begin, size),
            count=ffn_rows_each,
            pair=pair,
            high=high,
        )

    def ride_two(out, z, begin=0, size=None):
        return dict(
            kind="two",
            out=out,
            z=z,
            rows=(begin, ffn_rows_each if size is None else size),
            count=ffn_rows_each,
            pair=pair,
            high=high,
            steps=[("dp", b) for b in reversed(low_bits)],
        )

    def own_codes(value):
        lanes = value[:, width:]
        return jnp.where(first, lanes[:, : 2 * RANK], lanes[:, 2 * RANK : 4 * RANK])

    qb_rows, kvb_rows = query_up_matrix.shape[0], keyvalue_up_matrix.shape[0]
    out_rows = output_matrix.shape[1]

    def rows_at(start, step, count):
        return lambda dd, tt: (pl.ds(pl.multiple_of(start + dd * step, 16), count),)

    def group_block(dd, tt):
        return lax.rem(dd // pair, 2) * n_t + tt

    def group_jobs(src, out, ways):
        return [
            dict(
                src=src,
                src_at=pl.ds(at, half_rows),
                out=out,
                out_at=lambda dd, tt, at=at: (
                    pl.ds(pl.multiple_of(group_block(dd, tt) * rows + at, 16), half_rows),
                ),
                steps=steps + t_core,
                group="rows",
            )
            for at, steps in zip((0, half_rows), ways)
        ]

    group_a = t_slow + [("dp", pair)]
    group_b = [("dp", pair)] + t_slow
    pe_at = q_lat + 2 * RANK
    lat_wide = q_lat + CODE_LANES + kv_lat

    def token_jobs(src, out, parts, group=0):
        count = rows // parts
        return [
            dict(
                src=src,
                src_at=pl.ds(n * count, count),
                out=out,
                out_at=lambda dd, tt, n=n: (
                    pl.ds(pl.multiple_of(tt * rows + n * count, 16), count),
                ),
                steps=t_slow + t_core,
                group=group,
            )
            for n in range(parts)
        ]

    def latent_work(refs):
        x_ref, norm_ref, q_norm_ref, kv_norm_ref, in_ref, b_ref, qb_ref, kvb_ref = refs[12:20]
        latent_ref, codes_ref, w_ref, own_ref = refs[20:24]
        x_f = x_ref[...].astype(F32)
        scale = lax.rsqrt(jnp.mean(x_f * x_f, axis=-1, keepdims=True) + NORM_EPS)
        h_rows = narrow(x_f * scale * norm_ref[...])
        codes = narrow(dot_nt(h_rows, in_ref[...]))
        latent = dot_nn(h_rows, w_ref[...]) + ADAPT_SCALE * dot_nn(codes, b_ref[...])
        latent_ref[...] = latent
        codes_ref[...] = codes
        q_part = latent[:, :q_lat]
        kv_part = latent[:, q_lat : q_lat + kv_lat]
        q_scale = lax.rsqrt(jnp.mean(q_part * q_part, axis=-1, keepdims=True) + NORM_EPS)
        kv_scale = lax.rsqrt(jnp.mean(kv_part * kv_part, axis=-1, keepdims=True) + NORM_EPS)
        q_in = narrow(q_part * q_scale * q_norm_ref[...])
        kv_in = narrow(kv_part * kv_scale * kv_norm_ref[...])
        own_ref[:, :q_lat] = q_in
        own_ref[:, q_lat + CODE_LANES :] = kv_in
        code_block = dot_nt(q_in, qb_ref[...]) + dot_nt(kv_in, kvb_ref[...])
        pe_block = pltpu.roll(latent[:, q_lat + kv_lat :], 2 * RANK, 1)
        lane = lax.broadcasted_iota(jnp.int32, code_block.shape, 1)
        own_ref[:, q_lat : q_lat + CODE_LANES] = narrow(
            jnp.where(lane < 2 * RANK, code_block, pe_block)
        )

    down_steps = outer_first + (t_slow if shares == n_t else []) + t_core
    n_start_outs = 9
    latent_at, w_at, lat_own_at = n_start_outs, n_start_outs + 2, n_start_outs + 3
    n_start_sources = 20
    jobs = [
        dict(
            src=0,
            out=w_at,
            out_at=lambda dd, tt: (
                pl.ds(
                    pl.multiple_of(dd * down_shard + lax.rem(tt, shares) * share_rows, 16), share_rows
                ),
            ),
            steps=down_steps,
            group="down",
        ),
        dict(src=1, out=1, out_at=rows_at(0, qb_rows, qb_rows), steps=outer_first, group="up"),
        dict(src=2, out=2, out_at=rows_at(CODE_LANES, kvb_rows, kvb_rows), steps=outer_first, group="up"),
        dict(src=8, out=5, out_at=lambda dd, tt: (dd,), steps=outer_first, group="up"),
        dict(src=3, out=3, out_at=rows_at(0, out_rows, out_rows), steps=outer_first, group="out"),
    ]
    low_steps = [("dp", b) for b in reversed(low_bits)]
    for src, out in ((9, 6), (11, 7)):
        jobs.append(
            dict(
                src=src,
                out=out,
                out_at=rows_at(0, ffn_rows_each, ffn_rows_each),
                steps=low_steps,
                group="own",
            )
        )
    jobs += group_jobs(4, 4, (group_b, group_b))
    jobs += token_jobs(n_start_sources + 3, 8, 2, "latents")
    set_mark = jnp.full((16, 128), sequence_adapter_index[0].astype(F32)).astype(BF16)
    w_down, w_q, w_kv, w_out, g_all, set_marks, w_ffn0, w_ffn1, lat_all, latent, down_codes_in = (
        remote_gather(
            [
                down_mine,
                q_up_mine,
                keyvalue_up_matrix,
                output_matrix.T,
                g_own,
                q_aug_rows,
                kv_aug_rows,
                out_extra,
                set_mark,
                ffn_mine[0],
                ffn_other[0],
                ffn_mine[1],
                inputs[0],
                attention_norm_gain[None],
                query_latent_gain[None],
                keyvalue_latent_gain[None],
                down_in,
                down_b_rows,
                qb_in_wide,
                kvb_in_wide,
            ],
            jobs,
            [
                (5, 1, lambda dd, tt: (pl.ds(q_lat, CODE_LANES),)),
                (6, 2, lambda dd, tt: (pl.ds(0, CODE_LANES),)),
                (7, 3, lambda dd, tt: (pl.ds(width, CODE_LANES),)),
            ],
            [
                (width, down_wide),
                (q_lat + CODE_LANES, heads * HEAD_LANES),
                (CODE_LANES + kv_lat, heads * HEAD_LANES),
                (aug, heads * VALUE_HEAD_DIM),
                (2 * n_t * rows, aug),
                (n_dp, 16, 128),
                (width, ffn_wide[0]),
                (width, ffn_wide[1]),
                (length, lat_wide),
            ],
            "gather_start",
            1,
            riders=[ride_one(6, 9, 10, 0, ffn_rows_each)],
            order=["down", "up", "out", "down", "up", "down", "own", "out", "rows", "down"]
            + ["up", "out", "ride"]
            + ["down"] * (len(down_steps) - 4)
            + [("all", "down"), "work", "latents", "rows"]
            + ["latents"] * len(t_slow)
            + ["rows"],
            near_outs=[
                jax.ShapeDtypeStruct((rows, down_wide), F32),
                jax.ShapeDtypeStruct((rows, 2 * RANK), BF16),
            ],
            scratch=[
                jax.ShapeDtypeStruct((width, down_wide), BF16),
                jax.ShapeDtypeStruct((rows, lat_wide), BF16),
            ],
            work=latent_work,
            late=[(n_start_sources + 2, 0)],
        )
    )
    set_all = set_marks[:, 0, 0].astype(jnp.int32)
    set_peer = lax.dynamic_index_in_dim(set_all, jnp.bitwise_xor(d, pair), 0, keepdims=False)
    set_even = jnp.where(first, set_own, set_peer)
    set_odd = jnp.where(first, set_peer, set_own)
    ffn_extra = ffn_extras(
        jnp.stack([set_even, set_odd, zl]).astype(jnp.int32),
        gate_up_adapter_out,
        turned(down_adapter_in),
        mains,
        tail,
        tail_wide,
    )
    cut_a = ffn_rows_each // 48 * 16

    cos_part, sin_part = rope_tables(document_numbers)
    zeros_l = jnp.zeros((length, PLAIN_HEAD_DIM), F32)
    zeros_r = jnp.zeros((length, HEAD_LANES - 96), F32)
    none_16 = jnp.zeros_like(sin_part)
    rope = jnp.stack(
        [
            jnp.concatenate([zeros_l + 1.0, cos_part, cos_part, zeros_r], axis=1),
            jnp.concatenate([zeros_l, -sin_part, none_16, zeros_r], axis=1),
            jnp.concatenate([zeros_l, none_16, sin_part, zeros_r], axis=1),
        ],
        axis=0,
    )
    lane_ids = jnp.arange(HEAD_LANES, dtype=jnp.int32)[None, :]
    doc_lane = (lane_ids >= DOC_LANE) & (lane_ids < DOC_LANE + DOC_SLOTS)
    is_doc = document_numbers[0][:, None] == lane_ids - DOC_LANE
    doc_q = narrow(jnp.where(doc_lane & is_doc, 1.0, 0.0))
    doc_k = jnp.where(
        doc_lane & ~is_doc, -BIG, jnp.where((lane_ids >= 96) & (lane_ids < 99), 1.0, 0.0)
    )

    residual = inputs[0].astype(F32)
    attn_normed, attn_scale = normalize(residual, attention_norm_gain)
    attn_rows = narrow(attn_normed)
    q_latent = latent[:, :q_lat]
    kv_latent = latent[:, q_lat : q_lat + kv_lat]
    q_normed, q_scale = normalize(q_latent, query_latent_gain)
    kv_normed, kv_scale = normalize(kv_latent, keyvalue_latent_gain)
    q_input = narrow(q_normed)
    kv_input = narrow(kv_normed)
    pe_rows = lat_all[:, pe_at : pe_at + ROTARY_DIM].astype(F32)
    pe_a, pe_b = pe_rows[:, : ROTARY_DIM // 2], pe_rows[:, ROTARY_DIM // 2 :]
    pe_aug = narrow(
        jnp.concatenate(
            [
                zeros_l,
                pe_a * cos_part - pe_b * sin_part,
                pe_b * cos_part + pe_a * sin_part,
                zeros_r,
            ],
            axis=1,
        )
        + doc_k
    )
    q_aug, kv, head_out, w_ffn0, w_ffn1 = attend(
        lat_all,
        w_q,
        w_kv,
        rope,
        pe_aug,
        doc_q,
        q_lat + CODE_LANES,
        q_lat,
        [ride_two(0, 1), ride_two(0, 2, 0, cut_a), ride_one(1, 2, 3, 0, cut_a)],
        [w_ffn0, w_ffn1],
        [ffn_mine[1], ffn_other[1]],
    )
    tensor_keys = [(0, r) for r in reversed(range(0, n_t, 2))]

    def token_rows(key, place):
        at = jnp.bitwise_xor(place["tensor"], key[1]) * rows
        return pl.ds(pl.multiple_of(at, 16), rows)

    def out_term(held, place, key):
        return dot_nt(held[0][token_rows(key, place), :], held[1][...])

    def middle_work(at, total, extra, outs):
        x_ref, out_b_ref, norm_ref, lanes_ref = extra
        middle_ref, codes_ref, own_ref = outs
        codes = narrow(total[:, width : width + RANK])
        mid = x_ref[at, :].astype(F32) + RESIDUAL * (
            total[:, :width] + ADAPT_SCALE * dot_nn(codes, out_b_ref[...])
        )
        middle_ref[at, :] = mid
        codes_ref[at, :] = codes
        scale = lax.rsqrt(jnp.mean(mid * mid, axis=-1, keepdims=True) + NORM_EPS)
        normed = narrow(mid * scale * norm_ref[...])
        own_ref[at, :width] = normed
        own_ref[at, width:] = narrow(dot_nt(normed, lanes_ref[...]))

    middle, out_codes, x_own, w_ffn0, w_ffn1 = remote_reduce(
        [head_out, w_out],
        [head_out.shape, w_out.shape],
        out_term,
        tensor_keys,
        [t_slow[::-1]],
        rows,
        aug,
        "reduce_out",
        3,
        riders=[ride_two(0, 2, cut_a, ffn_rows_each - cut_a)]
        + [ride_two(0, z) for z in range(3, z_count)]
        + [ride_one(1, 2, 3, cut_a, ffn_rows_each - cut_a)],
        ridden=[w_ffn0, w_ffn1],
        carried=[ffn_mine[1], ffn_other[1]],
        after=middle_work,
        after_in=[inputs[0], out_out, feedforward_norm_gain[None], gu_in_lanes],
        after_out=[
            jax.ShapeDtypeStruct((rows, width), F32),
            jax.ShapeDtypeStruct((rows, RANK), BF16),
            jax.ShapeDtypeStruct((rows, aug), BF16),
        ],
    )
    ffn_rows = x_own[:, :width]
    ffn_scale = lax.rsqrt(jnp.mean(middle * middle, axis=-1, keepdims=True) + NORM_EPS)

    def group_block_of(key, place):
        return group_block(
            jnp.bitwise_xor(place["dp"], key[0]), jnp.bitwise_xor(place["tensor"], key[1])
        )

    x_codes, grads, hids, ffn_weights = remote_ffn(
        x_own,
        g_all,
        [w_ffn0, w_ffn1],
        ffn_extra,
        mains,
        tail,
        tail_wide,
        t_slow + [("dp", pair)],
        group_block_of,
        [ride_two(1, z) for z in range(1, z_count)],
        "feed_forward",
        4,
    )
    group_keys = [(p, r) for p in (pair, 0) for r in reversed(range(0, n_t, 2))]
    ffn_in_sum, down_chip, *code_terms = remote_ffn_back(
        grads,
        hids,
        ffn_weights,
        ffn_extra,
        x_codes,
        g_all[:, width:],
        mains,
        tail_wide,
        group_keys,
        [group_a[::-1], group_b[::-1]],
        group_block_of,
        rows,
        "feed_forward_back",
        5,
    )
    def grad_work(part, refs):
        at = slice(part * half_rows, (part + 1) * half_rows)
        sum_ref, mid_ref, cot_ref, norm_ref, gu_ref, out_ref = refs[0:6]
        middle_ref, codes_ref, aug_ref = refs[n_grad : n_grad + 3]
        lanes = sum_ref[at, width:]
        lanes = jnp.where(zl_of() == 0, lanes, pltpu.roll(lanes, CODE_LANES - 2 * RANK, 1))
        lane = lax.broadcasted_iota(jnp.int32, lanes.shape, 1)
        codes = narrow(jnp.where(lane < 2 * RANK, lanes, 0.0))
        codes_ref[at, :] = codes
        weighted = (sum_ref[at, :width] + dot_nn(codes, gu_ref[...])) * norm_ref[...]
        mid = mid_ref[at, :]
        scale = lax.rsqrt(jnp.mean(mid * mid, axis=-1, keepdims=True) + NORM_EPS)
        inner = jnp.mean(mid * weighted, axis=-1, keepdims=True)
        grad = cot_ref[at, :].astype(F32) + scale * weighted - mid * (scale * scale * scale * inner)
        middle_ref[at, :] = grad
        scaled = narrow(RESIDUAL * grad)
        aug_ref[at, :width] = scaled
        aug_ref[at, width:] = narrow(ADAPT_SCALE * dot_nt(scaled, out_ref[...]))

    def zl_of():
        return lax.rem(lax.axis_index("dp") // pair, 2)

    hidden_shape = (6 * RANK, half)

    def hidden_work(refs):
        gu_refs, down_refs = refs[6 : 6 + chunks], refs[6 + chunks : 6 + 2 * chunks]
        own_ref = refs[n_grad + 6]
        for kind, c, at, begin, count in chunk_places(mains, tail, tail_wide):
            for p in range(2):
                to = slice((3 * p + kind) * RANK, (3 * p + kind + 1) * RANK)
                if kind < 2:
                    top = 2 * RANK * p + kind * RANK
                    value = gu_refs[c][top : top + RANK, at : at + count] * ADAPT_SCALE
                else:
                    here = at - 2 * mains[c] - tails[c] if count == mains[c] else at
                    value = down_refs[c][2 * RANK * p : 2 * RANK * p + RANK, here : here + count]
                own_ref[to, begin : begin + count] = narrow(value)

    def dp_job(src, out):
        return dict(src=src, out=out, out_at=lambda dd, tt: (dd,), steps=outer_first)

    n_grad = 7 + 2 * chunks + (1 if n_t == 4 else 0)

    def heads_work(refs):
        w_ref, heads_ref, lanes_ref, all_ref = refs[6 + 2 * chunks], *refs[n_grad + 3 : n_grad + 6]
        for n in range(2):
            at = slice(n * length // 2, (n + 1) * length // 2)
            heads_ref[at, :] = narrow(dot_nn(all_ref[at, :], w_ref[...]))
        lanes_ref[...] = all_ref[:, width:]

    ride_down = n_t == 4
    n_far = 2 if ride_down else 1
    sent = remote_gather(
        [
            ffn_in_sum,
            middle,
            cotangent[0],
            feedforward_norm_gain[None],
            gu_in_wide,
            out_out_wide,
            *code_terms,
            w_out,
        ]
        + ([down_chip] if ride_down else []),
        token_jobs(n_grad + 2, n_far + 5, 2, "top")[:1]
        + token_jobs(n_grad + 2, n_far + 5, 2, "bottom")[1:]
        + [
            dict(
                src=n_grad + 6,
                out=0,
                out_at=rows_at(0, hidden_shape[0], hidden_shape[0]),
                steps=[("dp", high), ("dp", pair)],
                group="hidden",
            )
        ],
        [],
        [(n_dp * hidden_shape[0], half)] + ([(rows, aug)] if ride_down else []),
        "gather_grad",
        6,
        riders=[dict(kind="plain", src=n_grad - 1, src_at=0, out=1, step=("dp", pair))]
        if ride_down
        else [],
        distant=(n_grad - 1,) if ride_down else (),
        order=[
            functools.partial(grad_work, 0),
            "top",
            functools.partial(grad_work, 1),
            "bottom",
            hidden_work,
            "hidden",
            "hidden",
            "ride",
            "top",
            "bottom",
        ]
        + ["top", "bottom"] * (len(t_slow) - 1)
        + [("all", "top"), ("all", "bottom"), heads_work],
        near_outs=[
            jax.ShapeDtypeStruct((rows, width), F32),
            jax.ShapeDtypeStruct((rows, CODE_LANES), BF16),
            jax.ShapeDtypeStruct((rows, aug), BF16),
            jax.ShapeDtypeStruct((length, w_out.shape[1]), BF16),
            jax.ShapeDtypeStruct((length, CODE_LANES), BF16),
        ],
        scratch=[
            jax.ShapeDtypeStruct((length, aug), BF16),
            jax.ShapeDtypeStruct(hidden_shape, BF16),
        ],
    )
    middle_grad, gu_code_grad, attn_grad_aug, heads_grad, grad_lanes = sent[n_far:]
    gu_code_grad = gu_code_grad[:, : 2 * RANK]
    attn_grad = attn_grad_aug[:, :width]
    hidden_terms = sent[0]
    out_a = dot_tn(grad_lanes, head_out)[:RANK]
    hidden_ride = [
        dict(
            kind="two",
            out=0,
            z=z,
            count=hidden_shape[0],
            pair=pair,
            high=high,
            steps=[("dp", b) for b in reversed(low_bits)],
        )
        for z in range(z_count)
    ]
    if ride_down:
        down_far = narrow(down_chip[2].astype(F32) + sent[1].astype(F32))
        dq, dkv, dpe, hidden_terms, came_pair, came_y = attend_back(
            q_aug,
            kv,
            head_out,
            heads_grad,
            rope,
            pe_aug,
            [
                dict(kind="plain", src=1, src_at=1, out=1, step=("dp", pair)),
                dict(kind="plain", src=2, src_at=None, out=2, step=("tensor", 2)),
            ]
            + hidden_ride,
            [hidden_terms],
            [down_chip, down_far],
            [(rows, aug), (rows, aug)],
        )
    else:
        dq, dkv, dpe, hidden_terms = attend_back(
            q_aug, kv, head_out, heads_grad, rope, pe_aug, hidden_ride, [hidden_terms], [], []
        )
        places = n_t // 2
        ffn_out = down_chip[places:].astype(F32) + hop(down_chip[:places], ("dp", pair)).astype(F32)
        while places > 1:
            places //= 2
            ffn_out = ffn_out[places:] + hop(narrow(ffn_out[:places]), ("tensor", 2 * places)).astype(
                F32
            )
        ffn_out = ffn_out[0]
    pe_g = dpe[:, PLAIN_HEAD_DIM : PLAIN_HEAD_DIM + ROTARY_DIM]
    pe_ga, pe_gb = pe_g[:, : ROTARY_DIM // 2], pe_g[:, ROTARY_DIM // 2 :]
    pe_grad = jnp.concatenate(
        [pe_ga * cos_part + pe_gb * sin_part, pe_gb * cos_part - pe_ga * sin_part], axis=1
    )
    pe_padded = jnp.pad(pe_grad, ((0, 0), (2 * RANK, CODE_LANES - 2 * RANK - ROTARY_DIM)))
    def latent_term(held, place, key):
        at = token_rows(key, place)
        from_q = dot_nt(held[0][at, :], held[2][...])
        from_kv = dot_nt(held[1][at, :], held[3][...])
        return jnp.concatenate(
            [
                from_q[:, :q_lat],
                from_q[:, q_lat:] + from_kv[:, :CODE_LANES] + held[4][at, :],
                from_kv[:, CODE_LANES:],
            ],
            axis=1,
        )

    lat_codes = lat_all[:, q_lat : q_lat + CODE_LANES]
    qb_b = ADAPT_SCALE * dot_tn(lat_codes, dq)[:RANK]
    kvb_b = ADAPT_SCALE * dot_tn(lat_codes, dkv)[RANK : 2 * RANK]
    head_own = narrow(jnp.concatenate([qb_b, kvb_b, out_a], axis=1))
    operands = [dq, dkv, w_q, w_kv, pe_padded]
    small_at, small_wide = [0], []
    for value in (q_lat, kv_all, q_lat, kv_lat):
        small_wide.append(value)
        small_at.append(small_at[-1] + -(-value // 128) * 128)

    def latent_back(at, total, extra, outs):
        latent_ref, q_norm, kv_norm, qb_ref, kvb_ref, b_ref, rows_ref, codes_ref = extra
        grad_ref, code_ref, terms_ref = outs
        block = total[:, q_lat : q_lat + CODE_LANES]
        lane = lax.broadcasted_iota(jnp.int32, block.shape, 1)
        codes = narrow(jnp.where(lane < 2 * RANK, block, 0.0))
        latent_f = latent_ref[...]
        parts = []
        inputs_in = []
        for begin, size, grad, norm_ref, in_ref in (
            (0, q_lat, total[:, :q_lat], q_norm, qb_ref),
            (q_lat, kv_lat, total[:, q_lat + CODE_LANES :], kv_norm, kvb_ref),
        ):
            value = latent_f[:, begin : begin + size]
            scale = lax.rsqrt(jnp.mean(value * value, axis=-1, keepdims=True) + NORM_EPS)
            inputs_in.append(narrow(value * scale * norm_ref[...]))
            weighted = (grad + dot_nn(codes, in_ref[...])) * norm_ref[...]
            inner = jnp.mean(value * weighted, axis=-1, keepdims=True)
            parts.append(scale * weighted - value * (scale * scale * scale * inner))
        grad_ref[:, :q_lat] = narrow(parts[0])
        grad_ref[:, q_lat : q_lat + kv_lat] = narrow(parts[1])
        pe_block = pltpu.roll(block, CODE_LANES - 2 * RANK, 1)
        pe_block = jnp.where(lane < ROTARY_DIM, pe_block, 0.0)
        grad_ref[:, q_lat + kv_lat :] = narrow(pe_block[:, : down_wide - q_lat - kv_lat])
        grad_rows = grad_ref[...]
        code_grad = narrow(ADAPT_SCALE * dot_nt(grad_rows, b_ref[...]))
        code_ref[...] = code_grad
        terms_ref[...] = jnp.zeros_like(terms_ref)
        terms_ref[: 2 * RANK, :] = narrow(dot_tn(code_grad, rows_ref[...]))
        b_terms = ADAPT_SCALE * dot_tn(codes_ref[...], grad_rows)
        qb_a = dot_tn(codes, inputs_in[0])
        kvb_a = dot_tn(codes, inputs_in[1])
        small_values = (
            b_terms[:RANK, :q_lat],
            b_terms[RANK:, q_lat : q_lat + kv_all],
            qb_a[:RANK, :],
            kvb_a[RANK : 2 * RANK, :],
        )
        for value, begin, size in zip(small_values, small_at, small_wide):
            terms_ref[2 * RANK :, begin : begin + size] = narrow(value)

    latent_grad, code_grad, late_terms, head_terms = remote_reduce(
        operands,
        [o.shape for o in operands],
        latent_term,
        tensor_keys,
        [t_slow[::-1]],
        rows,
        lat_wide,
        "reduce_latents",
        7,
        jobs=[dp_job(0, 0)],
        job_sources=[head_own],
        job_outs=[(n_dp,) + head_own.shape],
        after=latent_back,
        after_in=[
            latent,
            query_latent_gain[None],
            keyvalue_latent_gain[None],
            qb_in_wide,
            kvb_in_wide,
            down_b_rows,
            attn_rows,
            down_codes_in,
        ],
        after_out=[
            jax.ShapeDtypeStruct((rows, down_wide), BF16),
            jax.ShapeDtypeStruct((rows, 2 * RANK), BF16),
            jax.ShapeDtypeStruct((3 * RANK, width), BF16),
        ],
    )
    if ride_down:
        ffn_out = (
            down_chip[3].astype(F32)
            + came_pair.astype(F32)
            + came_y.astype(F32)
        )
    down_codes = narrow(own_codes(ffn_out)[:, :RANK])
    outputs = narrow(
        middle + RESIDUAL * (ffn_out[:, :width] + ADAPT_SCALE * dot_nn(down_codes, down_out))
    )
    gu_a = dot_tn(gu_code_grad, ffn_rows)
    out_b = ADAPT_SCALE * dot_tn(out_codes, attn_grad)
    down_b = ADAPT_SCALE * dot_tn(down_codes, g_own[:, :width])
    table_orders = [outer_first + t_slow + t_core, t_slow + outer_first + t_core]
    shared = jnp.concatenate([narrow(gu_a), narrow(out_b), narrow(down_b), late_terms], axis=0)
    shared = jnp.pad(shared, ((0, -shared.shape[0] % (16 * n_t)), (0, 0)))

    def input_work(refs):
        grad_ref, code_ref, w_ref, in_ref, x_ref, norm_ref, mid_ref, out_ref = refs
        back = dot_nt(grad_ref[...], w_ref[...]) + dot_nn(code_ref[...], in_ref[...])
        value = x_ref[...].astype(F32)
        scale = lax.rsqrt(jnp.mean(value * value, axis=-1, keepdims=True) + NORM_EPS)
        weighted = back * norm_ref[...]
        inner = jnp.mean(value * weighted, axis=-1, keepdims=True)
        out_ref[...] = (
            mid_ref[...] + scale * weighted - value * (scale * scale * scale * inner)
        )

    shared_terms, input_grad = remote_share(
        shared,
        n_dp,
        n_t,
        table_orders,
        "share",
        8,
        [
            latent_grad,
            code_grad,
            w_down,
            down_in,
            inputs[0],
            attention_norm_gain[None],
            middle_grad,
        ],
        [jax.ShapeDtypeStruct((rows, width), F32)],
        input_work,
    )
    part_wide = width // 2

    def add_shared(s, refs, acc):
        for p in range(2):
            at = slice(p * part_wide, (p + 1) * part_wide)
            acc[:, at] += refs[0][p, s].astype(F32)

    def put_shared(acc, outs):
        outs[0][0, 0] = acc[:RANK, :]
        outs[0][1, 0] = acc[RANK : 2 * RANK, :]
        for n in range(4):
            outs[1 + n][0] = acc[(2 + n) * RANK : (3 + n) * RANK, :]
        for n, size in enumerate(small_wide):
            at = small_at[n]
            outs[5 + n][0] = acc[6 * RANK : 7 * RANK, at : at + size]

    shared_sets = set_sums(
        set_all,
        [shared_terms],
        (shared.shape[0], width),
        add_shared,
        [((2,), (RANK, width))]
        + [((), (RANK, width))] * 4
        + [((), (RANK, size)) for size in small_wide],
        put_shared,
        group_count,
        "sum_shared",
    )
    gu_a_t, out_b_grad, down_b_grad, qa_a_t, kva_a_t, qa_b_grad, kva_b_grad, qb_a_t, kvb_a_t = (
        shared_sets
    )
    wide = heads * HEAD_LANES
    head_wide = head_own.shape[1]

    def add_split(s, refs, acc):
        which = (s // pair) % 2
        base = s - which * pair
        for h in range(2):
            acc[: 3 * RANK, h * half : (h + 1) * half] += refs[0][
                base + h * pair, which * 3 * RANK : (which + 1) * 3 * RANK, :
            ].astype(F32)
        acc[3 * RANK :, :head_wide] += refs[1][s].astype(F32)

    def put_split(acc, outs):
        outs[0][0, 0] = acc[:RANK, :hidden]
        outs[0][1, 0] = acc[RANK : 2 * RANK, :hidden]
        outs[1][0] = acc[2 * RANK : 3 * RANK, :hidden]
        for h in range(heads):
            outs[2][0, :, h * head_q : (h + 1) * head_q] = acc[
                3 * RANK :, h * HEAD_LANES : h * HEAD_LANES + head_q
            ]
        outs[3][0] = acc[3 * RANK :, wide : 2 * wide]
        outs[4][0] = acc[3 * RANK :, 2 * wide : head_wide]

    gu_b_grad, down_a_t, qb_b_grad, kvb_b_grad, out_a_t = set_sums(
        set_all,
        [hidden_terms.reshape((n_dp,) + hidden_shape), head_terms],
        (4 * RANK, max(hidden, -(-head_wide // 128) * 128)),
        add_split,
        [
            ((2,), (RANK, hidden)),
            ((), (RANK, hidden)),
            ((), (RANK, heads * head_q)),
            ((), (RANK, wide)),
            ((), (RANK, head_wide - 2 * wide)),
        ],
        put_split,
        group_count,
        "sum_split",
    )
    return (
        outputs[None],
        input_grad[None],
        turned(qa_a_t),
        qa_b_grad,
        turned(kva_a_t),
        kva_b_grad,
        turned(qb_a_t),
        qb_b_grad,
        turned(kvb_a_t),
        kvb_b_grad,
        turned(out_a_t),
        out_b_grad,
        turned(gu_a_t),
        gu_b_grad,
        turned(down_a_t),
        down_b_grad,
    )


def solution(mesh):
    return jax.shard_map(
        functools.partial(per_device, mesh.shape["dp"], mesh.shape["tensor"]),
        mesh=mesh,
        in_specs=(
            P("dp", "tensor", None),
            P("dp", "tensor", None),
            P("dp", None),
            P("dp"),
            P(),
            P(),
            P(),
            P(),
            P("dp", None),
            P("dp", None),
            P("dp", "tensor"),
            P("dp", "tensor"),
            P("tensor", "dp"),
            P(None, "dp", "tensor"),
            P("tensor", "dp"),
            P(),
            P(),
            P(),
            P(),
            P(),
            P(None, None, "tensor"),
            P(),
            P(None, None, "tensor"),
            P(None, "tensor", None),
            P(),
            P(),
            P(None, None, None, "tensor"),
            P(None, "tensor", None),
            P(),
        ),
        out_specs=(
            P("dp", "tensor", None),
            P("dp", "tensor", None),
            P(),
            P(),
            P(),
            P(),
            P(),
            P(None, None, "tensor"),
            P(),
            P(None, None, "tensor"),
            P(None, "tensor", None),
            P(),
            P(),
            P(None, None, None, "tensor"),
            P(None, "tensor", None),
            P(),
        ),
        check_vma=False,
    )
```

```python
import functools
import math

import jax
import jax.numpy as jnp
from jax import lax
from jax.experimental import pallas as pl
from jax.experimental.pallas import tpu as pltpu
from jax.sharding import PartitionSpec as P

PLAIN_HEAD_DIM = 64
ROTARY_DIM = 32
VALUE_HEAD_DIM = 64
HEAD_LANES = 128
CODE_LANES = 128
RANK = 16
BLOCK_Q = 256
DOC_LANE = 99
DOC_SLOTS = 24

NORM_EPS = 1e-05
RESIDUAL = 1.4 / math.sqrt(62.0)
ADAPT_SCALE = 2.0
SCORE_SCALE = 1.0 / math.sqrt(PLAIN_HEAD_DIM + ROTARY_DIM)
EXP2_SCALE = SCORE_SCALE * math.log2(math.e)
BIG = 1e30
VMEM_LIMIT = 60 * 1024 * 1024
FREE = pl.CostEstimate(flops=0, bytes_accessed=0, transcendentals=0)
F32 = jnp.float32
BF16 = jnp.bfloat16


def narrow(value):
    return value.astype(BF16)


def dot_nn(a, b):
    return lax.dot_general(a, b, (((1,), (0,)), ((), ())), preferred_element_type=F32)


def dot_nt(a, b):
    return lax.dot_general(a, b, (((1,), (1,)), ((), ())), preferred_element_type=F32)


def dot_tn(a, b):
    return lax.dot_general(a, b, (((0,), (0,)), ((), ())), preferred_element_type=F32)


def normalize(value, gain_vec):
    scale_inv = lax.rsqrt(jnp.mean(value * value, axis=-1, keepdims=True) + NORM_EPS)
    return (value * scale_inv * gain_vec, scale_inv)


def normalize_back(value, scale_inv, gain_vec, grad_in):
    weighted = grad_in * gain_vec
    return scale_inv * weighted - value * scale_inv**3 * jnp.mean(
        value * weighted, axis=-1, keepdims=True
    )


def rope_tables(segments):
    places = jnp.arange(segments.shape[-1], dtype=jnp.int32)
    begins = jnp.concatenate(
        [jnp.ones_like(segments[:, :1]), (segments[:, 1:] != segments[:, :-1]).astype(jnp.int32)],
        axis=1,
    )
    first_place = lax.cummax(places[None, :] * begins, axis=1)
    offsets = (places[None, :] - first_place).astype(F32)
    inv_freq = 10000.0 ** (-2.0 * jnp.arange(ROTARY_DIM // 2, dtype=F32) / ROTARY_DIM)
    angles = offsets[..., None] * inv_freq
    return (jnp.cos(angles)[0], jnp.sin(angles)[0])


def swap(value, axis, bit, size):
    return lax.ppermute(value, axis, [(i, i ^ bit) for i in range(size)])


class Links:
    def __init__(self, send_sems, recv_sems):
        self.send_sems, self.recv_sems = send_sems, recv_sems
        self.place = {"dp": lax.axis_index("dp"), "tensor": lax.axis_index("tensor")}
        self.copies = []
        self.waited = set()

    def peer(self, step):
        place = dict(self.place)
        place[step[0]] = jnp.bitwise_xor(place[step[0]], step[1])
        return (place["dp"], place["tensor"])

    def greet(self, steps):
        barrier = pltpu.get_barrier_semaphore()
        for step in steps:
            pl.semaphore_signal(
                barrier, inc=1, device_id=self.peer(step), device_id_type=pl.DeviceIdType.MESH
            )
        pl.semaphore_wait(barrier, len(steps))

    def prepare(self, src, dst, step):
        n = len(self.copies)
        copy = pltpu.make_async_remote_copy(
            src_ref=src,
            dst_ref=dst,
            send_sem=self.send_sems.at[n],
            recv_sem=self.recv_sems.at[n],
            device_id=self.peer(step),
            device_id_type=pl.DeviceIdType.MESH,
        )
        self.copies.append(copy)
        return n

    def send(self, src, dst, step):
        n = self.prepare(src, dst, step)
        self.copies[n].start()
        return n

    def arrived(self, n):
        if n not in self.waited:
            self.copies[n].wait_recv()
            self.waited.add(n)

    def close(self):
        for n, copy in enumerate(self.copies):
            self.arrived(n)
            copy.wait_send()


class Riders:
    def __init__(self, links, riders, in_refs, out_refs):
        self.links = links
        self.rounds = []
        d = links.place["dp"]
        for rider in riders:
            full = out_refs[rider["out"]]
            if rider["kind"] == "plain":
                src = in_refs[rider["src"]]
                if rider["src_at"] is not None:
                    src = src.at[rider["src_at"]]
                self.add(0, src, full, rider["step"])
                continue
            if rider["kind"] == "block":
                held = [0]
                for k, step in enumerate(rider["steps"]):
                    for key in list(held):
                        here = full.at[rider["at"](links.place, key)]
                        self.add(k, here, here, step)
                        held.append(key ^ step[1])
                continue
            if rider["kind"] == "blocks":
                for key in rider["keys"]:
                    here = full.at[rider["at"](links.place, key)]
                    self.add(0, here, here, rider["step"])
                continue
            count, pair, high = rider["count"], rider["pair"], rider["high"]
            if rider["kind"] == "one":
                begin, size = rider["rows"]
                here = full.at[pl.ds(pl.multiple_of(d * count + begin, 16), size)]
                for name, bit in (("other", pair), ("mine", high), ("other", high ^ pair)):
                    src = in_refs[rider[name]].at[pl.ds(begin, size)]
                    self.add(0, src, here, ("dp", bit))
            else:
                held = [0]
                for k, step in enumerate(rider["steps"]):
                    for key in list(held):
                        place = jnp.bitwise_xor(d, rider["z"] * pair + key)
                        begin, size = rider.get("rows", (0, count))
                        at = pl.multiple_of(place * count + begin, 16)
                        here = full.at[pl.ds(at, size)]
                        self.add(k, here, here, step)
                        held.append(key ^ step[1])

    def add(self, k, src, dst, step):
        while len(self.rounds) <= k:
            self.rounds.append([])
        self.rounds[k].append(self.links.prepare(src, dst, step))

    def start(self):
        if self.rounds:
            for n in self.rounds[0]:
                self.links.copies[n].start()

    def finish(self):
        for k, numbers in enumerate(self.rounds):
            if k:
                for n in numbers:
                    self.links.copies[n].start()
            for n in numbers:
                self.links.arrived(n)


def rider_steps(riders):
    steps = []
    for rider in riders:
        if rider["kind"] in ("plain", "blocks"):
            steps.append(rider["step"])
        elif rider["kind"] == "one":
            pair, high = rider["pair"], rider["high"]
            steps += [("dp", pair), ("dp", high), ("dp", high ^ pair)]
        else:
            steps += rider["steps"]
    return steps


def rider_count(riders):
    total = 0
    for rider in riders:
        if rider["kind"] == "plain":
            total += 1
        elif rider["kind"] == "blocks":
            total += len(rider["keys"])
        elif rider["kind"] == "one":
            total += 3
        else:
            total += (1 << len(rider["steps"])) - 1
    return total


def distinct(steps):
    out = []
    for step in steps:
        if step not in out:
            out.append(step)
    return out


def flip(key, step):
    return (key[0] ^ step[1], key[1]) if step[0] == "dp" else (key[0], key[1] ^ step[1])


def has_bit(key, step):
    return bool((key[0] if step[0] == "dp" else key[1]) & step[1])


def gather_count(jobs):
    return sum((1 << len(job["steps"])) - 1 for job in jobs)


def gather_rounds(links, src_refs, out_refs, jobs):
    d, t = links.place["dp"], links.place["tensor"]

    def landing(job, key):
        at = job["out_at"](jnp.bitwise_xor(d, key[0]), jnp.bitwise_xor(t, key[1]))
        return out_refs[job["out"]].at[at]

    state = []
    for job in jobs:
        src = src_refs[job["src"]]
        if job.get("src_at") is not None:
            src = src.at[job["src_at"]]
        state.append({(0, 0): (src, None)})
    for k in range(max(len(job["steps"]) for job in jobs)):
        for job, held in zip(jobs, state):
            if k >= len(job["steps"]):
                continue
            step = job["steps"][k]
            for key in list(held):
                src, came = held[key]
                if came is not None:
                    links.arrived(came)
                n = links.send(src, landing(job, key), step)
                new = flip(key, step)
                held[new] = (landing(job, new), n)
        yield k


def remote_gather(
    sources,
    jobs,
    extra,
    outs,
    name,
    collective_id,
    riders=(),
    aliases=(),
    distant=(),
    order=(),
    near_outs=(),
    scratch=(),
    work=None,
    late=(),
):
    steps = distinct([s for job in jobs for s in job["steps"]] + rider_steps(riders))
    count = gather_count(jobs) + rider_count(riders)
    aliases = dict(aliases)
    n_src, n_out, n_near = len(sources), len(outs), len(near_outs)

    def kernel(*refs):
        src_refs, refs = refs[:n_src], refs[n_src:]
        out_refs, refs = refs[:n_out], refs[n_out:]
        near, refs = refs[: n_near + len(scratch)], refs[n_near + len(scratch) :]
        send_sems, recv_sems, local_sems = refs
        all_src, all_out = list(src_refs) + list(near), list(out_refs) + list(near)
        links = Links(send_sems, recv_sems)
        d, t = links.place["dp"], links.place["tensor"]
        links.greet(steps)
        ride = Riders(links, riders, src_refs, out_refs)
        local = []

        def keep(src, where):
            copy = pltpu.make_async_copy(src, where, local_sems.at[len(local)])
            copy.start()
            local.append(copy)
            return copy

        for src, out, at in extra:
            keep(all_src[src], all_out[out].at[at(d, t)])
        groups = {}
        for job in jobs:
            groups.setdefault(job.get("group", 0), []).append(job)
        turns = {}
        sent = {g: [] for g in groups}
        kept = {g: [] for g in groups}

        def advance(group):
            before = len(links.copies)
            if group not in turns:
                turns[group] = gather_rounds(links, all_src, all_out, groups[group])
                for job in groups[group]:
                    if not job.get("keep", True):
                        continue
                    src = all_src[job["src"]]
                    if job.get("src_at") is not None:
                        src = src.at[job["src_at"]]
                    kept[group].append(keep(src, all_out[job["out"]].at[job["out_at"](d, t)]))
            going = next(turns[group], None) is not None
            sent[group] += range(before, len(links.copies))
            return going

        waited = set()
        if "ride" not in order:
            ride.start()
        for turn in order:
            if turn == "ride":
                ride.start()
            elif callable(turn):
                turn(all_src)
            elif turn == "work":
                work(all_src)
                for src, out in late:
                    keep(all_src[src], all_out[out])
            elif isinstance(turn, tuple):
                for n in sent[turn[1]]:
                    links.arrived(n)
                for copy in kept[turn[1]]:
                    copy.wait()
                waited.add(turn[1])
            else:
                advance(turn)
        for group in groups:
            while advance(group):
                pass
        ride.finish()
        links.close()
        done = [copy for group in waited for copy in kept[group]]
        for copy in local:
            if not any(copy is other for other in done):
                copy.wait()

    vmem = pl.BlockSpec(memory_space=pltpu.VMEM)
    far = pl.BlockSpec(memory_space=pl.ANY)
    return pl.pallas_call(
        kernel,
        out_shape=[jax.ShapeDtypeStruct(o, BF16) for o in outs] + list(near_outs),
        in_specs=[far if n in aliases or n in distant else vmem for n in range(n_src)],
        out_specs=[far] * n_out + [vmem] * n_near,
        scratch_shapes=[pltpu.VMEM(o.shape, o.dtype) for o in scratch]
        + [
            pltpu.SemaphoreType.DMA((count,)),
            pltpu.SemaphoreType.DMA((count,)),
            pltpu.SemaphoreType.DMA((len(jobs) + len(extra) + len(late),)),
        ],
        input_output_aliases=aliases,
        compiler_params=pltpu.CompilerParams(
            collective_id=collective_id, has_side_effects=True, vmem_limit_bytes=VMEM_LIMIT
        ),
        cost_estimate=FREE,
        name=name,
    )(*sources)


def reduce_plan(keys, ways):
    plan = []
    for w, steps in enumerate(ways):
        live = list(keys)
        for k, step in enumerate(steps):
            plan += [(w, k, key) for key in live if has_bit(key, step)]
            live = [key for key in live if not has_bit(key, step)]
    return plan


def remote_reduce(
    operands, fetched, term, keys, ways, rows, wide, name, collective_id, riders=(), ridden=(), carried=(), jobs=(), job_sources=(), job_outs=(), after=None, after_in=(), after_out=()
):
    core_step = ("tensor", 1)
    part = rows // len(ways)
    plan = reduce_plan(keys, ways)
    slot = {entry: n for n, entry in enumerate(plan)}
    steps = distinct(
        [core_step]
        + [s for s in ways[0]]
        + rider_steps(riders)
        + [s for job in jobs for s in job["steps"]]
    )
    count = len(keys) + len(plan) + rider_count(riders) + gather_count(jobs)
    n_in = len(operands)
    n_ride = n_in + len(ridden) + len(carried)
    n_all = n_ride + len(job_sources)
    n_jobs = len(job_outs)
    after_out = list(after_out) or [jax.ShapeDtypeStruct((rows, wide), F32)]
    n_own = len(after_out)

    def kernel(*refs):
        in_refs = refs[:n_in]
        own_out = refs[n_all + len(after_in) : n_all + len(after_in) + n_own]
        extra_in = refs[n_all : n_all + len(after_in)]
        refs = refs[:n_all] + refs[n_all + len(after_in) + n_own - 1 :]
        ride_in = refs[n_in:n_ride]
        job_in = refs[n_ride:n_all]
        ride_out = refs[n_all + 1 : n_all + 1 + len(ridden)]
        job_out = refs[n_all + 1 + len(ridden) : n_all + 1 + len(ridden) + n_jobs]
        scratch = refs[n_all + 1 + len(ridden) + n_jobs :]
        held = scratch[:n_in]
        core_out, core_in, chip, hop_out, hop_in, send_sems, recv_sems, in_sems, job_sems = scratch[
            n_in:
        ]
        started = []
        for n in range(n_in):
            shape = fetched[n]
            src = in_refs[n].at[tuple(pl.ds(0, s) for s in shape)]
            copy = pltpu.make_async_copy(src, held[n], in_sems.at[n])
            copy.start()
            started.append(copy)
        links = Links(send_sems, recv_sems)
        links.greet(steps)
        ride = Riders(links, riders, ride_in, ride_out)
        ride.start()
        rounds = gather_rounds(links, job_in, job_out, jobs) if jobs else iter(())
        next(rounds, None)
        placed = []
        for n, job in enumerate(jobs):
            at = job["out_at"](links.place["dp"], links.place["tensor"])
            copy = pltpu.make_async_copy(
                job_in[job["src"]], job_out[job["out"]].at[at], job_sems.at[n]
            )
            copy.start()
            placed.append(copy)
        for copy in started:
            copy.wait()
        came = {}

        def send_part(w, k, key):
            entry = (w, k, key)
            came[entry] = links.send(hop_out.at[slot[entry]], hop_in.at[slot[entry]], ways[w][k])

        def so_far(w, k, key):
            total = chip[keys.index(key), w * part : (w + 1) * part, :]
            for j in range(k):
                entry = (w, j, flip(key, ways[w][j]))
                links.arrived(came[entry])
                total = total + hop_in[slot[entry]].astype(F32)
            return total

        for i, key in enumerate(keys):
            core_out[i] = narrow(term(held, links.place, (key[0], key[1] ^ 1)))
            crossing = links.send(core_out.at[i], core_in.at[i], core_step)
            mine = term(held, links.place, key)
            links.arrived(crossing)
            chip[i] = mine + core_in[i].astype(F32)
            for w, way in enumerate(ways):
                if way and has_bit(key, way[0]):
                    hop_out[slot[(w, 0, key)]] = narrow(chip[i, w * part : (w + 1) * part, :])
                    send_part(w, 0, key)
            next(rounds, None)
        for k in range(1, len(ways[0])):
            for w in range(len(ways)):
                for entry in plan:
                    if entry[0] == w and entry[1] == k:
                        hop_out[slot[entry]] = narrow(so_far(w, k, entry[2]))
                        send_part(w, k, entry[2])
        for w in range(len(ways)):
            total = so_far(w, len(ways[w]), (0, 0))
            if after is None:
                own_out[0][w * part : (w + 1) * part, :] = total
            else:
                after(slice(w * part, (w + 1) * part), total, extra_in, own_out)
        for _ in rounds:
            pass
        ride.finish()
        links.close()
        for copy in placed:
            copy.wait()

    any_spec = pl.BlockSpec(memory_space=pl.ANY)
    return pl.pallas_call(
        kernel,
        out_shape=after_out
        + [jax.ShapeDtypeStruct(r.shape, r.dtype) for r in ridden]
        + [jax.ShapeDtypeStruct(o, BF16) for o in job_outs],
        in_specs=[any_spec] * n_ride
        + [pl.BlockSpec(memory_space=pltpu.VMEM)] * (len(job_sources) + len(after_in)),
        out_specs=[pl.BlockSpec(memory_space=pltpu.VMEM)] * n_own
        + [any_spec] * (len(ridden) + n_jobs),
        input_output_aliases={n_in + n: n_own + n for n in range(len(ridden))},
        scratch_shapes=[pltpu.VMEM(s, o.dtype) for s, o in zip(fetched, operands)]
        + [
            pltpu.VMEM((len(keys), rows, wide), BF16),
            pltpu.VMEM((len(keys), rows, wide), BF16),
            pltpu.VMEM((len(keys), rows, wide), F32),
            pltpu.VMEM((max(len(plan), 1), part, wide), BF16),
            pltpu.VMEM((max(len(plan), 1), part, wide), BF16),
            pltpu.SemaphoreType.DMA((count,)),
            pltpu.SemaphoreType.DMA((count,)),
            pltpu.SemaphoreType.DMA((n_in,)),
            pltpu.SemaphoreType.DMA((max(len(jobs), 1),)),
        ],
        compiler_params=pltpu.CompilerParams(
            collective_id=collective_id, has_side_effects=True, vmem_limit_bytes=VMEM_LIMIT
        ),
        cost_estimate=FREE,
        name=name,
    )(*operands, *ridden, *carried, *job_sources, *after_in)


class Share:
    def __init__(self, links, n_t, orders, source, out, own, sums, came, went, terms, fetch_sem):
        self.links, self.terms, self.own = links, terms, own
        self.fetch = pltpu.make_async_copy(source, terms, fetch_sem.at[0])
        self.sums, self.came, self.went = sums, came, went
        self.count = terms.shape[0] // n_t
        self.wide = terms.shape[1] // len(orders)
        count = self.count
        t_steps = [("tensor", 1 << b) for b in range(n_t.bit_length() - 1)]
        self.rounds = []
        live, slot = list(range(n_t)), 0
        before = []
        for k, step in enumerate(t_steps):
            sent = []
            for r in live:
                if r & step[1]:
                    src = terms.at[self.block(r)] if k == 0 else went.at[slot]
                    sent.append((r, slot, links.prepare(src, came.at[slot], step)))
                    slot += 1
            live = [r for r in live if not r & step[1]]
            self.rounds.append(functools.partial(self.scatter, k, list(live), before, sent, step))
            before = [(r ^ step[1], at, n) for r, at, n in sent]
        d, t = links.place["dp"], links.place["tensor"]

        def landing(p, key):
            rows = pl.ds(pl.multiple_of(jnp.bitwise_xor(t, key[1]) * count, 16), count)
            return out.at[p, jnp.bitwise_xor(d, key[0]), rows]

        self.places = [landing(p, (0, 0)) for p in range(len(orders))]
        held = [{(0, 0): (own.at[p], None)} for p in range(len(orders))]
        seen = set()
        for k in range(len(orders[0])):
            work = []
            for p, order in enumerate(orders):
                step = order[k]
                for key in list(held[p]):
                    src, needs = held[p][key]
                    n = links.prepare(src, landing(p, key), step)
                    work.append((None if needs in seen else needs, n))
                    seen.add(needs)
                    new = flip(key, step)
                    held[p][new] = (landing(p, new), n)
            self.rounds.append(functools.partial(self.gather, k, before, work))

    def block(self, r):
        at = jnp.bitwise_xor(self.links.place["tensor"], r) * self.count
        return pl.ds(pl.multiple_of(at, 16), self.count)

    def scatter(self, k, live, before, sent, step):
        if k == 0:
            self.fetch.start()
            self.fetch.wait()
            for r in live:
                self.sums[r] = self.terms[self.block(r), :].astype(F32)
        self.add(before)
        for r, at, n in sent:
            if k:
                self.went[at] = narrow(self.sums[r])
            self.links.copies[n].start()

    def add(self, before):
        for r, at, n in before:
            self.links.arrived(n)
            self.sums[r] = self.sums[r] + self.came[at].astype(F32)

    def gather(self, k, before, work):
        if k == 0:
            self.add(before)
            for p in range(self.own.shape[0]):
                self.own[p] = narrow(self.sums[0, :, p * self.wide : (p + 1) * self.wide])
        for needs, n in work:
            if needs is not None:
                self.links.copies[needs].wait_recv()
                self.links.waited.add(needs)
            self.links.copies[n].start()

    def keep(self, sems):
        return [
            pltpu.make_async_copy(self.own.at[p], where, sems.at[p])
            for p, where in enumerate(self.places)
        ]


def share_shapes(shape, n_t, orders):
    count, parts = shape[0] // n_t, len(orders)
    copies = n_t - 1 + parts * ((1 << len(orders[0])) - 1)
    scratch = [
        pltpu.VMEM((parts, count, shape[1] // parts), BF16),
        pltpu.VMEM((n_t, count, shape[1]), F32),
        pltpu.VMEM((n_t - 1, count, shape[1]), BF16),
        pltpu.VMEM((n_t - 1, count, shape[1]), BF16),
        pltpu.VMEM(shape, BF16),
        pltpu.SemaphoreType.DMA((1,)),
        pltpu.SemaphoreType.DMA((parts,)),
    ]
    return scratch, copies


def remote_share(terms, n_dp, n_t, orders, name, collective_id, work_in, work_out, work):
    scratch, copies = share_shapes(terms.shape, n_t, orders)
    parts = len(orders)

    n_in, n_work = len(work_in), len(work_out)

    def kernel(source, *refs):
        work_refs = refs[:n_in] + refs[n_in + 1 : n_in + 1 + n_work]
        out_ref = refs[n_in]
        refs = refs[n_in + 1 + n_work :]
        held, refs = refs[:n_in], refs[n_in:]
        own_sems, send_sems, recv_sems, in_sems = refs[-4:]
        fetched = [
            pltpu.make_async_copy(work_refs[n], held[n], in_sems.at[n]) for n in range(n_in)
        ]
        for copy in fetched:
            copy.start()
        links = Links(send_sems, recv_sems)
        links.greet(orders[0])
        share = Share(links, n_t, orders, source, out_ref, *refs[:-4])
        for k, one in enumerate(share.rounds):
            one()
            if k == len(share.rounds) - 2:
                for copy in fetched:
                    copy.wait()
                work(list(held) + list(work_refs[n_in:]))
        kept = share.keep(own_sems)
        for copy in kept:
            copy.start()
        links.close()
        for copy in kept:
            copy.wait()

    return pl.pallas_call(
        kernel,
        out_shape=[
            jax.ShapeDtypeStruct((parts, n_dp, terms.shape[0], terms.shape[1] // parts), BF16)
        ]
        + list(work_out),
        in_specs=[pl.BlockSpec(memory_space=pl.ANY)]
        + [pl.BlockSpec(memory_space=pl.ANY)] * n_in,
        out_specs=[pl.BlockSpec(memory_space=pl.ANY)]
        + [pl.BlockSpec(memory_space=pltpu.VMEM)] * n_work,
        scratch_shapes=[pltpu.VMEM(a.shape, a.dtype) for a in work_in]
        + scratch
        + [
            pltpu.SemaphoreType.DMA((copies,)),
            pltpu.SemaphoreType.DMA((copies,)),
            pltpu.SemaphoreType.DMA((n_in,)),
        ],
        compiler_params=pltpu.CompilerParams(
            collective_id=collective_id, has_side_effects=True, vmem_limit_bytes=VMEM_LIMIT
        ),
        cost_estimate=FREE,
        name=name,
    )(terms, *work_in)


def set_sums(set_ids, sources, acc_shape, add, outs, put, groups, name):
    n_src = len(sources)
    count = set_ids.shape[0]

    def kernel(ids_ref, *refs):
        src_refs, out_refs, acc = refs[:n_src], refs[n_src:-1], refs[-1]
        k = pl.program_id(0)
        acc[...] = jnp.zeros_like(acc)
        for s in range(count):

            @pl.when(ids_ref[s] == k)
            def _(s=s):
                add(s, src_refs, acc)

        put(acc, out_refs)

    out_specs = []
    for before, after in outs:
        lead = len(before)
        block = tuple(before) + (1,) + tuple(after)
        out_specs.append(
            pl.BlockSpec(
                block, lambda k, ids, lead=lead, n=len(after): (0,) * lead + (k,) + (0,) * n
            )
        )
    return pl.pallas_call(
        kernel,
        grid_spec=pltpu.PrefetchScalarGridSpec(
            num_scalar_prefetch=1,
            grid=(groups,),
            in_specs=[
                pl.BlockSpec(a.shape, lambda k, ids, n=a.ndim: (0,) * n) for a in sources
            ],
            out_specs=out_specs,
            scratch_shapes=[pltpu.VMEM(acc_shape, F32)],
        ),
        out_shape=[
            jax.ShapeDtypeStruct(tuple(before) + (groups,) + tuple(after), F32)
            for before, after in outs
        ],
        compiler_params=pltpu.CompilerParams(vmem_limit_bytes=VMEM_LIMIT),
        cost_estimate=FREE,
        name=name,
    )(set_ids, *sources)


def split_three(value):
    high = narrow(value).astype(F32)
    middle = narrow(value - high).astype(F32)
    return high, middle, value - high - middle


def rope_mix(value, cos_l, sin_a, sin_b):
    return (
        value * cos_l
        + pltpu.roll(value, HEAD_LANES - ROTARY_DIM // 2, 1) * sin_a
        + pltpu.roll(value, ROTARY_DIM // 2, 1) * sin_b
    )


def attn_fwd_kernel(
    per_step, q_width, kv_at, xl_ref, wq_ref, wkv_ref, rope_ref, pe_ref, doc_ref, qa_ref, kv_ref, o_ref
):
    length = xl_ref.shape[0]
    lane = lax.broadcasted_iota(jnp.int32, (length, HEAD_LANES), 1)
    q_all = dot_nn(xl_ref[:, :q_width], wq_ref[...])
    kv_all = dot_nn(xl_ref[:, kv_at:], wkv_ref[...])
    kv_ref[...] = narrow(kv_all)
    doc_q = doc_ref[...].astype(F32)
    q_heads, k_heads, kv_turned = [], [], []
    for i in range(per_step):
        span = slice(i * HEAD_LANES, (i + 1) * HEAD_LANES)
        q_one = rope_mix(q_all[:, span], rope_ref[0], rope_ref[1], rope_ref[2]) + doc_q
        q_heads.append(narrow(q_one))
        kv_one = kv_all[:, span]
        k_heads.append(jnp.where(lane < PLAIN_HEAD_DIM, narrow(kv_one), pe_ref[...]))
        kv_turned.append(narrow(kv_one.T))
    key_at = lax.broadcasted_iota(jnp.int32, (BLOCK_Q, BLOCK_Q), 0)
    query_at = lax.broadcasted_iota(jnp.int32, (BLOCK_Q, BLOCK_Q), 1)
    row = lax.broadcasted_iota(jnp.int32, (HEAD_LANES, BLOCK_Q), 0)
    block_lane = lax.broadcasted_iota(jnp.int32, (BLOCK_Q, HEAD_LANES), 1)
    for j in range(length // BLOCK_Q):
        begin, end = j * BLOCK_Q, (j + 1) * BLOCK_Q
        mixed = []
        for i in range(per_step):
            q_part = q_heads[i][begin:end]
            scores = dot_nt(k_heads[i][:end], q_part)
            diag = jnp.where(key_at <= query_at, scores[begin:], -BIG)
            scores = diag if j == 0 else jnp.concatenate([scores[:begin], diag], axis=0)
            top = jnp.max(scores, axis=0, keepdims=True)
            terms = jnp.exp2((scores - top) * EXP2_SCALE)
            total = jnp.sum(terms, axis=0, keepdims=True)
            out_t = dot_nn(kv_turned[i][:, :end], narrow(terms)) * (1.0 / total)
            high, middle, low = split_three(top + jnp.log2(total) * (1.0 / EXP2_SCALE))
            out_t = jnp.where(
                row == 0, -high, jnp.where(row == 1, -middle, jnp.where(row == 2, -low, out_t))
            )
            out_n = out_t.T
            mixed.append(out_n)
            is_lse = (block_lane >= 96) & (block_lane < 99)
            q_saved = jnp.where(is_lse, narrow(pltpu.roll(out_n, 96, 1)), q_part)
            qa_ref[begin:end, i * HEAD_LANES : (i + 1) * HEAD_LANES] = q_saved
        if per_step == 2:
            both = jnp.where(block_lane < 64, pltpu.roll(mixed[0], 64, 1), mixed[1])
            o_ref[begin:end, :] = narrow(both)
        else:
            even = lax.rem(pl.program_id(0), 2) == 0
            moved = jnp.where(even, pltpu.roll(mixed[0], 64, 1), mixed[0])
            mine = (block_lane < 64) == even
            o_ref[begin:end, :] = jnp.where(mine, narrow(moved), o_ref[begin:end, :])


def attn_bwd_kernel(
    per_step,
    qa_ref,
    kv_ref,
    o_ref,
    do_ref,
    rope_ref,
    pe_ref,
    codes_ref,
    dq_ref,
    dkv_ref,
    dpe_ref,
    cq_ref,
    ckv_ref,
    dk_acc,
    dv_acc,
):
    length = qa_ref.shape[0]
    step = pl.program_id(0)
    lane = lax.broadcasted_iota(jnp.int32, (length, HEAD_LANES), 1)
    upper = lane >= 64
    key_at = lax.broadcasted_iota(jnp.int32, (BLOCK_Q, BLOCK_Q), 0)
    query_at = lax.broadcasted_iota(jnp.int32, (BLOCK_Q, BLOCK_Q), 1)
    causal = key_at <= query_at
    out_both = o_ref[...].astype(F32)
    grad_both = do_ref[...].astype(F32)

    @pl.when(step == 0)
    def _():
        dpe_ref[...] = jnp.zeros_like(dpe_ref)

    for i in range(per_step):
        span = slice(i * HEAD_LANES, (i + 1) * HEAD_LANES)
        if per_step == 2:
            turn = i == 0
            grad_one = pltpu.roll(grad_both, 64, 1) if turn else grad_both
            out_one = pltpu.roll(out_both, 64, 1) if turn else out_both
        else:
            even = lax.rem(step, 2) == 0
            grad_one = jnp.where(even, pltpu.roll(grad_both, 64, 1), grad_both)
            out_one = jnp.where(even, pltpu.roll(out_both, 64, 1), out_both)
        grad_one = jnp.where(upper, grad_one, 0.0)
        inner = jnp.sum(jnp.where(upper, grad_one * out_one, 0.0), axis=-1, keepdims=True)
        high, middle, low = split_three(inner)
        grad_aug = jnp.where(
            lane == 0, -high, jnp.where(lane == 1, -middle, jnp.where(lane == 2, -low, grad_one))
        )
        grad_aug = narrow(grad_aug)
        kv_one = kv_ref[:, span]
        ones = jnp.where(lane < 3, 1.0, 0.0).astype(BF16)
        v_aug = jnp.where(upper, kv_one, ones)
        k_aug = jnp.where(lane < 64, kv_one, pe_ref[...])
        k_turned = narrow(k_aug.astype(F32).T)
        for j in reversed(range(length // BLOCK_Q)):
            begin, end = j * BLOCK_Q, (j + 1) * BLOCK_Q
            q_part = qa_ref[begin:end, span]
            probs = jnp.exp2(dot_nt(k_aug[:end], q_part) * EXP2_SCALE)
            diag = jnp.where(causal, probs[begin:], 0.0)
            probs = diag if j == 0 else jnp.concatenate([probs[:begin], diag], axis=0)
            grads = narrow(probs * dot_nt(v_aug[:end], grad_aug[begin:end]))
            dq_part = dot_nn(k_turned[:, :end], grads).T * SCORE_SCALE
            dq_part = rope_mix(
                dq_part,
                rope_ref[0, begin:end, :],
                -rope_ref[1, begin:end, :],
                -rope_ref[2, begin:end, :],
            )
            dq_ref[begin:end, span] = narrow(dq_part)
            dk_part = dot_nn(grads, q_part)
            dv_part = dot_nn(narrow(probs), grad_aug[begin:end])
            if end == length:
                dk_acc[...] = dk_part
                dv_acc[...] = dv_part
            else:
                dk_acc[:end] += dk_part
                dv_acc[:end] += dv_part
        dk_all = dk_acc[...] * SCORE_SCALE
        dkv_ref[:, span] = narrow(jnp.where(upper, dv_acc[...], dk_all))
        dpe_ref[...] += jnp.where(upper & (lane < 96), dk_all, 0.0)
    cq_ref[...] = dot_tn(codes_ref[...], dq_ref[...])
    ckv_ref[...] = dot_tn(codes_ref[...], dkv_ref[...])

    @pl.when(step == pl.num_programs(0) - 1)
    def _():
        turned_back = rope_mix(dpe_ref[...], rope_ref[0], -rope_ref[1], -rope_ref[2])
        dpe_ref[...] = pltpu.roll(turned_back, PLAIN_HEAD_DIM + 2 * RANK, 1)


def ridden_call(
    kernel,
    grid,
    arrays,
    in_specs,
    out_shape,
    out_specs,
    scratch,
    riders,
    ridden,
    carried,
    fresh,
    name,
    collective_id,
):
    steps = distinct(rider_steps(riders))
    count = rider_count(riders)
    n_in, n_out = len(arrays), len(out_shape)
    n_ride_in = len(ridden) + len(carried)
    n_ride_out = len(ridden) + len(fresh)
    def body(*refs):
        own_in, rest = refs[:n_in], refs[n_in:]
        ride_in, rest = rest[:n_ride_in], rest[n_ride_in:]
        own_out, rest = rest[:n_out], rest[n_out:]
        ride_out, rest = rest[:n_ride_out], rest[n_ride_out:]
        send_sems, recv_sems = rest[-2:]
        links = Links(send_sems, recv_sems)
        ride = Riders(links, riders, ride_in, ride_out)

        @pl.when(pl.program_id(0) == 0)
        def _():
            links.greet(steps)
            ride.start()

        kernel(*own_in, *own_out, *rest[:-2])

        @pl.when(pl.program_id(0) == grid[0] - 1)
        def _():
            ride.finish()
            links.close()

    any_spec = pl.BlockSpec(memory_space=pl.ANY)
    return pl.pallas_call(
        body,
        grid=grid,
        in_specs=list(in_specs) + [any_spec] * n_ride_in,
        out_specs=list(out_specs) + [any_spec] * n_ride_out,
        out_shape=list(out_shape)
        + [jax.ShapeDtypeStruct(r.shape, r.dtype) for r in ridden]
        + [jax.ShapeDtypeStruct(f, BF16) for f in fresh],
        scratch_shapes=list(scratch)
        + [pltpu.SemaphoreType.DMA((count,)), pltpu.SemaphoreType.DMA((count,))],
        input_output_aliases={n_in + n: n_out + n for n in range(len(ridden))},
        compiler_params=pltpu.CompilerParams(
            collective_id=collective_id, has_side_effects=True, vmem_limit_bytes=VMEM_LIMIT
        ),
        cost_estimate=FREE,
        name=name,
    )(*arrays, *ridden, *carried)


def attend(latents, w_q, w_kv, rope, pe_aug, doc_q, q_width, kv_at, riders, ridden, carried):
    length = latents.shape[0]
    heads = w_q.shape[1] // HEAD_LANES
    per_step = 2 if heads % 2 == 0 else 1
    wide = per_step * HEAD_LANES
    whole = lambda a: pl.BlockSpec(a.shape, lambda h: (0,) * a.ndim)
    return ridden_call(
        functools.partial(attn_fwd_kernel, per_step, q_width, kv_at),
        (heads // per_step,),
        [latents, w_q, w_kv, rope, pe_aug, doc_q],
        [
            whole(latents),
            pl.BlockSpec((w_q.shape[0], wide), lambda h: (0, h)),
            pl.BlockSpec((w_kv.shape[0], wide), lambda h: (0, h)),
            whole(rope),
            whole(pe_aug),
            whole(doc_q),
        ],
        [
            jax.ShapeDtypeStruct((length, heads * HEAD_LANES), BF16),
            jax.ShapeDtypeStruct((length, heads * HEAD_LANES), BF16),
            jax.ShapeDtypeStruct((length, heads * VALUE_HEAD_DIM), BF16),
        ],
        [
            pl.BlockSpec((length, wide), lambda h: (0, h)),
            pl.BlockSpec((length, wide), lambda h: (0, h)),
            pl.BlockSpec((length, HEAD_LANES), lambda h: (0, h * per_step // 2)),
        ],
        [],
        riders,
        ridden,
        carried,
        [],
        "attend",
        10,
    )


def attend_back(q_aug, kv, heads_out, heads_grad, rope, pe_aug, codes, riders, ridden, carried, fresh):
    length = q_aug.shape[0]
    heads = q_aug.shape[1] // HEAD_LANES
    per_step = 2 if heads % 2 == 0 else 1
    wide = per_step * HEAD_LANES
    whole = lambda a: pl.BlockSpec(a.shape, lambda h: (0,) * a.ndim)
    columns = pl.BlockSpec((length, wide), lambda h: (0, h))
    packed = pl.BlockSpec((length, HEAD_LANES), lambda h: (0, h * per_step // 2))
    rows_in, lane_block = codes
    arrays = [q_aug, kv, heads_out, heads_grad, rope, pe_aug, rows_in]
    in_specs = [columns, columns, packed, packed, whole(rope), whole(pe_aug)]
    in_specs.append(pl.BlockSpec((length, CODE_LANES), lambda h: (0, lane_block)))
    out_shape = [
        jax.ShapeDtypeStruct((length, heads * HEAD_LANES), BF16),
        jax.ShapeDtypeStruct((length, heads * HEAD_LANES), BF16),
        jax.ShapeDtypeStruct((length, HEAD_LANES), F32),
    ] + [jax.ShapeDtypeStruct((CODE_LANES, heads * HEAD_LANES), F32)] * 2
    out_specs = [columns, columns, pl.BlockSpec((length, HEAD_LANES), lambda h: (0, 0))]
    out_specs += [pl.BlockSpec((CODE_LANES, wide), lambda h: (0, h))] * 2
    scratch = [pltpu.VMEM((length, HEAD_LANES), F32), pltpu.VMEM((length, HEAD_LANES), F32)]
    return ridden_call(
        functools.partial(attn_bwd_kernel, per_step),
        (heads // per_step,),
        arrays,
        in_specs,
        out_shape,
        out_specs,
        scratch,
        riders,
        ridden,
        carried,
        fresh,
        "attend_back",
        11,
    )


def gate_middle(gate, up, hid_grad):
    sig = 1.0 / (1.0 + jnp.exp(-gate))
    silu = gate * sig
    gate_grad = hid_grad * up * (sig * (1.0 + gate * (1.0 - sig)))
    return silu * up, gate_grad, hid_grad * silu


def tail_middle(pre, back, tail):
    wide = pre.shape[1]
    up = pltpu.roll(pre, wide - tail, 1)
    hid_grad = pltpu.roll(back, wide - 2 * tail, 1)
    hid, gate_grad, up_grad = gate_middle(pre, up, hid_grad)
    lane = lax.broadcasted_iota(jnp.int32, pre.shape, 1)
    hid = jnp.where((lane >= 2 * tail) & (lane < 3 * tail), pltpu.roll(hid, 2 * tail, 1), 0.0)
    both = jnp.where(
        lane < tail, gate_grad, jnp.where(lane < 2 * tail, pltpu.roll(up_grad, tail, 1), 0.0)
    )
    return hid, both


def remote_ffn(x_own, g_all, weights, extras, mains, tail, tail_wide, slow, block_of, riders, name, collective_id):
    rows, aug = x_own.shape
    total = g_all.shape[0]
    blocks = total // rows
    both = 2 * rows
    width = aug - CODE_LANES
    chunks = len(mains)
    tails = [0] * (chunks - 1) + [tail_wide]
    gu = [2 * m + w for m, w in zip(mains, tails)]
    core_step = ("tensor", 1)
    keys = [(0, 0)]
    for step in slow:
        keys += [flip(key, step) for key in keys]
    bits_of = {key: [s for s in slow if has_bit(key, s)] for key in keys}
    keys.sort(key=lambda k: len(bits_of[k]))

    def part_rows(key, step):
        n = len(bits_of[key])
        i = bits_of[key].index(step)
        size = -(-rows // (16 * n)) * 16
        begin = i * size
        return begin, min(size, rows - begin)

    count = len(keys) + sum(len(bits_of[k]) for k in keys) + rider_count(riders)
    steps = distinct([core_step] + slow + rider_steps(riders))

    def kernel(x_ref, g_ref, *refs):
        e_refs = refs[chunks : 2 * chunks]
        refs = refs[2 * chunks :]
        codes_ref = refs[0]
        grad_refs = refs[1 : 1 + chunks]
        hid_refs = refs[1 + chunks : 1 + 2 * chunks]
        w_refs = refs[1 + 2 * chunks : 1 + 3 * chunks]
        x_held, back_held, g_held = refs[1 + 3 * chunks : 4 + 3 * chunks]
        w_held = refs[4 + 3 * chunks : 4 + 4 * chunks]
        send_sems, recv_sems, w_sems, g_sems = refs[4 + 4 * chunks :]
        links = Links(send_sems, recv_sems)
        place = links.place
        fetch = [
            pltpu.make_async_copy(w_refs[c], w_held[c].at[pl.ds(0, width)], w_sems.at[c])
            for c in range(chunks)
        ]
        fetch_extra = [
            pltpu.make_async_copy(
                e_refs[c], w_held[c].at[pl.ds(width, CODE_LANES)], w_sems.at[chunks + c]
            )
            for c in range(chunks)
        ]
        fetch[0].start()
        for copy in fetch_extra:
            copy.start()
        links.greet(steps)

        def landing(key):
            at = pl.multiple_of(block_of(key, place) * rows, 16)
            return x_held.at[pl.ds(at, rows)]

        arrivals = {key: [] for key in keys}

        def pass_on(key, src):
            for step in slow:
                if has_bit(key, step):
                    continue
                there = flip(key, step)
                begin, size = part_rows(there, step)
                at = pl.ds(begin, size)
                n = links.send(src.at[at], landing(key).at[at], step)
                arrivals[there].append(n)

        crossing = {}
        pass_on((0, 0), x_ref)
        crossing[(0, 0)] = links.send(x_ref, landing((0, 0)), core_step)
        ride = Riders(links, riders, w_refs, w_refs)
        ride.start()
        x_held[pl.ds(pl.multiple_of(block_of((0, 0), place) * rows, 16), rows), :] = x_ref[...]

        def g_copy(b, slot):
            at = pl.ds(pl.multiple_of(b * both, 16), both)
            return pltpu.make_async_copy(g_ref.at[at], g_held.at[slot], g_sems.at[slot])

        def over_blocks(work):
            g_copy(0, 0).start()

            def one(b, carry):
                slot = lax.rem(b, 2)

                @pl.when(b + 1 < blocks // 2)
                def _():
                    g_copy(b + 1, 1 - slot).start()

                g_copy(b, slot).wait()
                work(b, g_held[slot])
                return carry

            lax.fori_loop(0, blocks // 2, one, 0)

        fetch[0].wait()
        for copy in fetch_extra:
            copy.wait()

        def back_first(b, g_rows):
            back_held[b] = dot_nn(g_rows, w_held[0][:, gu[0] :])

        over_blocks(back_first)

        def forward(b, c, back):
            main = mains[c]
            at = pl.ds(pl.multiple_of(b * both, 16), both)
            pre = dot_nn(x_held[at, :], w_held[c][:, : gu[c]])
            hid, gate_grad, up_grad = gate_middle(pre[:, :main], pre[:, gu[c] - main :], back)
            hid_refs[c][at, :main] = narrow(hid)
            grad_refs[c][at, :main] = narrow(gate_grad)
            grad_refs[c][at, gu[c] - main :] = narrow(up_grad)
            return pre, at

        def first_chunk(key):
            b = block_of(key, place) // 2
            forward(b, 0, back_held[b])

        links.arrived(crossing[(0, 0)])
        first_chunk((0, 0))

        def later(b, g_rows, c):
            main = mains[c]
            back = dot_nn(g_rows, w_held[c][:, gu[c] :])
            pre, at = forward(b, c, back)
            if tails[c]:
                at_tail = slice(main, main + tail_wide)
                hid, both_grads = tail_middle(
                    pre[:, at_tail], dot_nn(g_rows, w_held[c][:, at_tail]), tail
                )
                hid_refs[c][at, main:] = narrow(hid)
                grad_refs[c][at, at_tail] = narrow(both_grads)

        def later_chunks(pairs):
            places = [block_of(key, place) // 2 for key in pairs]
            g_copy(places[0], 0).start()
            for n, b in enumerate(places):
                if n + 1 < len(places):
                    g_copy(places[n + 1], (n + 1) % 2).start()
                g_copy(b, n % 2).wait()
                for c in range(1, chunks):
                    later(b, g_held[n % 2], c)

        waiting = [(0, 0)]
        for level in range(1, len(slow) + 1):
            here = [key for key in keys if len(bits_of[key]) == level]
            for key in here:
                for n in arrivals[key]:
                    links.arrived(n)
                pass_on(key, landing(key))
                crossing[key] = links.send(landing(key), landing(key), core_step)
            for key in here:
                links.arrived(crossing[key])
                first_chunk(key)
            waiting += here
            if level == len(slow) - 1:
                ride.finish()
                for c in range(1, chunks):
                    fetch[c].start()
                    fetch[c].wait()
                later_chunks(waiting)
                waiting = []
        later_chunks(waiting)
        codes_ref[...] = x_held[:, width:]
        links.close()

    any_spec = pl.BlockSpec(memory_space=pl.ANY)
    vmem_spec = pl.BlockSpec(memory_space=pltpu.VMEM)
    outs = pl.pallas_call(
        kernel,
        in_specs=[vmem_spec, any_spec] + [any_spec] * (2 * chunks),
        out_specs=[vmem_spec] * (1 + 2 * chunks) + [any_spec] * chunks,
        out_shape=[jax.ShapeDtypeStruct((total, CODE_LANES), BF16)]
        + [jax.ShapeDtypeStruct((total, g), BF16) for g in gu]
        + [jax.ShapeDtypeStruct((total, m + w), BF16) for m, w in zip(mains, tails)]
        + [jax.ShapeDtypeStruct(w.shape, BF16) for w in weights],
        scratch_shapes=[
            pltpu.VMEM((total, aug), BF16),
            pltpu.VMEM((blocks // 2, both, mains[0]), F32),
            pltpu.VMEM((2, both, aug), BF16),
        ]
        + [pltpu.VMEM((aug, w.shape[1]), BF16) for w in weights]
        + [
            pltpu.SemaphoreType.DMA((count,)),
            pltpu.SemaphoreType.DMA((count,)),
            pltpu.SemaphoreType.DMA((2 * chunks,)),
            pltpu.SemaphoreType.DMA((2,)),
        ],
        input_output_aliases={2 + c: 1 + 2 * chunks + c for c in range(chunks)},
        compiler_params=pltpu.CompilerParams(
            collective_id=collective_id, has_side_effects=True, vmem_limit_bytes=VMEM_LIMIT
        ),
        cost_estimate=FREE,
        name=name,
    )(x_own, g_all, *weights, *extras)
    return (
        outs[0],
        outs[1 : 1 + chunks],
        outs[1 + chunks : 1 + 2 * chunks],
        outs[1 + 2 * chunks :],
    )


def remote_ffn_back(
    grads, hids, weights, extras, x_codes, g_all, mains, tail_wide, keys, ways, block_of, rows, name, collective_id
):
    width = weights[0].shape[0]
    aug = width + CODE_LANES
    chunks = len(mains)
    tails = [0] * (chunks - 1) + [tail_wide]
    gu = [2 * m + w for m, w in zip(mains, tails)]
    core_step = ("tensor", 1)
    part = rows // len(ways)
    plan = reduce_plan(keys, ways)
    later = [entry for entry in plan if entry[1] > 0]
    slot = {entry: n for n, entry in enumerate(plan)}
    later_slot = {entry: n for n, entry in enumerate(later)}
    steps = distinct([core_step] + ways[0])
    count = 2 * len(keys) + len(plan)
    operands = list(grads) + list(hids) + list(weights) + [x_codes, g_all]
    shapes = [o.shape for o in operands]
    for c in range(chunks):
        shapes[2 * chunks + c] = (aug, weights[c].shape[1])
    shapes[3 * chunks + 1] = x_codes.shape

    def kernel(*refs):
        n_in = len(operands)
        in_refs, e_refs, refs = refs[:n_in], refs[n_in : n_in + chunks], refs[n_in + chunks :]
        refs = in_refs + refs
        out_ref, terms_ref = refs[n_in : n_in + 2]
        gu_refs = refs[n_in + 2 : n_in + 2 + chunks]
        down_refs = refs[n_in + 2 + chunks : n_in + 2 + 2 * chunks]
        held = refs[n_in + 2 + 2 * chunks : 2 * n_in + 2 + 2 * chunks]
        rest = refs[2 * n_in + 2 + 2 * chunks :]
        core_out, core_in, chip, hop_out, hop_in, stage, send_sems, recv_sems, in_sems, out_sems, free = rest
        g_held, h_held = held[:chunks], held[chunks : 2 * chunks]
        w_held = held[2 * chunks : 3 * chunks]
        started = []
        order = [n for c in range(chunks) for n in (2 * chunks + c, c)]
        order += list(range(chunks, 2 * chunks)) + [3 * chunks, 3 * chunks + 1]
        for n in order:
            is_weight = 2 * chunks <= n < 3 * chunks
            to = held[n].at[pl.ds(0, width)] if is_weight else held[n]
            src = in_refs[n]
            if n == 3 * chunks + 1:
                src = src.at[:, pl.ds(width, CODE_LANES)]
            copy = pltpu.make_async_copy(src, to, in_sems.at[n])
            copy.start()
            started.append(copy)
        for c in range(chunks):
            copy = pltpu.make_async_copy(
                e_refs[c], w_held[c].at[pl.ds(width, CODE_LANES)], in_sems.at[n_in + c]
            )
            copy.start()
            started.append(copy)
        links = Links(send_sems, recv_sems)
        place = links.place
        links.greet(steps)
        for copy in started[: 2 * chunks] + started[n_in:]:
            copy.wait()
        came = {}

        def rows_of(key):
            return pl.ds(pl.multiple_of(block_of(key, place) * rows, 16), rows)

        def in_term(key):
            at = rows_of(key)
            out = dot_nt(g_held[0][at, :], w_held[0][:, : gu[0]])
            for c in range(1, chunks):
                out = out + dot_nt(g_held[c][at, :], w_held[c][:, : gu[c]])
            return out

        def down_term(key):
            at = rows_of(key)
            out = 0.0
            for c in range(chunks):
                out = out + dot_nt(h_held[c][at, : mains[c]], w_held[c][:, gu[c] :])
                if tails[c]:
                    out = out + dot_nt(
                        h_held[c][at, mains[c] :], w_held[c][:, mains[c] : mains[c] + tails[c]]
                    )
            return out

        def so_far(w, k, key):
            if key == (0, 0):
                total = out_ref[w * part : (w + 1) * part, :]
            else:
                total = chip[keys.index(key), w * part : (w + 1) * part, :].astype(F32)
            for j in range(k):
                entry = (w, j, flip(key, ways[w][j]))
                links.arrived(came[entry])
                total = total + hop_in[slot[entry]].astype(F32)
            return total

        crossings = []

        def cross(i, value):
            n = len(crossings)
            if n >= 2:
                links.copies[crossings[n - 2]].wait_send()
            core_out[n % 2] = narrow(value)
            crossings.append(links.send(core_out.at[n % 2], core_in.at[i], core_step))
            return crossings[-1]

        for i, key in enumerate(keys):
            crossing = cross(i, in_term((key[0], key[1] ^ 1)))
            mine = in_term(key)
            links.arrived(crossing)
            mine = mine + core_in[i].astype(F32)
            if key == (0, 0):
                out_ref[...] = mine
            else:
                chip[i] = narrow(mine)
                for w, way in enumerate(ways):
                    if has_bit(key, way[0]):
                        at = slice(w * part, (w + 1) * part)
                        entry = (w, 0, key)
                        came[entry] = links.send(
                            chip.at[i, pl.ds(w * part, part)], hop_in.at[slot[entry]], way[0]
                        )
        pl.semaphore_signal(
            free, inc=1, device_id=links.peer(core_step), device_id_type=pl.DeviceIdType.MESH
        )
        pl.semaphore_wait(free, 1)
        for copy in started[2 * chunks : n_in]:
            copy.wait()
        stored = []
        for i, key in enumerate(keys):
            crossing = cross(i, down_term((key[0], key[1] ^ 1)))
            mine = down_term(key)
            links.arrived(crossing)
            if i >= 2:
                stored[i - 2].wait()
            stage[i % 2] = narrow(mine + core_in[i].astype(F32))
            copy = pltpu.make_async_copy(stage.at[i % 2], terms_ref.at[i], out_sems.at[i])
            copy.start()
            stored.append(copy)
            if i == len(keys) // 2 - 1:
                for k in range(1, len(ways[0])):
                    for w in range(len(ways)):
                        for entry in plan:
                            if entry[0] == w and entry[1] == k:
                                hop_out[later_slot[entry]] = narrow(so_far(w, k, entry[2]))
                                came[entry] = links.send(
                                    hop_out.at[later_slot[entry]],
                                    hop_in.at[slot[entry]],
                                    ways[w][k],
                                )
        x_held, gc_held = held[3 * chunks :]
        for c in range(chunks):
            gu_refs[c][...] = dot_tn(x_held[...], g_held[c][...])
            down_refs[c][...] = dot_tn(gc_held[...], h_held[c][...])
        for w in range(len(ways)):
            out_ref[w * part : (w + 1) * part, :] = so_far(w, len(ways[w]), (0, 0))
        for copy in stored[max(0, len(keys) - 2) :]:
            copy.wait()
        for n, copy in enumerate(links.copies):
            links.arrived(n)
            if n not in crossings[:-2]:
                copy.wait_send()

    any_spec = pl.BlockSpec(memory_space=pl.ANY)
    return pl.pallas_call(
        kernel,
        out_shape=[
            jax.ShapeDtypeStruct((rows, aug), F32),
            jax.ShapeDtypeStruct((len(keys), rows, aug), BF16),
        ]
        + [jax.ShapeDtypeStruct((CODE_LANES, g.shape[1]), F32) for g in grads]
        + [jax.ShapeDtypeStruct((CODE_LANES, h.shape[1]), F32) for h in hids],
        in_specs=[any_spec] * (len(operands) + chunks),
        out_specs=[pl.BlockSpec(memory_space=pltpu.VMEM), any_spec]
        + [pl.BlockSpec(memory_space=pltpu.VMEM)] * (2 * chunks),
        scratch_shapes=[pltpu.VMEM(n, o.dtype) for n, o in zip(shapes, operands)]
        + [
            pltpu.VMEM((2, rows, aug), BF16),
            pltpu.VMEM((len(keys), rows, aug), BF16),
            pltpu.VMEM((len(keys) - 1, rows, aug), BF16),
            pltpu.VMEM((max(len(later), 1), part, aug), BF16),
            pltpu.VMEM((len(plan), part, aug), BF16),
            pltpu.VMEM((2, rows, aug), BF16),
            pltpu.SemaphoreType.DMA((count,)),
            pltpu.SemaphoreType.DMA((count,)),
            pltpu.SemaphoreType.DMA((len(operands) + chunks,)),
            pltpu.SemaphoreType.DMA((len(keys),)),
            pltpu.SemaphoreType.REGULAR,
        ],
        compiler_params=pltpu.CompilerParams(
            collective_id=collective_id, has_side_effects=True, vmem_limit_bytes=VMEM_LIMIT
        ),
        cost_estimate=FREE,
        name=name,
    )(*operands, *extras)


def ffn_extras(places, gate_up_out, down_in, mains, tail, tail_wide):
    half = down_in.shape[2] // 2
    chunks = len(mains)
    tails = [0] * (chunks - 1) + [tail_wide]
    wide = [3 * m + w for m, w in zip(mains, tails)]

    def kernel(places_ref, gu_ref, down_ref, *outs):
        for out in outs:
            out[...] = jnp.zeros_like(out)
        lower = places_ref[2] == 0
        for p in range(2):
            which = places_ref[p]

            def half_of(value):
                return jnp.where(lower, value[:, :half], value[:, half:])

            parts = [
                half_of(gu_ref[0, which]) * 2,
                half_of(gu_ref[1, which]) * 2,
                half_of(down_ref[which]),
            ]
            for kind, value in enumerate(parts):
                top = 2 * RANK * p + (RANK if kind == 1 else 0)
                at_rows = slice(top, top + RANK)
                begin = 0
                for c in range(chunks):
                    main = mains[c]
                    at = [0, main + tails[c], 2 * main + tails[c]][kind]
                    outs[c][at_rows, at : at + main] = value[:, begin : begin + main]
                    begin += main
                if tail:
                    at = mains[-1] + kind * tail
                    outs[-1][at_rows, at : at + tail] = value[:, begin:]

    return pl.pallas_call(
        kernel,
        grid_spec=pltpu.PrefetchScalarGridSpec(
            num_scalar_prefetch=1,
            grid=(1,),
            in_specs=[
                pl.BlockSpec(a.shape, lambda i, ids, n=a.ndim: (0,) * n)
                for a in (gate_up_out, down_in)
            ],
            out_specs=[pl.BlockSpec((CODE_LANES, w), lambda i, ids: (0, 0)) for w in wide],
        ),
        out_shape=[jax.ShapeDtypeStruct((CODE_LANES, w), BF16) for w in wide],
        compiler_params=pltpu.CompilerParams(vmem_limit_bytes=VMEM_LIMIT),
        cost_estimate=FREE,
        name="ffn_extras",
    )(places, gate_up_out, down_in)


def chunk_places(mains, tail, tail_wide):
    out = []
    begin = 0
    for c, main in enumerate(mains):
        wide = tail_wide if c == len(mains) - 1 else 0
        for kind, at in enumerate((0, main + wide, 2 * main + wide)):
            out.append((kind, c, at, begin, main))
        begin += main
    if tail:
        for kind in range(3):
            out.append((kind, len(mains) - 1, mains[-1] + kind * tail, begin, tail))
    return out


def prepare(places, tables, shards, sizes, mains, tail, tail_wide):
    heads, head_q, shares, down_wide = sizes
    qa_in, kva_in, qb_in, kvb_in, out_in, gu_in, qa_out, kva_out, qb_out, kvb_out, out_out, down_out = (
        tables
    )
    q_down, kv_down, q_up, gate_up, down_t, cotangent = shards
    width, q_lat, kv_all = qa_in.shape[2], q_down.shape[1], kv_down.shape[1]
    rows = cotangent.shape[0]
    share_rows = q_down.shape[0] // shares
    wide = heads * HEAD_LANES
    half = down_t.shape[1] // 2
    wides = [3 * m for m in mains[:-1]] + [3 * mains[-1] + tail_wide]

    def kernel(places_ref, *refs):
        ins, outs = refs[: len(tables) + len(shards)], refs[len(tables) + len(shards) :]
        qa_i, kva_i, qb_i, kvb_i, out_i, gu_i, qa_o, kva_o, qb_o, kvb_o, out_o, down_o = ins[
            : len(tables)
        ]
        qd, kvd, qu, gu_w, down_w, cot = ins[len(tables) :]
        down_in_o, down_b_o, qb_w, kvb_w, q_aug, kv_aug, out_x, gu_lanes, out_p, down_p, gu_p = outs[:11]
        mine_d, q_pad, g_own = outs[11:14]
        pieces = outs[14:]
        first = places_ref[1] == 0
        for out in (down_b_o, qb_w, kvb_w, q_aug, kv_aug, out_x, gu_lanes, out_p, gu_p, mine_d, q_pad):
            out[...] = jnp.zeros_like(out)
        for out in pieces:
            out[...] = jnp.zeros_like(out)
        down_in_o[:RANK, :] = qa_i[0]
        down_in_o[RANK:, :] = kva_i[0]
        down_b_o[:RANK, :q_lat] = qa_o[0]
        down_b_o[RANK:, q_lat : q_lat + kv_all] = kva_o[0]
        qb_w[:RANK, :] = qb_i[0]
        kvb_w[RANK : 2 * RANK, :] = kvb_i[0]
        out_x[:RANK, :] = out_i[0]
        kv_aug[RANK : 2 * RANK, :] = narrow(kvb_o[0].astype(F32) * ADAPT_SCALE)
        q_out = narrow(qb_o[0].astype(F32) * ADAPT_SCALE)
        q_up_all = qu[...]
        for h in range(heads):
            at = slice(h * HEAD_LANES, h * HEAD_LANES + head_q)
            q_aug[:RANK, at] = q_out[:, h * head_q : (h + 1) * head_q]
            q_pad[:, at] = q_up_all[:, h * head_q : (h + 1) * head_q]
        for n in range(2):
            both = gu_i[n, 0]
            none = jnp.zeros_like(both)
            gu_p[n * RANK : (n + 1) * RANK, :] = both
            gu_lanes[n * RANK : (n + 1) * RANK, :] = jnp.where(first, both, none)
            gu_lanes[(2 + n) * RANK : (3 + n) * RANK, :] = jnp.where(first, none, both)
        out_p[:RANK, :] = out_o[0]
        down_p[...] = down_o[0]
        mine_d[:, :q_lat] = qd[...]
        mine_d[:, q_lat : q_lat + kv_all] = kvd[...]
        grad = narrow(RESIDUAL * cot[...].astype(F32))
        g_own[:, :width] = grad
        codes = dot_nt(grad, jnp.concatenate([down_o[0]] * 8, axis=0)) * ADAPT_SCALE
        lane = lax.broadcasted_iota(jnp.int32, codes.shape, 1)
        begin = jnp.where(first, 0, 2 * RANK)
        g_own[:, width:] = narrow(jnp.where((lane >= begin) & (lane < begin + RANK), codes, 0.0))
        sources = [gu_w[0], gu_w[1], down_w[...]]
        sides = [(v[:, :half], v[:, half:]) for v in sources]
        for kind, c, at, begin, count in chunk_places(mains, tail, tail_wide):
            left = sides[kind][0][:, begin : begin + count]
            right = sides[kind][1][:, begin : begin + count]
            pieces[2 * c][:, at : at + count] = jnp.where(first, left, right)
            pieces[2 * c + 1][:, at : at + count] = jnp.where(first, right, left)

    def picked(table):
        if table.ndim == 4:
            return pl.BlockSpec((2, 1) + table.shape[2:], lambda i, ids: (0, ids[0], 0, 0))
        return pl.BlockSpec((1,) + table.shape[1:], lambda i, ids: (ids[0], 0, 0))

    def shared(shard):
        return pl.BlockSpec((share_rows, shard.shape[1]), lambda i, ids: (ids[2], 0))

    def whole(shape):
        return pl.BlockSpec(shape, lambda i, ids: (0,) * len(shape))

    out_shapes = [
        (2 * RANK, width),
        (2 * RANK, down_wide),
        (CODE_LANES, qb_in.shape[2]),
        (CODE_LANES, kvb_in.shape[2]),
        (CODE_LANES, wide),
        (CODE_LANES, wide),
        (CODE_LANES, out_in.shape[2]),
        (CODE_LANES, width),
        (CODE_LANES, width),
        (RANK, width),
        (CODE_LANES, width),
        (share_rows, down_wide),
        (q_up.shape[0], wide),
        (rows, width + CODE_LANES),
    ]
    for w in wides:
        out_shapes += [(down_t.shape[0], w)] * 2
    return pl.pallas_call(
        kernel,
        grid_spec=pltpu.PrefetchScalarGridSpec(
            num_scalar_prefetch=1,
            grid=(1,),
            in_specs=[picked(a) for a in tables]
            + [shared(q_down), shared(kv_down)]
            + [whole(a.shape) for a in shards[2:]],
            out_specs=[whole(o) for o in out_shapes],
        ),
        out_shape=[jax.ShapeDtypeStruct(o, BF16) for o in out_shapes],
        compiler_params=pltpu.CompilerParams(vmem_limit_bytes=VMEM_LIMIT),
        cost_estimate=FREE,
        name="prepare",
    )(places, *tables, *shards)


def per_device(
    n_dp,
    n_t,
    inputs,
    cotangent,
    document_numbers,
    sequence_adapter_index,
    attention_norm_gain,
    query_latent_gain,
    keyvalue_latent_gain,
    feedforward_norm_gain,
    query_down_matrix,
    keyvalue_down_matrix,
    query_up_matrix,
    keyvalue_up_matrix,
    output_matrix,
    gate_up_matrix,
    down_matrix,
    query_down_adapter_in,
    query_down_adapter_out,
    keyvalue_down_adapter_in,
    keyvalue_down_adapter_out,
    query_up_adapter_in,
    query_up_adapter_out,
    keyvalue_up_adapter_in,
    keyvalue_up_adapter_out,
    output_adapter_in,
    output_adapter_out,
    gate_up_adapter_in,
    gate_up_adapter_out,
    down_adapter_in,
    down_adapter_out,
):
    d = lax.axis_index("dp")
    t = lax.axis_index("tensor")
    pair = n_dp // 4
    low_bits = [b for b in (1, 2, 4, 8, 16) if b < pair]
    high = n_dp // 2
    y_bits = [b for b in (2, 4, 8, 16) if b < n_t]
    zl = lax.rem(d // pair, 2)
    core = lax.rem(t, 2)
    first = zl == 0
    size = {"dp": n_dp, "tensor": n_t}
    rows = inputs.shape[1]
    width = inputs.shape[2]
    length = document_numbers.shape[1]
    q_lat = query_down_matrix.shape[1]
    kv_all = keyvalue_down_matrix.shape[1]
    kv_lat = kv_all - ROTARY_DIM
    heads = keyvalue_up_matrix.shape[1] // HEAD_LANES
    group_count = query_down_adapter_in.shape[0]
    aug = width + CODE_LANES
    half_rows = rows // 2

    def hop(value, step):
        return swap(value, step[0], step[1], size[step[0]])

    outer_first = [("dp", high), ("dp", pair)] + [("dp", b) for b in reversed(low_bits)]
    inner_first = [("dp", b) for b in low_bits] + [("dp", high), ("dp", pair)]
    t_slow = [("tensor", b) for b in reversed(y_bits)]
    t_core = [("tensor", 1)]

    set_own = sequence_adapter_index[0]

    def pick(table, index):
        return lax.dynamic_index_in_dim(table, index, 0, keepdims=False)

    def turned(table):
        return jnp.swapaxes(table, -1, -2)

    hidden = down_matrix.shape[0]
    half = hidden // 2
    tiles = half // 128
    main = tiles * 128
    tail = half - main
    tail_wide = -(-3 * tail // 128) * 128
    first_tiles = (2 * tiles + 2) // 3
    mains = [first_tiles * 128, main - first_tiles * 128]
    chunks = len(mains)
    tails = [0] * (chunks - 1) + [tail_wide]
    gu_wide = [2 * m + w for m, w in zip(mains, tails)]

    head_q = PLAIN_HEAD_DIM + ROTARY_DIM
    down_shard = query_down_matrix.shape[0]
    shares = n_t if down_shard % (16 * n_t) == 0 else 2
    share_rows = down_shard // shares
    down_wide = -(-(q_lat + kv_all) // 128) * 128
    down_pad = down_wide - q_lat - kv_all
    (
        down_in,
        down_b_rows,
        qb_in_wide,
        kvb_in_wide,
        q_aug_rows,
        kv_aug_rows,
        out_extra,
        gu_in_lanes,
        out_out_wide,
        down_out,
        gu_in_wide,
        down_mine,
        q_up_mine,
        g_own,
        *ffn_pieces,
    ) = prepare(
        jnp.stack([set_own, zl, lax.rem(t, shares)]).astype(jnp.int32),
        [
            turned(query_down_adapter_in),
            turned(keyvalue_down_adapter_in),
            turned(query_up_adapter_in),
            turned(keyvalue_up_adapter_in),
            turned(output_adapter_in),
            turned(gate_up_adapter_in),
            query_down_adapter_out,
            keyvalue_down_adapter_out,
            query_up_adapter_out,
            keyvalue_up_adapter_out,
            output_adapter_out,
            down_adapter_out,
        ],
        [
            query_down_matrix,
            keyvalue_down_matrix,
            query_up_matrix,
            gate_up_matrix,
            down_matrix.T,
            cotangent[0],
        ],
        (heads, head_q, shares, down_wide),
        mains,
        tail,
        tail_wide,
    )
    qb_in, kvb_in = qb_in_wide[:RANK], kvb_in_wide[RANK : 2 * RANK]
    out_out, gu_in = out_out_wide[:RANK], gu_in_wide[: 2 * RANK]
    ffn_mine, ffn_other = ffn_pieces[::2], ffn_pieces[1::2]
    ffn_rows_each = gate_up_matrix.shape[1]
    z_count = n_dp // pair
    ffn_wide = [m.shape[1] for m in ffn_mine]

    def ride_one(out, mine, other, begin, size):
        return dict(
            kind="one",
            out=out,
            mine=mine,
            other=other,
            rows=(begin, size),
            count=ffn_rows_each,
            pair=pair,
            high=high,
        )

    def ride_two(out, z, begin=0, size=None):
        return dict(
            kind="two",
            out=out,
            z=z,
            rows=(begin, ffn_rows_each if size is None else size),
            count=ffn_rows_each,
            pair=pair,
            high=high,
            steps=[("dp", b) for b in reversed(low_bits)],
        )

    def own_codes(value):
        lanes = value[:, width:]
        return jnp.where(first, lanes[:, : 2 * RANK], lanes[:, 2 * RANK : 4 * RANK])

    qb_rows, kvb_rows = query_up_matrix.shape[0], keyvalue_up_matrix.shape[0]
    out_rows = output_matrix.shape[1]

    def rows_at(start, step, count):
        return lambda dd, tt: (pl.ds(pl.multiple_of(start + dd * step, 16), count),)

    def group_block(dd, tt):
        return lax.rem(dd // pair, 2) * n_t + tt

    def group_jobs(src, out, ways):
        return [
            dict(
                src=src,
                src_at=pl.ds(at, half_rows),
                out=out,
                out_at=lambda dd, tt, at=at: (
                    pl.ds(pl.multiple_of(group_block(dd, tt) * rows + at, 16), half_rows),
                ),
                steps=steps + t_core,
                group="rows",
            )
            for at, steps in zip((0, half_rows), ways)
        ]

    group_a = t_slow + [("dp", pair)]
    group_b = [("dp", pair)] + t_slow
    pe_at = q_lat + 2 * RANK
    lat_wide = q_lat + CODE_LANES + kv_lat

    def token_jobs(src, out, parts, group=0):
        count = rows // parts
        return [
            dict(
                src=src,
                src_at=pl.ds(n * count, count),
                out=out,
                out_at=lambda dd, tt, n=n: (
                    pl.ds(pl.multiple_of(tt * rows + n * count, 16), count),
                ),
                steps=t_slow + t_core,
                group=group,
            )
            for n in range(parts)
        ]

    def latent_work(refs):
        x_ref, norm_ref, q_norm_ref, kv_norm_ref, in_ref, b_ref, qb_ref, kvb_ref = refs[12:20]
        latent_ref, codes_ref, rows_ref, w_ref, own_ref = refs[20:25]
        x_f = x_ref[...].astype(F32)
        scale = lax.rsqrt(jnp.mean(x_f * x_f, axis=-1, keepdims=True) + NORM_EPS)
        h_rows = narrow(x_f * scale * norm_ref[...])
        rows_ref[...] = h_rows
        codes = narrow(dot_nt(h_rows, in_ref[...]))
        latent = dot_nn(h_rows, w_ref[...]) + ADAPT_SCALE * dot_nn(codes, b_ref[...])
        latent_ref[...] = latent
        codes_ref[...] = codes
        q_part = latent[:, :q_lat]
        kv_part = latent[:, q_lat : q_lat + kv_lat]
        q_scale = lax.rsqrt(jnp.mean(q_part * q_part, axis=-1, keepdims=True) + NORM_EPS)
        kv_scale = lax.rsqrt(jnp.mean(kv_part * kv_part, axis=-1, keepdims=True) + NORM_EPS)
        q_in = narrow(q_part * q_scale * q_norm_ref[...])
        kv_in = narrow(kv_part * kv_scale * kv_norm_ref[...])
        own_ref[:, :q_lat] = q_in
        own_ref[:, q_lat + CODE_LANES :] = kv_in
        code_block = dot_nt(q_in, qb_ref[...]) + dot_nt(kv_in, kvb_ref[...])
        pe_block = pltpu.roll(latent[:, q_lat + kv_lat :], 2 * RANK, 1)
        lane = lax.broadcasted_iota(jnp.int32, code_block.shape, 1)
        own_ref[:, q_lat : q_lat + CODE_LANES] = narrow(
            jnp.where(lane < 2 * RANK, code_block, pe_block)
        )

    down_steps = outer_first + (t_slow if shares == n_t else []) + t_core
    n_start_outs = 9
    w_at, lat_own_at = n_start_outs + 3, n_start_outs + 4
    n_start_sources = 20
    jobs = [
        dict(
            src=0,
            out=w_at,
            out_at=lambda dd, tt: (
                pl.ds(
                    pl.multiple_of(dd * down_shard + lax.rem(tt, shares) * share_rows, 16), share_rows
                ),
            ),
            steps=down_steps,
            group="down",
        ),
        dict(src=1, out=1, out_at=rows_at(0, qb_rows, qb_rows), steps=outer_first, group="up"),
        dict(src=2, out=2, out_at=rows_at(CODE_LANES, kvb_rows, kvb_rows), steps=outer_first, group="up"),
        dict(src=8, out=5, out_at=lambda dd, tt: (dd,), steps=outer_first, group="up"),
        dict(src=3, out=3, out_at=rows_at(0, out_rows, out_rows), steps=outer_first, group="out"),
    ]
    low_steps = [("dp", b) for b in reversed(low_bits)]
    for src, out in ((9, 6), (11, 7)):
        jobs.append(
            dict(
                src=src,
                out=out,
                out_at=rows_at(0, ffn_rows_each, ffn_rows_each),
                steps=low_steps,
                group="own",
            )
        )
    def own_block(dd, tt):
        return (pl.ds(pl.multiple_of(group_block(dd, tt) * rows, 16), rows),)

    jobs.append(dict(src=4, out=4, out_at=own_block, steps=t_slow + t_core, group="rows"))
    jobs.append(
        dict(src=4, out=4, out_at=own_block, steps=[("dp", pair)], group="pair", keep=False)
    )
    jobs += token_jobs(n_start_sources + 4, 8, 2, "latents")
    set_mark = jnp.full((16, 128), sequence_adapter_index[0].astype(F32)).astype(BF16)
    start = (
        remote_gather(
            [
                down_mine,
                q_up_mine,
                keyvalue_up_matrix,
                output_matrix.T,
                g_own,
                q_aug_rows,
                kv_aug_rows,
                out_extra,
                set_mark,
                ffn_mine[0],
                ffn_other[0],
                ffn_mine[1],
                inputs[0],
                attention_norm_gain[None],
                query_latent_gain[None],
                keyvalue_latent_gain[None],
                down_in,
                down_b_rows,
                qb_in_wide,
                kvb_in_wide,
            ],
            jobs,
            [
                (5, 1, lambda dd, tt: (pl.ds(q_lat, CODE_LANES),)),
                (6, 2, lambda dd, tt: (pl.ds(0, CODE_LANES),)),
                (7, 3, lambda dd, tt: (pl.ds(width, CODE_LANES),)),
            ],
            [
                (width, down_wide),
                (q_lat + CODE_LANES, heads * HEAD_LANES),
                (CODE_LANES + kv_lat, heads * HEAD_LANES),
                (aug, heads * VALUE_HEAD_DIM),
                (2 * n_t * rows, aug),
                (n_dp, 16, 128),
                (width, ffn_wide[0]),
                (width, ffn_wide[1]),
                (length, lat_wide),
            ],
            "gather_start",
            1,
            riders=[ride_one(6, 9, 10, 0, ffn_rows_each)],
            order=["down", "up", "out", "rows", "down", "up", "down", "own", "out", "pair"]
            + ["down", "up", "out", "ride"]
            + ["down"] * (len(down_steps) - 4)
            + [("all", "down"), "work", "latents"]
            + ["latents"] * len(t_slow)
            + ["rows"],
            near_outs=[
                jax.ShapeDtypeStruct((rows, down_wide), F32),
                jax.ShapeDtypeStruct((rows, 2 * RANK), BF16),
                jax.ShapeDtypeStruct((rows, width), BF16),
            ],
            scratch=[
                jax.ShapeDtypeStruct((width, down_wide), BF16),
                jax.ShapeDtypeStruct((rows, lat_wide), BF16),
            ],
            work=latent_work,
            late=[(n_start_sources + 3, 0)],
        )
    )
    w_down, w_q, w_kv, w_out, g_all, set_marks, w_ffn0, w_ffn1, lat_all = start[:9]
    latent, down_codes_in, attn_rows = start[9:]
    set_all = set_marks[:, 0, 0].astype(jnp.int32)
    set_peer = lax.dynamic_index_in_dim(set_all, jnp.bitwise_xor(d, pair), 0, keepdims=False)
    set_even = jnp.where(first, set_own, set_peer)
    set_odd = jnp.where(first, set_peer, set_own)
    ffn_extra = ffn_extras(
        jnp.stack([set_even, set_odd, zl]).astype(jnp.int32),
        gate_up_adapter_out,
        turned(down_adapter_in),
        mains,
        tail,
        tail_wide,
    )
    cut_a = ffn_rows_each // 48 * 16

    cos_part, sin_part = rope_tables(document_numbers)
    zeros_l = jnp.zeros((length, PLAIN_HEAD_DIM), F32)
    zeros_r = jnp.zeros((length, HEAD_LANES - 96), F32)
    none_16 = jnp.zeros_like(sin_part)
    rope = jnp.stack(
        [
            jnp.concatenate([zeros_l + 1.0, cos_part, cos_part, zeros_r], axis=1),
            jnp.concatenate([zeros_l, -sin_part, none_16, zeros_r], axis=1),
            jnp.concatenate([zeros_l, none_16, sin_part, zeros_r], axis=1),
        ],
        axis=0,
    )
    lane_ids = jnp.arange(HEAD_LANES, dtype=jnp.int32)[None, :]
    doc_lane = (lane_ids >= DOC_LANE) & (lane_ids < DOC_LANE + DOC_SLOTS)
    is_doc = document_numbers[0][:, None] == lane_ids - DOC_LANE
    doc_q = narrow(jnp.where(doc_lane & is_doc, 1.0, 0.0))
    doc_k = jnp.where(
        doc_lane & ~is_doc, -BIG, jnp.where((lane_ids >= 96) & (lane_ids < 99), 1.0, 0.0)
    )

    pe_rows = lat_all[:, pe_at : pe_at + ROTARY_DIM].astype(F32)
    pe_a, pe_b = pe_rows[:, : ROTARY_DIM // 2], pe_rows[:, ROTARY_DIM // 2 :]
    pe_aug = narrow(
        jnp.concatenate(
            [
                zeros_l,
                pe_a * cos_part - pe_b * sin_part,
                pe_b * cos_part + pe_a * sin_part,
                zeros_r,
            ],
            axis=1,
        )
        + doc_k
    )
    def pair_rows(place, key):
        block = group_block(jnp.bitwise_xor(place["dp"], pair), jnp.bitwise_xor(place["tensor"], key))
        return pl.ds(pl.multiple_of(block * rows, 16), rows)

    q_aug, kv, head_out, w_ffn0, w_ffn1, g_all = attend(
        lat_all,
        w_q,
        w_kv,
        rope,
        pe_aug,
        doc_q,
        q_lat + CODE_LANES,
        q_lat,
        [
            ride_two(0, 1),
            ride_two(0, 2, 0, cut_a),
            ride_one(1, 3, 4, 0, cut_a),
            dict(kind="block", out=2, at=pair_rows, steps=t_slow),
        ],
        [w_ffn0, w_ffn1, g_all],
        [ffn_mine[1], ffn_other[1]],
    )
    tensor_keys = [(0, r) for r in reversed(range(0, n_t, 2))]

    def token_rows(key, place):
        at = jnp.bitwise_xor(place["tensor"], key[1]) * rows
        return pl.ds(pl.multiple_of(at, 16), rows)

    def out_term(held, place, key):
        return dot_nt(held[0][token_rows(key, place), :], held[1][...])

    def middle_work(at, total, extra, outs):
        x_ref, out_b_ref, norm_ref, lanes_ref = extra
        middle_ref, codes_ref, own_ref = outs
        codes = narrow(total[:, width : width + RANK])
        mid = x_ref[at, :].astype(F32) + RESIDUAL * (
            total[:, :width] + ADAPT_SCALE * dot_nn(codes, out_b_ref[...])
        )
        middle_ref[at, :] = mid
        codes_ref[at, :] = codes
        scale = lax.rsqrt(jnp.mean(mid * mid, axis=-1, keepdims=True) + NORM_EPS)
        normed = narrow(mid * scale * norm_ref[...])
        own_ref[at, :width] = normed
        own_ref[at, width:] = narrow(dot_nt(normed, lanes_ref[...]))

    middle, out_codes, x_own, w_ffn0, w_ffn1, g_all = remote_reduce(
        [head_out, w_out],
        [head_out.shape, w_out.shape],
        out_term,
        tensor_keys,
        [t_slow[::-1]],
        rows,
        aug,
        "reduce_out",
        3,
        riders=[ride_two(0, 2, cut_a, ffn_rows_each - cut_a)]
        + [ride_two(0, z) for z in range(3, z_count)]
        + [
            ride_one(1, 3, 4, cut_a, ffn_rows_each - cut_a),
            dict(
                kind="blocks",
                out=2,
                at=pair_rows,
                keys=list(range(0, n_t, 2)),
                step=t_core[0],
            ),
        ],
        ridden=[w_ffn0, w_ffn1, g_all],
        carried=[ffn_mine[1], ffn_other[1]],
        after=middle_work,
        after_in=[inputs[0], out_out, feedforward_norm_gain[None], gu_in_lanes],
        after_out=[
            jax.ShapeDtypeStruct((rows, width), F32),
            jax.ShapeDtypeStruct((rows, RANK), BF16),
            jax.ShapeDtypeStruct((rows, aug), BF16),
        ],
    )

    def group_block_of(key, place):
        return group_block(
            jnp.bitwise_xor(place["dp"], key[0]), jnp.bitwise_xor(place["tensor"], key[1])
        )

    x_codes, grads, hids, ffn_weights = remote_ffn(
        x_own,
        g_all,
        [w_ffn0, w_ffn1],
        ffn_extra,
        mains,
        tail,
        tail_wide,
        t_slow + [("dp", pair)],
        group_block_of,
        [ride_two(1, z) for z in range(1, z_count)],
        "feed_forward",
        4,
    )
    group_keys = [(p, r) for p in (pair, 0) for r in reversed(range(0, n_t, 2))]
    ffn_in_sum, down_chip, *code_terms = remote_ffn_back(
        grads,
        hids,
        ffn_weights,
        ffn_extra,
        x_codes,
        g_all,
        mains,
        tail_wide,
        group_keys,
        [group_a[::-1], group_b[::-1]],
        group_block_of,
        rows,
        "feed_forward_back",
        5,
    )
    def grad_work(part, refs):
        at = slice(part * half_rows, (part + 1) * half_rows)
        sum_ref, mid_ref, cot_ref, norm_ref, gu_ref, out_ref = refs[0:6]
        middle_ref, codes_ref, aug_ref = refs[n_grad : n_grad + 3]
        lanes = sum_ref[at, width:]
        lanes = jnp.where(zl_of() == 0, lanes, pltpu.roll(lanes, CODE_LANES - 2 * RANK, 1))
        lane = lax.broadcasted_iota(jnp.int32, lanes.shape, 1)
        codes = narrow(jnp.where(lane < 2 * RANK, lanes, 0.0))
        codes_ref[at, :] = codes
        weighted = (sum_ref[at, :width] + dot_nn(codes, gu_ref[...])) * norm_ref[...]
        mid = mid_ref[at, :]
        scale = lax.rsqrt(jnp.mean(mid * mid, axis=-1, keepdims=True) + NORM_EPS)
        inner = jnp.mean(mid * weighted, axis=-1, keepdims=True)
        grad = cot_ref[at, :].astype(F32) + scale * weighted - mid * (scale * scale * scale * inner)
        middle_ref[at, :] = grad
        scaled = narrow(RESIDUAL * grad)
        aug_ref[at, :width] = scaled
        aug_ref[at, width:] = narrow(ADAPT_SCALE * dot_nt(scaled, out_ref[...]))

    def zl_of():
        return lax.rem(lax.axis_index("dp") // pair, 2)

    hidden_shape = (6 * RANK, half)

    def hidden_work(refs):
        gu_refs, down_refs = refs[6 : 6 + chunks], refs[6 + chunks : 6 + 2 * chunks]
        own_ref = refs[n_grad + 6]
        for kind, c, at, begin, count in chunk_places(mains, tail, tail_wide):
            for p in range(2):
                to = slice((3 * p + kind) * RANK, (3 * p + kind + 1) * RANK)
                if kind < 2:
                    top = 2 * RANK * p + kind * RANK
                    value = gu_refs[c][top : top + RANK, at : at + count] * ADAPT_SCALE
                else:
                    here = at - 2 * mains[c] - tails[c] if count == mains[c] else at
                    value = down_refs[c][2 * RANK * p : 2 * RANK * p + RANK, here : here + count]
                own_ref[to, begin : begin + count] = narrow(value)

    def dp_job(src, out):
        return dict(src=src, out=out, out_at=lambda dd, tt: (dd,), steps=outer_first)

    n_grad = 7 + 2 * chunks + (1 if n_t == 4 else 0)

    def heads_work(refs):
        w_ref, heads_ref, lanes_ref, all_ref = refs[6 + 2 * chunks], *refs[n_grad + 3 : n_grad + 6]
        for n in range(2):
            at = slice(n * length // 2, (n + 1) * length // 2)
            heads_ref[at, :] = narrow(dot_nn(all_ref[at, :], w_ref[...]))
        lanes_ref[...] = all_ref[:, width:]

    ride_down = n_t == 4
    n_far = 2 if ride_down else 1
    sent = remote_gather(
        [
            ffn_in_sum,
            middle,
            cotangent[0],
            feedforward_norm_gain[None],
            gu_in_wide,
            out_out_wide,
            *code_terms,
            w_out,
        ]
        + ([down_chip] if ride_down else []),
        token_jobs(n_grad + 2, n_far + 5, 2, "top")[:1]
        + token_jobs(n_grad + 2, n_far + 5, 2, "bottom")[1:]
        + [
            dict(
                src=n_grad + 6,
                out=0,
                out_at=rows_at(0, hidden_shape[0], hidden_shape[0]),
                steps=[("dp", high), ("dp", pair)],
                group="hidden",
            )
        ],
        [],
        [(n_dp * hidden_shape[0], half)] + ([(rows, aug)] if ride_down else []),
        "gather_grad",
        6,
        riders=[dict(kind="plain", src=n_grad - 1, src_at=0, out=1, step=("dp", pair))]
        if ride_down
        else [],
        distant=(n_grad - 1,) if ride_down else (),
        order=[
            hidden_work,
            "hidden",
            functools.partial(grad_work, 0),
            "top",
            "ride",
            functools.partial(grad_work, 1),
            "bottom",
            "hidden",
            "top",
            "bottom",
        ]
        + ["top", "bottom"] * (len(t_slow) - 1)
        + [("all", "top"), ("all", "bottom"), heads_work],
        near_outs=[
            jax.ShapeDtypeStruct((rows, width), F32),
            jax.ShapeDtypeStruct((rows, CODE_LANES), BF16),
            jax.ShapeDtypeStruct((rows, aug), BF16),
            jax.ShapeDtypeStruct((length, w_out.shape[1]), BF16),
            jax.ShapeDtypeStruct((length, CODE_LANES), BF16),
        ],
        scratch=[
            jax.ShapeDtypeStruct((length, aug), BF16),
            jax.ShapeDtypeStruct(hidden_shape, BF16),
        ],
    )
    middle_grad, gu_code_grad, attn_grad_aug, heads_grad, grad_lanes = sent[n_far:]
    gu_code_grad = gu_code_grad[:, : 2 * RANK]
    hidden_terms = sent[0]
    out_a = dot_tn(grad_lanes, head_out)[:RANK]
    hidden_ride = [
        dict(
            kind="two",
            out=0,
            z=z,
            count=hidden_shape[0],
            pair=pair,
            high=high,
            steps=[("dp", b) for b in reversed(low_bits)],
        )
        for z in range(z_count)
    ]
    if ride_down:
        down_far = narrow(down_chip[2].astype(F32) + sent[1].astype(F32))
        dq, dkv, pe_padded, cq, ckv, hidden_terms, came_pair, came_y = attend_back(
            q_aug,
            kv,
            head_out,
            heads_grad,
            rope,
            pe_aug,
            (lat_all, q_lat // CODE_LANES),
            [
                dict(kind="plain", src=1, src_at=1, out=1, step=("dp", pair)),
                dict(kind="plain", src=2, src_at=None, out=2, step=("tensor", 2)),
            ]
            + hidden_ride,
            [hidden_terms],
            [down_chip, down_far],
            [(rows, aug), (rows, aug)],
        )
    else:
        dq, dkv, pe_padded, cq, ckv, hidden_terms = attend_back(
            q_aug, kv, head_out, heads_grad, rope, pe_aug, (lat_all, q_lat // CODE_LANES), hidden_ride, [hidden_terms], [], []
        )
        places = n_t // 2
        ffn_out = down_chip[places:].astype(F32) + hop(down_chip[:places], ("dp", pair)).astype(F32)
        while places > 1:
            places //= 2
            ffn_out = ffn_out[places:] + hop(narrow(ffn_out[:places]), ("tensor", 2 * places)).astype(
                F32
            )
        ffn_out = ffn_out[0]
    def latent_term(held, place, key):
        at = token_rows(key, place)
        from_q = dot_nt(held[0][at, :], held[2][...])
        from_kv = dot_nt(held[1][at, :], held[3][...])
        return jnp.concatenate(
            [
                from_q[:, :q_lat],
                from_q[:, q_lat:] + from_kv[:, :CODE_LANES] + held[4][at, :],
                from_kv[:, CODE_LANES:],
            ],
            axis=1,
        )

    qb_b = ADAPT_SCALE * cq[:RANK]
    kvb_b = ADAPT_SCALE * ckv[RANK : 2 * RANK]
    head_own = narrow(jnp.concatenate([qb_b, kvb_b, out_a], axis=1))
    operands = [dq, dkv, w_q, w_kv, pe_padded]
    small_at, small_wide = [0], []
    for value in (q_lat, kv_all, q_lat, kv_lat):
        small_wide.append(value)
        small_at.append(small_at[-1] + -(-value // 128) * 128)

    def latent_back(at, total, extra, outs):
        latent_ref, q_norm, kv_norm, qb_ref, kvb_ref, b_ref, rows_ref, codes_ref = extra
        grad_ref, code_ref, terms_ref = outs
        block = total[:, q_lat : q_lat + CODE_LANES]
        lane = lax.broadcasted_iota(jnp.int32, block.shape, 1)
        codes = narrow(jnp.where(lane < 2 * RANK, block, 0.0))
        latent_f = latent_ref[...]
        parts = []
        inputs_in = []
        for begin, size, grad, norm_ref, in_ref in (
            (0, q_lat, total[:, :q_lat], q_norm, qb_ref),
            (q_lat, kv_lat, total[:, q_lat + CODE_LANES :], kv_norm, kvb_ref),
        ):
            value = latent_f[:, begin : begin + size]
            scale = lax.rsqrt(jnp.mean(value * value, axis=-1, keepdims=True) + NORM_EPS)
            inputs_in.append(narrow(value * scale * norm_ref[...]))
            weighted = (grad + dot_nn(codes, in_ref[...])) * norm_ref[...]
            inner = jnp.mean(value * weighted, axis=-1, keepdims=True)
            parts.append(scale * weighted - value * (scale * scale * scale * inner))
        grad_ref[:, :q_lat] = narrow(parts[0])
        grad_ref[:, q_lat : q_lat + kv_lat] = narrow(parts[1])
        pe_block = pltpu.roll(block, CODE_LANES - 2 * RANK, 1)
        pe_block = jnp.where(lane < ROTARY_DIM, pe_block, 0.0)
        grad_ref[:, q_lat + kv_lat :] = narrow(pe_block[:, : down_wide - q_lat - kv_lat])
        grad_rows = grad_ref[...]
        code_grad = narrow(ADAPT_SCALE * dot_nt(grad_rows, b_ref[...]))
        code_ref[...] = code_grad
        terms_ref[...] = jnp.zeros_like(terms_ref)
        terms_ref[: 2 * RANK, :] = narrow(dot_tn(code_grad, rows_ref[...]))
        b_terms = ADAPT_SCALE * dot_tn(codes_ref[...], grad_rows)
        qb_a = dot_tn(codes, inputs_in[0])
        kvb_a = dot_tn(codes, inputs_in[1])
        small_values = (
            b_terms[:RANK, :q_lat],
            b_terms[RANK:, q_lat : q_lat + kv_all],
            qb_a[:RANK, :],
            kvb_a[RANK : 2 * RANK, :],
        )
        for value, begin, size in zip(small_values, small_at, small_wide):
            terms_ref[2 * RANK :, begin : begin + size] = narrow(value)

    latent_grad, code_grad, late_terms, head_terms = remote_reduce(
        operands,
        [o.shape for o in operands],
        latent_term,
        tensor_keys,
        [t_slow[::-1]],
        rows,
        lat_wide,
        "reduce_latents",
        7,
        jobs=[dp_job(0, 0)],
        job_sources=[head_own],
        job_outs=[(n_dp,) + head_own.shape],
        after=latent_back,
        after_in=[
            latent,
            query_latent_gain[None],
            keyvalue_latent_gain[None],
            qb_in_wide,
            kvb_in_wide,
            down_b_rows,
            attn_rows,
            down_codes_in,
        ],
        after_out=[
            jax.ShapeDtypeStruct((rows, down_wide), BF16),
            jax.ShapeDtypeStruct((rows, 2 * RANK), BF16),
            jax.ShapeDtypeStruct((3 * RANK, width), BF16),
        ],
    )
    if ride_down:
        ffn_out = (
            down_chip[3].astype(F32)
            + came_pair.astype(F32)
            + came_y.astype(F32)
        )
    down_codes = narrow(own_codes(ffn_out)[:, :RANK])
    outputs = narrow(
        middle + RESIDUAL * (ffn_out[:, :width] + ADAPT_SCALE * dot_nn(down_codes, down_out))
    )
    gu_a = dot_tn(gu_code_grad, x_own)[:, :width]
    out_b = ADAPT_SCALE * dot_tn(out_codes, attn_grad_aug)[:, :width]
    down_b = ADAPT_SCALE * dot_tn(down_codes, g_own)[:, :width]
    table_orders = [outer_first + t_slow + t_core, t_slow + outer_first + t_core]
    shared = jnp.concatenate([narrow(gu_a), narrow(out_b), narrow(down_b), late_terms], axis=0)
    shared = jnp.pad(shared, ((0, -shared.shape[0] % (16 * n_t)), (0, 0)))

    def input_work(refs):
        grad_ref, code_ref, w_ref, in_ref, x_ref, norm_ref, mid_ref, out_ref = refs
        back = dot_nt(grad_ref[...], w_ref[...]) + dot_nn(code_ref[...], in_ref[...])
        value = x_ref[...].astype(F32)
        scale = lax.rsqrt(jnp.mean(value * value, axis=-1, keepdims=True) + NORM_EPS)
        weighted = back * norm_ref[...]
        inner = jnp.mean(value * weighted, axis=-1, keepdims=True)
        out_ref[...] = (
            mid_ref[...] + scale * weighted - value * (scale * scale * scale * inner)
        )

    shared_terms, input_grad = remote_share(
        shared,
        n_dp,
        n_t,
        table_orders,
        "share",
        8,
        [
            latent_grad,
            code_grad,
            w_down,
            down_in,
            inputs[0],
            attention_norm_gain[None],
            middle_grad,
        ],
        [jax.ShapeDtypeStruct((rows, width), F32)],
        input_work,
    )
    part_wide = width // 2

    def add_shared(s, refs, acc):
        for p in range(2):
            at = slice(p * part_wide, (p + 1) * part_wide)
            acc[:, at] += refs[0][p, s].astype(F32)

    def put_shared(acc, outs):
        outs[0][0, 0] = acc[:RANK, :]
        outs[0][1, 0] = acc[RANK : 2 * RANK, :]
        for n in range(4):
            outs[1 + n][0] = acc[(2 + n) * RANK : (3 + n) * RANK, :]
        for n, size in enumerate(small_wide):
            at = small_at[n]
            outs[5 + n][0] = acc[6 * RANK : 7 * RANK, at : at + size]

    shared_sets = set_sums(
        set_all,
        [shared_terms],
        (shared.shape[0], width),
        add_shared,
        [((2,), (RANK, width))]
        + [((), (RANK, width))] * 4
        + [((), (RANK, size)) for size in small_wide],
        put_shared,
        group_count,
        "sum_shared",
    )
    gu_a_t, out_b_grad, down_b_grad, qa_a_t, kva_a_t, qa_b_grad, kva_b_grad, qb_a_t, kvb_a_t = (
        shared_sets
    )
    wide = heads * HEAD_LANES
    head_wide = head_own.shape[1]

    def add_split(s, refs, acc):
        which = (s // pair) % 2
        base = s - which * pair
        for h in range(2):
            acc[: 3 * RANK, h * half : (h + 1) * half] += refs[0][
                base + h * pair, which * 3 * RANK : (which + 1) * 3 * RANK, :
            ].astype(F32)
        acc[3 * RANK :, :head_wide] += refs[1][s].astype(F32)

    def put_split(acc, outs):
        outs[0][0, 0] = acc[:RANK, :hidden]
        outs[0][1, 0] = acc[RANK : 2 * RANK, :hidden]
        outs[1][0] = acc[2 * RANK : 3 * RANK, :hidden]
        for h in range(heads):
            outs[2][0, :, h * head_q : (h + 1) * head_q] = acc[
                3 * RANK :, h * HEAD_LANES : h * HEAD_LANES + head_q
            ]
        outs[3][0] = acc[3 * RANK :, wide : 2 * wide]
        outs[4][0] = acc[3 * RANK :, 2 * wide : head_wide]

    gu_b_grad, down_a_t, qb_b_grad, kvb_b_grad, out_a_t = set_sums(
        set_all,
        [hidden_terms.reshape((n_dp,) + hidden_shape), head_terms],
        (4 * RANK, max(hidden, -(-head_wide // 128) * 128)),
        add_split,
        [
            ((2,), (RANK, hidden)),
            ((), (RANK, hidden)),
            ((), (RANK, heads * head_q)),
            ((), (RANK, wide)),
            ((), (RANK, head_wide - 2 * wide)),
        ],
        put_split,
        group_count,
        "sum_split",
    )
    return (
        outputs[None],
        input_grad[None],
        turned(qa_a_t),
        qa_b_grad,
        turned(kva_a_t),
        kva_b_grad,
        turned(qb_a_t),
        qb_b_grad,
        turned(kvb_a_t),
        kvb_b_grad,
        turned(out_a_t),
        out_b_grad,
        turned(gu_a_t),
        gu_b_grad,
        turned(down_a_t),
        down_b_grad,
    )


def solution(mesh):
    return jax.shard_map(
        functools.partial(per_device, mesh.shape["dp"], mesh.shape["tensor"]),
        mesh=mesh,
        in_specs=(
            P("dp", "tensor", None),
            P("dp", "tensor", None),
            P("dp", None),
            P("dp"),
            P(),
            P(),
            P(),
            P(),
            P("dp", None),
            P("dp", None),
            P("dp", "tensor"),
            P("dp", "tensor"),
            P("tensor", "dp"),
            P(None, "dp", "tensor"),
            P("tensor", "dp"),
            P(),
            P(),
            P(),
            P(),
            P(),
            P(None, None, "tensor"),
            P(),
            P(None, None, "tensor"),
            P(None, "tensor", None),
            P(),
            P(),
            P(None, None, None, "tensor"),
            P(None, "tensor", None),
            P(),
        ),
        out_specs=(
            P("dp", "tensor", None),
            P("dp", "tensor", None),
            P(),
            P(),
            P(),
            P(),
            P(),
            P(None, None, "tensor"),
            P(),
            P(None, None, "tensor"),
            P(None, "tensor", None),
            P(),
            P(),
            P(None, None, None, "tensor"),
            P(None, "tensor", None),
            P(),
        ),
        check_vma=False,
    )
```

```python
import functools
import math

import jax
import jax.numpy as jnp
from jax import lax
from jax.experimental import pallas as pl
from jax.experimental.pallas import tpu as pltpu
from jax.sharding import PartitionSpec as P

PLAIN_HEAD_DIM = 64
ROTARY_DIM = 32
VALUE_HEAD_DIM = 64
HEAD_LANES = 128
CODE_LANES = 128
RANK = 16
BLOCK_Q = 256
DOC_LANE = 99
DOC_SLOTS = 24

NORM_EPS = 1e-05
RESIDUAL = 1.4 / math.sqrt(62.0)
ADAPT_SCALE = 2.0
SCORE_SCALE = 1.0 / math.sqrt(PLAIN_HEAD_DIM + ROTARY_DIM)
EXP2_SCALE = SCORE_SCALE * math.log2(math.e)
BIG = 1e30
VMEM_LIMIT = 60 * 1024 * 1024
FREE = pl.CostEstimate(flops=0, bytes_accessed=0, transcendentals=0)
F32 = jnp.float32
BF16 = jnp.bfloat16


def narrow(value):
    return value.astype(BF16)


def dot_nn(a, b):
    return lax.dot_general(a, b, (((1,), (0,)), ((), ())), preferred_element_type=F32)


def dot_nt(a, b):
    return lax.dot_general(a, b, (((1,), (1,)), ((), ())), preferred_element_type=F32)


def dot_tn(a, b):
    return lax.dot_general(a, b, (((0,), (0,)), ((), ())), preferred_element_type=F32)


def normalize(value, gain_vec):
    scale_inv = lax.rsqrt(jnp.mean(value * value, axis=-1, keepdims=True) + NORM_EPS)
    return (value * scale_inv * gain_vec, scale_inv)


def normalize_back(value, scale_inv, gain_vec, grad_in):
    weighted = grad_in * gain_vec
    return scale_inv * weighted - value * scale_inv**3 * jnp.mean(
        value * weighted, axis=-1, keepdims=True
    )


def rope_tables(segments):
    places = jnp.arange(segments.shape[-1], dtype=jnp.int32)
    begins = jnp.concatenate(
        [jnp.ones_like(segments[:, :1]), (segments[:, 1:] != segments[:, :-1]).astype(jnp.int32)],
        axis=1,
    )
    first_place = lax.cummax(places[None, :] * begins, axis=1)
    offsets = (places[None, :] - first_place).astype(F32)
    inv_freq = 10000.0 ** (-2.0 * jnp.arange(ROTARY_DIM // 2, dtype=F32) / ROTARY_DIM)
    angles = offsets[..., None] * inv_freq
    return (jnp.cos(angles)[0], jnp.sin(angles)[0])


def swap(value, axis, bit, size):
    return lax.ppermute(value, axis, [(i, i ^ bit) for i in range(size)])


class Links:
    def __init__(self, send_sems, recv_sems):
        self.send_sems, self.recv_sems = send_sems, recv_sems
        self.place = {"dp": lax.axis_index("dp"), "tensor": lax.axis_index("tensor")}
        self.copies = []
        self.waited = set()

    def peer(self, step):
        place = dict(self.place)
        place[step[0]] = jnp.bitwise_xor(place[step[0]], step[1])
        return (place["dp"], place["tensor"])

    def greet(self, steps):
        barrier = pltpu.get_barrier_semaphore()
        for step in steps:
            pl.semaphore_signal(
                barrier, inc=1, device_id=self.peer(step), device_id_type=pl.DeviceIdType.MESH
            )
        pl.semaphore_wait(barrier, len(steps))

    def prepare(self, src, dst, step):
        n = len(self.copies)
        copy = pltpu.make_async_remote_copy(
            src_ref=src,
            dst_ref=dst,
            send_sem=self.send_sems.at[n],
            recv_sem=self.recv_sems.at[n],
            device_id=self.peer(step),
            device_id_type=pl.DeviceIdType.MESH,
        )
        self.copies.append(copy)
        return n

    def send(self, src, dst, step):
        n = self.prepare(src, dst, step)
        self.copies[n].start()
        return n

    def arrived(self, n):
        if n not in self.waited:
            self.copies[n].wait_recv()
            self.waited.add(n)

    def close(self):
        for n, copy in enumerate(self.copies):
            self.arrived(n)
            copy.wait_send()


class Riders:
    def __init__(self, links, riders, in_refs, out_refs):
        self.links = links
        self.rounds = []
        d = links.place["dp"]
        for rider in riders:
            full = out_refs[rider["out"]]
            if rider["kind"] == "plain":
                src = in_refs[rider["src"]]
                if rider["src_at"] is not None:
                    src = src.at[rider["src_at"]]
                self.add(0, src, full, rider["step"])
                continue
            if rider["kind"] == "block":
                held = [0]
                for k, step in enumerate(rider["steps"]):
                    for key in list(held):
                        here = full.at[rider["at"](links.place, key)]
                        self.add(k, here, here, step)
                        held.append(key ^ step[1])
                continue
            if rider["kind"] == "blocks":
                for key in rider["keys"]:
                    here = full.at[rider["at"](links.place, key)]
                    self.add(0, here, here, rider["step"])
                continue
            count, pair, high = rider["count"], rider["pair"], rider["high"]
            if rider["kind"] == "one":
                begin, size = rider["rows"]
                here = full.at[pl.ds(pl.multiple_of(d * count + begin, 16), size)]
                for name, bit in (("other", pair), ("mine", high), ("other", high ^ pair)):
                    src = in_refs[rider[name]].at[pl.ds(begin, size)]
                    self.add(0, src, here, ("dp", bit))
            else:
                held = [0]
                for k, step in enumerate(rider["steps"]):
                    for key in list(held):
                        place = jnp.bitwise_xor(d, rider["z"] * pair + key)
                        begin, size = rider.get("rows", (0, count))
                        at = pl.multiple_of(place * count + begin, 16)
                        here = full.at[pl.ds(at, size)]
                        self.add(k, here, here, step)
                        held.append(key ^ step[1])

    def add(self, k, src, dst, step):
        while len(self.rounds) <= k:
            self.rounds.append([])
        self.rounds[k].append(self.links.prepare(src, dst, step))

    def start(self):
        if self.rounds:
            for n in self.rounds[0]:
                self.links.copies[n].start()

    def finish(self):
        for k, numbers in enumerate(self.rounds):
            if k:
                for n in numbers:
                    self.links.copies[n].start()
            for n in numbers:
                self.links.arrived(n)


def rider_steps(riders):
    steps = []
    for rider in riders:
        if rider["kind"] in ("plain", "blocks"):
            steps.append(rider["step"])
        elif rider["kind"] == "one":
            pair, high = rider["pair"], rider["high"]
            steps += [("dp", pair), ("dp", high), ("dp", high ^ pair)]
        else:
            steps += rider["steps"]
    return steps


def rider_count(riders):
    total = 0
    for rider in riders:
        if rider["kind"] == "plain":
            total += 1
        elif rider["kind"] == "blocks":
            total += len(rider["keys"])
        elif rider["kind"] == "one":
            total += 3
        else:
            total += (1 << len(rider["steps"])) - 1
    return total


def distinct(steps):
    out = []
    for step in steps:
        if step not in out:
            out.append(step)
    return out


def flip(key, step):
    return (key[0] ^ step[1], key[1]) if step[0] == "dp" else (key[0], key[1] ^ step[1])


def has_bit(key, step):
    return bool((key[0] if step[0] == "dp" else key[1]) & step[1])


def gather_count(jobs):
    return sum((1 << len(job["steps"])) - 1 for job in jobs)


def gather_rounds(links, src_refs, out_refs, jobs):
    d, t = links.place["dp"], links.place["tensor"]

    def landing(job, key):
        at = job["out_at"](jnp.bitwise_xor(d, key[0]), jnp.bitwise_xor(t, key[1]))
        return out_refs[job["out"]].at[at]

    state = []
    for job in jobs:
        src = src_refs[job["src"]]
        if job.get("src_at") is not None:
            src = src.at[job["src_at"]]
        state.append({(0, 0): (src, None)})
    for k in range(max(len(job["steps"]) for job in jobs)):
        for job, held in zip(jobs, state):
            if k >= len(job["steps"]):
                continue
            step = job["steps"][k]
            for key in list(held):
                src, came = held[key]
                if came is not None:
                    links.arrived(came)
                n = links.send(src, landing(job, key), step)
                new = flip(key, step)
                held[new] = (landing(job, new), n)
        yield k


def remote_gather(
    sources,
    jobs,
    extra,
    outs,
    name,
    collective_id,
    riders=(),
    aliases=(),
    distant=(),
    order=(),
    near_outs=(),
    scratch=(),
    work=None,
    late=(),
):
    steps = distinct([s for job in jobs for s in job["steps"]] + rider_steps(riders))
    count = gather_count(jobs) + rider_count(riders)
    aliases = dict(aliases)
    n_src, n_out, n_near = len(sources), len(outs), len(near_outs)

    def kernel(*refs):
        src_refs, refs = refs[:n_src], refs[n_src:]
        out_refs, refs = refs[:n_out], refs[n_out:]
        near, refs = refs[: n_near + len(scratch)], refs[n_near + len(scratch) :]
        send_sems, recv_sems, local_sems = refs
        all_src, all_out = list(src_refs) + list(near), list(out_refs) + list(near)
        links = Links(send_sems, recv_sems)
        d, t = links.place["dp"], links.place["tensor"]
        links.greet(steps)
        ride = Riders(links, riders, src_refs, out_refs)
        local = []

        def keep(src, where):
            copy = pltpu.make_async_copy(src, where, local_sems.at[len(local)])
            copy.start()
            local.append(copy)
            return copy

        for src, out, at in extra:
            keep(all_src[src], all_out[out].at[at(d, t)])
        groups = {}
        for job in jobs:
            groups.setdefault(job.get("group", 0), []).append(job)
        turns = {}
        sent = {g: [] for g in groups}
        kept = {g: [] for g in groups}

        def advance(group):
            before = len(links.copies)
            if group not in turns:
                turns[group] = gather_rounds(links, all_src, all_out, groups[group])
                for job in groups[group]:
                    if not job.get("keep", True):
                        continue
                    src = all_src[job["src"]]
                    if job.get("src_at") is not None:
                        src = src.at[job["src_at"]]
                    kept[group].append(keep(src, all_out[job["out"]].at[job["out_at"](d, t)]))
            going = next(turns[group], None) is not None
            sent[group] += range(before, len(links.copies))
            return going

        waited = set()
        if "ride" not in order:
            ride.start()
        for turn in order:
            if turn == "ride":
                ride.start()
            elif callable(turn):
                turn(all_src)
            elif turn == "work":
                work(all_src)
                for src, out in late:
                    keep(all_src[src], all_out[out])
            elif isinstance(turn, tuple):
                for n in sent[turn[1]]:
                    links.arrived(n)
                for copy in kept[turn[1]]:
                    copy.wait()
                waited.add(turn[1])
            else:
                advance(turn)
        for group in groups:
            while advance(group):
                pass
        ride.finish()
        links.close()
        done = [copy for group in waited for copy in kept[group]]
        for copy in local:
            if not any(copy is other for other in done):
                copy.wait()

    vmem = pl.BlockSpec(memory_space=pltpu.VMEM)
    far = pl.BlockSpec(memory_space=pl.ANY)
    return pl.pallas_call(
        kernel,
        out_shape=[jax.ShapeDtypeStruct(o, BF16) for o in outs] + list(near_outs),
        in_specs=[far if n in aliases or n in distant else vmem for n in range(n_src)],
        out_specs=[far] * n_out + [vmem] * n_near,
        scratch_shapes=[pltpu.VMEM(o.shape, o.dtype) for o in scratch]
        + [
            pltpu.SemaphoreType.DMA((count,)),
            pltpu.SemaphoreType.DMA((count,)),
            pltpu.SemaphoreType.DMA((len(jobs) + len(extra) + len(late),)),
        ],
        input_output_aliases=aliases,
        compiler_params=pltpu.CompilerParams(
            collective_id=collective_id, has_side_effects=True, vmem_limit_bytes=VMEM_LIMIT
        ),
        cost_estimate=FREE,
        name=name,
    )(*sources)


def reduce_plan(keys, ways):
    plan = []
    for w, steps in enumerate(ways):
        live = list(keys)
        for k, step in enumerate(steps):
            plan += [(w, k, key) for key in live if has_bit(key, step)]
            live = [key for key in live if not has_bit(key, step)]
    return plan


def remote_reduce(
    operands, fetched, term, keys, ways, rows, wide, name, collective_id, riders=(), ridden=(), carried=(), jobs=(), job_sources=(), job_outs=(), after=None, after_in=(), after_out=()
):
    core_step = ("tensor", 1)
    part = rows // len(ways)
    plan = reduce_plan(keys, ways)
    slot = {entry: n for n, entry in enumerate(plan)}
    steps = distinct(
        [core_step]
        + [s for s in ways[0]]
        + rider_steps(riders)
        + [s for job in jobs for s in job["steps"]]
    )
    count = len(keys) + len(plan) + rider_count(riders) + gather_count(jobs)
    n_in = len(operands)
    n_ride = n_in + len(ridden) + len(carried)
    n_all = n_ride + len(job_sources)
    n_jobs = len(job_outs)
    after_out = list(after_out) or [jax.ShapeDtypeStruct((rows, wide), F32)]
    n_own = len(after_out)

    def kernel(*refs):
        in_refs = refs[:n_in]
        own_out = refs[n_all + len(after_in) : n_all + len(after_in) + n_own]
        extra_in = refs[n_all : n_all + len(after_in)]
        refs = refs[:n_all] + refs[n_all + len(after_in) + n_own - 1 :]
        ride_in = refs[n_in:n_ride]
        job_in = refs[n_ride:n_all]
        ride_out = refs[n_all + 1 : n_all + 1 + len(ridden)]
        job_out = refs[n_all + 1 + len(ridden) : n_all + 1 + len(ridden) + n_jobs]
        scratch = refs[n_all + 1 + len(ridden) + n_jobs :]
        held = scratch[:n_in]
        core_out, core_in, chip, hop_out, hop_in, send_sems, recv_sems, in_sems, job_sems = scratch[
            n_in:
        ]
        started = []
        for n in range(n_in):
            shape = fetched[n]
            src = in_refs[n].at[tuple(pl.ds(0, s) for s in shape)]
            copy = pltpu.make_async_copy(src, held[n], in_sems.at[n])
            copy.start()
            started.append(copy)
        links = Links(send_sems, recv_sems)
        links.greet(steps)
        ride = Riders(links, riders, ride_in, ride_out)
        ride.start()
        rounds = gather_rounds(links, job_in, job_out, jobs) if jobs else iter(())
        next(rounds, None)
        placed = []
        for n, job in enumerate(jobs):
            at = job["out_at"](links.place["dp"], links.place["tensor"])
            copy = pltpu.make_async_copy(
                job_in[job["src"]], job_out[job["out"]].at[at], job_sems.at[n]
            )
            copy.start()
            placed.append(copy)
        for copy in started:
            copy.wait()
        came = {}

        def send_part(w, k, key):
            entry = (w, k, key)
            came[entry] = links.send(hop_out.at[slot[entry]], hop_in.at[slot[entry]], ways[w][k])

        def so_far(w, k, key):
            total = chip[keys.index(key), w * part : (w + 1) * part, :]
            for j in range(k):
                entry = (w, j, flip(key, ways[w][j]))
                links.arrived(came[entry])
                total = total + hop_in[slot[entry]].astype(F32)
            return total

        for i, key in enumerate(keys):
            core_out[i] = narrow(term(held, links.place, (key[0], key[1] ^ 1)))
            crossing = links.send(core_out.at[i], core_in.at[i], core_step)
            mine = term(held, links.place, key)
            links.arrived(crossing)
            chip[i] = mine + core_in[i].astype(F32)
            for w, way in enumerate(ways):
                if way and has_bit(key, way[0]):
                    hop_out[slot[(w, 0, key)]] = narrow(chip[i, w * part : (w + 1) * part, :])
                    send_part(w, 0, key)
            next(rounds, None)
        for k in range(1, len(ways[0])):
            for w in range(len(ways)):
                for entry in plan:
                    if entry[0] == w and entry[1] == k:
                        hop_out[slot[entry]] = narrow(so_far(w, k, entry[2]))
                        send_part(w, k, entry[2])
        for w in range(len(ways)):
            total = so_far(w, len(ways[w]), (0, 0))
            if after is None:
                own_out[0][w * part : (w + 1) * part, :] = total
            else:
                after(slice(w * part, (w + 1) * part), total, extra_in, own_out)
        for _ in rounds:
            pass
        ride.finish()
        links.close()
        for copy in placed:
            copy.wait()

    any_spec = pl.BlockSpec(memory_space=pl.ANY)
    return pl.pallas_call(
        kernel,
        out_shape=after_out
        + [jax.ShapeDtypeStruct(r.shape, r.dtype) for r in ridden]
        + [jax.ShapeDtypeStruct(o, BF16) for o in job_outs],
        in_specs=[any_spec] * n_ride
        + [pl.BlockSpec(memory_space=pltpu.VMEM)] * (len(job_sources) + len(after_in)),
        out_specs=[pl.BlockSpec(memory_space=pltpu.VMEM)] * n_own
        + [any_spec] * (len(ridden) + n_jobs),
        input_output_aliases={n_in + n: n_own + n for n in range(len(ridden))},
        scratch_shapes=[pltpu.VMEM(s, o.dtype) for s, o in zip(fetched, operands)]
        + [
            pltpu.VMEM((len(keys), rows, wide), BF16),
            pltpu.VMEM((len(keys), rows, wide), BF16),
            pltpu.VMEM((len(keys), rows, wide), F32),
            pltpu.VMEM((max(len(plan), 1), part, wide), BF16),
            pltpu.VMEM((max(len(plan), 1), part, wide), BF16),
            pltpu.SemaphoreType.DMA((count,)),
            pltpu.SemaphoreType.DMA((count,)),
            pltpu.SemaphoreType.DMA((n_in,)),
            pltpu.SemaphoreType.DMA((max(len(jobs), 1),)),
        ],
        compiler_params=pltpu.CompilerParams(
            collective_id=collective_id, has_side_effects=True, vmem_limit_bytes=VMEM_LIMIT
        ),
        cost_estimate=FREE,
        name=name,
    )(*operands, *ridden, *carried, *job_sources, *after_in)


class Share:
    def __init__(self, links, n_t, orders, source, out, own, sums, came, went, terms, fetch_sem):
        self.links, self.terms, self.own = links, terms, own
        self.fetch = pltpu.make_async_copy(source, terms, fetch_sem.at[0])
        self.sums, self.came, self.went = sums, came, went
        self.count = terms.shape[0] // n_t
        self.wide = terms.shape[1] // len(orders)
        count = self.count
        t_steps = [("tensor", 1 << b) for b in range(n_t.bit_length() - 1)]
        self.rounds = []
        live, slot = list(range(n_t)), 0
        before = []
        for k, step in enumerate(t_steps):
            sent = []
            for r in live:
                if r & step[1]:
                    src = terms.at[self.block(r)] if k == 0 else went.at[slot]
                    sent.append((r, slot, links.prepare(src, came.at[slot], step)))
                    slot += 1
            live = [r for r in live if not r & step[1]]
            self.rounds.append(functools.partial(self.scatter, k, list(live), before, sent, step))
            before = [(r ^ step[1], at, n) for r, at, n in sent]
        d, t = links.place["dp"], links.place["tensor"]

        def landing(p, key):
            rows = pl.ds(pl.multiple_of(jnp.bitwise_xor(t, key[1]) * count, 16), count)
            return out.at[p, jnp.bitwise_xor(d, key[0]), rows]

        self.places = [landing(p, (0, 0)) for p in range(len(orders))]
        held = [{(0, 0): (own.at[p], None)} for p in range(len(orders))]
        seen = set()
        for k in range(len(orders[0])):
            work = []
            for p, order in enumerate(orders):
                step = order[k]
                for key in list(held[p]):
                    src, needs = held[p][key]
                    n = links.prepare(src, landing(p, key), step)
                    work.append((None if needs in seen else needs, n))
                    seen.add(needs)
                    new = flip(key, step)
                    held[p][new] = (landing(p, new), n)
            self.rounds.append(functools.partial(self.gather, k, before, work))

    def block(self, r):
        at = jnp.bitwise_xor(self.links.place["tensor"], r) * self.count
        return pl.ds(pl.multiple_of(at, 16), self.count)

    def scatter(self, k, live, before, sent, step):
        if k == 0:
            self.fetch.start()
            self.fetch.wait()
            for r in live:
                self.sums[r] = self.terms[self.block(r), :].astype(F32)
        self.add(before)
        for r, at, n in sent:
            if k:
                self.went[at] = narrow(self.sums[r])
            self.links.copies[n].start()

    def add(self, before):
        for r, at, n in before:
            self.links.arrived(n)
            self.sums[r] = self.sums[r] + self.came[at].astype(F32)

    def gather(self, k, before, work):
        if k == 0:
            self.add(before)
            for p in range(self.own.shape[0]):
                self.own[p] = narrow(self.sums[0, :, p * self.wide : (p + 1) * self.wide])
        for needs, n in work:
            if needs is not None:
                self.links.copies[needs].wait_recv()
                self.links.waited.add(needs)
            self.links.copies[n].start()

    def keep(self, sems):
        return [
            pltpu.make_async_copy(self.own.at[p], where, sems.at[p])
            for p, where in enumerate(self.places)
        ]


def share_shapes(shape, n_t, orders):
    count, parts = shape[0] // n_t, len(orders)
    copies = n_t - 1 + parts * ((1 << len(orders[0])) - 1)
    scratch = [
        pltpu.VMEM((parts, count, shape[1] // parts), BF16),
        pltpu.VMEM((n_t, count, shape[1]), F32),
        pltpu.VMEM((n_t - 1, count, shape[1]), BF16),
        pltpu.VMEM((n_t - 1, count, shape[1]), BF16),
        pltpu.VMEM(shape, BF16),
        pltpu.SemaphoreType.DMA((1,)),
        pltpu.SemaphoreType.DMA((parts,)),
    ]
    return scratch, copies


def remote_share(terms, n_dp, n_t, orders, name, collective_id, work_in, work_out, work):
    scratch, copies = share_shapes(terms.shape, n_t, orders)
    parts = len(orders)

    n_in, n_work = len(work_in), len(work_out)

    def kernel(source, *refs):
        work_refs = refs[:n_in] + refs[n_in + 1 : n_in + 1 + n_work]
        out_ref = refs[n_in]
        refs = refs[n_in + 1 + n_work :]
        held, refs = refs[:n_in], refs[n_in:]
        own_sems, send_sems, recv_sems, in_sems = refs[-4:]
        fetched = [
            pltpu.make_async_copy(work_refs[n], held[n], in_sems.at[n]) for n in range(n_in)
        ]
        for copy in fetched:
            copy.start()
        links = Links(send_sems, recv_sems)
        links.greet(orders[0])
        share = Share(links, n_t, orders, source, out_ref, *refs[:-4])
        for k, one in enumerate(share.rounds):
            one()
            if k == len(share.rounds) - 2:
                for copy in fetched:
                    copy.wait()
                work(list(held) + list(work_refs[n_in:]))
        kept = share.keep(own_sems)
        for copy in kept:
            copy.start()
        links.close()
        for copy in kept:
            copy.wait()

    return pl.pallas_call(
        kernel,
        out_shape=[
            jax.ShapeDtypeStruct((parts, n_dp, terms.shape[0], terms.shape[1] // parts), BF16)
        ]
        + list(work_out),
        in_specs=[pl.BlockSpec(memory_space=pl.ANY)]
        + [pl.BlockSpec(memory_space=pl.ANY)] * n_in,
        out_specs=[pl.BlockSpec(memory_space=pl.ANY)]
        + [pl.BlockSpec(memory_space=pltpu.VMEM)] * n_work,
        scratch_shapes=[pltpu.VMEM(a.shape, a.dtype) for a in work_in]
        + scratch
        + [
            pltpu.SemaphoreType.DMA((copies,)),
            pltpu.SemaphoreType.DMA((copies,)),
            pltpu.SemaphoreType.DMA((n_in,)),
        ],
        compiler_params=pltpu.CompilerParams(
            collective_id=collective_id, has_side_effects=True, vmem_limit_bytes=VMEM_LIMIT
        ),
        cost_estimate=FREE,
        name=name,
    )(terms, *work_in)


def set_sums(set_ids, sources, acc_shape, add, outs, put, groups, name):
    n_src = len(sources)
    count = set_ids.shape[0]

    def kernel(ids_ref, *refs):
        src_refs, out_refs, acc = refs[:n_src], refs[n_src:-1], refs[-1]
        k = pl.program_id(0)
        acc[...] = jnp.zeros_like(acc)
        for s in range(count):

            @pl.when(ids_ref[s] == k)
            def _(s=s):
                add(s, src_refs, acc)

        put(acc, out_refs)

    out_specs = []
    for before, after in outs:
        lead = len(before)
        block = tuple(before) + (1,) + tuple(after)
        out_specs.append(
            pl.BlockSpec(
                block, lambda k, ids, lead=lead, n=len(after): (0,) * lead + (k,) + (0,) * n
            )
        )
    return pl.pallas_call(
        kernel,
        grid_spec=pltpu.PrefetchScalarGridSpec(
            num_scalar_prefetch=1,
            grid=(groups,),
            in_specs=[
                pl.BlockSpec(a.shape, lambda k, ids, n=a.ndim: (0,) * n) for a in sources
            ],
            out_specs=out_specs,
            scratch_shapes=[pltpu.VMEM(acc_shape, F32)],
        ),
        out_shape=[
            jax.ShapeDtypeStruct(tuple(before) + (groups,) + tuple(after), F32)
            for before, after in outs
        ],
        compiler_params=pltpu.CompilerParams(vmem_limit_bytes=VMEM_LIMIT),
        cost_estimate=FREE,
        name=name,
    )(set_ids, *sources)


def split_three(value):
    high = narrow(value).astype(F32)
    middle = narrow(value - high).astype(F32)
    return high, middle, value - high - middle


def rope_mix(value, cos_l, sin_a, sin_b):
    return (
        value * cos_l
        + pltpu.roll(value, HEAD_LANES - ROTARY_DIM // 2, 1) * sin_a
        + pltpu.roll(value, ROTARY_DIM // 2, 1) * sin_b
    )


def attn_fwd_kernel(
    per_step, q_width, kv_at, xl_ref, wq_ref, wkv_ref, rope_ref, pe_ref, doc_ref, qa_ref, kv_ref, o_ref
):
    length = xl_ref.shape[0]
    lane = lax.broadcasted_iota(jnp.int32, (length, HEAD_LANES), 1)
    q_all = dot_nn(xl_ref[:, :q_width], wq_ref[...])
    kv_all = dot_nn(xl_ref[:, kv_at:], wkv_ref[...])
    kv_ref[...] = narrow(kv_all)
    doc_q = doc_ref[...].astype(F32)
    q_heads, k_heads, kv_turned = [], [], []
    for i in range(per_step):
        span = slice(i * HEAD_LANES, (i + 1) * HEAD_LANES)
        q_one = rope_mix(q_all[:, span], rope_ref[0], rope_ref[1], rope_ref[2]) + doc_q
        q_heads.append(narrow(q_one))
        kv_one = kv_all[:, span]
        k_heads.append(jnp.where(lane < PLAIN_HEAD_DIM, narrow(kv_one), pe_ref[...]))
        kv_turned.append(narrow(kv_one.T))
    key_at = lax.broadcasted_iota(jnp.int32, (BLOCK_Q, BLOCK_Q), 0)
    query_at = lax.broadcasted_iota(jnp.int32, (BLOCK_Q, BLOCK_Q), 1)
    row = lax.broadcasted_iota(jnp.int32, (HEAD_LANES, BLOCK_Q), 0)
    block_lane = lax.broadcasted_iota(jnp.int32, (BLOCK_Q, HEAD_LANES), 1)
    for j in range(length // BLOCK_Q):
        begin, end = j * BLOCK_Q, (j + 1) * BLOCK_Q
        mixed = []
        for i in range(per_step):
            q_part = q_heads[i][begin:end]
            scores = dot_nt(k_heads[i][:end], q_part)
            diag = jnp.where(key_at <= query_at, scores[begin:], -BIG)
            scores = diag if j == 0 else jnp.concatenate([scores[:begin], diag], axis=0)
            top = jnp.max(scores, axis=0, keepdims=True)
            terms = jnp.exp2((scores - top) * EXP2_SCALE)
            total = jnp.sum(terms, axis=0, keepdims=True)
            out_t = dot_nn(kv_turned[i][:, :end], narrow(terms)) * (1.0 / total)
            high, middle, low = split_three(top + jnp.log2(total) * (1.0 / EXP2_SCALE))
            out_t = jnp.where(
                row == 0, -high, jnp.where(row == 1, -middle, jnp.where(row == 2, -low, out_t))
            )
            out_n = out_t.T
            mixed.append(out_n)
            is_lse = (block_lane >= 96) & (block_lane < 99)
            q_saved = jnp.where(is_lse, narrow(pltpu.roll(out_n, 96, 1)), q_part)
            qa_ref[begin:end, i * HEAD_LANES : (i + 1) * HEAD_LANES] = q_saved
        if per_step == 2:
            both = jnp.where(block_lane < 64, pltpu.roll(mixed[0], 64, 1), mixed[1])
            o_ref[begin:end, :] = narrow(both)
        else:
            even = lax.rem(pl.program_id(0), 2) == 0
            moved = jnp.where(even, pltpu.roll(mixed[0], 64, 1), mixed[0])
            mine = (block_lane < 64) == even
            o_ref[begin:end, :] = jnp.where(mine, narrow(moved), o_ref[begin:end, :])


def attn_bwd_kernel(
    per_step,
    qa_ref,
    kv_ref,
    o_ref,
    do_ref,
    rope_ref,
    pe_ref,
    codes_ref,
    dq_ref,
    dkv_ref,
    dpe_ref,
    cq_ref,
    ckv_ref,
    dk_acc,
    dv_acc,
):
    length = qa_ref.shape[0]
    step = pl.program_id(0)
    lane = lax.broadcasted_iota(jnp.int32, (length, HEAD_LANES), 1)
    upper = lane >= 64
    key_at = lax.broadcasted_iota(jnp.int32, (BLOCK_Q, BLOCK_Q), 0)
    query_at = lax.broadcasted_iota(jnp.int32, (BLOCK_Q, BLOCK_Q), 1)
    causal = key_at <= query_at
    out_both = o_ref[...].astype(F32)
    grad_both = do_ref[...].astype(F32)

    @pl.when(step == 0)
    def _():
        dpe_ref[...] = jnp.zeros_like(dpe_ref)

    for i in range(per_step):
        span = slice(i * HEAD_LANES, (i + 1) * HEAD_LANES)
        if per_step == 2:
            turn = i == 0
            grad_one = pltpu.roll(grad_both, 64, 1) if turn else grad_both
            out_one = pltpu.roll(out_both, 64, 1) if turn else out_both
        else:
            even = lax.rem(step, 2) == 0
            grad_one = jnp.where(even, pltpu.roll(grad_both, 64, 1), grad_both)
            out_one = jnp.where(even, pltpu.roll(out_both, 64, 1), out_both)
        grad_one = jnp.where(upper, grad_one, 0.0)
        inner = jnp.sum(jnp.where(upper, grad_one * out_one, 0.0), axis=-1, keepdims=True)
        high, middle, low = split_three(inner)
        grad_aug = jnp.where(
            lane == 0, -high, jnp.where(lane == 1, -middle, jnp.where(lane == 2, -low, grad_one))
        )
        grad_aug = narrow(grad_aug)
        kv_one = kv_ref[:, span]
        ones = jnp.where(lane < 3, 1.0, 0.0).astype(BF16)
        v_aug = jnp.where(upper, kv_one, ones)
        k_aug = jnp.where(lane < 64, kv_one, pe_ref[...])
        k_turned = narrow(k_aug.astype(F32).T)
        for j in reversed(range(length // BLOCK_Q)):
            begin, end = j * BLOCK_Q, (j + 1) * BLOCK_Q
            q_part = qa_ref[begin:end, span]
            probs = jnp.exp2(dot_nt(k_aug[:end], q_part) * EXP2_SCALE)
            diag = jnp.where(causal, probs[begin:], 0.0)
            probs = diag if j == 0 else jnp.concatenate([probs[:begin], diag], axis=0)
            grads = narrow(probs * dot_nt(v_aug[:end], grad_aug[begin:end]))
            dq_part = dot_nn(k_turned[:, :end], grads).T * SCORE_SCALE
            dq_part = rope_mix(
                dq_part,
                rope_ref[0, begin:end, :],
                -rope_ref[1, begin:end, :],
                -rope_ref[2, begin:end, :],
            )
            dq_ref[begin:end, span] = narrow(dq_part)
            dk_part = dot_nn(grads, q_part)
            dv_part = dot_nn(narrow(probs), grad_aug[begin:end])
            if end == length:
                dk_acc[...] = dk_part
                dv_acc[...] = dv_part
            else:
                dk_acc[:end] += dk_part
                dv_acc[:end] += dv_part
        dk_all = dk_acc[...] * SCORE_SCALE
        dkv_ref[:, span] = narrow(jnp.where(upper, dv_acc[...], dk_all))
        dpe_ref[...] += jnp.where(upper & (lane < 96), dk_all, 0.0)
    cq_ref[...] = dot_tn(codes_ref[...], dq_ref[...])
    ckv_ref[...] = dot_tn(codes_ref[...], dkv_ref[...])

    @pl.when(step == pl.num_programs(0) - 1)
    def _():
        turned_back = rope_mix(dpe_ref[...], rope_ref[0], -rope_ref[1], -rope_ref[2])
        dpe_ref[...] = pltpu.roll(turned_back, PLAIN_HEAD_DIM + 2 * RANK, 1)


def ridden_call(
    kernel,
    grid,
    arrays,
    in_specs,
    out_shape,
    out_specs,
    scratch,
    riders,
    ridden,
    carried,
    fresh,
    name,
    collective_id,
):
    steps = distinct(rider_steps(riders))
    count = rider_count(riders)
    n_in, n_out = len(arrays), len(out_shape)
    n_ride_in = len(ridden) + len(carried)
    n_ride_out = len(ridden) + len(fresh)
    def body(*refs):
        own_in, rest = refs[:n_in], refs[n_in:]
        ride_in, rest = rest[:n_ride_in], rest[n_ride_in:]
        own_out, rest = rest[:n_out], rest[n_out:]
        ride_out, rest = rest[:n_ride_out], rest[n_ride_out:]
        send_sems, recv_sems = rest[-2:]
        links = Links(send_sems, recv_sems)
        ride = Riders(links, riders, ride_in, ride_out)

        @pl.when(pl.program_id(0) == 0)
        def _():
            links.greet(steps)
            ride.start()

        kernel(*own_in, *own_out, *rest[:-2])

        @pl.when(pl.program_id(0) == grid[0] - 1)
        def _():
            ride.finish()
            links.close()

    any_spec = pl.BlockSpec(memory_space=pl.ANY)
    return pl.pallas_call(
        body,
        grid=grid,
        in_specs=list(in_specs) + [any_spec] * n_ride_in,
        out_specs=list(out_specs) + [any_spec] * n_ride_out,
        out_shape=list(out_shape)
        + [jax.ShapeDtypeStruct(r.shape, r.dtype) for r in ridden]
        + [jax.ShapeDtypeStruct(f, BF16) for f in fresh],
        scratch_shapes=list(scratch)
        + [pltpu.SemaphoreType.DMA((count,)), pltpu.SemaphoreType.DMA((count,))],
        input_output_aliases={n_in + n: n_out + n for n in range(len(ridden))},
        compiler_params=pltpu.CompilerParams(
            collective_id=collective_id, has_side_effects=True, vmem_limit_bytes=VMEM_LIMIT
        ),
        cost_estimate=FREE,
        name=name,
    )(*arrays, *ridden, *carried)


def attend(latents, w_q, w_kv, rope, pe_aug, doc_q, q_width, kv_at, riders, ridden, carried):
    length = latents.shape[0]
    heads = w_q.shape[1] // HEAD_LANES
    per_step = 2 if heads % 2 == 0 else 1
    wide = per_step * HEAD_LANES
    whole = lambda a: pl.BlockSpec(a.shape, lambda h: (0,) * a.ndim)
    return ridden_call(
        functools.partial(attn_fwd_kernel, per_step, q_width, kv_at),
        (heads // per_step,),
        [latents, w_q, w_kv, rope, pe_aug, doc_q],
        [
            whole(latents),
            pl.BlockSpec((w_q.shape[0], wide), lambda h: (0, h)),
            pl.BlockSpec((w_kv.shape[0], wide), lambda h: (0, h)),
            whole(rope),
            whole(pe_aug),
            whole(doc_q),
        ],
        [
            jax.ShapeDtypeStruct((length, heads * HEAD_LANES), BF16),
            jax.ShapeDtypeStruct((length, heads * HEAD_LANES), BF16),
            jax.ShapeDtypeStruct((length, heads * VALUE_HEAD_DIM), BF16),
        ],
        [
            pl.BlockSpec((length, wide), lambda h: (0, h)),
            pl.BlockSpec((length, wide), lambda h: (0, h)),
            pl.BlockSpec((length, HEAD_LANES), lambda h: (0, h * per_step // 2)),
        ],
        [],
        riders,
        ridden,
        carried,
        [],
        "attend",
        10,
    )


def attend_back(q_aug, kv, heads_out, heads_grad, rope, pe_aug, codes, riders, ridden, carried, fresh):
    length = q_aug.shape[0]
    heads = q_aug.shape[1] // HEAD_LANES
    per_step = 2 if heads % 2 == 0 else 1
    wide = per_step * HEAD_LANES
    whole = lambda a: pl.BlockSpec(a.shape, lambda h: (0,) * a.ndim)
    columns = pl.BlockSpec((length, wide), lambda h: (0, h))
    packed = pl.BlockSpec((length, HEAD_LANES), lambda h: (0, h * per_step // 2))
    rows_in, lane_block = codes
    arrays = [q_aug, kv, heads_out, heads_grad, rope, pe_aug, rows_in]
    in_specs = [columns, columns, packed, packed, whole(rope), whole(pe_aug)]
    in_specs.append(pl.BlockSpec((length, CODE_LANES), lambda h: (0, lane_block)))
    out_shape = [
        jax.ShapeDtypeStruct((length, heads * HEAD_LANES), BF16),
        jax.ShapeDtypeStruct((length, heads * HEAD_LANES), BF16),
        jax.ShapeDtypeStruct((length, HEAD_LANES), F32),
    ] + [jax.ShapeDtypeStruct((CODE_LANES, heads * HEAD_LANES), F32)] * 2
    out_specs = [columns, columns, pl.BlockSpec((length, HEAD_LANES), lambda h: (0, 0))]
    out_specs += [pl.BlockSpec((CODE_LANES, wide), lambda h: (0, h))] * 2
    scratch = [pltpu.VMEM((length, HEAD_LANES), F32), pltpu.VMEM((length, HEAD_LANES), F32)]
    return ridden_call(
        functools.partial(attn_bwd_kernel, per_step),
        (heads // per_step,),
        arrays,
        in_specs,
        out_shape,
        out_specs,
        scratch,
        riders,
        ridden,
        carried,
        fresh,
        "attend_back",
        11,
    )


def gate_middle(gate, up, hid_grad):
    sig = 1.0 / (1.0 + jnp.exp(-gate))
    silu = gate * sig
    gate_grad = hid_grad * up * (sig * (1.0 + gate * (1.0 - sig)))
    return silu * up, gate_grad, hid_grad * silu


def tail_middle(pre, back, tail):
    wide = pre.shape[1]
    up = pltpu.roll(pre, wide - tail, 1)
    hid_grad = pltpu.roll(back, wide - 2 * tail, 1)
    hid, gate_grad, up_grad = gate_middle(pre, up, hid_grad)
    lane = lax.broadcasted_iota(jnp.int32, pre.shape, 1)
    hid = jnp.where((lane >= 2 * tail) & (lane < 3 * tail), pltpu.roll(hid, 2 * tail, 1), 0.0)
    both = jnp.where(
        lane < tail, gate_grad, jnp.where(lane < 2 * tail, pltpu.roll(up_grad, tail, 1), 0.0)
    )
    return hid, both


def remote_ffn(x_own, g_all, weights, extras, mains, tail, tail_wide, slow, block_of, riders, name, collective_id):
    rows, aug = x_own.shape
    total = g_all.shape[0]
    blocks = total // rows
    both = 2 * rows
    width = aug - CODE_LANES
    chunks = len(mains)
    tails = [0] * (chunks - 1) + [tail_wide]
    gu = [2 * m + w for m, w in zip(mains, tails)]
    core_step = ("tensor", 1)
    keys = [(0, 0)]
    for step in slow:
        keys += [flip(key, step) for key in keys]
    bits_of = {key: [s for s in slow if has_bit(key, s)] for key in keys}
    keys.sort(key=lambda k: len(bits_of[k]))

    def part_rows(key, step):
        n = len(bits_of[key])
        i = bits_of[key].index(step)
        size = -(-rows // (16 * n)) * 16
        begin = i * size
        return begin, min(size, rows - begin)

    count = len(keys) + sum(len(bits_of[k]) for k in keys) + rider_count(riders)
    steps = distinct([core_step] + slow + rider_steps(riders))

    def kernel(x_ref, g_ref, *refs):
        e_refs = refs[chunks : 2 * chunks]
        refs = refs[2 * chunks :]
        codes_ref = refs[0]
        grad_refs = refs[1 : 1 + chunks]
        hid_refs = refs[1 + chunks : 1 + 2 * chunks]
        w_refs = refs[1 + 2 * chunks : 1 + 3 * chunks]
        x_held, back_held, g_held = refs[1 + 3 * chunks : 4 + 3 * chunks]
        w_held = refs[4 + 3 * chunks : 4 + 4 * chunks]
        send_sems, recv_sems, w_sems, g_sems = refs[4 + 4 * chunks :]
        links = Links(send_sems, recv_sems)
        place = links.place
        fetch = [
            pltpu.make_async_copy(w_refs[c], w_held[c].at[pl.ds(0, width)], w_sems.at[c])
            for c in range(chunks)
        ]
        fetch_extra = [
            pltpu.make_async_copy(
                e_refs[c], w_held[c].at[pl.ds(width, CODE_LANES)], w_sems.at[chunks + c]
            )
            for c in range(chunks)
        ]
        fetch[0].start()
        for copy in fetch_extra:
            copy.start()
        links.greet(steps)

        def landing(key):
            at = pl.multiple_of(block_of(key, place) * rows, 16)
            return x_held.at[pl.ds(at, rows)]

        arrivals = {key: [] for key in keys}

        def pass_on(key, src):
            for step in slow:
                if has_bit(key, step):
                    continue
                there = flip(key, step)
                begin, size = part_rows(there, step)
                at = pl.ds(begin, size)
                n = links.send(src.at[at], landing(key).at[at], step)
                arrivals[there].append(n)

        crossing = {}
        pass_on((0, 0), x_ref)
        crossing[(0, 0)] = links.send(x_ref, landing((0, 0)), core_step)
        ride = Riders(links, riders, w_refs, w_refs)
        ride.start()
        x_held[pl.ds(pl.multiple_of(block_of((0, 0), place) * rows, 16), rows), :] = x_ref[...]

        def g_copy(b, slot):
            at = pl.ds(pl.multiple_of(b * both, 16), both)
            return pltpu.make_async_copy(g_ref.at[at], g_held.at[slot], g_sems.at[slot])

        def over_blocks(work):
            g_copy(0, 0).start()

            def one(b, carry):
                slot = lax.rem(b, 2)

                @pl.when(b + 1 < blocks // 2)
                def _():
                    g_copy(b + 1, 1 - slot).start()

                g_copy(b, slot).wait()
                work(b, g_held[slot])
                return carry

            lax.fori_loop(0, blocks // 2, one, 0)

        fetch[0].wait()
        for copy in fetch_extra:
            copy.wait()

        def back_first(b, g_rows):
            back_held[b] = dot_nn(g_rows, w_held[0][:, gu[0] :])

        over_blocks(back_first)

        def forward(b, c, back):
            main = mains[c]
            at = pl.ds(pl.multiple_of(b * both, 16), both)
            pre = dot_nn(x_held[at, :], w_held[c][:, : gu[c]])
            hid, gate_grad, up_grad = gate_middle(pre[:, :main], pre[:, gu[c] - main :], back)
            hid_refs[c][at, :main] = narrow(hid)
            grad_refs[c][at, :main] = narrow(gate_grad)
            grad_refs[c][at, gu[c] - main :] = narrow(up_grad)
            return pre, at

        def first_chunk(key):
            b = block_of(key, place) // 2
            forward(b, 0, back_held[b])

        links.arrived(crossing[(0, 0)])
        first_chunk((0, 0))

        def later(b, g_rows, c):
            main = mains[c]
            back = dot_nn(g_rows, w_held[c][:, gu[c] :])
            pre, at = forward(b, c, back)
            if tails[c]:
                at_tail = slice(main, main + tail_wide)
                hid, both_grads = tail_middle(
                    pre[:, at_tail], dot_nn(g_rows, w_held[c][:, at_tail]), tail
                )
                hid_refs[c][at, main:] = narrow(hid)
                grad_refs[c][at, at_tail] = narrow(both_grads)

        def later_chunks(pairs):
            places = [block_of(key, place) // 2 for key in pairs]
            g_copy(places[0], 0).start()
            for n, b in enumerate(places):
                if n + 1 < len(places):
                    g_copy(places[n + 1], (n + 1) % 2).start()
                g_copy(b, n % 2).wait()
                for c in range(1, chunks):
                    later(b, g_held[n % 2], c)

        waiting = [(0, 0)]
        for level in range(1, len(slow) + 1):
            here = [key for key in keys if len(bits_of[key]) == level]
            for key in here:
                for n in arrivals[key]:
                    links.arrived(n)
                pass_on(key, landing(key))
                crossing[key] = links.send(landing(key), landing(key), core_step)
            for key in here:
                links.arrived(crossing[key])
                first_chunk(key)
            waiting += here
            if level == len(slow) - 1:
                ride.finish()
                for c in range(1, chunks):
                    fetch[c].start()
                    fetch[c].wait()
                later_chunks(waiting)
                waiting = []
        later_chunks(waiting)
        codes_ref[...] = x_held[:, width:]
        links.close()

    any_spec = pl.BlockSpec(memory_space=pl.ANY)
    vmem_spec = pl.BlockSpec(memory_space=pltpu.VMEM)
    outs = pl.pallas_call(
        kernel,
        in_specs=[vmem_spec, any_spec] + [any_spec] * (2 * chunks),
        out_specs=[vmem_spec] * (1 + 2 * chunks) + [any_spec] * chunks,
        out_shape=[jax.ShapeDtypeStruct((total, CODE_LANES), BF16)]
        + [jax.ShapeDtypeStruct((total, g), BF16) for g in gu]
        + [jax.ShapeDtypeStruct((total, m + w), BF16) for m, w in zip(mains, tails)]
        + [jax.ShapeDtypeStruct(w.shape, BF16) for w in weights],
        scratch_shapes=[
            pltpu.VMEM((total, aug), BF16),
            pltpu.VMEM((blocks // 2, both, mains[0]), F32),
            pltpu.VMEM((2, both, aug), BF16),
        ]
        + [pltpu.VMEM((aug, w.shape[1]), BF16) for w in weights]
        + [
            pltpu.SemaphoreType.DMA((count,)),
            pltpu.SemaphoreType.DMA((count,)),
            pltpu.SemaphoreType.DMA((2 * chunks,)),
            pltpu.SemaphoreType.DMA((2,)),
        ],
        input_output_aliases={2 + c: 1 + 2 * chunks + c for c in range(chunks)},
        compiler_params=pltpu.CompilerParams(
            collective_id=collective_id, has_side_effects=True, vmem_limit_bytes=VMEM_LIMIT
        ),
        cost_estimate=FREE,
        name=name,
    )(x_own, g_all, *weights, *extras)
    return (
        outs[0],
        outs[1 : 1 + chunks],
        outs[1 + chunks : 1 + 2 * chunks],
        outs[1 + 2 * chunks :],
    )


def remote_ffn_back(
    grads, hids, weights, extras, x_codes, g_all, mains, tail_wide, keys, ways, block_of, rows, name, collective_id
):
    width = weights[0].shape[0]
    aug = width + CODE_LANES
    chunks = len(mains)
    tails = [0] * (chunks - 1) + [tail_wide]
    gu = [2 * m + w for m, w in zip(mains, tails)]
    core_step = ("tensor", 1)
    part = rows // len(ways)
    plan = reduce_plan(keys, ways)
    later = [entry for entry in plan if entry[1] > 0]
    slot = {entry: n for n, entry in enumerate(plan)}
    later_slot = {entry: n for n, entry in enumerate(later)}
    steps = distinct([core_step] + ways[0])
    count = 2 * len(keys) + len(plan)
    operands = list(grads) + list(hids) + list(weights) + [x_codes, g_all]
    shapes = [o.shape for o in operands]
    for c in range(chunks):
        shapes[2 * chunks + c] = (aug, weights[c].shape[1])
    shapes[3 * chunks + 1] = x_codes.shape

    def kernel(*refs):
        n_in = len(operands)
        in_refs, e_refs, refs = refs[:n_in], refs[n_in : n_in + chunks], refs[n_in + chunks :]
        refs = in_refs + refs
        out_ref, terms_ref = refs[n_in : n_in + 2]
        gu_refs = refs[n_in + 2 : n_in + 2 + chunks]
        down_refs = refs[n_in + 2 + chunks : n_in + 2 + 2 * chunks]
        held = refs[n_in + 2 + 2 * chunks : 2 * n_in + 2 + 2 * chunks]
        rest = refs[2 * n_in + 2 + 2 * chunks :]
        core_out, core_in, chip, hop_out, hop_in, stage, send_sems, recv_sems, in_sems, out_sems, free = rest
        g_held, h_held = held[:chunks], held[chunks : 2 * chunks]
        w_held = held[2 * chunks : 3 * chunks]
        started = []
        order = [n for c in range(chunks) for n in (2 * chunks + c, c)]
        order += list(range(chunks, 2 * chunks)) + [3 * chunks, 3 * chunks + 1]
        for n in order:
            is_weight = 2 * chunks <= n < 3 * chunks
            to = held[n].at[pl.ds(0, width)] if is_weight else held[n]
            src = in_refs[n]
            if n == 3 * chunks + 1:
                src = src.at[:, pl.ds(width, CODE_LANES)]
            copy = pltpu.make_async_copy(src, to, in_sems.at[n])
            copy.start()
            started.append(copy)
        for c in range(chunks):
            copy = pltpu.make_async_copy(
                e_refs[c], w_held[c].at[pl.ds(width, CODE_LANES)], in_sems.at[n_in + c]
            )
            copy.start()
            started.append(copy)
        links = Links(send_sems, recv_sems)
        place = links.place
        links.greet(steps)
        for copy in started[: 2 * chunks] + started[n_in:]:
            copy.wait()
        came = {}

        def rows_of(key):
            return pl.ds(pl.multiple_of(block_of(key, place) * rows, 16), rows)

        def in_term(key):
            at = rows_of(key)
            out = dot_nt(g_held[0][at, :], w_held[0][:, : gu[0]])
            for c in range(1, chunks):
                out = out + dot_nt(g_held[c][at, :], w_held[c][:, : gu[c]])
            return out

        def down_term(key):
            at = rows_of(key)
            out = 0.0
            for c in range(chunks):
                out = out + dot_nt(h_held[c][at, : mains[c]], w_held[c][:, gu[c] :])
                if tails[c]:
                    out = out + dot_nt(
                        h_held[c][at, mains[c] :], w_held[c][:, mains[c] : mains[c] + tails[c]]
                    )
            return out

        def so_far(w, k, key):
            if key == (0, 0):
                total = out_ref[w * part : (w + 1) * part, :]
            else:
                total = chip[keys.index(key), w * part : (w + 1) * part, :].astype(F32)
            for j in range(k):
                entry = (w, j, flip(key, ways[w][j]))
                links.arrived(came[entry])
                total = total + hop_in[slot[entry]].astype(F32)
            return total

        crossings = []

        def cross(i, value):
            n = len(crossings)
            if n >= 2:
                links.copies[crossings[n - 2]].wait_send()
            core_out[n % 2] = narrow(value)
            crossings.append(links.send(core_out.at[n % 2], core_in.at[i], core_step))
            return crossings[-1]

        for i, key in enumerate(keys):
            crossing = cross(i, in_term((key[0], key[1] ^ 1)))
            mine = in_term(key)
            links.arrived(crossing)
            mine = mine + core_in[i].astype(F32)
            if key == (0, 0):
                out_ref[...] = mine
            else:
                chip[i] = narrow(mine)
                for w, way in enumerate(ways):
                    if has_bit(key, way[0]):
                        at = slice(w * part, (w + 1) * part)
                        entry = (w, 0, key)
                        came[entry] = links.send(
                            chip.at[i, pl.ds(w * part, part)], hop_in.at[slot[entry]], way[0]
                        )
        pl.semaphore_signal(
            free, inc=1, device_id=links.peer(core_step), device_id_type=pl.DeviceIdType.MESH
        )
        pl.semaphore_wait(free, 1)
        for copy in started[2 * chunks : n_in]:
            copy.wait()
        stored = []
        for i, key in enumerate(keys):
            crossing = cross(i, down_term((key[0], key[1] ^ 1)))
            mine = down_term(key)
            links.arrived(crossing)
            if i >= 2:
                stored[i - 2].wait()
            stage[i % 2] = narrow(mine + core_in[i].astype(F32))
            copy = pltpu.make_async_copy(stage.at[i % 2], terms_ref.at[i], out_sems.at[i])
            copy.start()
            stored.append(copy)
            if i == len(keys) // 2 - 1:
                for k in range(1, len(ways[0])):
                    for w in range(len(ways)):
                        for entry in plan:
                            if entry[0] == w and entry[1] == k:
                                hop_out[later_slot[entry]] = narrow(so_far(w, k, entry[2]))
                                came[entry] = links.send(
                                    hop_out.at[later_slot[entry]],
                                    hop_in.at[slot[entry]],
                                    ways[w][k],
                                )
        x_held, gc_held = held[3 * chunks :]
        for c in range(chunks):
            gu_refs[c][...] = dot_tn(x_held[...], g_held[c][...])
            down_refs[c][...] = dot_tn(gc_held[...], h_held[c][...])
        for w in range(len(ways)):
            out_ref[w * part : (w + 1) * part, :] = so_far(w, len(ways[w]), (0, 0))
        for copy in stored[max(0, len(keys) - 2) :]:
            copy.wait()
        for n, copy in enumerate(links.copies):
            links.arrived(n)
            if n not in crossings[:-2]:
                copy.wait_send()

    any_spec = pl.BlockSpec(memory_space=pl.ANY)
    return pl.pallas_call(
        kernel,
        out_shape=[
            jax.ShapeDtypeStruct((rows, aug), F32),
            jax.ShapeDtypeStruct((len(keys), rows, aug), BF16),
        ]
        + [jax.ShapeDtypeStruct((CODE_LANES, g.shape[1]), F32) for g in grads]
        + [jax.ShapeDtypeStruct((CODE_LANES, h.shape[1]), F32) for h in hids],
        in_specs=[any_spec] * (len(operands) + chunks),
        out_specs=[pl.BlockSpec(memory_space=pltpu.VMEM), any_spec]
        + [pl.BlockSpec(memory_space=pltpu.VMEM)] * (2 * chunks),
        scratch_shapes=[pltpu.VMEM(n, o.dtype) for n, o in zip(shapes, operands)]
        + [
            pltpu.VMEM((2, rows, aug), BF16),
            pltpu.VMEM((len(keys), rows, aug), BF16),
            pltpu.VMEM((len(keys) - 1, rows, aug), BF16),
            pltpu.VMEM((max(len(later), 1), part, aug), BF16),
            pltpu.VMEM((len(plan), part, aug), BF16),
            pltpu.VMEM((2, rows, aug), BF16),
            pltpu.SemaphoreType.DMA((count,)),
            pltpu.SemaphoreType.DMA((count,)),
            pltpu.SemaphoreType.DMA((len(operands) + chunks,)),
            pltpu.SemaphoreType.DMA((len(keys),)),
            pltpu.SemaphoreType.REGULAR,
        ],
        compiler_params=pltpu.CompilerParams(
            collective_id=collective_id, has_side_effects=True, vmem_limit_bytes=VMEM_LIMIT
        ),
        cost_estimate=FREE,
        name=name,
    )(*operands, *extras)


def ffn_extras(places, gate_up_out, down_in, mains, tail, tail_wide):
    half = down_in.shape[2] // 2
    chunks = len(mains)
    tails = [0] * (chunks - 1) + [tail_wide]
    wide = [3 * m + w for m, w in zip(mains, tails)]

    def kernel(places_ref, gu_ref, down_ref, *outs):
        for out in outs:
            out[...] = jnp.zeros_like(out)
        lower = places_ref[2] == 0
        for p in range(2):
            which = places_ref[p]

            def half_of(value):
                return jnp.where(lower, value[:, :half], value[:, half:])

            parts = [
                half_of(gu_ref[0, which]) * 2,
                half_of(gu_ref[1, which]) * 2,
                half_of(down_ref[which]),
            ]
            for kind, value in enumerate(parts):
                top = 2 * RANK * p + (RANK if kind == 1 else 0)
                at_rows = slice(top, top + RANK)
                begin = 0
                for c in range(chunks):
                    main = mains[c]
                    at = [0, main + tails[c], 2 * main + tails[c]][kind]
                    outs[c][at_rows, at : at + main] = value[:, begin : begin + main]
                    begin += main
                if tail:
                    at = mains[-1] + kind * tail
                    outs[-1][at_rows, at : at + tail] = value[:, begin:]

    return pl.pallas_call(
        kernel,
        grid_spec=pltpu.PrefetchScalarGridSpec(
            num_scalar_prefetch=1,
            grid=(1,),
            in_specs=[
                pl.BlockSpec(a.shape, lambda i, ids, n=a.ndim: (0,) * n)
                for a in (gate_up_out, down_in)
            ],
            out_specs=[pl.BlockSpec((CODE_LANES, w), lambda i, ids: (0, 0)) for w in wide],
        ),
        out_shape=[jax.ShapeDtypeStruct((CODE_LANES, w), BF16) for w in wide],
        compiler_params=pltpu.CompilerParams(vmem_limit_bytes=VMEM_LIMIT),
        cost_estimate=FREE,
        name="ffn_extras",
    )(places, gate_up_out, down_in)


def chunk_places(mains, tail, tail_wide):
    out = []
    begin = 0
    for c, main in enumerate(mains):
        wide = tail_wide if c == len(mains) - 1 else 0
        for kind, at in enumerate((0, main + wide, 2 * main + wide)):
            out.append((kind, c, at, begin, main))
        begin += main
    if tail:
        for kind in range(3):
            out.append((kind, len(mains) - 1, mains[-1] + kind * tail, begin, tail))
    return out


def prepare(places, tables, shards, sizes, mains, tail, tail_wide):
    heads, head_q, shares, down_wide = sizes
    qa_in, kva_in, qb_in, kvb_in, out_in, gu_in, qa_out, kva_out, qb_out, kvb_out, out_out, down_out = (
        tables
    )
    q_down, kv_down, q_up, gate_up, down_t, cotangent = shards
    width, q_lat, kv_all = qa_in.shape[2], q_down.shape[1], kv_down.shape[1]
    rows = cotangent.shape[0]
    share_rows = q_down.shape[0] // shares
    wide = heads * HEAD_LANES
    half = down_t.shape[1] // 2
    wides = [3 * m for m in mains[:-1]] + [3 * mains[-1] + tail_wide]

    def kernel(places_ref, *refs):
        ins, outs = refs[: len(tables) + len(shards)], refs[len(tables) + len(shards) :]
        qa_i, kva_i, qb_i, kvb_i, out_i, gu_i, qa_o, kva_o, qb_o, kvb_o, out_o, down_o = ins[
            : len(tables)
        ]
        qd, kvd, qu, gu_w, down_w, cot = ins[len(tables) :]
        down_in_o, down_b_o, qb_w, kvb_w, q_aug, kv_aug, out_x, gu_lanes, out_p, down_p, gu_p = outs[:11]
        mine_d, q_pad, g_own = outs[11:14]
        pieces = outs[14:]
        first = places_ref[1] == 0
        for out in (down_b_o, qb_w, kvb_w, q_aug, kv_aug, out_x, gu_lanes, out_p, gu_p, mine_d, q_pad):
            out[...] = jnp.zeros_like(out)
        for out in pieces:
            out[...] = jnp.zeros_like(out)
        down_in_o[:RANK, :] = qa_i[0]
        down_in_o[RANK:, :] = kva_i[0]
        down_b_o[:RANK, :q_lat] = qa_o[0]
        down_b_o[RANK:, q_lat : q_lat + kv_all] = kva_o[0]
        qb_w[:RANK, :] = qb_i[0]
        kvb_w[RANK : 2 * RANK, :] = kvb_i[0]
        out_x[:RANK, :] = out_i[0]
        kv_aug[RANK : 2 * RANK, :] = narrow(kvb_o[0].astype(F32) * ADAPT_SCALE)
        q_out = narrow(qb_o[0].astype(F32) * ADAPT_SCALE)
        q_up_all = qu[...]
        for h in range(heads):
            at = slice(h * HEAD_LANES, h * HEAD_LANES + head_q)
            q_aug[:RANK, at] = q_out[:, h * head_q : (h + 1) * head_q]
            q_pad[:, at] = q_up_all[:, h * head_q : (h + 1) * head_q]
        for n in range(2):
            both = gu_i[n, 0]
            none = jnp.zeros_like(both)
            gu_p[n * RANK : (n + 1) * RANK, :] = both
            gu_lanes[n * RANK : (n + 1) * RANK, :] = jnp.where(first, both, none)
            gu_lanes[(2 + n) * RANK : (3 + n) * RANK, :] = jnp.where(first, none, both)
        out_p[:RANK, :] = out_o[0]
        down_p[...] = down_o[0]
        mine_d[:, :q_lat] = qd[...]
        mine_d[:, q_lat : q_lat + kv_all] = kvd[...]
        grad = narrow(RESIDUAL * cot[...].astype(F32))
        g_own[:, :width] = grad
        codes = dot_nt(grad, jnp.concatenate([down_o[0]] * 8, axis=0)) * ADAPT_SCALE
        lane = lax.broadcasted_iota(jnp.int32, codes.shape, 1)
        begin = jnp.where(first, 0, 2 * RANK)
        g_own[:, width:] = narrow(jnp.where((lane >= begin) & (lane < begin + RANK), codes, 0.0))
        sources = [gu_w[0], gu_w[1], down_w[...]]
        sides = [(v[:, :half], v[:, half:]) for v in sources]
        for kind, c, at, begin, count in chunk_places(mains, tail, tail_wide):
            left = sides[kind][0][:, begin : begin + count]
            right = sides[kind][1][:, begin : begin + count]
            pieces[2 * c][:, at : at + count] = jnp.where(first, left, right)
            pieces[2 * c + 1][:, at : at + count] = jnp.where(first, right, left)

    def picked(table):
        if table.ndim == 4:
            return pl.BlockSpec((2, 1) + table.shape[2:], lambda i, ids: (0, ids[0], 0, 0))
        return pl.BlockSpec((1,) + table.shape[1:], lambda i, ids: (ids[0], 0, 0))

    def shared(shard):
        return pl.BlockSpec((share_rows, shard.shape[1]), lambda i, ids: (ids[2], 0))

    def whole(shape):
        return pl.BlockSpec(shape, lambda i, ids: (0,) * len(shape))

    out_shapes = [
        (2 * RANK, width),
        (2 * RANK, down_wide),
        (CODE_LANES, qb_in.shape[2]),
        (CODE_LANES, kvb_in.shape[2]),
        (CODE_LANES, wide),
        (CODE_LANES, wide),
        (CODE_LANES, out_in.shape[2]),
        (CODE_LANES, width),
        (CODE_LANES, width),
        (RANK, width),
        (CODE_LANES, width),
        (share_rows, down_wide),
        (q_up.shape[0], wide),
        (rows, width + CODE_LANES),
    ]
    for w in wides:
        out_shapes += [(down_t.shape[0], w)] * 2
    return pl.pallas_call(
        kernel,
        grid_spec=pltpu.PrefetchScalarGridSpec(
            num_scalar_prefetch=1,
            grid=(1,),
            in_specs=[picked(a) for a in tables]
            + [shared(q_down), shared(kv_down)]
            + [whole(a.shape) for a in shards[2:]],
            out_specs=[whole(o) for o in out_shapes],
        ),
        out_shape=[jax.ShapeDtypeStruct(o, BF16) for o in out_shapes],
        compiler_params=pltpu.CompilerParams(vmem_limit_bytes=VMEM_LIMIT),
        cost_estimate=FREE,
        name="prepare",
    )(places, *tables, *shards)


def per_device(
    n_dp,
    n_t,
    inputs,
    cotangent,
    document_numbers,
    sequence_adapter_index,
    attention_norm_gain,
    query_latent_gain,
    keyvalue_latent_gain,
    feedforward_norm_gain,
    query_down_matrix,
    keyvalue_down_matrix,
    query_up_matrix,
    keyvalue_up_matrix,
    output_matrix,
    gate_up_matrix,
    down_matrix,
    query_down_adapter_in,
    query_down_adapter_out,
    keyvalue_down_adapter_in,
    keyvalue_down_adapter_out,
    query_up_adapter_in,
    query_up_adapter_out,
    keyvalue_up_adapter_in,
    keyvalue_up_adapter_out,
    output_adapter_in,
    output_adapter_out,
    gate_up_adapter_in,
    gate_up_adapter_out,
    down_adapter_in,
    down_adapter_out,
):
    d = lax.axis_index("dp")
    t = lax.axis_index("tensor")
    pair = n_dp // 4
    low_bits = [b for b in (1, 2, 4, 8, 16) if b < pair]
    high = n_dp // 2
    y_bits = [b for b in (2, 4, 8, 16) if b < n_t]
    zl = lax.rem(d // pair, 2)
    core = lax.rem(t, 2)
    first = zl == 0
    size = {"dp": n_dp, "tensor": n_t}
    rows = inputs.shape[1]
    width = inputs.shape[2]
    length = document_numbers.shape[1]
    q_lat = query_down_matrix.shape[1]
    kv_all = keyvalue_down_matrix.shape[1]
    kv_lat = kv_all - ROTARY_DIM
    heads = keyvalue_up_matrix.shape[1] // HEAD_LANES
    group_count = query_down_adapter_in.shape[0]
    aug = width + CODE_LANES
    half_rows = rows // 2

    def hop(value, step):
        return swap(value, step[0], step[1], size[step[0]])

    outer_first = [("dp", high), ("dp", pair)] + [("dp", b) for b in reversed(low_bits)]
    inner_first = [("dp", b) for b in low_bits] + [("dp", high), ("dp", pair)]
    t_slow = [("tensor", b) for b in reversed(y_bits)]
    t_core = [("tensor", 1)]

    set_own = sequence_adapter_index[0]

    def pick(table, index):
        return lax.dynamic_index_in_dim(table, index, 0, keepdims=False)

    def turned(table):
        return jnp.swapaxes(table, -1, -2)

    hidden = down_matrix.shape[0]
    half = hidden // 2
    tiles = half // 128
    main = tiles * 128
    tail = half - main
    tail_wide = -(-3 * tail // 128) * 128
    first_tiles = (2 * tiles + 2) // 3
    mains = [first_tiles * 128, main - first_tiles * 128]
    chunks = len(mains)
    tails = [0] * (chunks - 1) + [tail_wide]
    gu_wide = [2 * m + w for m, w in zip(mains, tails)]

    head_q = PLAIN_HEAD_DIM + ROTARY_DIM
    down_shard = query_down_matrix.shape[0]
    shares = n_t if down_shard % (16 * n_t) == 0 else 2
    share_rows = down_shard // shares
    down_wide = -(-(q_lat + kv_all) // 128) * 128
    down_pad = down_wide - q_lat - kv_all
    (
        down_in,
        down_b_rows,
        qb_in_wide,
        kvb_in_wide,
        q_aug_rows,
        kv_aug_rows,
        out_extra,
        gu_in_lanes,
        out_out_wide,
        down_out,
        gu_in_wide,
        down_mine,
        q_up_mine,
        g_own,
        *ffn_pieces,
    ) = prepare(
        jnp.stack([set_own, zl, lax.rem(t, shares)]).astype(jnp.int32),
        [
            turned(query_down_adapter_in),
            turned(keyvalue_down_adapter_in),
            turned(query_up_adapter_in),
            turned(keyvalue_up_adapter_in),
            turned(output_adapter_in),
            turned(gate_up_adapter_in),
            query_down_adapter_out,
            keyvalue_down_adapter_out,
            query_up_adapter_out,
            keyvalue_up_adapter_out,
            output_adapter_out,
            down_adapter_out,
        ],
        [
            query_down_matrix,
            keyvalue_down_matrix,
            query_up_matrix,
            gate_up_matrix,
            down_matrix.T,
            cotangent[0],
        ],
        (heads, head_q, shares, down_wide),
        mains,
        tail,
        tail_wide,
    )
    qb_in, kvb_in = qb_in_wide[:RANK], kvb_in_wide[RANK : 2 * RANK]
    out_out, gu_in = out_out_wide[:RANK], gu_in_wide[: 2 * RANK]
    ffn_mine, ffn_other = ffn_pieces[::2], ffn_pieces[1::2]
    ffn_rows_each = gate_up_matrix.shape[1]
    z_count = n_dp // pair
    ffn_wide = [m.shape[1] for m in ffn_mine]

    def ride_one(out, mine, other, begin, size):
        return dict(
            kind="one",
            out=out,
            mine=mine,
            other=other,
            rows=(begin, size),
            count=ffn_rows_each,
            pair=pair,
            high=high,
        )

    def ride_two(out, z, begin=0, size=None):
        return dict(
            kind="two",
            out=out,
            z=z,
            rows=(begin, ffn_rows_each if size is None else size),
            count=ffn_rows_each,
            pair=pair,
            high=high,
            steps=[("dp", b) for b in reversed(low_bits)],
        )

    def own_codes(value):
        lanes = value[:, width:]
        return jnp.where(first, lanes[:, : 2 * RANK], lanes[:, 2 * RANK : 4 * RANK])

    qb_rows, kvb_rows = query_up_matrix.shape[0], keyvalue_up_matrix.shape[0]
    out_rows = output_matrix.shape[1]

    def rows_at(start, step, count):
        return lambda dd, tt: (pl.ds(pl.multiple_of(start + dd * step, 16), count),)

    def group_block(dd, tt):
        return lax.rem(dd // pair, 2) * n_t + tt

    def group_jobs(src, out, ways):
        return [
            dict(
                src=src,
                src_at=pl.ds(at, half_rows),
                out=out,
                out_at=lambda dd, tt, at=at: (
                    pl.ds(pl.multiple_of(group_block(dd, tt) * rows + at, 16), half_rows),
                ),
                steps=steps + t_core,
                group="rows",
            )
            for at, steps in zip((0, half_rows), ways)
        ]

    group_a = t_slow + [("dp", pair)]
    group_b = [("dp", pair)] + t_slow
    pe_at = q_lat + 2 * RANK
    lat_wide = q_lat + CODE_LANES + kv_lat

    def token_jobs(src, out, parts, group=0):
        count = rows // parts
        return [
            dict(
                src=src,
                src_at=pl.ds(n * count, count),
                out=out,
                out_at=lambda dd, tt, n=n: (
                    pl.ds(pl.multiple_of(tt * rows + n * count, 16), count),
                ),
                steps=t_slow + t_core,
                group=group,
            )
            for n in range(parts)
        ]

    def latent_work(refs):
        x_ref, norm_ref, q_norm_ref, kv_norm_ref, in_ref, b_ref, qb_ref, kvb_ref = refs[12:20]
        latent_ref, codes_ref, rows_ref, w_ref, own_ref = refs[20:25]
        x_f = x_ref[...].astype(F32)
        scale = lax.rsqrt(jnp.mean(x_f * x_f, axis=-1, keepdims=True) + NORM_EPS)
        h_rows = narrow(x_f * scale * norm_ref[...])
        rows_ref[...] = h_rows
        codes = narrow(dot_nt(h_rows, in_ref[...]))
        latent = dot_nn(h_rows, w_ref[...]) + ADAPT_SCALE * dot_nn(codes, b_ref[...])
        latent_ref[...] = latent
        codes_ref[...] = codes
        q_part = latent[:, :q_lat]
        kv_part = latent[:, q_lat : q_lat + kv_lat]
        q_scale = lax.rsqrt(jnp.mean(q_part * q_part, axis=-1, keepdims=True) + NORM_EPS)
        kv_scale = lax.rsqrt(jnp.mean(kv_part * kv_part, axis=-1, keepdims=True) + NORM_EPS)
        q_in = narrow(q_part * q_scale * q_norm_ref[...])
        kv_in = narrow(kv_part * kv_scale * kv_norm_ref[...])
        own_ref[:, :q_lat] = q_in
        own_ref[:, q_lat + CODE_LANES :] = kv_in
        code_block = dot_nt(q_in, qb_ref[...]) + dot_nt(kv_in, kvb_ref[...])
        pe_block = pltpu.roll(latent[:, q_lat + kv_lat :], 2 * RANK, 1)
        lane = lax.broadcasted_iota(jnp.int32, code_block.shape, 1)
        own_ref[:, q_lat : q_lat + CODE_LANES] = narrow(
            jnp.where(lane < 2 * RANK, code_block, pe_block)
        )

    down_steps = outer_first + (t_slow if shares == n_t else []) + t_core
    cut_c = ffn_rows_each * 4 // 5 // 16 * 16
    n_start_outs = 9
    w_at, lat_own_at = n_start_outs + 3, n_start_outs + 4
    n_start_sources = 20
    jobs = [
        dict(
            src=0,
            out=w_at,
            out_at=lambda dd, tt: (
                pl.ds(
                    pl.multiple_of(dd * down_shard + lax.rem(tt, shares) * share_rows, 16), share_rows
                ),
            ),
            steps=down_steps,
            group="down",
        ),
        dict(src=1, out=1, out_at=rows_at(0, qb_rows, qb_rows), steps=outer_first, group="up"),
        dict(src=2, out=2, out_at=rows_at(CODE_LANES, kvb_rows, kvb_rows), steps=outer_first, group="up"),
        dict(src=8, out=5, out_at=lambda dd, tt: (dd,), steps=outer_first, group="up"),
        dict(src=3, out=3, out_at=rows_at(0, out_rows, out_rows), steps=outer_first, group="out"),
    ]
    low_steps = [("dp", b) for b in reversed(low_bits)]
    for src, out in ((9, 6), (11, 7)):
        jobs.append(
            dict(
                src=src,
                out=out,
                out_at=rows_at(0, ffn_rows_each, ffn_rows_each),
                steps=low_steps,
                group="own",
            )
        )
    def own_block(dd, tt):
        return (pl.ds(pl.multiple_of(group_block(dd, tt) * rows, 16), rows),)

    jobs.append(dict(src=4, out=4, out_at=own_block, steps=t_slow + t_core, group="rows"))
    jobs.append(
        dict(src=4, out=4, out_at=own_block, steps=[("dp", pair)], group="pair", keep=False)
    )
    jobs += token_jobs(n_start_sources + 4, 8, 2, "latents")
    set_mark = jnp.full((16, 128), sequence_adapter_index[0].astype(F32)).astype(BF16)
    start = (
        remote_gather(
            [
                down_mine,
                q_up_mine,
                keyvalue_up_matrix,
                output_matrix.T,
                g_own,
                q_aug_rows,
                kv_aug_rows,
                out_extra,
                set_mark,
                ffn_mine[0],
                ffn_other[0],
                ffn_mine[1],
                inputs[0],
                attention_norm_gain[None],
                query_latent_gain[None],
                keyvalue_latent_gain[None],
                down_in,
                down_b_rows,
                qb_in_wide,
                kvb_in_wide,
            ],
            jobs,
            [
                (5, 1, lambda dd, tt: (pl.ds(q_lat, CODE_LANES),)),
                (6, 2, lambda dd, tt: (pl.ds(0, CODE_LANES),)),
                (7, 3, lambda dd, tt: (pl.ds(width, CODE_LANES),)),
            ],
            [
                (width, down_wide),
                (q_lat + CODE_LANES, heads * HEAD_LANES),
                (CODE_LANES + kv_lat, heads * HEAD_LANES),
                (aug, heads * VALUE_HEAD_DIM),
                (2 * n_t * rows, aug),
                (n_dp, 16, 128),
                (width, ffn_wide[0]),
                (width, ffn_wide[1]),
                (length, lat_wide),
            ],
            "gather_start",
            1,
            riders=[ride_one(6, 9, 10, 0, cut_c)],
            order=["down", "up", "out", "rows", "down", "up", "down", "own", "out", "pair"]
            + ["down", "up", "out", "ride"]
            + ["down"] * (len(down_steps) - 4)
            + [("all", "down"), "work", "latents"]
            + ["latents"] * len(t_slow)
            + ["rows"],
            near_outs=[
                jax.ShapeDtypeStruct((rows, down_wide), F32),
                jax.ShapeDtypeStruct((rows, 2 * RANK), BF16),
                jax.ShapeDtypeStruct((rows, width), BF16),
            ],
            scratch=[
                jax.ShapeDtypeStruct((width, down_wide), BF16),
                jax.ShapeDtypeStruct((rows, lat_wide), BF16),
            ],
            work=latent_work,
            late=[(n_start_sources + 3, 0)],
        )
    )
    w_down, w_q, w_kv, w_out, g_all, set_marks, w_ffn0, w_ffn1, lat_all = start[:9]
    latent, down_codes_in, attn_rows = start[9:]
    set_all = set_marks[:, 0, 0].astype(jnp.int32)
    set_peer = lax.dynamic_index_in_dim(set_all, jnp.bitwise_xor(d, pair), 0, keepdims=False)
    set_even = jnp.where(first, set_own, set_peer)
    set_odd = jnp.where(first, set_peer, set_own)
    ffn_extra = ffn_extras(
        jnp.stack([set_even, set_odd, zl]).astype(jnp.int32),
        gate_up_adapter_out,
        turned(down_adapter_in),
        mains,
        tail,
        tail_wide,
    )
    cut_a = ffn_rows_each // 48 * 16
    cut_d = ffn_rows_each // 32 * 16

    cos_part, sin_part = rope_tables(document_numbers)
    zeros_l = jnp.zeros((length, PLAIN_HEAD_DIM), F32)
    zeros_r = jnp.zeros((length, HEAD_LANES - 96), F32)
    none_16 = jnp.zeros_like(sin_part)
    rope = jnp.stack(
        [
            jnp.concatenate([zeros_l + 1.0, cos_part, cos_part, zeros_r], axis=1),
            jnp.concatenate([zeros_l, -sin_part, none_16, zeros_r], axis=1),
            jnp.concatenate([zeros_l, none_16, sin_part, zeros_r], axis=1),
        ],
        axis=0,
    )
    lane_ids = jnp.arange(HEAD_LANES, dtype=jnp.int32)[None, :]
    doc_lane = (lane_ids >= DOC_LANE) & (lane_ids < DOC_LANE + DOC_SLOTS)
    is_doc = document_numbers[0][:, None] == lane_ids - DOC_LANE
    doc_q = narrow(jnp.where(doc_lane & is_doc, 1.0, 0.0))
    doc_k = jnp.where(
        doc_lane & ~is_doc, -BIG, jnp.where((lane_ids >= 96) & (lane_ids < 99), 1.0, 0.0)
    )

    pe_rows = lat_all[:, pe_at : pe_at + ROTARY_DIM].astype(F32)
    pe_a, pe_b = pe_rows[:, : ROTARY_DIM // 2], pe_rows[:, ROTARY_DIM // 2 :]
    pe_aug = narrow(
        jnp.concatenate(
            [
                zeros_l,
                pe_a * cos_part - pe_b * sin_part,
                pe_b * cos_part + pe_a * sin_part,
                zeros_r,
            ],
            axis=1,
        )
        + doc_k
    )
    def pair_rows(place, key):
        block = group_block(jnp.bitwise_xor(place["dp"], pair), jnp.bitwise_xor(place["tensor"], key))
        return pl.ds(pl.multiple_of(block * rows, 16), rows)

    q_aug, kv, head_out, w_ffn0, w_ffn1, g_all = attend(
        lat_all,
        w_q,
        w_kv,
        rope,
        pe_aug,
        doc_q,
        q_lat + CODE_LANES,
        q_lat,
        [
            ride_two(0, 1, 0, cut_c),
            ride_two(0, 2, 0, cut_d),
            ride_one(0, 5, 6, cut_c, ffn_rows_each - cut_c),
            ride_one(1, 3, 4, 0, cut_a),
            dict(kind="block", out=2, at=pair_rows, steps=t_slow),
        ],
        [w_ffn0, w_ffn1, g_all],
        [ffn_mine[1], ffn_other[1], ffn_mine[0], ffn_other[0]],
    )
    tensor_keys = [(0, r) for r in reversed(range(0, n_t, 2))]

    def token_rows(key, place):
        at = jnp.bitwise_xor(place["tensor"], key[1]) * rows
        return pl.ds(pl.multiple_of(at, 16), rows)

    def out_term(held, place, key):
        return dot_nt(held[0][token_rows(key, place), :], held[1][...])

    def middle_work(at, total, extra, outs):
        x_ref, out_b_ref, norm_ref, lanes_ref = extra
        middle_ref, codes_ref, own_ref = outs
        codes = narrow(total[:, width : width + RANK])
        mid = x_ref[at, :].astype(F32) + RESIDUAL * (
            total[:, :width] + ADAPT_SCALE * dot_nn(codes, out_b_ref[:RANK, :])
        )
        middle_ref[at, :] = mid
        codes_ref[at, :] = codes
        scale = lax.rsqrt(jnp.mean(mid * mid, axis=-1, keepdims=True) + NORM_EPS)
        normed = narrow(mid * scale * norm_ref[...])
        own_ref[at, :width] = normed
        own_ref[at, width:] = narrow(dot_nt(normed, lanes_ref[...]))

    middle, out_codes, x_own, w_ffn0, w_ffn1, g_all = remote_reduce(
        [head_out, w_out],
        [head_out.shape, w_out.shape],
        out_term,
        tensor_keys,
        [t_slow[::-1]],
        rows,
        aug,
        "reduce_out",
        3,
        riders=[ride_two(0, 2, cut_d, cut_c - cut_d)]
        + [ride_two(0, z, 0, cut_c) for z in range(3, z_count)]
        + [ride_two(0, z, cut_c, ffn_rows_each - cut_c) for z in range(1, z_count)]
        + [
            ride_one(1, 3, 4, cut_a, ffn_rows_each - cut_a),
            dict(
                kind="blocks",
                out=2,
                at=pair_rows,
                keys=list(range(0, n_t, 2)),
                step=t_core[0],
            ),
        ],
        ridden=[w_ffn0, w_ffn1, g_all],
        carried=[ffn_mine[1], ffn_other[1]],
        after=middle_work,
        after_in=[inputs[0], out_out_wide, feedforward_norm_gain[None], gu_in_lanes],
        after_out=[
            jax.ShapeDtypeStruct((rows, width), F32),
            jax.ShapeDtypeStruct((rows, RANK), BF16),
            jax.ShapeDtypeStruct((rows, aug), BF16),
        ],
    )

    def group_block_of(key, place):
        return group_block(
            jnp.bitwise_xor(place["dp"], key[0]), jnp.bitwise_xor(place["tensor"], key[1])
        )

    x_codes, grads, hids, ffn_weights = remote_ffn(
        x_own,
        g_all,
        [w_ffn0, w_ffn1],
        ffn_extra,
        mains,
        tail,
        tail_wide,
        t_slow + [("dp", pair)],
        group_block_of,
        [ride_two(1, z) for z in range(1, z_count)],
        "feed_forward",
        4,
    )
    group_keys = [(p, r) for p in (pair, 0) for r in reversed(range(0, n_t, 2))]
    ffn_in_sum, down_chip, *code_terms = remote_ffn_back(
        grads,
        hids,
        ffn_weights,
        ffn_extra,
        x_codes,
        g_all,
        mains,
        tail_wide,
        group_keys,
        [group_a[::-1], group_b[::-1]],
        group_block_of,
        rows,
        "feed_forward_back",
        5,
    )
    def grad_work(part, refs):
        at = slice(part * half_rows, (part + 1) * half_rows)
        sum_ref, mid_ref, cot_ref, norm_ref, gu_ref, out_ref = refs[0:6]
        middle_ref, codes_ref, aug_ref = refs[n_grad : n_grad + 3]
        lanes = sum_ref[at, width:]
        lanes = jnp.where(zl_of() == 0, lanes, pltpu.roll(lanes, CODE_LANES - 2 * RANK, 1))
        lane = lax.broadcasted_iota(jnp.int32, lanes.shape, 1)
        codes = narrow(jnp.where(lane < 2 * RANK, lanes, 0.0))
        codes_ref[at, :] = codes
        weighted = (sum_ref[at, :width] + dot_nn(codes, gu_ref[...])) * norm_ref[...]
        mid = mid_ref[at, :]
        scale = lax.rsqrt(jnp.mean(mid * mid, axis=-1, keepdims=True) + NORM_EPS)
        inner = jnp.mean(mid * weighted, axis=-1, keepdims=True)
        grad = cot_ref[at, :].astype(F32) + scale * weighted - mid * (scale * scale * scale * inner)
        middle_ref[at, :] = grad
        scaled = narrow(RESIDUAL * grad)
        aug_ref[at, :width] = scaled
        aug_ref[at, width:] = narrow(ADAPT_SCALE * dot_nt(scaled, out_ref[...]))

    def zl_of():
        return lax.rem(lax.axis_index("dp") // pair, 2)

    hidden_shape = (6 * RANK, half)

    def hidden_work(refs):
        gu_refs, down_refs = refs[6 : 6 + chunks], refs[6 + chunks : 6 + 2 * chunks]
        own_ref = refs[n_grad + 6]
        for kind, c, at, begin, count in chunk_places(mains, tail, tail_wide):
            for p in range(2):
                to = slice((3 * p + kind) * RANK, (3 * p + kind + 1) * RANK)
                if kind < 2:
                    top = 2 * RANK * p + kind * RANK
                    value = gu_refs[c][top : top + RANK, at : at + count] * ADAPT_SCALE
                else:
                    here = at - 2 * mains[c] - tails[c] if count == mains[c] else at
                    value = down_refs[c][2 * RANK * p : 2 * RANK * p + RANK, here : here + count]
                own_ref[to, begin : begin + count] = narrow(value)

    def dp_job(src, out):
        return dict(src=src, out=out, out_at=lambda dd, tt: (dd,), steps=outer_first)

    n_grad = 7 + 2 * chunks + (1 if n_t == 4 else 0)

    def heads_work(refs):
        w_ref, heads_ref, lanes_ref, all_ref = refs[6 + 2 * chunks], *refs[n_grad + 3 : n_grad + 6]
        for n in range(2):
            at = slice(n * length // 2, (n + 1) * length // 2)
            heads_ref[at, :] = narrow(dot_nn(all_ref[at, :], w_ref[...]))
        lanes_ref[...] = all_ref[:, width:]

    ride_down = n_t == 4
    n_far = 2 if ride_down else 1
    sent = remote_gather(
        [
            ffn_in_sum,
            middle,
            cotangent[0],
            feedforward_norm_gain[None],
            gu_in_wide,
            out_out_wide,
            *code_terms,
            w_out,
        ]
        + ([down_chip] if ride_down else []),
        token_jobs(n_grad + 2, n_far + 5, 2, "top")[:1]
        + token_jobs(n_grad + 2, n_far + 5, 2, "bottom")[1:]
        + [
            dict(
                src=n_grad + 6,
                out=0,
                out_at=rows_at(0, hidden_shape[0], hidden_shape[0]),
                steps=[("dp", high), ("dp", pair)],
                group="hidden",
            )
        ],
        [],
        [(n_dp * hidden_shape[0], half)] + ([(rows, aug)] if ride_down else []),
        "gather_grad",
        6,
        riders=[dict(kind="plain", src=n_grad - 1, src_at=0, out=1, step=("dp", pair))]
        if ride_down
        else [],
        distant=(n_grad - 1,) if ride_down else (),
        order=[
            hidden_work,
            "hidden",
            functools.partial(grad_work, 0),
            "top",
            "ride",
            functools.partial(grad_work, 1),
            "bottom",
            "hidden",
            "top",
            "bottom",
        ]
        + ["top", "bottom"] * (len(t_slow) - 1)
        + [("all", "top"), ("all", "bottom"), heads_work],
        near_outs=[
            jax.ShapeDtypeStruct((rows, width), F32),
            jax.ShapeDtypeStruct((rows, CODE_LANES), BF16),
            jax.ShapeDtypeStruct((rows, aug), BF16),
            jax.ShapeDtypeStruct((length, w_out.shape[1]), BF16),
            jax.ShapeDtypeStruct((length, CODE_LANES), BF16),
        ],
        scratch=[
            jax.ShapeDtypeStruct((length, aug), BF16),
            jax.ShapeDtypeStruct(hidden_shape, BF16),
        ],
    )
    middle_grad, gu_code_grad, attn_grad_aug, heads_grad, grad_lanes = sent[n_far:]
    gu_code_grad = gu_code_grad[:, : 2 * RANK]
    hidden_terms = sent[0]
    out_a = dot_tn(grad_lanes, head_out)[:RANK]
    hidden_ride = [
        dict(
            kind="two",
            out=0,
            z=z,
            count=hidden_shape[0],
            pair=pair,
            high=high,
            steps=[("dp", b) for b in reversed(low_bits)],
        )
        for z in range(z_count)
    ]
    if ride_down:
        down_far = narrow(down_chip[2].astype(F32) + sent[1].astype(F32))
        dq, dkv, pe_padded, cq, ckv, hidden_terms, came_pair, came_y = attend_back(
            q_aug,
            kv,
            head_out,
            heads_grad,
            rope,
            pe_aug,
            (lat_all, q_lat // CODE_LANES),
            [
                dict(kind="plain", src=1, src_at=1, out=1, step=("dp", pair)),
                dict(kind="plain", src=2, src_at=None, out=2, step=("tensor", 2)),
            ]
            + hidden_ride,
            [hidden_terms],
            [down_chip, down_far],
            [(rows, aug), (rows, aug)],
        )
    else:
        dq, dkv, pe_padded, cq, ckv, hidden_terms = attend_back(
            q_aug, kv, head_out, heads_grad, rope, pe_aug, (lat_all, q_lat // CODE_LANES), hidden_ride, [hidden_terms], [], []
        )
        places = n_t // 2
        ffn_out = down_chip[places:].astype(F32) + hop(down_chip[:places], ("dp", pair)).astype(F32)
        while places > 1:
            places //= 2
            ffn_out = ffn_out[places:] + hop(narrow(ffn_out[:places]), ("tensor", 2 * places)).astype(
                F32
            )
        ffn_out = ffn_out[0]
    def latent_term(held, place, key):
        at = token_rows(key, place)
        from_q = dot_nt(held[0][at, :], held[2][...])
        from_kv = dot_nt(held[1][at, :], held[3][...])
        return jnp.concatenate(
            [
                from_q[:, :q_lat],
                from_q[:, q_lat:] + from_kv[:, :CODE_LANES] + held[4][at, :],
                from_kv[:, CODE_LANES:],
            ],
            axis=1,
        )

    qb_b = ADAPT_SCALE * cq[:RANK]
    kvb_b = ADAPT_SCALE * ckv[RANK : 2 * RANK]
    head_own = narrow(jnp.concatenate([qb_b, kvb_b, out_a], axis=1))
    operands = [dq, dkv, w_q, w_kv, pe_padded]
    small_at, small_wide = [0], []
    for value in (q_lat, kv_all, q_lat, kv_lat):
        small_wide.append(value)
        small_at.append(small_at[-1] + -(-value // 128) * 128)

    def latent_back(at, total, extra, outs):
        latent_ref, q_norm, kv_norm, qb_ref, kvb_ref, b_ref, rows_ref, codes_ref = extra
        grad_ref, code_ref, terms_ref = outs
        block = total[:, q_lat : q_lat + CODE_LANES]
        lane = lax.broadcasted_iota(jnp.int32, block.shape, 1)
        codes = narrow(jnp.where(lane < 2 * RANK, block, 0.0))
        latent_f = latent_ref[...]
        parts = []
        inputs_in = []
        for begin, size, grad, norm_ref, in_ref in (
            (0, q_lat, total[:, :q_lat], q_norm, qb_ref),
            (q_lat, kv_lat, total[:, q_lat + CODE_LANES :], kv_norm, kvb_ref),
        ):
            value = latent_f[:, begin : begin + size]
            scale = lax.rsqrt(jnp.mean(value * value, axis=-1, keepdims=True) + NORM_EPS)
            inputs_in.append(narrow(value * scale * norm_ref[...]))
            weighted = (grad + dot_nn(codes, in_ref[...])) * norm_ref[...]
            inner = jnp.mean(value * weighted, axis=-1, keepdims=True)
            parts.append(scale * weighted - value * (scale * scale * scale * inner))
        grad_ref[:, :q_lat] = narrow(parts[0])
        grad_ref[:, q_lat : q_lat + kv_lat] = narrow(parts[1])
        pe_block = pltpu.roll(block, CODE_LANES - 2 * RANK, 1)
        pe_block = jnp.where(lane < ROTARY_DIM, pe_block, 0.0)
        grad_ref[:, q_lat + kv_lat :] = narrow(pe_block[:, : down_wide - q_lat - kv_lat])
        grad_rows = grad_ref[...]
        code_grad = narrow(ADAPT_SCALE * dot_nt(grad_rows, b_ref[...]))
        code_ref[...] = code_grad
        terms_ref[...] = jnp.zeros_like(terms_ref)
        terms_ref[: 2 * RANK, :] = narrow(dot_tn(code_grad, rows_ref[...]))
        b_terms = ADAPT_SCALE * dot_tn(codes_ref[...], grad_rows)
        qb_a = dot_tn(codes, inputs_in[0])
        kvb_a = dot_tn(codes, inputs_in[1])
        small_values = (
            b_terms[:RANK, :q_lat],
            b_terms[RANK:, q_lat : q_lat + kv_all],
            qb_a[:RANK, :],
            kvb_a[RANK : 2 * RANK, :],
        )
        for value, begin, size in zip(small_values, small_at, small_wide):
            terms_ref[2 * RANK :, begin : begin + size] = narrow(value)

    latent_grad, code_grad, late_terms, head_terms = remote_reduce(
        operands,
        [o.shape for o in operands],
        latent_term,
        tensor_keys,
        [t_slow[::-1]],
        rows,
        lat_wide,
        "reduce_latents",
        7,
        jobs=[dp_job(0, 0)],
        job_sources=[head_own],
        job_outs=[(n_dp,) + head_own.shape],
        after=latent_back,
        after_in=[
            latent,
            query_latent_gain[None],
            keyvalue_latent_gain[None],
            qb_in_wide,
            kvb_in_wide,
            down_b_rows,
            attn_rows,
            down_codes_in,
        ],
        after_out=[
            jax.ShapeDtypeStruct((rows, down_wide), BF16),
            jax.ShapeDtypeStruct((rows, 2 * RANK), BF16),
            jax.ShapeDtypeStruct((3 * RANK, width), BF16),
        ],
    )
    if ride_down:
        ffn_out = (
            down_chip[3].astype(F32)
            + came_pair.astype(F32)
            + came_y.astype(F32)
        )
    down_codes = narrow(own_codes(ffn_out)[:, :RANK])
    outputs = narrow(
        middle + RESIDUAL * (ffn_out[:, :width] + ADAPT_SCALE * dot_nn(down_codes, down_out))
    )
    gu_a = dot_tn(gu_code_grad, x_own)[:, :width]
    out_b = ADAPT_SCALE * dot_tn(out_codes, attn_grad_aug)[:, :width]
    down_b = ADAPT_SCALE * dot_tn(down_codes, g_own)[:, :width]
    table_orders = [outer_first + t_slow + t_core, t_slow + outer_first + t_core]
    shared = jnp.concatenate([narrow(gu_a), narrow(out_b), narrow(down_b), late_terms], axis=0)
    shared = jnp.pad(shared, ((0, -shared.shape[0] % (16 * n_t)), (0, 0)))

    def input_work(refs):
        grad_ref, code_ref, w_ref, in_ref, x_ref, norm_ref, mid_ref, out_ref = refs
        back = dot_nt(grad_ref[...], w_ref[...]) + dot_nn(code_ref[...], in_ref[...])
        value = x_ref[...].astype(F32)
        scale = lax.rsqrt(jnp.mean(value * value, axis=-1, keepdims=True) + NORM_EPS)
        weighted = back * norm_ref[...]
        inner = jnp.mean(value * weighted, axis=-1, keepdims=True)
        out_ref[...] = (
            mid_ref[...] + scale * weighted - value * (scale * scale * scale * inner)
        )

    shared_terms, input_grad = remote_share(
        shared,
        n_dp,
        n_t,
        table_orders,
        "share",
        8,
        [
            latent_grad,
            code_grad,
            w_down,
            down_in,
            inputs[0],
            attention_norm_gain[None],
            middle_grad,
        ],
        [jax.ShapeDtypeStruct((rows, width), F32)],
        input_work,
    )
    part_wide = width // 2

    def add_shared(s, refs, acc):
        for p in range(2):
            at = slice(p * part_wide, (p + 1) * part_wide)
            acc[:, at] += refs[0][p, s].astype(F32)

    def put_shared(acc, outs):
        outs[0][0, 0] = acc[:RANK, :]
        outs[0][1, 0] = acc[RANK : 2 * RANK, :]
        for n in range(4):
            outs[1 + n][0] = acc[(2 + n) * RANK : (3 + n) * RANK, :]
        for n, size in enumerate(small_wide):
            at = small_at[n]
            outs[5 + n][0] = acc[6 * RANK : 7 * RANK, at : at + size]

    shared_sets = set_sums(
        set_all,
        [shared_terms],
        (shared.shape[0], width),
        add_shared,
        [((2,), (RANK, width))]
        + [((), (RANK, width))] * 4
        + [((), (RANK, size)) for size in small_wide],
        put_shared,
        group_count,
        "sum_shared",
    )
    gu_a_t, out_b_grad, down_b_grad, qa_a_t, kva_a_t, qa_b_grad, kva_b_grad, qb_a_t, kvb_a_t = (
        shared_sets
    )
    wide = heads * HEAD_LANES
    head_wide = head_own.shape[1]

    def add_split(s, refs, acc):
        which = (s // pair) % 2
        base = s - which * pair
        for h in range(2):
            acc[: 3 * RANK, h * half : (h + 1) * half] += refs[0][
                base + h * pair, which * 3 * RANK : (which + 1) * 3 * RANK, :
            ].astype(F32)
        acc[3 * RANK :, :head_wide] += refs[1][s].astype(F32)

    def put_split(acc, outs):
        outs[0][0, 0] = acc[:RANK, :hidden]
        outs[0][1, 0] = acc[RANK : 2 * RANK, :hidden]
        outs[1][0] = acc[2 * RANK : 3 * RANK, :hidden]
        for h in range(heads):
            outs[2][0, :, h * head_q : (h + 1) * head_q] = acc[
                3 * RANK :, h * HEAD_LANES : h * HEAD_LANES + head_q
            ]
        outs[3][0] = acc[3 * RANK :, wide : 2 * wide]
        outs[4][0] = acc[3 * RANK :, 2 * wide : head_wide]

    gu_b_grad, down_a_t, qb_b_grad, kvb_b_grad, out_a_t = set_sums(
        set_all,
        [hidden_terms.reshape((n_dp,) + hidden_shape), head_terms],
        (4 * RANK, max(hidden, -(-head_wide // 128) * 128)),
        add_split,
        [
            ((2,), (RANK, hidden)),
            ((), (RANK, hidden)),
            ((), (RANK, heads * head_q)),
            ((), (RANK, wide)),
            ((), (RANK, head_wide - 2 * wide)),
        ],
        put_split,
        group_count,
        "sum_split",
    )
    return (
        outputs[None],
        input_grad[None],
        turned(qa_a_t),
        qa_b_grad,
        turned(kva_a_t),
        kva_b_grad,
        turned(qb_a_t),
        qb_b_grad,
        turned(kvb_a_t),
        kvb_b_grad,
        turned(out_a_t),
        out_b_grad,
        turned(gu_a_t),
        gu_b_grad,
        turned(down_a_t),
        down_b_grad,
    )


def solution(mesh):
    return jax.shard_map(
        functools.partial(per_device, mesh.shape["dp"], mesh.shape["tensor"]),
        mesh=mesh,
        in_specs=(
            P("dp", "tensor", None),
            P("dp", "tensor", None),
            P("dp", None),
            P("dp"),
            P(),
            P(),
            P(),
            P(),
            P("dp", None),
            P("dp", None),
            P("dp", "tensor"),
            P("dp", "tensor"),
            P("tensor", "dp"),
            P(None, "dp", "tensor"),
            P("tensor", "dp"),
            P(),
            P(),
            P(),
            P(),
            P(),
            P(None, None, "tensor"),
            P(),
            P(None, None, "tensor"),
            P(None, "tensor", None),
            P(),
            P(),
            P(None, None, None, "tensor"),
            P(None, "tensor", None),
            P(),
        ),
        out_specs=(
            P("dp", "tensor", None),
            P("dp", "tensor", None),
            P(),
            P(),
            P(),
            P(),
            P(),
            P(None, None, "tensor"),
            P(),
            P(None, None, "tensor"),
            P(None, "tensor", None),
            P(),
            P(),
            P(None, None, None, "tensor"),
            P(None, "tensor", None),
            P(),
        ),
        check_vma=False,
    )
```

```python
import functools
import math

import jax
import jax.numpy as jnp
from jax import lax
from jax.experimental import pallas as pl
from jax.experimental.pallas import tpu as pltpu
from jax.sharding import PartitionSpec as P

PLAIN_HEAD_DIM = 64
ROTARY_DIM = 32
VALUE_HEAD_DIM = 64
HEAD_LANES = 128
CODE_LANES = 128
RANK = 16
BLOCK_Q = 256
DOC_LANE = 99
DOC_SLOTS = 24

NORM_EPS = 1e-05
RESIDUAL = 1.4 / math.sqrt(62.0)
ADAPT_SCALE = 2.0
SCORE_SCALE = 1.0 / math.sqrt(PLAIN_HEAD_DIM + ROTARY_DIM)
EXP2_SCALE = SCORE_SCALE * math.log2(math.e)
BIG = 1e30
VMEM_LIMIT = 60 * 1024 * 1024
FREE = pl.CostEstimate(flops=0, bytes_accessed=0, transcendentals=0)
F32 = jnp.float32
BF16 = jnp.bfloat16


def narrow(value):
    return value.astype(BF16)


def dot_nn(a, b):
    return lax.dot_general(a, b, (((1,), (0,)), ((), ())), preferred_element_type=F32)


def dot_nt(a, b):
    return lax.dot_general(a, b, (((1,), (1,)), ((), ())), preferred_element_type=F32)


def dot_tn(a, b):
    return lax.dot_general(a, b, (((0,), (0,)), ((), ())), preferred_element_type=F32)


def normalize(value, gain_vec):
    scale_inv = lax.rsqrt(jnp.mean(value * value, axis=-1, keepdims=True) + NORM_EPS)
    return (value * scale_inv * gain_vec, scale_inv)


def normalize_back(value, scale_inv, gain_vec, grad_in):
    weighted = grad_in * gain_vec
    return scale_inv * weighted - value * scale_inv**3 * jnp.mean(
        value * weighted, axis=-1, keepdims=True
    )


def rope_tables(segments):
    places = jnp.arange(segments.shape[-1], dtype=jnp.int32)
    begins = jnp.concatenate(
        [jnp.ones_like(segments[:, :1]), (segments[:, 1:] != segments[:, :-1]).astype(jnp.int32)],
        axis=1,
    )
    first_place = lax.cummax(places[None, :] * begins, axis=1)
    offsets = (places[None, :] - first_place).astype(F32)
    inv_freq = 10000.0 ** (-2.0 * jnp.arange(ROTARY_DIM // 2, dtype=F32) / ROTARY_DIM)
    angles = offsets[..., None] * inv_freq
    return (jnp.cos(angles)[0], jnp.sin(angles)[0])


def swap(value, axis, bit, size):
    return lax.ppermute(value, axis, [(i, i ^ bit) for i in range(size)])


class Links:
    def __init__(self, send_sems, recv_sems):
        self.send_sems, self.recv_sems = send_sems, recv_sems
        self.place = {"dp": lax.axis_index("dp"), "tensor": lax.axis_index("tensor")}
        self.copies = []
        self.waited = set()

    def peer(self, step):
        place = dict(self.place)
        place[step[0]] = jnp.bitwise_xor(place[step[0]], step[1])
        return (place["dp"], place["tensor"])

    def greet(self, steps):
        barrier = pltpu.get_barrier_semaphore()
        for step in steps:
            pl.semaphore_signal(
                barrier, inc=1, device_id=self.peer(step), device_id_type=pl.DeviceIdType.MESH
            )
        pl.semaphore_wait(barrier, len(steps))

    def prepare(self, src, dst, step):
        n = len(self.copies)
        copy = pltpu.make_async_remote_copy(
            src_ref=src,
            dst_ref=dst,
            send_sem=self.send_sems.at[n],
            recv_sem=self.recv_sems.at[n],
            device_id=self.peer(step),
            device_id_type=pl.DeviceIdType.MESH,
        )
        self.copies.append(copy)
        return n

    def send(self, src, dst, step):
        n = self.prepare(src, dst, step)
        self.copies[n].start()
        return n

    def arrived(self, n):
        if n not in self.waited:
            self.copies[n].wait_recv()
            self.waited.add(n)

    def close(self):
        for n, copy in enumerate(self.copies):
            self.arrived(n)
            copy.wait_send()


class Riders:
    def __init__(self, links, riders, in_refs, out_refs):
        self.links = links
        self.rounds = []
        d = links.place["dp"]
        for rider in riders:
            full = out_refs[rider["out"]]
            if rider["kind"] == "plain":
                src = in_refs[rider["src"]]
                if rider["src_at"] is not None:
                    src = src.at[rider["src_at"]]
                self.add(0, src, full, rider["step"])
                continue
            if rider["kind"] == "block":
                held = [0]
                for k, step in enumerate(rider["steps"]):
                    for key in list(held):
                        here = full.at[rider["at"](links.place, key)]
                        self.add(k, here, here, step)
                        held.append(key ^ step[1])
                continue
            if rider["kind"] == "blocks":
                for key in rider["keys"]:
                    here = full.at[rider["at"](links.place, key)]
                    self.add(0, here, here, rider["step"])
                continue
            count, pair, high = rider["count"], rider["pair"], rider["high"]
            if rider["kind"] == "one":
                begin, size = rider["rows"]
                here = full.at[pl.ds(pl.multiple_of(d * count + begin, 16), size)]
                for name, bit in (("other", pair), ("mine", high), ("other", high ^ pair)):
                    src = in_refs[rider[name]].at[pl.ds(begin, size)]
                    self.add(0, src, here, ("dp", bit))
            else:
                held = [0]
                for k, step in enumerate(rider["steps"]):
                    for key in list(held):
                        place = jnp.bitwise_xor(d, rider["z"] * pair + key)
                        begin, size = rider.get("rows", (0, count))
                        at = pl.multiple_of(place * count + begin, 16)
                        here = full.at[pl.ds(at, size)]
                        self.add(k, here, here, step)
                        held.append(key ^ step[1])

    def add(self, k, src, dst, step):
        while len(self.rounds) <= k:
            self.rounds.append([])
        self.rounds[k].append(self.links.prepare(src, dst, step))

    def start(self):
        if self.rounds:
            for n in self.rounds[0]:
                self.links.copies[n].start()

    def finish(self):
        for k, numbers in enumerate(self.rounds):
            if k:
                for n in numbers:
                    self.links.copies[n].start()
            for n in numbers:
                self.links.arrived(n)


def rider_steps(riders):
    steps = []
    for rider in riders:
        if rider["kind"] in ("plain", "blocks"):
            steps.append(rider["step"])
        elif rider["kind"] == "one":
            pair, high = rider["pair"], rider["high"]
            steps += [("dp", pair), ("dp", high), ("dp", high ^ pair)]
        else:
            steps += rider["steps"]
    return steps


def rider_count(riders):
    total = 0
    for rider in riders:
        if rider["kind"] == "plain":
            total += 1
        elif rider["kind"] == "blocks":
            total += len(rider["keys"])
        elif rider["kind"] == "one":
            total += 3
        else:
            total += (1 << len(rider["steps"])) - 1
    return total


def distinct(steps):
    out = []
    for step in steps:
        if step not in out:
            out.append(step)
    return out


def flip(key, step):
    return (key[0] ^ step[1], key[1]) if step[0] == "dp" else (key[0], key[1] ^ step[1])


def has_bit(key, step):
    return bool((key[0] if step[0] == "dp" else key[1]) & step[1])


def gather_count(jobs):
    return sum((1 << len(job["steps"])) - 1 for job in jobs)


def gather_rounds(links, src_refs, out_refs, jobs):
    d, t = links.place["dp"], links.place["tensor"]

    def landing(job, key):
        at = job["out_at"](jnp.bitwise_xor(d, key[0]), jnp.bitwise_xor(t, key[1]))
        return out_refs[job["out"]].at[at]

    state = []
    for job in jobs:
        src = src_refs[job["src"]]
        if job.get("src_at") is not None:
            src = src.at[job["src_at"]]
        state.append({(0, 0): (src, None)})
    for k in range(max(len(job["steps"]) for job in jobs)):
        for job, held in zip(jobs, state):
            if k >= len(job["steps"]):
                continue
            step = job["steps"][k]
            for key in list(held):
                src, came = held[key]
                if came is not None:
                    links.arrived(came)
                n = links.send(src, landing(job, key), step)
                new = flip(key, step)
                held[new] = (landing(job, new), n)
        yield k


def remote_gather(
    sources,
    jobs,
    extra,
    outs,
    name,
    collective_id,
    riders=(),
    aliases=(),
    distant=(),
    order=(),
    near_outs=(),
    scratch=(),
    work=None,
    late=(),
):
    steps = distinct([s for job in jobs for s in job["steps"]] + rider_steps(riders))
    count = gather_count(jobs) + rider_count(riders)
    aliases = dict(aliases)
    n_src, n_out, n_near = len(sources), len(outs), len(near_outs)

    def kernel(*refs):
        src_refs, refs = refs[:n_src], refs[n_src:]
        out_refs, refs = refs[:n_out], refs[n_out:]
        near, refs = refs[: n_near + len(scratch)], refs[n_near + len(scratch) :]
        send_sems, recv_sems, local_sems = refs
        all_src, all_out = list(src_refs) + list(near), list(out_refs) + list(near)
        links = Links(send_sems, recv_sems)
        d, t = links.place["dp"], links.place["tensor"]
        links.greet(steps)
        ride = Riders(links, riders, src_refs, out_refs)
        local = []

        def keep(src, where):
            copy = pltpu.make_async_copy(src, where, local_sems.at[len(local)])
            copy.start()
            local.append(copy)
            return copy

        for src, out, at in extra:
            keep(all_src[src], all_out[out].at[at(d, t)])
        groups = {}
        for job in jobs:
            groups.setdefault(job.get("group", 0), []).append(job)
        turns = {}
        sent = {g: [] for g in groups}
        kept = {g: [] for g in groups}

        def advance(group):
            before = len(links.copies)
            if group not in turns:
                turns[group] = gather_rounds(links, all_src, all_out, groups[group])
                for job in groups[group]:
                    if not job.get("keep", True):
                        continue
                    src = all_src[job["src"]]
                    if job.get("src_at") is not None:
                        src = src.at[job["src_at"]]
                    kept[group].append(keep(src, all_out[job["out"]].at[job["out_at"](d, t)]))
            going = next(turns[group], None) is not None
            sent[group] += range(before, len(links.copies))
            return going

        waited = set()
        if "ride" not in order:
            ride.start()
        for turn in order:
            if turn == "ride":
                ride.start()
            elif callable(turn):
                turn(all_src)
            elif turn == "work":
                work(all_src)
                for src, out in late:
                    keep(all_src[src], all_out[out])
            elif isinstance(turn, tuple):
                for n in sent[turn[1]]:
                    links.arrived(n)
                for copy in kept[turn[1]]:
                    copy.wait()
                waited.add(turn[1])
            else:
                advance(turn)
        for group in groups:
            while advance(group):
                pass
        ride.finish()
        links.close()
        done = [copy for group in waited for copy in kept[group]]
        for copy in local:
            if not any(copy is other for other in done):
                copy.wait()

    vmem = pl.BlockSpec(memory_space=pltpu.VMEM)
    far = pl.BlockSpec(memory_space=pl.ANY)
    return pl.pallas_call(
        kernel,
        out_shape=[jax.ShapeDtypeStruct(o, BF16) for o in outs] + list(near_outs),
        in_specs=[far if n in aliases or n in distant else vmem for n in range(n_src)],
        out_specs=[far] * n_out + [vmem] * n_near,
        scratch_shapes=[pltpu.VMEM(o.shape, o.dtype) for o in scratch]
        + [
            pltpu.SemaphoreType.DMA((count,)),
            pltpu.SemaphoreType.DMA((count,)),
            pltpu.SemaphoreType.DMA((len(jobs) + len(extra) + len(late),)),
        ],
        input_output_aliases=aliases,
        compiler_params=pltpu.CompilerParams(
            collective_id=collective_id, has_side_effects=True, vmem_limit_bytes=VMEM_LIMIT
        ),
        cost_estimate=FREE,
        name=name,
    )(*sources)


def reduce_plan(keys, ways):
    plan = []
    for w, steps in enumerate(ways):
        live = list(keys)
        for k, step in enumerate(steps):
            plan += [(w, k, key) for key in live if has_bit(key, step)]
            live = [key for key in live if not has_bit(key, step)]
    return plan


def remote_reduce(
    operands, fetched, term, keys, ways, rows, wide, name, collective_id, riders=(), ridden=(), carried=(), jobs=(), job_sources=(), job_outs=(), after=None, after_in=(), after_out=()
):
    core_step = ("tensor", 1)
    part = rows // len(ways)
    plan = reduce_plan(keys, ways)
    slot = {entry: n for n, entry in enumerate(plan)}
    steps = distinct(
        [core_step]
        + [s for s in ways[0]]
        + rider_steps(riders)
        + [s for job in jobs for s in job["steps"]]
    )
    count = len(keys) + len(plan) + rider_count(riders) + gather_count(jobs)
    n_in = len(operands)
    n_ride = n_in + len(ridden) + len(carried)
    n_all = n_ride + len(job_sources)
    n_jobs = len(job_outs)
    after_out = list(after_out) or [jax.ShapeDtypeStruct((rows, wide), F32)]
    n_own = len(after_out)

    def kernel(*refs):
        in_refs = refs[:n_in]
        own_out = refs[n_all + len(after_in) : n_all + len(after_in) + n_own]
        extra_in = refs[n_all : n_all + len(after_in)]
        refs = refs[:n_all] + refs[n_all + len(after_in) + n_own - 1 :]
        ride_in = refs[n_in:n_ride]
        job_in = refs[n_ride:n_all]
        ride_out = refs[n_all + 1 : n_all + 1 + len(ridden)]
        job_out = refs[n_all + 1 + len(ridden) : n_all + 1 + len(ridden) + n_jobs]
        scratch = refs[n_all + 1 + len(ridden) + n_jobs :]
        held = scratch[:n_in]
        core_out, core_in, chip, hop_out, hop_in, send_sems, recv_sems, in_sems, job_sems = scratch[
            n_in:
        ]
        started = []
        for n in range(n_in):
            shape = fetched[n]
            src = in_refs[n].at[tuple(pl.ds(0, s) for s in shape)]
            copy = pltpu.make_async_copy(src, held[n], in_sems.at[n])
            copy.start()
            started.append(copy)
        links = Links(send_sems, recv_sems)
        links.greet(steps)
        ride = Riders(links, riders, ride_in, ride_out)
        ride.start()
        rounds = gather_rounds(links, job_in, job_out, jobs) if jobs else iter(())
        next(rounds, None)
        placed = []
        for n, job in enumerate(jobs):
            at = job["out_at"](links.place["dp"], links.place["tensor"])
            copy = pltpu.make_async_copy(
                job_in[job["src"]], job_out[job["out"]].at[at], job_sems.at[n]
            )
            copy.start()
            placed.append(copy)
        for copy in started:
            copy.wait()
        came = {}

        def send_part(w, k, key):
            entry = (w, k, key)
            came[entry] = links.send(hop_out.at[slot[entry]], hop_in.at[slot[entry]], ways[w][k])

        def so_far(w, k, key):
            total = chip[keys.index(key), w * part : (w + 1) * part, :]
            for j in range(k):
                entry = (w, j, flip(key, ways[w][j]))
                links.arrived(came[entry])
                total = total + hop_in[slot[entry]].astype(F32)
            return total

        for i, key in enumerate(keys):
            core_out[i] = narrow(term(held, links.place, (key[0], key[1] ^ 1)))
            crossing = links.send(core_out.at[i], core_in.at[i], core_step)
            mine = term(held, links.place, key)
            links.arrived(crossing)
            chip[i] = mine + core_in[i].astype(F32)
            for w, way in enumerate(ways):
                if way and has_bit(key, way[0]):
                    hop_out[slot[(w, 0, key)]] = narrow(chip[i, w * part : (w + 1) * part, :])
                    send_part(w, 0, key)
            next(rounds, None)
        for k in range(1, len(ways[0])):
            for w in range(len(ways)):
                for entry in plan:
                    if entry[0] == w and entry[1] == k:
                        hop_out[slot[entry]] = narrow(so_far(w, k, entry[2]))
                        send_part(w, k, entry[2])
        for w in range(len(ways)):
            total = so_far(w, len(ways[w]), (0, 0))
            if after is None:
                own_out[0][w * part : (w + 1) * part, :] = total
            else:
                after(slice(w * part, (w + 1) * part), total, extra_in, own_out)
        for _ in rounds:
            pass
        ride.finish()
        links.close()
        for copy in placed:
            copy.wait()

    any_spec = pl.BlockSpec(memory_space=pl.ANY)
    return pl.pallas_call(
        kernel,
        out_shape=after_out
        + [jax.ShapeDtypeStruct(r.shape, r.dtype) for r in ridden]
        + [jax.ShapeDtypeStruct(o, BF16) for o in job_outs],
        in_specs=[any_spec] * n_ride
        + [pl.BlockSpec(memory_space=pltpu.VMEM)] * (len(job_sources) + len(after_in)),
        out_specs=[pl.BlockSpec(memory_space=pltpu.VMEM)] * n_own
        + [any_spec] * (len(ridden) + n_jobs),
        input_output_aliases={n_in + n: n_own + n for n in range(len(ridden))},
        scratch_shapes=[pltpu.VMEM(s, o.dtype) for s, o in zip(fetched, operands)]
        + [
            pltpu.VMEM((len(keys), rows, wide), BF16),
            pltpu.VMEM((len(keys), rows, wide), BF16),
            pltpu.VMEM((len(keys), rows, wide), F32),
            pltpu.VMEM((max(len(plan), 1), part, wide), BF16),
            pltpu.VMEM((max(len(plan), 1), part, wide), BF16),
            pltpu.SemaphoreType.DMA((count,)),
            pltpu.SemaphoreType.DMA((count,)),
            pltpu.SemaphoreType.DMA((n_in,)),
            pltpu.SemaphoreType.DMA((max(len(jobs), 1),)),
        ],
        compiler_params=pltpu.CompilerParams(
            collective_id=collective_id, has_side_effects=True, vmem_limit_bytes=VMEM_LIMIT
        ),
        cost_estimate=FREE,
        name=name,
    )(*operands, *ridden, *carried, *job_sources, *after_in)


class Share:
    def __init__(self, links, n_t, orders, source, out, own, sums, came, went, terms, fetch_sem):
        self.links, self.terms, self.own = links, terms, own
        self.fetch = pltpu.make_async_copy(source, terms, fetch_sem.at[0])
        self.sums, self.came, self.went = sums, came, went
        self.count = terms.shape[0] // n_t
        self.wide = terms.shape[1] // len(orders)
        count = self.count
        t_steps = [("tensor", 1 << b) for b in range(n_t.bit_length() - 1)]
        self.rounds = []
        live, slot = list(range(n_t)), 0
        before = []
        for k, step in enumerate(t_steps):
            sent = []
            for r in live:
                if r & step[1]:
                    src = terms.at[self.block(r)] if k == 0 else went.at[slot]
                    sent.append((r, slot, links.prepare(src, came.at[slot], step)))
                    slot += 1
            live = [r for r in live if not r & step[1]]
            self.rounds.append(functools.partial(self.scatter, k, list(live), before, sent, step))
            before = [(r ^ step[1], at, n) for r, at, n in sent]
        d, t = links.place["dp"], links.place["tensor"]

        def landing(p, key):
            rows = pl.ds(pl.multiple_of(jnp.bitwise_xor(t, key[1]) * count, 16), count)
            return out.at[p, jnp.bitwise_xor(d, key[0]), rows]

        self.places = [landing(p, (0, 0)) for p in range(len(orders))]
        held = [{(0, 0): (own.at[p], None)} for p in range(len(orders))]
        seen = set()
        for k in range(len(orders[0])):
            work = []
            for p, order in enumerate(orders):
                step = order[k]
                for key in list(held[p]):
                    src, needs = held[p][key]
                    n = links.prepare(src, landing(p, key), step)
                    work.append((None if needs in seen else needs, n))
                    seen.add(needs)
                    new = flip(key, step)
                    held[p][new] = (landing(p, new), n)
            self.rounds.append(functools.partial(self.gather, k, before, work))

    def block(self, r):
        at = jnp.bitwise_xor(self.links.place["tensor"], r) * self.count
        return pl.ds(pl.multiple_of(at, 16), self.count)

    def scatter(self, k, live, before, sent, step):
        if k == 0:
            self.fetch.start()
            self.fetch.wait()
            for r in live:
                self.sums[r] = self.terms[self.block(r), :].astype(F32)
        self.add(before)
        for r, at, n in sent:
            if k:
                self.went[at] = narrow(self.sums[r])
            self.links.copies[n].start()

    def add(self, before):
        for r, at, n in before:
            self.links.arrived(n)
            self.sums[r] = self.sums[r] + self.came[at].astype(F32)

    def gather(self, k, before, work):
        if k == 0:
            self.add(before)
            for p in range(self.own.shape[0]):
                self.own[p] = narrow(self.sums[0, :, p * self.wide : (p + 1) * self.wide])
        for needs, n in work:
            if needs is not None:
                self.links.copies[needs].wait_recv()
                self.links.waited.add(needs)
            self.links.copies[n].start()

    def keep(self, sems):
        return [
            pltpu.make_async_copy(self.own.at[p], where, sems.at[p])
            for p, where in enumerate(self.places)
        ]


def share_shapes(shape, n_t, orders):
    count, parts = shape[0] // n_t, len(orders)
    copies = n_t - 1 + parts * ((1 << len(orders[0])) - 1)
    scratch = [
        pltpu.VMEM((parts, count, shape[1] // parts), BF16),
        pltpu.VMEM((n_t, count, shape[1]), F32),
        pltpu.VMEM((n_t - 1, count, shape[1]), BF16),
        pltpu.VMEM((n_t - 1, count, shape[1]), BF16),
        pltpu.VMEM(shape, BF16),
        pltpu.SemaphoreType.DMA((1,)),
        pltpu.SemaphoreType.DMA((parts,)),
    ]
    return scratch, copies


def remote_share(terms, n_dp, n_t, orders, name, collective_id, work_in, work_out, work):
    scratch, copies = share_shapes(terms.shape, n_t, orders)
    parts = len(orders)

    n_in, n_work = len(work_in), len(work_out)

    def kernel(source, *refs):
        work_refs = refs[:n_in] + refs[n_in + 1 : n_in + 1 + n_work]
        out_ref = refs[n_in]
        refs = refs[n_in + 1 + n_work :]
        held, refs = refs[:n_in], refs[n_in:]
        own_sems, send_sems, recv_sems, in_sems = refs[-4:]
        fetched = [
            pltpu.make_async_copy(work_refs[n], held[n], in_sems.at[n]) for n in range(n_in)
        ]
        for copy in fetched:
            copy.start()
        links = Links(send_sems, recv_sems)
        links.greet(orders[0])
        share = Share(links, n_t, orders, source, out_ref, *refs[:-4])
        for k, one in enumerate(share.rounds):
            one()
            if k == len(share.rounds) - 2:
                for copy in fetched:
                    copy.wait()
                work(list(held) + list(work_refs[n_in:]))
        kept = share.keep(own_sems)
        for copy in kept:
            copy.start()
        links.close()
        for copy in kept:
            copy.wait()

    return pl.pallas_call(
        kernel,
        out_shape=[
            jax.ShapeDtypeStruct((parts, n_dp, terms.shape[0], terms.shape[1] // parts), BF16)
        ]
        + list(work_out),
        in_specs=[pl.BlockSpec(memory_space=pl.ANY)]
        + [pl.BlockSpec(memory_space=pl.ANY)] * n_in,
        out_specs=[pl.BlockSpec(memory_space=pl.ANY)]
        + [pl.BlockSpec(memory_space=pltpu.VMEM)] * n_work,
        scratch_shapes=[pltpu.VMEM(a.shape, a.dtype) for a in work_in]
        + scratch
        + [
            pltpu.SemaphoreType.DMA((copies,)),
            pltpu.SemaphoreType.DMA((copies,)),
            pltpu.SemaphoreType.DMA((n_in,)),
        ],
        compiler_params=pltpu.CompilerParams(
            collective_id=collective_id, has_side_effects=True, vmem_limit_bytes=VMEM_LIMIT
        ),
        cost_estimate=FREE,
        name=name,
    )(terms, *work_in)


def set_sums(set_ids, sources, acc_shape, add, outs, put, groups, name):
    n_src = len(sources)
    count = set_ids.shape[0]

    def kernel(ids_ref, *refs):
        src_refs, out_refs, acc = refs[:n_src], refs[n_src:-1], refs[-1]
        k = pl.program_id(0)
        acc[...] = jnp.zeros_like(acc)
        for s in range(count):

            @pl.when(ids_ref[s] == k)
            def _(s=s):
                add(s, src_refs, acc)

        put(acc, out_refs)

    out_specs = []
    for before, after in outs:
        lead = len(before)
        block = tuple(before) + (1,) + tuple(after)
        out_specs.append(
            pl.BlockSpec(
                block, lambda k, ids, lead=lead, n=len(after): (0,) * lead + (k,) + (0,) * n
            )
        )
    return pl.pallas_call(
        kernel,
        grid_spec=pltpu.PrefetchScalarGridSpec(
            num_scalar_prefetch=1,
            grid=(groups,),
            in_specs=[
                pl.BlockSpec(a.shape, lambda k, ids, n=a.ndim: (0,) * n) for a in sources
            ],
            out_specs=out_specs,
            scratch_shapes=[pltpu.VMEM(acc_shape, F32)],
        ),
        out_shape=[
            jax.ShapeDtypeStruct(tuple(before) + (groups,) + tuple(after), F32)
            for before, after in outs
        ],
        compiler_params=pltpu.CompilerParams(vmem_limit_bytes=VMEM_LIMIT),
        cost_estimate=FREE,
        name=name,
    )(set_ids, *sources)


def split_three(value):
    high = narrow(value).astype(F32)
    middle = narrow(value - high).astype(F32)
    return high, middle, value - high - middle


def rope_mix(value, cos_l, sin_a, sin_b):
    return (
        value * cos_l
        + pltpu.roll(value, HEAD_LANES - ROTARY_DIM // 2, 1) * sin_a
        + pltpu.roll(value, ROTARY_DIM // 2, 1) * sin_b
    )


def attn_fwd_kernel(
    per_step, q_width, kv_at, xl_ref, wq_ref, wkv_ref, rope_ref, pe_ref, doc_ref, qa_ref, kv_ref, o_ref
):
    length = xl_ref.shape[0]
    lane = lax.broadcasted_iota(jnp.int32, (length, HEAD_LANES), 1)
    q_all = dot_nn(xl_ref[:, :q_width], wq_ref[...])
    kv_all = dot_nn(xl_ref[:, kv_at:], wkv_ref[...])
    kv_ref[...] = narrow(kv_all)
    doc_q = doc_ref[...].astype(F32)
    q_heads, k_heads, kv_turned = [], [], []
    for i in range(per_step):
        span = slice(i * HEAD_LANES, (i + 1) * HEAD_LANES)
        q_one = rope_mix(q_all[:, span], rope_ref[0], rope_ref[1], rope_ref[2]) + doc_q
        q_heads.append(narrow(q_one))
        kv_one = kv_all[:, span]
        k_heads.append(jnp.where(lane < PLAIN_HEAD_DIM, narrow(kv_one), pe_ref[...]))
        kv_turned.append(narrow(kv_one.T))
    key_at = lax.broadcasted_iota(jnp.int32, (BLOCK_Q, BLOCK_Q), 0)
    query_at = lax.broadcasted_iota(jnp.int32, (BLOCK_Q, BLOCK_Q), 1)
    row = lax.broadcasted_iota(jnp.int32, (HEAD_LANES, BLOCK_Q), 0)
    block_lane = lax.broadcasted_iota(jnp.int32, (BLOCK_Q, HEAD_LANES), 1)
    for j in range(length // BLOCK_Q):
        begin, end = j * BLOCK_Q, (j + 1) * BLOCK_Q
        mixed = []
        for i in range(per_step):
            q_part = q_heads[i][begin:end]
            scores = dot_nt(k_heads[i][:end], q_part)
            diag = jnp.where(key_at <= query_at, scores[begin:], -BIG)
            scores = diag if j == 0 else jnp.concatenate([scores[:begin], diag], axis=0)
            top = jnp.max(scores, axis=0, keepdims=True)
            terms = jnp.exp2((scores - top) * EXP2_SCALE)
            total = jnp.sum(terms, axis=0, keepdims=True)
            out_t = dot_nn(kv_turned[i][:, :end], narrow(terms)) * (1.0 / total)
            high, middle, low = split_three(top + jnp.log2(total) * (1.0 / EXP2_SCALE))
            out_t = jnp.where(
                row == 0, -high, jnp.where(row == 1, -middle, jnp.where(row == 2, -low, out_t))
            )
            out_n = out_t.T
            mixed.append(out_n)
            is_lse = (block_lane >= 96) & (block_lane < 99)
            q_saved = jnp.where(is_lse, narrow(pltpu.roll(out_n, 96, 1)), q_part)
            qa_ref[begin:end, i * HEAD_LANES : (i + 1) * HEAD_LANES] = q_saved
        if per_step == 2:
            both = jnp.where(block_lane < 64, pltpu.roll(mixed[0], 64, 1), mixed[1])
            o_ref[begin:end, :] = narrow(both)
        else:
            even = lax.rem(pl.program_id(0), 2) == 0
            moved = jnp.where(even, pltpu.roll(mixed[0], 64, 1), mixed[0])
            mine = (block_lane < 64) == even
            o_ref[begin:end, :] = jnp.where(mine, narrow(moved), o_ref[begin:end, :])


def attn_bwd_kernel(
    per_step,
    qa_ref,
    kv_ref,
    o_ref,
    do_ref,
    rope_ref,
    pe_ref,
    codes_ref,
    dq_ref,
    dkv_ref,
    dpe_ref,
    cq_ref,
    ckv_ref,
    dk_acc,
    dv_acc,
):
    length = qa_ref.shape[0]
    step = pl.program_id(0)
    lane = lax.broadcasted_iota(jnp.int32, (length, HEAD_LANES), 1)
    upper = lane >= 64
    key_at = lax.broadcasted_iota(jnp.int32, (BLOCK_Q, BLOCK_Q), 0)
    query_at = lax.broadcasted_iota(jnp.int32, (BLOCK_Q, BLOCK_Q), 1)
    causal = key_at <= query_at
    out_both = o_ref[...].astype(F32)
    grad_both = do_ref[...].astype(F32)

    @pl.when(step == 0)
    def _():
        dpe_ref[...] = jnp.zeros_like(dpe_ref)

    for i in range(per_step):
        span = slice(i * HEAD_LANES, (i + 1) * HEAD_LANES)
        if per_step == 2:
            turn = i == 0
            grad_one = pltpu.roll(grad_both, 64, 1) if turn else grad_both
            out_one = pltpu.roll(out_both, 64, 1) if turn else out_both
        else:
            even = lax.rem(step, 2) == 0
            grad_one = jnp.where(even, pltpu.roll(grad_both, 64, 1), grad_both)
            out_one = jnp.where(even, pltpu.roll(out_both, 64, 1), out_both)
        grad_one = jnp.where(upper, grad_one, 0.0)
        inner = jnp.sum(jnp.where(upper, grad_one * out_one, 0.0), axis=-1, keepdims=True)
        high, middle, low = split_three(inner)
        grad_aug = jnp.where(
            lane == 0, -high, jnp.where(lane == 1, -middle, jnp.where(lane == 2, -low, grad_one))
        )
        grad_aug = narrow(grad_aug)
        kv_one = kv_ref[:, span]
        ones = jnp.where(lane < 3, 1.0, 0.0).astype(BF16)
        v_aug = jnp.where(upper, kv_one, ones)
        k_aug = jnp.where(lane < 64, kv_one, pe_ref[...])
        k_turned = narrow(k_aug.astype(F32).T)
        for j in reversed(range(length // BLOCK_Q)):
            begin, end = j * BLOCK_Q, (j + 1) * BLOCK_Q
            q_part = qa_ref[begin:end, span]
            probs = jnp.exp2(dot_nt(k_aug[:end], q_part) * EXP2_SCALE)
            diag = jnp.where(causal, probs[begin:], 0.0)
            probs = diag if j == 0 else jnp.concatenate([probs[:begin], diag], axis=0)
            grads = narrow(probs * dot_nt(v_aug[:end], grad_aug[begin:end]))
            dq_part = dot_nn(k_turned[:, :end], grads).T * SCORE_SCALE
            dq_part = rope_mix(
                dq_part,
                rope_ref[0, begin:end, :],
                -rope_ref[1, begin:end, :],
                -rope_ref[2, begin:end, :],
            )
            dq_ref[begin:end, span] = narrow(dq_part)
            dk_part = dot_nn(grads, q_part)
            dv_part = dot_nn(narrow(probs), grad_aug[begin:end])
            if end == length:
                dk_acc[...] = dk_part
                dv_acc[...] = dv_part
            else:
                dk_acc[:end] += dk_part
                dv_acc[:end] += dv_part
        dk_all = dk_acc[...] * SCORE_SCALE
        dkv_ref[:, span] = narrow(jnp.where(upper, dv_acc[...], dk_all))
        dpe_ref[...] += jnp.where(upper & (lane < 96), dk_all, 0.0)
    cq_ref[...] = dot_tn(codes_ref[...], dq_ref[...])
    ckv_ref[...] = dot_tn(codes_ref[...], dkv_ref[...])

    @pl.when(step == pl.num_programs(0) - 1)
    def _():
        turned_back = rope_mix(dpe_ref[...], rope_ref[0], -rope_ref[1], -rope_ref[2])
        dpe_ref[...] = pltpu.roll(turned_back, PLAIN_HEAD_DIM + 2 * RANK, 1)


def ridden_call(
    kernel,
    grid,
    arrays,
    in_specs,
    out_shape,
    out_specs,
    scratch,
    riders,
    ridden,
    carried,
    fresh,
    name,
    collective_id,
):
    steps = distinct(rider_steps(riders))
    count = rider_count(riders)
    n_in, n_out = len(arrays), len(out_shape)
    n_ride_in = len(ridden) + len(carried)
    n_ride_out = len(ridden) + len(fresh)
    def body(*refs):
        own_in, rest = refs[:n_in], refs[n_in:]
        ride_in, rest = rest[:n_ride_in], rest[n_ride_in:]
        own_out, rest = rest[:n_out], rest[n_out:]
        ride_out, rest = rest[:n_ride_out], rest[n_ride_out:]
        send_sems, recv_sems = rest[-2:]
        links = Links(send_sems, recv_sems)
        ride = Riders(links, riders, ride_in, ride_out)

        @pl.when(pl.program_id(0) == 0)
        def _():
            links.greet(steps)
            ride.start()

        kernel(*own_in, *own_out, *rest[:-2])

        @pl.when(pl.program_id(0) == grid[0] - 1)
        def _():
            ride.finish()
            links.close()

    any_spec = pl.BlockSpec(memory_space=pl.ANY)
    return pl.pallas_call(
        body,
        grid=grid,
        in_specs=list(in_specs) + [any_spec] * n_ride_in,
        out_specs=list(out_specs) + [any_spec] * n_ride_out,
        out_shape=list(out_shape)
        + [jax.ShapeDtypeStruct(r.shape, r.dtype) for r in ridden]
        + [jax.ShapeDtypeStruct(f, BF16) for f in fresh],
        scratch_shapes=list(scratch)
        + [pltpu.SemaphoreType.DMA((count,)), pltpu.SemaphoreType.DMA((count,))],
        input_output_aliases={n_in + n: n_out + n for n in range(len(ridden))},
        compiler_params=pltpu.CompilerParams(
            collective_id=collective_id, has_side_effects=True, vmem_limit_bytes=VMEM_LIMIT
        ),
        cost_estimate=FREE,
        name=name,
    )(*arrays, *ridden, *carried)


def attend(latents, w_q, w_kv, rope, pe_aug, doc_q, q_width, kv_at, riders, ridden, carried):
    length = latents.shape[0]
    heads = w_q.shape[1] // HEAD_LANES
    per_step = 2 if heads % 2 == 0 else 1
    wide = per_step * HEAD_LANES
    whole = lambda a: pl.BlockSpec(a.shape, lambda h: (0,) * a.ndim)
    return ridden_call(
        functools.partial(attn_fwd_kernel, per_step, q_width, kv_at),
        (heads // per_step,),
        [latents, w_q, w_kv, rope, pe_aug, doc_q],
        [
            whole(latents),
            pl.BlockSpec((w_q.shape[0], wide), lambda h: (0, h)),
            pl.BlockSpec((w_kv.shape[0], wide), lambda h: (0, h)),
            whole(rope),
            whole(pe_aug),
            whole(doc_q),
        ],
        [
            jax.ShapeDtypeStruct((length, heads * HEAD_LANES), BF16),
            jax.ShapeDtypeStruct((length, heads * HEAD_LANES), BF16),
            jax.ShapeDtypeStruct((length, heads * VALUE_HEAD_DIM), BF16),
        ],
        [
            pl.BlockSpec((length, wide), lambda h: (0, h)),
            pl.BlockSpec((length, wide), lambda h: (0, h)),
            pl.BlockSpec((length, HEAD_LANES), lambda h: (0, h * per_step // 2)),
        ],
        [],
        riders,
        ridden,
        carried,
        [],
        "attend",
        10,
    )


def attend_back(q_aug, kv, heads_out, heads_grad, rope, pe_aug, codes, riders, ridden, carried, fresh):
    length = q_aug.shape[0]
    heads = q_aug.shape[1] // HEAD_LANES
    per_step = 2 if heads % 2 == 0 else 1
    wide = per_step * HEAD_LANES
    whole = lambda a: pl.BlockSpec(a.shape, lambda h: (0,) * a.ndim)
    columns = pl.BlockSpec((length, wide), lambda h: (0, h))
    packed = pl.BlockSpec((length, HEAD_LANES), lambda h: (0, h * per_step // 2))
    rows_in, lane_block = codes
    arrays = [q_aug, kv, heads_out, heads_grad, rope, pe_aug, rows_in]
    in_specs = [columns, columns, packed, packed, whole(rope), whole(pe_aug)]
    in_specs.append(pl.BlockSpec((length, CODE_LANES), lambda h: (0, lane_block)))
    out_shape = [
        jax.ShapeDtypeStruct((length, heads * HEAD_LANES), BF16),
        jax.ShapeDtypeStruct((length, heads * HEAD_LANES), BF16),
        jax.ShapeDtypeStruct((length, HEAD_LANES), F32),
    ] + [jax.ShapeDtypeStruct((CODE_LANES, heads * HEAD_LANES), F32)] * 2
    out_specs = [columns, columns, pl.BlockSpec((length, HEAD_LANES), lambda h: (0, 0))]
    out_specs += [pl.BlockSpec((CODE_LANES, wide), lambda h: (0, h))] * 2
    scratch = [pltpu.VMEM((length, HEAD_LANES), F32), pltpu.VMEM((length, HEAD_LANES), F32)]
    return ridden_call(
        functools.partial(attn_bwd_kernel, per_step),
        (heads // per_step,),
        arrays,
        in_specs,
        out_shape,
        out_specs,
        scratch,
        riders,
        ridden,
        carried,
        fresh,
        "attend_back",
        11,
    )


def gate_middle(gate, up, hid_grad):
    sig = 1.0 / (1.0 + jnp.exp(-gate))
    silu = gate * sig
    gate_grad = hid_grad * up * (sig * (1.0 + gate * (1.0 - sig)))
    return silu * up, gate_grad, hid_grad * silu


def tail_middle(pre, back, tail):
    wide = pre.shape[1]
    up = pltpu.roll(pre, wide - tail, 1)
    hid_grad = pltpu.roll(back, wide - 2 * tail, 1)
    hid, gate_grad, up_grad = gate_middle(pre, up, hid_grad)
    lane = lax.broadcasted_iota(jnp.int32, pre.shape, 1)
    hid = jnp.where((lane >= 2 * tail) & (lane < 3 * tail), pltpu.roll(hid, 2 * tail, 1), 0.0)
    both = jnp.where(
        lane < tail, gate_grad, jnp.where(lane < 2 * tail, pltpu.roll(up_grad, tail, 1), 0.0)
    )
    return hid, both


def remote_ffn(x_own, g_all, weights, extras, mains, tail, tail_wide, slow, block_of, riders, name, collective_id):
    rows, aug = x_own.shape
    total = g_all.shape[0]
    blocks = total // rows
    both = 2 * rows
    width = aug - CODE_LANES
    chunks = len(mains)
    tails = [0] * (chunks - 1) + [tail_wide]
    gu = [2 * m + w for m, w in zip(mains, tails)]
    core_step = ("tensor", 1)
    keys = [(0, 0)]
    for step in slow:
        keys += [flip(key, step) for key in keys]
    bits_of = {key: [s for s in slow if has_bit(key, s)] for key in keys}
    keys.sort(key=lambda k: len(bits_of[k]))

    def part_rows(key, step):
        n = len(bits_of[key])
        i = bits_of[key].index(step)
        size = -(-rows // (16 * n)) * 16
        begin = i * size
        return begin, min(size, rows - begin)

    count = len(keys) + sum(len(bits_of[k]) for k in keys) + rider_count(riders)
    steps = distinct([core_step] + slow + rider_steps(riders))

    def kernel(x_ref, g_ref, *refs):
        e_refs = refs[chunks : 2 * chunks]
        refs = refs[2 * chunks :]
        codes_ref = refs[0]
        grad_refs = refs[1 : 1 + chunks]
        hid_refs = refs[1 + chunks : 1 + 2 * chunks]
        w_refs = refs[1 + 2 * chunks : 1 + 3 * chunks]
        x_held, back_held, g_held = refs[1 + 3 * chunks : 4 + 3 * chunks]
        w_held = refs[4 + 3 * chunks : 4 + 4 * chunks]
        send_sems, recv_sems, w_sems, g_sems = refs[4 + 4 * chunks :]
        links = Links(send_sems, recv_sems)
        place = links.place
        fetch = [
            pltpu.make_async_copy(w_refs[c], w_held[c].at[pl.ds(0, width)], w_sems.at[c])
            for c in range(chunks)
        ]
        fetch_extra = [
            pltpu.make_async_copy(
                e_refs[c], w_held[c].at[pl.ds(width, CODE_LANES)], w_sems.at[chunks + c]
            )
            for c in range(chunks)
        ]
        fetch[0].start()
        for copy in fetch_extra:
            copy.start()
        links.greet(steps)

        def landing(key):
            at = pl.multiple_of(block_of(key, place) * rows, 16)
            return x_held.at[pl.ds(at, rows)]

        arrivals = {key: [] for key in keys}

        def pass_on(key, src):
            for step in slow:
                if has_bit(key, step):
                    continue
                there = flip(key, step)
                begin, size = part_rows(there, step)
                at = pl.ds(begin, size)
                n = links.send(src.at[at], landing(key).at[at], step)
                arrivals[there].append(n)

        crossing = {}
        pass_on((0, 0), x_ref)
        crossing[(0, 0)] = links.send(x_ref, landing((0, 0)), core_step)
        ride = Riders(links, riders, w_refs, w_refs)
        ride.start()
        x_held[pl.ds(pl.multiple_of(block_of((0, 0), place) * rows, 16), rows), :] = x_ref[...]

        def g_copy(b, slot):
            at = pl.ds(pl.multiple_of(b * both, 16), both)
            return pltpu.make_async_copy(g_ref.at[at], g_held.at[slot], g_sems.at[slot])

        def over_blocks(work):
            g_copy(0, 0).start()

            def one(b, carry):
                slot = lax.rem(b, 2)

                @pl.when(b + 1 < blocks // 2)
                def _():
                    g_copy(b + 1, 1 - slot).start()

                g_copy(b, slot).wait()
                work(b, g_held[slot])
                return carry

            lax.fori_loop(0, blocks // 2, one, 0)

        fetch[0].wait()
        for copy in fetch_extra:
            copy.wait()

        def back_first(b, g_rows):
            back_held[b] = dot_nn(g_rows, w_held[0][:, gu[0] :])

        over_blocks(back_first)

        def forward(b, c, back):
            main = mains[c]
            at = pl.ds(pl.multiple_of(b * both, 16), both)
            pre = dot_nn(x_held[at, :], w_held[c][:, : gu[c]])
            hid, gate_grad, up_grad = gate_middle(pre[:, :main], pre[:, gu[c] - main :], back)
            hid_refs[c][at, :main] = narrow(hid)
            grad_refs[c][at, :main] = narrow(gate_grad)
            grad_refs[c][at, gu[c] - main :] = narrow(up_grad)
            return pre, at

        def first_chunk(key):
            b = block_of(key, place) // 2
            forward(b, 0, back_held[b])

        links.arrived(crossing[(0, 0)])
        first_chunk((0, 0))

        def later(b, g_rows, c):
            main = mains[c]
            back = dot_nn(g_rows, w_held[c][:, gu[c] :])
            pre, at = forward(b, c, back)
            if tails[c]:
                at_tail = slice(main, main + tail_wide)
                hid, both_grads = tail_middle(
                    pre[:, at_tail], dot_nn(g_rows, w_held[c][:, at_tail]), tail
                )
                hid_refs[c][at, main:] = narrow(hid)
                grad_refs[c][at, at_tail] = narrow(both_grads)

        def later_chunks(pairs):
            places = [block_of(key, place) // 2 for key in pairs]
            g_copy(places[0], 0).start()
            for n, b in enumerate(places):
                if n + 1 < len(places):
                    g_copy(places[n + 1], (n + 1) % 2).start()
                g_copy(b, n % 2).wait()
                for c in range(1, chunks):
                    later(b, g_held[n % 2], c)

        waiting = [(0, 0)]
        for level in range(1, len(slow) + 1):
            here = [key for key in keys if len(bits_of[key]) == level]
            for key in here:
                for n in arrivals[key]:
                    links.arrived(n)
                pass_on(key, landing(key))
                crossing[key] = links.send(landing(key), landing(key), core_step)
            for key in here:
                links.arrived(crossing[key])
                first_chunk(key)
            waiting += here
            if level == len(slow) - 1:
                ride.finish()
                for c in range(1, chunks):
                    fetch[c].start()
                    fetch[c].wait()
                later_chunks(waiting)
                waiting = []
        later_chunks(waiting)
        codes_ref[...] = x_held[:, width:]
        links.close()

    any_spec = pl.BlockSpec(memory_space=pl.ANY)
    vmem_spec = pl.BlockSpec(memory_space=pltpu.VMEM)
    outs = pl.pallas_call(
        kernel,
        in_specs=[vmem_spec, any_spec] + [any_spec] * (2 * chunks),
        out_specs=[vmem_spec] * (1 + 2 * chunks) + [any_spec] * chunks,
        out_shape=[jax.ShapeDtypeStruct((total, CODE_LANES), BF16)]
        + [jax.ShapeDtypeStruct((total, g), BF16) for g in gu]
        + [jax.ShapeDtypeStruct((total, m + w), BF16) for m, w in zip(mains, tails)]
        + [jax.ShapeDtypeStruct(w.shape, BF16) for w in weights],
        scratch_shapes=[
            pltpu.VMEM((total, aug), BF16),
            pltpu.VMEM((blocks // 2, both, mains[0]), F32),
            pltpu.VMEM((2, both, aug), BF16),
        ]
        + [pltpu.VMEM((aug, w.shape[1]), BF16) for w in weights]
        + [
            pltpu.SemaphoreType.DMA((count,)),
            pltpu.SemaphoreType.DMA((count,)),
            pltpu.SemaphoreType.DMA((2 * chunks,)),
            pltpu.SemaphoreType.DMA((2,)),
        ],
        input_output_aliases={2 + c: 1 + 2 * chunks + c for c in range(chunks)},
        compiler_params=pltpu.CompilerParams(
            collective_id=collective_id, has_side_effects=True, vmem_limit_bytes=VMEM_LIMIT
        ),
        cost_estimate=FREE,
        name=name,
    )(x_own, g_all, *weights, *extras)
    return (
        outs[0],
        outs[1 : 1 + chunks],
        outs[1 + chunks : 1 + 2 * chunks],
        outs[1 + 2 * chunks :],
    )


def remote_ffn_back(
    grads, hids, weights, extras, x_codes, g_all, mains, tail_wide, keys, ways, block_of, rows, name, collective_id
):
    width = weights[0].shape[0]
    aug = width + CODE_LANES
    chunks = len(mains)
    tails = [0] * (chunks - 1) + [tail_wide]
    gu = [2 * m + w for m, w in zip(mains, tails)]
    core_step = ("tensor", 1)
    part = rows // len(ways)
    plan = reduce_plan(keys, ways)
    later = [entry for entry in plan if entry[1] > 0]
    slot = {entry: n for n, entry in enumerate(plan)}
    later_slot = {entry: n for n, entry in enumerate(later)}
    steps = distinct([core_step] + ways[0])
    count = 2 * len(keys) + len(plan)
    operands = list(grads) + list(hids) + list(weights) + [x_codes, g_all]
    shapes = [o.shape for o in operands]
    for c in range(chunks):
        shapes[2 * chunks + c] = (aug, weights[c].shape[1])
    shapes[3 * chunks + 1] = x_codes.shape

    def kernel(*refs):
        n_in = len(operands)
        in_refs, e_refs, refs = refs[:n_in], refs[n_in : n_in + chunks], refs[n_in + chunks :]
        refs = in_refs + refs
        out_ref, terms_ref = refs[n_in : n_in + 2]
        gu_refs = refs[n_in + 2 : n_in + 2 + chunks]
        down_refs = refs[n_in + 2 + chunks : n_in + 2 + 2 * chunks]
        held = refs[n_in + 2 + 2 * chunks : 2 * n_in + 2 + 2 * chunks]
        rest = refs[2 * n_in + 2 + 2 * chunks :]
        core_out, core_in, chip, hop_out, hop_in, stage, send_sems, recv_sems, in_sems, out_sems, free = rest
        g_held, h_held = held[:chunks], held[chunks : 2 * chunks]
        w_held = held[2 * chunks : 3 * chunks]
        started = []
        order = [n for c in range(chunks) for n in (2 * chunks + c, c)]
        order += list(range(chunks, 2 * chunks)) + [3 * chunks, 3 * chunks + 1]
        for n in order:
            is_weight = 2 * chunks <= n < 3 * chunks
            to = held[n].at[pl.ds(0, width)] if is_weight else held[n]
            src = in_refs[n]
            if n == 3 * chunks + 1:
                src = src.at[:, pl.ds(width, CODE_LANES)]
            copy = pltpu.make_async_copy(src, to, in_sems.at[n])
            copy.start()
            started.append(copy)
        for c in range(chunks):
            copy = pltpu.make_async_copy(
                e_refs[c], w_held[c].at[pl.ds(width, CODE_LANES)], in_sems.at[n_in + c]
            )
            copy.start()
            started.append(copy)
        links = Links(send_sems, recv_sems)
        place = links.place
        links.greet(steps)
        for copy in started[: 2 * chunks] + started[n_in:]:
            copy.wait()
        came = {}

        def rows_of(key):
            return pl.ds(pl.multiple_of(block_of(key, place) * rows, 16), rows)

        def in_term(key):
            at = rows_of(key)
            out = dot_nt(g_held[0][at, :], w_held[0][:, : gu[0]])
            for c in range(1, chunks):
                out = out + dot_nt(g_held[c][at, :], w_held[c][:, : gu[c]])
            return out

        def down_term(key):
            at = rows_of(key)
            out = 0.0
            for c in range(chunks):
                out = out + dot_nt(h_held[c][at, : mains[c]], w_held[c][:, gu[c] :])
                if tails[c]:
                    out = out + dot_nt(
                        h_held[c][at, mains[c] :], w_held[c][:, mains[c] : mains[c] + tails[c]]
                    )
            return out

        def so_far(w, k, key):
            if key == (0, 0):
                total = out_ref[w * part : (w + 1) * part, :]
            else:
                total = chip[keys.index(key), w * part : (w + 1) * part, :].astype(F32)
            for j in range(k):
                entry = (w, j, flip(key, ways[w][j]))
                links.arrived(came[entry])
                total = total + hop_in[slot[entry]].astype(F32)
            return total

        crossings = []

        def cross(i, value):
            n = len(crossings)
            if n >= 2:
                links.copies[crossings[n - 2]].wait_send()
            core_out[n % 2] = narrow(value)
            crossings.append(links.send(core_out.at[n % 2], core_in.at[i], core_step))
            return crossings[-1]

        for i, key in enumerate(keys):
            crossing = cross(i, in_term((key[0], key[1] ^ 1)))
            mine = in_term(key)
            links.arrived(crossing)
            mine = mine + core_in[i].astype(F32)
            if key == (0, 0):
                out_ref[...] = mine
            else:
                chip[i] = narrow(mine)
                for w, way in enumerate(ways):
                    if has_bit(key, way[0]):
                        at = slice(w * part, (w + 1) * part)
                        entry = (w, 0, key)
                        came[entry] = links.send(
                            chip.at[i, pl.ds(w * part, part)], hop_in.at[slot[entry]], way[0]
                        )
        pl.semaphore_signal(
            free, inc=1, device_id=links.peer(core_step), device_id_type=pl.DeviceIdType.MESH
        )
        pl.semaphore_wait(free, 1)
        for copy in started[2 * chunks : n_in]:
            copy.wait()
        stored = []
        for i, key in enumerate(keys):
            crossing = cross(i, down_term((key[0], key[1] ^ 1)))
            mine = down_term(key)
            links.arrived(crossing)
            if i >= 2:
                stored[i - 2].wait()
            stage[i % 2] = narrow(mine + core_in[i].astype(F32))
            copy = pltpu.make_async_copy(stage.at[i % 2], terms_ref.at[i], out_sems.at[i])
            copy.start()
            stored.append(copy)
            if i == len(keys) // 2 - 1:
                for k in range(1, len(ways[0])):
                    for w in range(len(ways)):
                        for entry in plan:
                            if entry[0] == w and entry[1] == k:
                                hop_out[later_slot[entry]] = narrow(so_far(w, k, entry[2]))
                                came[entry] = links.send(
                                    hop_out.at[later_slot[entry]],
                                    hop_in.at[slot[entry]],
                                    ways[w][k],
                                )
        x_held, gc_held = held[3 * chunks :]
        for c in range(chunks):
            gu_refs[c][...] = dot_tn(x_held[...], g_held[c][...])
            down_refs[c][...] = dot_tn(gc_held[...], h_held[c][...])
        for w in range(len(ways)):
            out_ref[w * part : (w + 1) * part, :] = so_far(w, len(ways[w]), (0, 0))
        for copy in stored[max(0, len(keys) - 2) :]:
            copy.wait()
        for n, copy in enumerate(links.copies):
            links.arrived(n)
            if n not in crossings[:-2]:
                copy.wait_send()

    any_spec = pl.BlockSpec(memory_space=pl.ANY)
    return pl.pallas_call(
        kernel,
        out_shape=[
            jax.ShapeDtypeStruct((rows, aug), F32),
            jax.ShapeDtypeStruct((len(keys), rows, aug), BF16),
        ]
        + [jax.ShapeDtypeStruct((CODE_LANES, g.shape[1]), F32) for g in grads]
        + [jax.ShapeDtypeStruct((CODE_LANES, h.shape[1]), F32) for h in hids],
        in_specs=[any_spec] * (len(operands) + chunks),
        out_specs=[pl.BlockSpec(memory_space=pltpu.VMEM), any_spec]
        + [pl.BlockSpec(memory_space=pltpu.VMEM)] * (2 * chunks),
        scratch_shapes=[pltpu.VMEM(n, o.dtype) for n, o in zip(shapes, operands)]
        + [
            pltpu.VMEM((2, rows, aug), BF16),
            pltpu.VMEM((len(keys), rows, aug), BF16),
            pltpu.VMEM((len(keys) - 1, rows, aug), BF16),
            pltpu.VMEM((max(len(later), 1), part, aug), BF16),
            pltpu.VMEM((len(plan), part, aug), BF16),
            pltpu.VMEM((2, rows, aug), BF16),
            pltpu.SemaphoreType.DMA((count,)),
            pltpu.SemaphoreType.DMA((count,)),
            pltpu.SemaphoreType.DMA((len(operands) + chunks,)),
            pltpu.SemaphoreType.DMA((len(keys),)),
            pltpu.SemaphoreType.REGULAR,
        ],
        compiler_params=pltpu.CompilerParams(
            collective_id=collective_id, has_side_effects=True, vmem_limit_bytes=VMEM_LIMIT
        ),
        cost_estimate=FREE,
        name=name,
    )(*operands, *extras)


def ffn_extras(places, gate_up_out, down_in, mains, tail, tail_wide):
    half = down_in.shape[2] // 2
    chunks = len(mains)
    tails = [0] * (chunks - 1) + [tail_wide]
    wide = [3 * m + w for m, w in zip(mains, tails)]

    def kernel(places_ref, gu_ref, down_ref, *outs):
        for out in outs:
            out[...] = jnp.zeros_like(out)
        lower = places_ref[2] == 0
        for p in range(2):
            which = places_ref[p]

            def half_of(value):
                return jnp.where(lower, value[:, :half], value[:, half:])

            parts = [
                half_of(gu_ref[0, which]) * 2,
                half_of(gu_ref[1, which]) * 2,
                half_of(down_ref[which]),
            ]
            for kind, value in enumerate(parts):
                top = 2 * RANK * p + (RANK if kind == 1 else 0)
                at_rows = slice(top, top + RANK)
                begin = 0
                for c in range(chunks):
                    main = mains[c]
                    at = [0, main + tails[c], 2 * main + tails[c]][kind]
                    outs[c][at_rows, at : at + main] = value[:, begin : begin + main]
                    begin += main
                if tail:
                    at = mains[-1] + kind * tail
                    outs[-1][at_rows, at : at + tail] = value[:, begin:]

    return pl.pallas_call(
        kernel,
        grid_spec=pltpu.PrefetchScalarGridSpec(
            num_scalar_prefetch=1,
            grid=(1,),
            in_specs=[
                pl.BlockSpec(a.shape, lambda i, ids, n=a.ndim: (0,) * n)
                for a in (gate_up_out, down_in)
            ],
            out_specs=[pl.BlockSpec((CODE_LANES, w), lambda i, ids: (0, 0)) for w in wide],
        ),
        out_shape=[jax.ShapeDtypeStruct((CODE_LANES, w), BF16) for w in wide],
        compiler_params=pltpu.CompilerParams(vmem_limit_bytes=VMEM_LIMIT),
        cost_estimate=FREE,
        name="ffn_extras",
    )(places, gate_up_out, down_in)


def chunk_places(mains, tail, tail_wide):
    out = []
    begin = 0
    for c, main in enumerate(mains):
        wide = tail_wide if c == len(mains) - 1 else 0
        for kind, at in enumerate((0, main + wide, 2 * main + wide)):
            out.append((kind, c, at, begin, main))
        begin += main
    if tail:
        for kind in range(3):
            out.append((kind, len(mains) - 1, mains[-1] + kind * tail, begin, tail))
    return out


def prepare(places, tables, shards, sizes, mains, tail, tail_wide):
    heads, head_q, shares, down_wide = sizes
    qa_in, kva_in, qb_in, kvb_in, out_in, gu_in, qa_out, kva_out, qb_out, kvb_out, out_out, down_out = (
        tables
    )
    q_down, kv_down, q_up, gate_up, down_t, cotangent = shards
    width, q_lat, kv_all = qa_in.shape[2], q_down.shape[1], kv_down.shape[1]
    rows = cotangent.shape[0]
    share_rows = q_down.shape[0] // shares
    wide = heads * HEAD_LANES
    half = down_t.shape[1] // 2
    wides = [3 * m for m in mains[:-1]] + [3 * mains[-1] + tail_wide]

    def kernel(places_ref, *refs):
        ins, outs = refs[: len(tables) + len(shards)], refs[len(tables) + len(shards) :]
        qa_i, kva_i, qb_i, kvb_i, out_i, gu_i, qa_o, kva_o, qb_o, kvb_o, out_o, down_o = ins[
            : len(tables)
        ]
        qd, kvd, qu, gu_w, down_w, cot = ins[len(tables) :]
        down_in_o, down_b_o, qb_w, kvb_w, q_aug, kv_aug, out_x, gu_lanes, out_p, down_p, gu_p = outs[:11]
        mine_d, q_pad, g_own = outs[11:14]
        pieces = outs[14:]
        first = places_ref[1] == 0
        for out in (down_b_o, qb_w, kvb_w, q_aug, kv_aug, out_x, gu_lanes, out_p, gu_p, mine_d, q_pad):
            out[...] = jnp.zeros_like(out)
        for out in pieces:
            out[...] = jnp.zeros_like(out)
        down_in_o[:RANK, :] = qa_i[0]
        down_in_o[RANK:, :] = kva_i[0]
        down_b_o[:RANK, :q_lat] = qa_o[0]
        down_b_o[RANK:, q_lat : q_lat + kv_all] = kva_o[0]
        qb_w[:RANK, :] = qb_i[0]
        kvb_w[RANK : 2 * RANK, :] = kvb_i[0]
        out_x[:RANK, :] = out_i[0]
        kv_aug[RANK : 2 * RANK, :] = narrow(kvb_o[0].astype(F32) * ADAPT_SCALE)
        q_out = narrow(qb_o[0].astype(F32) * ADAPT_SCALE)
        q_up_all = qu[...]
        for h in range(heads):
            at = slice(h * HEAD_LANES, h * HEAD_LANES + head_q)
            q_aug[:RANK, at] = q_out[:, h * head_q : (h + 1) * head_q]
            q_pad[:, at] = q_up_all[:, h * head_q : (h + 1) * head_q]
        for n in range(2):
            both = gu_i[n, 0]
            none = jnp.zeros_like(both)
            gu_p[n * RANK : (n + 1) * RANK, :] = both
            gu_lanes[n * RANK : (n + 1) * RANK, :] = jnp.where(first, both, none)
            gu_lanes[(2 + n) * RANK : (3 + n) * RANK, :] = jnp.where(first, none, both)
        out_p[:RANK, :] = out_o[0]
        down_p[...] = down_o[0]
        mine_d[:, :q_lat] = qd[...]
        mine_d[:, q_lat : q_lat + kv_all] = kvd[...]
        grad = narrow(RESIDUAL * cot[...].astype(F32))
        g_own[:, :width] = grad
        codes = dot_nt(grad, jnp.concatenate([down_o[0]] * 8, axis=0)) * ADAPT_SCALE
        lane = lax.broadcasted_iota(jnp.int32, codes.shape, 1)
        begin = jnp.where(first, 0, 2 * RANK)
        g_own[:, width:] = narrow(jnp.where((lane >= begin) & (lane < begin + RANK), codes, 0.0))
        sources = [gu_w[0], gu_w[1], down_w[...]]
        sides = [(v[:, :half], v[:, half:]) for v in sources]
        for kind, c, at, begin, count in chunk_places(mains, tail, tail_wide):
            left = sides[kind][0][:, begin : begin + count]
            right = sides[kind][1][:, begin : begin + count]
            pieces[2 * c][:, at : at + count] = jnp.where(first, left, right)
            pieces[2 * c + 1][:, at : at + count] = jnp.where(first, right, left)

    def picked(table):
        if table.ndim == 4:
            return pl.BlockSpec((2, 1) + table.shape[2:], lambda i, ids: (0, ids[0], 0, 0))
        return pl.BlockSpec((1,) + table.shape[1:], lambda i, ids: (ids[0], 0, 0))

    def shared(shard):
        return pl.BlockSpec((share_rows, shard.shape[1]), lambda i, ids: (ids[2], 0))

    def whole(shape):
        return pl.BlockSpec(shape, lambda i, ids: (0,) * len(shape))

    out_shapes = [
        (2 * RANK, width),
        (2 * RANK, down_wide),
        (CODE_LANES, qb_in.shape[2]),
        (CODE_LANES, kvb_in.shape[2]),
        (CODE_LANES, wide),
        (CODE_LANES, wide),
        (CODE_LANES, out_in.shape[2]),
        (CODE_LANES, width),
        (CODE_LANES, width),
        (RANK, width),
        (CODE_LANES, width),
        (share_rows, down_wide),
        (q_up.shape[0], wide),
        (rows, width + CODE_LANES),
    ]
    for w in wides:
        out_shapes += [(down_t.shape[0], w)] * 2
    return pl.pallas_call(
        kernel,
        grid_spec=pltpu.PrefetchScalarGridSpec(
            num_scalar_prefetch=1,
            grid=(1,),
            in_specs=[picked(a) for a in tables]
            + [shared(q_down), shared(kv_down)]
            + [whole(a.shape) for a in shards[2:]],
            out_specs=[whole(o) for o in out_shapes],
        ),
        out_shape=[jax.ShapeDtypeStruct(o, BF16) for o in out_shapes],
        compiler_params=pltpu.CompilerParams(vmem_limit_bytes=VMEM_LIMIT),
        cost_estimate=FREE,
        name="prepare",
    )(places, *tables, *shards)


def per_device(
    n_dp,
    n_t,
    inputs,
    cotangent,
    document_numbers,
    sequence_adapter_index,
    attention_norm_gain,
    query_latent_gain,
    keyvalue_latent_gain,
    feedforward_norm_gain,
    query_down_matrix,
    keyvalue_down_matrix,
    query_up_matrix,
    keyvalue_up_matrix,
    output_matrix,
    gate_up_matrix,
    down_matrix,
    query_down_adapter_in,
    query_down_adapter_out,
    keyvalue_down_adapter_in,
    keyvalue_down_adapter_out,
    query_up_adapter_in,
    query_up_adapter_out,
    keyvalue_up_adapter_in,
    keyvalue_up_adapter_out,
    output_adapter_in,
    output_adapter_out,
    gate_up_adapter_in,
    gate_up_adapter_out,
    down_adapter_in,
    down_adapter_out,
):
    d = lax.axis_index("dp")
    t = lax.axis_index("tensor")
    pair = n_dp // 4
    low_bits = [b for b in (1, 2, 4, 8, 16) if b < pair]
    high = n_dp // 2
    y_bits = [b for b in (2, 4, 8, 16) if b < n_t]
    zl = lax.rem(d // pair, 2)
    core = lax.rem(t, 2)
    first = zl == 0
    size = {"dp": n_dp, "tensor": n_t}
    rows = inputs.shape[1]
    width = inputs.shape[2]
    length = document_numbers.shape[1]
    q_lat = query_down_matrix.shape[1]
    kv_all = keyvalue_down_matrix.shape[1]
    kv_lat = kv_all - ROTARY_DIM
    heads = keyvalue_up_matrix.shape[1] // HEAD_LANES
    group_count = query_down_adapter_in.shape[0]
    aug = width + CODE_LANES
    half_rows = rows // 2

    def hop(value, step):
        return swap(value, step[0], step[1], size[step[0]])

    outer_first = [("dp", high), ("dp", pair)] + [("dp", b) for b in reversed(low_bits)]
    inner_first = [("dp", b) for b in low_bits] + [("dp", high), ("dp", pair)]
    t_slow = [("tensor", b) for b in reversed(y_bits)]
    t_core = [("tensor", 1)]

    set_own = sequence_adapter_index[0]

    def pick(table, index):
        return lax.dynamic_index_in_dim(table, index, 0, keepdims=False)

    def turned(table):
        return jnp.swapaxes(table, -1, -2)

    hidden = down_matrix.shape[0]
    half = hidden // 2
    tiles = half // 128
    main = tiles * 128
    tail = half - main
    tail_wide = -(-3 * tail // 128) * 128
    first_tiles = (2 * tiles + 2) // 3
    mains = [first_tiles * 128, main - first_tiles * 128]
    chunks = len(mains)
    tails = [0] * (chunks - 1) + [tail_wide]
    gu_wide = [2 * m + w for m, w in zip(mains, tails)]

    head_q = PLAIN_HEAD_DIM + ROTARY_DIM
    down_shard = query_down_matrix.shape[0]
    shares = n_t if down_shard % (16 * n_t) == 0 else 2
    share_rows = down_shard // shares
    down_wide = -(-(q_lat + kv_all) // 128) * 128
    down_pad = down_wide - q_lat - kv_all
    (
        down_in,
        down_b_rows,
        qb_in_wide,
        kvb_in_wide,
        q_aug_rows,
        kv_aug_rows,
        out_extra,
        gu_in_lanes,
        out_out_wide,
        down_out,
        gu_in_wide,
        down_mine,
        q_up_mine,
        g_own,
        *ffn_pieces,
    ) = prepare(
        jnp.stack([set_own, zl, lax.rem(t, shares)]).astype(jnp.int32),
        [
            turned(query_down_adapter_in),
            turned(keyvalue_down_adapter_in),
            turned(query_up_adapter_in),
            turned(keyvalue_up_adapter_in),
            turned(output_adapter_in),
            turned(gate_up_adapter_in),
            query_down_adapter_out,
            keyvalue_down_adapter_out,
            query_up_adapter_out,
            keyvalue_up_adapter_out,
            output_adapter_out,
            down_adapter_out,
        ],
        [
            query_down_matrix,
            keyvalue_down_matrix,
            query_up_matrix,
            gate_up_matrix,
            down_matrix.T,
            cotangent[0],
        ],
        (heads, head_q, shares, down_wide),
        mains,
        tail,
        tail_wide,
    )
    qb_in, kvb_in = qb_in_wide[:RANK], kvb_in_wide[RANK : 2 * RANK]
    out_out, gu_in = out_out_wide[:RANK], gu_in_wide[: 2 * RANK]
    ffn_mine, ffn_other = ffn_pieces[::2], ffn_pieces[1::2]
    ffn_rows_each = gate_up_matrix.shape[1]
    z_count = n_dp // pair
    ffn_wide = [m.shape[1] for m in ffn_mine]

    def ride_one(out, mine, other, begin, size):
        return dict(
            kind="one",
            out=out,
            mine=mine,
            other=other,
            rows=(begin, size),
            count=ffn_rows_each,
            pair=pair,
            high=high,
        )

    def ride_two(out, z, begin=0, size=None):
        return dict(
            kind="two",
            out=out,
            z=z,
            rows=(begin, ffn_rows_each if size is None else size),
            count=ffn_rows_each,
            pair=pair,
            high=high,
            steps=[("dp", b) for b in reversed(low_bits)],
        )

    def own_codes(value):
        lanes = value[:, width:]
        return jnp.where(first, lanes[:, : 2 * RANK], lanes[:, 2 * RANK : 4 * RANK])

    qb_rows, kvb_rows = query_up_matrix.shape[0], keyvalue_up_matrix.shape[0]
    out_rows = output_matrix.shape[1]

    def rows_at(start, step, count):
        return lambda dd, tt: (pl.ds(pl.multiple_of(start + dd * step, 16), count),)

    def group_block(dd, tt):
        return lax.rem(dd // pair, 2) * n_t + tt

    def group_jobs(src, out, ways):
        return [
            dict(
                src=src,
                src_at=pl.ds(at, half_rows),
                out=out,
                out_at=lambda dd, tt, at=at: (
                    pl.ds(pl.multiple_of(group_block(dd, tt) * rows + at, 16), half_rows),
                ),
                steps=steps + t_core,
                group="rows",
            )
            for at, steps in zip((0, half_rows), ways)
        ]

    group_a = t_slow + [("dp", pair)]
    group_b = [("dp", pair)] + t_slow
    pe_at = q_lat + 2 * RANK
    lat_wide = q_lat + CODE_LANES + kv_lat

    def token_jobs(src, out, parts, group=0):
        count = rows // parts
        return [
            dict(
                src=src,
                src_at=pl.ds(n * count, count),
                out=out,
                out_at=lambda dd, tt, n=n: (
                    pl.ds(pl.multiple_of(tt * rows + n * count, 16), count),
                ),
                steps=t_slow + t_core,
                group=group,
            )
            for n in range(parts)
        ]

    def latent_work(refs):
        x_ref, norm_ref, q_norm_ref, kv_norm_ref, in_ref, b_ref, qb_ref, kvb_ref = refs[12:20]
        latent_ref, codes_ref, rows_ref, w_ref, own_ref = refs[20:25]
        x_f = x_ref[...].astype(F32)
        scale = lax.rsqrt(jnp.mean(x_f * x_f, axis=-1, keepdims=True) + NORM_EPS)
        h_rows = narrow(x_f * scale * norm_ref[...])
        rows_ref[...] = h_rows
        codes = narrow(dot_nt(h_rows, in_ref[...]))
        latent = dot_nn(h_rows, w_ref[...]) + ADAPT_SCALE * dot_nn(codes, b_ref[...])
        latent_ref[...] = latent
        codes_ref[...] = codes
        q_part = latent[:, :q_lat]
        kv_part = latent[:, q_lat : q_lat + kv_lat]
        q_scale = lax.rsqrt(jnp.mean(q_part * q_part, axis=-1, keepdims=True) + NORM_EPS)
        kv_scale = lax.rsqrt(jnp.mean(kv_part * kv_part, axis=-1, keepdims=True) + NORM_EPS)
        q_in = narrow(q_part * q_scale * q_norm_ref[...])
        kv_in = narrow(kv_part * kv_scale * kv_norm_ref[...])
        own_ref[:, :q_lat] = q_in
        own_ref[:, q_lat + CODE_LANES :] = kv_in
        code_block = dot_nt(q_in, qb_ref[...]) + dot_nt(kv_in, kvb_ref[...])
        pe_block = pltpu.roll(latent[:, q_lat + kv_lat :], 2 * RANK, 1)
        lane = lax.broadcasted_iota(jnp.int32, code_block.shape, 1)
        own_ref[:, q_lat : q_lat + CODE_LANES] = narrow(
            jnp.where(lane < 2 * RANK, code_block, pe_block)
        )

    down_steps = outer_first + (t_slow if shares == n_t else []) + t_core
    cut_c = ffn_rows_each * 3 // 4 // 16 * 16
    n_start_outs = 9
    w_at, lat_own_at = n_start_outs + 3, n_start_outs + 4
    n_start_sources = 20
    jobs = [
        dict(
            src=0,
            out=w_at,
            out_at=lambda dd, tt: (
                pl.ds(
                    pl.multiple_of(dd * down_shard + lax.rem(tt, shares) * share_rows, 16), share_rows
                ),
            ),
            steps=down_steps,
            group="down",
        ),
        dict(src=1, out=1, out_at=rows_at(0, qb_rows, qb_rows), steps=outer_first, group="up"),
        dict(src=2, out=2, out_at=rows_at(CODE_LANES, kvb_rows, kvb_rows), steps=outer_first, group="up"),
        dict(src=8, out=5, out_at=lambda dd, tt: (dd,), steps=outer_first, group="up"),
        dict(src=3, out=3, out_at=rows_at(0, out_rows, out_rows), steps=outer_first, group="out"),
    ]
    low_steps = [("dp", b) for b in reversed(low_bits)]
    for src, out in ((9, 6), (11, 7)):
        jobs.append(
            dict(
                src=src,
                out=out,
                out_at=rows_at(0, ffn_rows_each, ffn_rows_each),
                steps=low_steps,
                group="own",
            )
        )
    def own_block(dd, tt):
        return (pl.ds(pl.multiple_of(group_block(dd, tt) * rows, 16), rows),)

    jobs.append(dict(src=4, out=4, out_at=own_block, steps=t_slow + t_core, group="rows"))
    jobs.append(
        dict(src=4, out=4, out_at=own_block, steps=[("dp", pair)], group="pair", keep=False)
    )
    jobs += token_jobs(n_start_sources + 4, 8, 2, "latents")
    set_mark = jnp.full((16, 128), sequence_adapter_index[0].astype(F32)).astype(BF16)
    start = (
        remote_gather(
            [
                down_mine,
                q_up_mine,
                keyvalue_up_matrix,
                output_matrix.T,
                g_own,
                q_aug_rows,
                kv_aug_rows,
                out_extra,
                set_mark,
                ffn_mine[0],
                ffn_other[0],
                ffn_mine[1],
                inputs[0],
                attention_norm_gain[None],
                query_latent_gain[None],
                keyvalue_latent_gain[None],
                down_in,
                down_b_rows,
                qb_in_wide,
                kvb_in_wide,
            ],
            jobs,
            [
                (5, 1, lambda dd, tt: (pl.ds(q_lat, CODE_LANES),)),
                (6, 2, lambda dd, tt: (pl.ds(0, CODE_LANES),)),
                (7, 3, lambda dd, tt: (pl.ds(width, CODE_LANES),)),
            ],
            [
                (width, down_wide),
                (q_lat + CODE_LANES, heads * HEAD_LANES),
                (CODE_LANES + kv_lat, heads * HEAD_LANES),
                (aug, heads * VALUE_HEAD_DIM),
                (2 * n_t * rows, aug),
                (n_dp, 16, 128),
                (width, ffn_wide[0]),
                (width, ffn_wide[1]),
                (length, lat_wide),
            ],
            "gather_start",
            1,
            riders=[ride_one(6, 9, 10, 0, cut_c)],
            order=["down", "up", "out", "rows", "down", "up", "down", "own", "out", "pair"]
            + ["down", "up", "out", "ride"]
            + ["down"] * (len(down_steps) - 4)
            + [("all", "down"), "work", "latents"]
            + ["latents"] * len(t_slow)
            + ["rows"],
            near_outs=[
                jax.ShapeDtypeStruct((rows, down_wide), F32),
                jax.ShapeDtypeStruct((rows, 2 * RANK), BF16),
                jax.ShapeDtypeStruct((rows, width), BF16),
            ],
            scratch=[
                jax.ShapeDtypeStruct((width, down_wide), BF16),
                jax.ShapeDtypeStruct((rows, lat_wide), BF16),
            ],
            work=latent_work,
            late=[(n_start_sources + 3, 0)],
        )
    )
    w_down, w_q, w_kv, w_out, g_all, set_marks, w_ffn0, w_ffn1, lat_all = start[:9]
    latent, down_codes_in, attn_rows = start[9:]
    set_all = set_marks[:, 0, 0].astype(jnp.int32)
    set_peer = lax.dynamic_index_in_dim(set_all, jnp.bitwise_xor(d, pair), 0, keepdims=False)
    set_even = jnp.where(first, set_own, set_peer)
    set_odd = jnp.where(first, set_peer, set_own)
    ffn_extra = ffn_extras(
        jnp.stack([set_even, set_odd, zl]).astype(jnp.int32),
        gate_up_adapter_out,
        turned(down_adapter_in),
        mains,
        tail,
        tail_wide,
    )
    cut_a = ffn_rows_each // 48 * 16
    cut_d = ffn_rows_each // 32 * 16

    cos_part, sin_part = rope_tables(document_numbers)
    zeros_l = jnp.zeros((length, PLAIN_HEAD_DIM), F32)
    zeros_r = jnp.zeros((length, HEAD_LANES - 96), F32)
    none_16 = jnp.zeros_like(sin_part)
    rope = jnp.stack(
        [
            jnp.concatenate([zeros_l + 1.0, cos_part, cos_part, zeros_r], axis=1),
            jnp.concatenate([zeros_l, -sin_part, none_16, zeros_r], axis=1),
            jnp.concatenate([zeros_l, none_16, sin_part, zeros_r], axis=1),
        ],
        axis=0,
    )
    lane_ids = jnp.arange(HEAD_LANES, dtype=jnp.int32)[None, :]
    doc_lane = (lane_ids >= DOC_LANE) & (lane_ids < DOC_LANE + DOC_SLOTS)
    is_doc = document_numbers[0][:, None] == lane_ids - DOC_LANE
    doc_q = narrow(jnp.where(doc_lane & is_doc, 1.0, 0.0))
    doc_k = jnp.where(
        doc_lane & ~is_doc, -BIG, jnp.where((lane_ids >= 96) & (lane_ids < 99), 1.0, 0.0)
    )

    pe_rows = lat_all[:, pe_at : pe_at + ROTARY_DIM].astype(F32)
    pe_a, pe_b = pe_rows[:, : ROTARY_DIM // 2], pe_rows[:, ROTARY_DIM // 2 :]
    pe_aug = narrow(
        jnp.concatenate(
            [
                zeros_l,
                pe_a * cos_part - pe_b * sin_part,
                pe_b * cos_part + pe_a * sin_part,
                zeros_r,
            ],
            axis=1,
        )
        + doc_k
    )
    def pair_rows(place, key):
        block = group_block(jnp.bitwise_xor(place["dp"], pair), jnp.bitwise_xor(place["tensor"], key))
        return pl.ds(pl.multiple_of(block * rows, 16), rows)

    q_aug, kv, head_out, w_ffn0, w_ffn1, g_all = attend(
        lat_all,
        w_q,
        w_kv,
        rope,
        pe_aug,
        doc_q,
        q_lat + CODE_LANES,
        q_lat,
        [
            ride_two(0, 1, 0, cut_c),
            ride_two(0, 2, 0, cut_d),
            ride_one(0, 5, 6, cut_c, ffn_rows_each - cut_c),
            ride_one(1, 3, 4, 0, cut_a),
            dict(kind="block", out=2, at=pair_rows, steps=t_slow),
        ],
        [w_ffn0, w_ffn1, g_all],
        [ffn_mine[1], ffn_other[1], ffn_mine[0], ffn_other[0]],
    )
    tensor_keys = [(0, r) for r in reversed(range(0, n_t, 2))]

    def token_rows(key, place):
        at = jnp.bitwise_xor(place["tensor"], key[1]) * rows
        return pl.ds(pl.multiple_of(at, 16), rows)

    def out_term(held, place, key):
        return dot_nt(held[0][token_rows(key, place), :], held[1][...])

    def middle_work(at, total, extra, outs):
        x_ref, out_b_ref, norm_ref, lanes_ref = extra
        middle_ref, codes_ref, own_ref = outs
        codes = narrow(total[:, width : width + RANK])
        mid = x_ref[at, :].astype(F32) + RESIDUAL * (
            total[:, :width] + ADAPT_SCALE * dot_nn(codes, out_b_ref[:RANK, :])
        )
        middle_ref[at, :] = mid
        codes_ref[at, :] = codes
        scale = lax.rsqrt(jnp.mean(mid * mid, axis=-1, keepdims=True) + NORM_EPS)
        normed = narrow(mid * scale * norm_ref[...])
        own_ref[at, :width] = normed
        own_ref[at, width:] = narrow(dot_nt(normed, lanes_ref[...]))

    middle, out_codes, x_own, w_ffn0, w_ffn1, g_all = remote_reduce(
        [head_out, w_out],
        [head_out.shape, w_out.shape],
        out_term,
        tensor_keys,
        [t_slow[::-1]],
        rows,
        aug,
        "reduce_out",
        3,
        riders=[ride_two(0, 2, cut_d, cut_c - cut_d)]
        + [ride_two(0, z, 0, cut_c) for z in range(3, z_count)]
        + [ride_two(0, z, cut_c, ffn_rows_each - cut_c) for z in range(1, z_count)]
        + [
            ride_one(1, 3, 4, cut_a, ffn_rows_each - cut_a),
            dict(
                kind="blocks",
                out=2,
                at=pair_rows,
                keys=list(range(0, n_t, 2)),
                step=t_core[0],
            ),
        ],
        ridden=[w_ffn0, w_ffn1, g_all],
        carried=[ffn_mine[1], ffn_other[1]],
        after=middle_work,
        after_in=[inputs[0], out_out_wide, feedforward_norm_gain[None], gu_in_lanes],
        after_out=[
            jax.ShapeDtypeStruct((rows, width), F32),
            jax.ShapeDtypeStruct((rows, RANK), BF16),
            jax.ShapeDtypeStruct((rows, aug), BF16),
        ],
    )

    def group_block_of(key, place):
        return group_block(
            jnp.bitwise_xor(place["dp"], key[0]), jnp.bitwise_xor(place["tensor"], key[1])
        )

    x_codes, grads, hids, ffn_weights = remote_ffn(
        x_own,
        g_all,
        [w_ffn0, w_ffn1],
        ffn_extra,
        mains,
        tail,
        tail_wide,
        t_slow + [("dp", pair)],
        group_block_of,
        [ride_two(1, z) for z in range(1, z_count)],
        "feed_forward",
        4,
    )
    group_keys = [(p, r) for p in (pair, 0) for r in reversed(range(0, n_t, 2))]
    ffn_in_sum, down_chip, *code_terms = remote_ffn_back(
        grads,
        hids,
        ffn_weights,
        ffn_extra,
        x_codes,
        g_all,
        mains,
        tail_wide,
        group_keys,
        [group_a[::-1], group_b[::-1]],
        group_block_of,
        rows,
        "feed_forward_back",
        5,
    )
    def grad_work(part, refs):
        at = slice(part * half_rows, (part + 1) * half_rows)
        sum_ref, mid_ref, cot_ref, norm_ref, gu_ref, out_ref = refs[0:6]
        middle_ref, codes_ref, aug_ref = refs[n_grad : n_grad + 3]
        lanes = sum_ref[at, width:]
        lanes = jnp.where(zl_of() == 0, lanes, pltpu.roll(lanes, CODE_LANES - 2 * RANK, 1))
        lane = lax.broadcasted_iota(jnp.int32, lanes.shape, 1)
        codes = narrow(jnp.where(lane < 2 * RANK, lanes, 0.0))
        codes_ref[at, :] = codes
        weighted = (sum_ref[at, :width] + dot_nn(codes, gu_ref[...])) * norm_ref[...]
        mid = mid_ref[at, :]
        scale = lax.rsqrt(jnp.mean(mid * mid, axis=-1, keepdims=True) + NORM_EPS)
        inner = jnp.mean(mid * weighted, axis=-1, keepdims=True)
        grad = cot_ref[at, :].astype(F32) + scale * weighted - mid * (scale * scale * scale * inner)
        middle_ref[at, :] = grad
        scaled = narrow(RESIDUAL * grad)
        aug_ref[at, :width] = scaled
        aug_ref[at, width:] = narrow(ADAPT_SCALE * dot_nt(scaled, out_ref[...]))

    def zl_of():
        return lax.rem(lax.axis_index("dp") // pair, 2)

    hidden_shape = (6 * RANK, half)

    def hidden_work(refs):
        gu_refs, down_refs = refs[6 : 6 + chunks], refs[6 + chunks : 6 + 2 * chunks]
        own_ref = refs[n_grad + 6]
        for kind, c, at, begin, count in chunk_places(mains, tail, tail_wide):
            for p in range(2):
                to = slice((3 * p + kind) * RANK, (3 * p + kind + 1) * RANK)
                if kind < 2:
                    top = 2 * RANK * p + kind * RANK
                    value = gu_refs[c][top : top + RANK, at : at + count] * ADAPT_SCALE
                else:
                    here = at - 2 * mains[c] - tails[c] if count == mains[c] else at
                    value = down_refs[c][2 * RANK * p : 2 * RANK * p + RANK, here : here + count]
                own_ref[to, begin : begin + count] = narrow(value)

    def dp_job(src, out):
        return dict(src=src, out=out, out_at=lambda dd, tt: (dd,), steps=outer_first)

    n_grad = 7 + 2 * chunks + (1 if n_t == 4 else 0)

    def heads_work(refs):
        w_ref, heads_ref, lanes_ref, all_ref = refs[6 + 2 * chunks], *refs[n_grad + 3 : n_grad + 6]
        for n in range(2):
            at = slice(n * length // 2, (n + 1) * length // 2)
            heads_ref[at, :] = narrow(dot_nn(all_ref[at, :], w_ref[...]))
        lanes_ref[...] = all_ref[:, width:]

    ride_down = n_t == 4
    n_far = 2 if ride_down else 1
    sent = remote_gather(
        [
            ffn_in_sum,
            middle,
            cotangent[0],
            feedforward_norm_gain[None],
            gu_in_wide,
            out_out_wide,
            *code_terms,
            w_out,
        ]
        + ([down_chip] if ride_down else []),
        token_jobs(n_grad + 2, n_far + 5, 2, "top")[:1]
        + token_jobs(n_grad + 2, n_far + 5, 2, "bottom")[1:]
        + [
            dict(
                src=n_grad + 6,
                out=0,
                out_at=rows_at(0, hidden_shape[0], hidden_shape[0]),
                steps=[("dp", high), ("dp", pair)],
                group="hidden",
            )
        ],
        [],
        [(n_dp * hidden_shape[0], half)] + ([(rows, aug)] if ride_down else []),
        "gather_grad",
        6,
        riders=[dict(kind="plain", src=n_grad - 1, src_at=0, out=1, step=("dp", pair))]
        if ride_down
        else [],
        distant=(n_grad - 1,) if ride_down else (),
        order=[
            hidden_work,
            "hidden",
            functools.partial(grad_work, 0),
            "top",
            "ride",
            functools.partial(grad_work, 1),
            "bottom",
            "hidden",
            "top",
            "bottom",
        ]
        + ["top", "bottom"] * (len(t_slow) - 1)
        + [("all", "top"), ("all", "bottom"), heads_work],
        near_outs=[
            jax.ShapeDtypeStruct((rows, width), F32),
            jax.ShapeDtypeStruct((rows, CODE_LANES), BF16),
            jax.ShapeDtypeStruct((rows, aug), BF16),
            jax.ShapeDtypeStruct((length, w_out.shape[1]), BF16),
            jax.ShapeDtypeStruct((length, CODE_LANES), BF16),
        ],
        scratch=[
            jax.ShapeDtypeStruct((length, aug), BF16),
            jax.ShapeDtypeStruct(hidden_shape, BF16),
        ],
    )
    middle_grad, gu_code_grad, attn_grad_aug, heads_grad, grad_lanes = sent[n_far:]
    gu_code_grad = gu_code_grad[:, : 2 * RANK]
    hidden_terms = sent[0]
    out_a = dot_tn(grad_lanes, head_out)[:RANK]
    hidden_ride = [
        dict(
            kind="two",
            out=0,
            z=z,
            count=hidden_shape[0],
            pair=pair,
            high=high,
            steps=[("dp", b) for b in reversed(low_bits)],
        )
        for z in range(z_count)
    ]
    if ride_down:
        down_far = narrow(down_chip[2].astype(F32) + sent[1].astype(F32))
        dq, dkv, pe_padded, cq, ckv, hidden_terms, came_pair, came_y = attend_back(
            q_aug,
            kv,
            head_out,
            heads_grad,
            rope,
            pe_aug,
            (lat_all, q_lat // CODE_LANES),
            [
                dict(kind="plain", src=1, src_at=1, out=1, step=("dp", pair)),
                dict(kind="plain", src=2, src_at=None, out=2, step=("tensor", 2)),
            ]
            + hidden_ride,
            [hidden_terms],
            [down_chip, down_far],
            [(rows, aug), (rows, aug)],
        )
    else:
        dq, dkv, pe_padded, cq, ckv, hidden_terms = attend_back(
            q_aug, kv, head_out, heads_grad, rope, pe_aug, (lat_all, q_lat // CODE_LANES), hidden_ride, [hidden_terms], [], []
        )
        places = n_t // 2
        ffn_out = down_chip[places:].astype(F32) + hop(down_chip[:places], ("dp", pair)).astype(F32)
        while places > 1:
            places //= 2
            ffn_out = ffn_out[places:] + hop(narrow(ffn_out[:places]), ("tensor", 2 * places)).astype(
                F32
            )
        ffn_out = ffn_out[0]
    def latent_term(held, place, key):
        at = token_rows(key, place)
        from_q = dot_nt(held[0][at, :], held[2][...])
        from_kv = dot_nt(held[1][at, :], held[3][...])
        return jnp.concatenate(
            [
                from_q[:, :q_lat],
                from_q[:, q_lat:] + from_kv[:, :CODE_LANES] + held[4][at, :],
                from_kv[:, CODE_LANES:],
            ],
            axis=1,
        )

    qb_b = ADAPT_SCALE * cq[:RANK]
    kvb_b = ADAPT_SCALE * ckv[RANK : 2 * RANK]
    head_own = narrow(jnp.concatenate([qb_b, kvb_b, out_a], axis=1))
    operands = [dq, dkv, w_q, w_kv, pe_padded]
    small_at, small_wide = [0], []
    for value in (q_lat, kv_all, q_lat, kv_lat):
        small_wide.append(value)
        small_at.append(small_at[-1] + -(-value // 128) * 128)

    def latent_back(at, total, extra, outs):
        latent_ref, q_norm, kv_norm, qb_ref, kvb_ref, b_ref, rows_ref, codes_ref = extra
        grad_ref, code_ref, terms_ref = outs
        block = total[:, q_lat : q_lat + CODE_LANES]
        lane = lax.broadcasted_iota(jnp.int32, block.shape, 1)
        codes = narrow(jnp.where(lane < 2 * RANK, block, 0.0))
        latent_f = latent_ref[...]
        parts = []
        inputs_in = []
        for begin, size, grad, norm_ref, in_ref in (
            (0, q_lat, total[:, :q_lat], q_norm, qb_ref),
            (q_lat, kv_lat, total[:, q_lat + CODE_LANES :], kv_norm, kvb_ref),
        ):
            value = latent_f[:, begin : begin + size]
            scale = lax.rsqrt(jnp.mean(value * value, axis=-1, keepdims=True) + NORM_EPS)
            inputs_in.append(narrow(value * scale * norm_ref[...]))
            weighted = (grad + dot_nn(codes, in_ref[...])) * norm_ref[...]
            inner = jnp.mean(value * weighted, axis=-1, keepdims=True)
            parts.append(scale * weighted - value * (scale * scale * scale * inner))
        grad_ref[:, :q_lat] = narrow(parts[0])
        grad_ref[:, q_lat : q_lat + kv_lat] = narrow(parts[1])
        pe_block = pltpu.roll(block, CODE_LANES - 2 * RANK, 1)
        pe_block = jnp.where(lane < ROTARY_DIM, pe_block, 0.0)
        grad_ref[:, q_lat + kv_lat :] = narrow(pe_block[:, : down_wide - q_lat - kv_lat])
        grad_rows = grad_ref[...]
        code_grad = narrow(ADAPT_SCALE * dot_nt(grad_rows, b_ref[...]))
        code_ref[...] = code_grad
        terms_ref[...] = jnp.zeros_like(terms_ref)
        terms_ref[: 2 * RANK, :] = narrow(dot_tn(code_grad, rows_ref[...]))
        b_terms = ADAPT_SCALE * dot_tn(codes_ref[...], grad_rows)
        qb_a = dot_tn(codes, inputs_in[0])
        kvb_a = dot_tn(codes, inputs_in[1])
        small_values = (
            b_terms[:RANK, :q_lat],
            b_terms[RANK:, q_lat : q_lat + kv_all],
            qb_a[:RANK, :],
            kvb_a[RANK : 2 * RANK, :],
        )
        for value, begin, size in zip(small_values, small_at, small_wide):
            terms_ref[2 * RANK :, begin : begin + size] = narrow(value)

    latent_grad, code_grad, late_terms, head_terms = remote_reduce(
        operands,
        [o.shape for o in operands],
        latent_term,
        tensor_keys,
        [t_slow[::-1]],
        rows,
        lat_wide,
        "reduce_latents",
        7,
        jobs=[dp_job(0, 0)],
        job_sources=[head_own],
        job_outs=[(n_dp,) + head_own.shape],
        after=latent_back,
        after_in=[
            latent,
            query_latent_gain[None],
            keyvalue_latent_gain[None],
            qb_in_wide,
            kvb_in_wide,
            down_b_rows,
            attn_rows,
            down_codes_in,
        ],
        after_out=[
            jax.ShapeDtypeStruct((rows, down_wide), BF16),
            jax.ShapeDtypeStruct((rows, 2 * RANK), BF16),
            jax.ShapeDtypeStruct((3 * RANK, width), BF16),
        ],
    )
    if ride_down:
        ffn_out = (
            down_chip[3].astype(F32)
            + came_pair.astype(F32)
            + came_y.astype(F32)
        )
    down_codes = narrow(own_codes(ffn_out)[:, :RANK])
    outputs = narrow(
        middle + RESIDUAL * (ffn_out[:, :width] + ADAPT_SCALE * dot_nn(down_codes, down_out))
    )
    gu_a = dot_tn(gu_code_grad, x_own)[:, :width]
    out_b = ADAPT_SCALE * dot_tn(out_codes, attn_grad_aug)[:, :width]
    down_b = ADAPT_SCALE * dot_tn(down_codes, g_own)[:, :width]
    table_orders = [outer_first + t_slow + t_core, t_slow + outer_first + t_core]
    shared = jnp.concatenate([narrow(gu_a), narrow(out_b), narrow(down_b), late_terms], axis=0)
    shared = jnp.pad(shared, ((0, -shared.shape[0] % (16 * n_t)), (0, 0)))

    def input_work(refs):
        grad_ref, code_ref, w_ref, in_ref, x_ref, norm_ref, mid_ref, out_ref = refs
        back = dot_nt(grad_ref[...], w_ref[...]) + dot_nn(code_ref[...], in_ref[...])
        value = x_ref[...].astype(F32)
        scale = lax.rsqrt(jnp.mean(value * value, axis=-1, keepdims=True) + NORM_EPS)
        weighted = back * norm_ref[...]
        inner = jnp.mean(value * weighted, axis=-1, keepdims=True)
        out_ref[...] = (
            mid_ref[...] + scale * weighted - value * (scale * scale * scale * inner)
        )

    shared_terms, input_grad = remote_share(
        shared,
        n_dp,
        n_t,
        table_orders,
        "share",
        8,
        [
            latent_grad,
            code_grad,
            w_down,
            down_in,
            inputs[0],
            attention_norm_gain[None],
            middle_grad,
        ],
        [jax.ShapeDtypeStruct((rows, width), F32)],
        input_work,
    )
    part_wide = width // 2

    def add_shared(s, refs, acc):
        for p in range(2):
            at = slice(p * part_wide, (p + 1) * part_wide)
            acc[:, at] += refs[0][p, s].astype(F32)

    def put_shared(acc, outs):
        outs[0][0, 0] = acc[:RANK, :]
        outs[0][1, 0] = acc[RANK : 2 * RANK, :]
        for n in range(4):
            outs[1 + n][0] = acc[(2 + n) * RANK : (3 + n) * RANK, :]
        for n, size in enumerate(small_wide):
            at = small_at[n]
            outs[5 + n][0] = acc[6 * RANK : 7 * RANK, at : at + size]

    shared_sets = set_sums(
        set_all,
        [shared_terms],
        (shared.shape[0], width),
        add_shared,
        [((2,), (RANK, width))]
        + [((), (RANK, width))] * 4
        + [((), (RANK, size)) for size in small_wide],
        put_shared,
        group_count,
        "sum_shared",
    )
    gu_a_t, out_b_grad, down_b_grad, qa_a_t, kva_a_t, qa_b_grad, kva_b_grad, qb_a_t, kvb_a_t = (
        shared_sets
    )
    wide = heads * HEAD_LANES
    head_wide = head_own.shape[1]

    def add_split(s, refs, acc):
        which = (s // pair) % 2
        base = s - which * pair
        for h in range(2):
            acc[: 3 * RANK, h * half : (h + 1) * half] += refs[0][
                base + h * pair, which * 3 * RANK : (which + 1) * 3 * RANK, :
            ].astype(F32)
        acc[3 * RANK :, :head_wide] += refs[1][s].astype(F32)

    def put_split(acc, outs):
        outs[0][0, 0] = acc[:RANK, :hidden]
        outs[0][1, 0] = acc[RANK : 2 * RANK, :hidden]
        outs[1][0] = acc[2 * RANK : 3 * RANK, :hidden]
        for h in range(heads):
            outs[2][0, :, h * head_q : (h + 1) * head_q] = acc[
                3 * RANK :, h * HEAD_LANES : h * HEAD_LANES + head_q
            ]
        outs[3][0] = acc[3 * RANK :, wide : 2 * wide]
        outs[4][0] = acc[3 * RANK :, 2 * wide : head_wide]

    gu_b_grad, down_a_t, qb_b_grad, kvb_b_grad, out_a_t = set_sums(
        set_all,
        [hidden_terms.reshape((n_dp,) + hidden_shape), head_terms],
        (4 * RANK, max(hidden, -(-head_wide // 128) * 128)),
        add_split,
        [
            ((2,), (RANK, hidden)),
            ((), (RANK, hidden)),
            ((), (RANK, heads * head_q)),
            ((), (RANK, wide)),
            ((), (RANK, head_wide - 2 * wide)),
        ],
        put_split,
        group_count,
        "sum_split",
    )
    return (
        outputs[None],
        input_grad[None],
        turned(qa_a_t),
        qa_b_grad,
        turned(kva_a_t),
        kva_b_grad,
        turned(qb_a_t),
        qb_b_grad,
        turned(kvb_a_t),
        kvb_b_grad,
        turned(out_a_t),
        out_b_grad,
        turned(gu_a_t),
        gu_b_grad,
        turned(down_a_t),
        down_b_grad,
    )


def solution(mesh):
    return jax.shard_map(
        functools.partial(per_device, mesh.shape["dp"], mesh.shape["tensor"]),
        mesh=mesh,
        in_specs=(
            P("dp", "tensor", None),
            P("dp", "tensor", None),
            P("dp", None),
            P("dp"),
            P(),
            P(),
            P(),
            P(),
            P("dp", None),
            P("dp", None),
            P("dp", "tensor"),
            P("dp", "tensor"),
            P("tensor", "dp"),
            P(None, "dp", "tensor"),
            P("tensor", "dp"),
            P(),
            P(),
            P(),
            P(),
            P(),
            P(None, None, "tensor"),
            P(),
            P(None, None, "tensor"),
            P(None, "tensor", None),
            P(),
            P(),
            P(None, None, None, "tensor"),
            P(None, "tensor", None),
            P(),
        ),
        out_specs=(
            P("dp", "tensor", None),
            P("dp", "tensor", None),
            P(),
            P(),
            P(),
            P(),
            P(),
            P(None, None, "tensor"),
            P(),
            P(None, None, "tensor"),
            P(None, "tensor", None),
            P(),
            P(),
            P(None, None, None, "tensor"),
            P(None, "tensor", None),
            P(),
        ),
        check_vma=False,
    )
```
